32 devices in a mesh: dp: 8 (over y, x, core), band: 4 (over z).
Axes of the slice: x: 2, y: 2, z: 4, core: 2. Of those that a mesh axis runs over, the one named last changes fastest.
Arguments:
- tokens: bfloat16 [16, 1024, 1152], P('dp', 'band'), may hold values from -6 to 6
- condition: bfloat16 [16, 1152], P('dp'), may hold values from -6 to 6
- patch_grid: int32 [16, 2], P('dp'), may hold values from 16 to 64, as said below
- ada_weight: bfloat16 [1152, 6912], P('band'), may hold values from -0.1875 to 0.1875
- ada_bias: bfloat16 [6912], P('band'), may hold values from -3 to 3
- qkv_weight: bfloat16 [1152, 3456], P('band'), may hold values from -0.25 to 0.25
- query_bias: bfloat16 [1152], P('band'), may hold values from -3 to 3
- value_bias: bfloat16 [1152], P('band'), may hold values from -3 to 3
- proj_weight: bfloat16 [1152, 1152], P('band'), may hold values from -0.75 to 0.75
- proj_bias: bfloat16 [1152], P('band'), may hold values from -2 to 2
- inner_weight: bfloat16 [1152, 4608], P('band'), may hold values from -0.1875 to 0.1875
- inner_bias: bfloat16 [4608], P('band'), may hold values from -3 to 3
- outer_weight: bfloat16 [4608, 1152], P('band'), may hold values from -0.09375 to 0.09375
- outer_bias: bfloat16 [1152], P('band'), may hold values from -2 to 2
- cotangent: bfloat16 [16, 1024, 1152], P('dp', 'band'), may hold values from -6 to 6
Outputs:
- block_out: bfloat16 [16, 1024, 1152], P('dp', 'band')
- grad_tokens: float32 [16, 1024, 1152], P('dp', 'band')
- grad_condition: float32 [16, 1152], P('dp')
- grad_ada_weight: float32 [1152, 6912], P('band')
- grad_ada_bias: float32 [6912], P('band')
- grad_qkv_weight: float32 [1152, 3456], P('band')
- grad_query_bias: float32 [1152], P('band')
- grad_value_bias: float32 [1152], P('band')
- grad_proj_weight: float32 [1152, 1152], P('band')
- grad_proj_bias: float32 [1152], P('band')
- grad_inner_weight: float32 [1152, 4608], P('band')
- grad_inner_bias: float32 [4608], P('band')
- grad_outer_weight: float32 [4608, 1152], P('band')
- grad_outer_bias: float32 [1152], P('band')
The draws below stay inside these ranges and needn't reach their ends.
Inputs may be any that keep to these rules, and one draw needn't show every extreme that they name: `patch_grid`: each image's grid is either 4 * 4 rows by 64 columns or 24 rows by 40 columns; each kind covers exactly half of the images, which ones is drawn.
All inputs are finite; a program needn't handle non-finite values.
Results may differ from the reference program's by a relative error of at most 0.02.
The reference program's roundings to bfloat16 on the way count: a program that leaves them out, or rounds other values in their place, can miss the bound.
Values may be sent and summed in bfloat16 or wider, within the bound.
A program may use at most 320 MiB of HBM per device.

```python
import jax
import jax.numpy as jnp
from jax import lax

D = 1152
HEADS = 16
HEAD_DIM = 72
FF = 4608
SLOTS = 1024
IMAGES = 16
BAND_SLOTS = 256
N_BAND = 4


def draw_patch_grid(key, part):
    key = jax.random.fold_in(key, 7)
    kinds = jax.random.permutation(key, IMAGES) % 2
    band_slots = SLOTS // N_BAND
    grid_rows = jnp.where(kinds == 0, 4 * N_BAND, 6 * N_BAND)
    grid_cols = jnp.where(kinds == 0, band_slots // 4, band_slots * 5 // 32)
    return jnp.stack([grid_rows, grid_cols], 1).astype(jnp.int32)


def shard_levels(own_key, shape, split, smallest, top_value):
    def one(position, shards_of):
        draws = jax.random.uniform(jax.random.fold_in(jax.random.fold_in(own_key, 6), position), (shards_of,), jnp.float32, smallest / len(split), top_value / len(split))
        return jnp.repeat(jnp.exp(draws), shape[position] // shards_of).reshape((-1,) + (1,) * (len(shape) - position - 1))

    gain = one(*split[0])
    for cut in split[1:]:
        gain = gain * one(*cut)
    return gain


def gaussian(own_key, shape, spread, most, split=(), held_as=jnp.bfloat16):
    values = jax.random.normal(own_key, shape, jnp.float32) * spread
    if len(split) > 0:
        values = shard_levels(own_key, shape, split, -0.22, 0.18) * values
    return jnp.clip(values, min=-most, max=most).astype(held_as)


def setup_inputs(seed: int = 0) -> dict:
    keys = jax.random.split(jax.random.key(seed), 16)
    return {
        "tokens": gaussian(keys[0], (IMAGES, SLOTS, D), 1.0, 6.0, ((0, 8), (1, 4))),
        "condition": gaussian(keys[1], (IMAGES, D), 1.0, 6.0, ((0, 8),)),
        "patch_grid": draw_patch_grid(jax.random.fold_in(keys[15], 71), 0),
        "ada_weight": gaussian(keys[3], (D, 6 * D), D ** -0.5, 0.1875, ((0, 4),)),
        "ada_bias": gaussian(keys[4], (6 * D,), 0.5, 3.0, ((0, 4),)),
        "qkv_weight": gaussian(keys[5], (D, 3 * D), (D // 2) ** -0.5, 0.25, ((0, 4),)),
        "query_bias": gaussian(keys[6], (D,), 0.5, 3.0, ((0, 4),)),
        "value_bias": gaussian(keys[7], (D,), 0.5, 3.0, ((0, 4),)),
        "proj_weight": gaussian(keys[8], (D, D), (D // 16) ** -0.5, 0.75, ((0, 4),)),
        "proj_bias": gaussian(keys[9], (D,), 0.3, 2.0, ((0, 4),)),
        "inner_weight": gaussian(keys[10], (D, FF), D ** -0.5, 0.1875, ((0, 4),)),
        "inner_bias": gaussian(keys[11], (FF,), 0.5, 3.0, ((0, 4),)),
        "outer_weight": gaussian(keys[12], (FF, D), FF ** -0.5, 0.09375, ((0, 4),)),
        "outer_bias": gaussian(keys[13], (D,), 0.3, 2.0, ((0, 4),)),
        "cotangent": gaussian(keys[14], (IMAGES, SLOTS, D), 1.0, 6.0, ((0, 8), (1, 4))),
    }


@jax.custom_vjp
def low(v):
    return lax.optimization_barrier(v.astype(jnp.bfloat16)).astype(jnp.float32)

@jax.custom_vjp
def low_back(v):
    return v

def low_keep(v):
    return (low(v), None)

def low_pass(kept, grad):
    return (grad,)

def back_keep(v):
    return (v, None)

def back_low(kept, grad):
    return (low(grad),)
low.defvjp(low_keep, low_pass)
low_back.defvjp(back_keep, back_low)

def matmul(operand, weights):
    return jnp.dot(operand, weights, precision=lax.Precision.HIGHEST)

def slot_layout(patch_grid, start, count, band_slots, band_count):
    slot_ids = start + jnp.arange(count, dtype=jnp.int32)
    band_ids = slot_ids // band_slots
    within = slot_ids % band_slots
    grid_rows = patch_grid[:, 0:1]
    grid_cols = patch_grid[:, 1:2]
    band_rows = grid_rows // band_count
    is_valid = within < band_rows * grid_cols
    row_index = band_ids * band_rows + within // grid_cols
    col_index = within % grid_cols
    return (row_index, col_index, is_valid)

def position_table(row_index, col_index, width):
    quarter = width // 4
    frequency = 10000.0 ** (-jnp.arange(quarter, dtype=jnp.float32) / quarter)
    rows_angle = row_index.astype(jnp.float32)[..., None] * frequency
    cols_angle = col_index.astype(jnp.float32)[..., None] * frequency
    return jnp.concatenate([jnp.sin(rows_angle), jnp.cos(rows_angle), jnp.sin(cols_angle), jnp.cos(cols_angle)], -1)

def normalize(values):
    average = lax.optimization_barrier(jnp.mean(values, -1, keepdims=True))
    centered = values - average
    variance = lax.optimization_barrier(jnp.mean(centered * centered, -1, keepdims=True))
    return centered * lax.rsqrt(variance + 1e-06)

def image_attention(packed):
    query_rows, key_rows, value_rows, key_valid = packed
    head_query = query_rows.reshape(SLOTS, HEADS, HEAD_DIM)
    head_key = key_rows.reshape(SLOTS, HEADS, HEAD_DIM)
    head_value = value_rows.reshape(SLOTS, HEADS, HEAD_DIM)
    scores = jnp.einsum('qhd,khd->hqk', head_query, head_key, precision=lax.Precision.HIGHEST) * HEAD_DIM ** (-0.5)
    scores = jnp.where(key_valid[None, None, :], low_back(scores), -1e+30)
    soft_weights = low(jax.nn.softmax(scores, axis=-1))
    mixed_rows = jnp.einsum('hqk,khd->qhd', soft_weights, head_value, precision=lax.Precision.HIGHEST)
    return mixed_rows.reshape(SLOTS, D)

def reference(tokens, condition, patch_grid, ada_weight, ada_bias, qkv_weight, query_bias, value_bias, proj_weight, proj_bias, inner_weight, inner_bias, outer_weight, outer_bias, cotangent):
    row_index, col_index, is_valid = slot_layout(patch_grid, 0, SLOTS, BAND_SLOTS, N_BAND)
    positions = position_table(row_index, col_index, D)

    def forward(tokens, condition, ada_weight, ada_bias, qkv_weight, query_bias, value_bias, proj_weight, proj_bias, inner_weight, inner_bias, outer_weight, outer_bias):
        activated = low(jax.nn.silu(condition))
        modulation = low_back(matmul(activated, ada_weight) + ada_bias)
        blocks = [modulation[:, None, block_index * D:(block_index + 1) * D] for block_index in range(6)]
        shift_one, scale_one, gate_one, shift_two, scale_two, gate_two = blocks
        residual = tokens + positions
        normed_one = normalize(residual)
        attn_in = low(normed_one * (1.0 + scale_one) + shift_one)
        projected = matmul(attn_in.reshape(-1, D), qkv_weight).reshape(IMAGES, SLOTS, 3 * D)
        query_rows = low_back(low(projected[..., :D] + query_bias))
        key_rows = low_back(low(projected[..., D:2 * D]))
        value_rows = low_back(low(projected[..., 2 * D:] + value_bias))
        mixed_rows = lax.map(jax.checkpoint(image_attention), (query_rows, key_rows, value_rows, is_valid))
        mixed_rows = low_back(low(mixed_rows))
        attended = low_back(matmul(mixed_rows.reshape(-1, D), proj_weight).reshape(IMAGES, SLOTS, D) + proj_bias)
        middle = residual + gate_one * attended
        normed_two = normalize(middle)
        mlp_in = low(normed_two * (1.0 + scale_two) + shift_two)
        hidden_pre = low_back(matmul(mlp_in.reshape(-1, D), inner_weight).reshape(IMAGES, SLOTS, FF) + inner_bias)
        hidden_act = low(jax.nn.gelu(hidden_pre, approximate=True))
        mlp_out = low_back(matmul(hidden_act.reshape(-1, FF), outer_weight).reshape(IMAGES, SLOTS, D) + outer_bias)
        return middle + gate_two * mlp_out
    arguments = tuple((member.astype(jnp.float32) for member in (tokens, condition, ada_weight, ada_bias, qkv_weight, query_bias, value_bias, proj_weight, proj_bias, inner_weight, inner_bias, outer_weight, outer_bias)))
    block_out, pullback = jax.vjp(forward, *arguments)
    grads = pullback(cotangent.astype(jnp.float32) * is_valid[..., None].astype(jnp.float32))
    return (block_out.astype(jnp.bfloat16), grads[0], grads[1], grads[2], grads[3], grads[4], grads[5], grads[6], grads[7], grads[8], grads[9], grads[10], grads[11], grads[12])
```

```python
import functools
from functools import partial

import jax
import jax.numpy as jnp
from jax import lax
from jax.experimental import pallas as pl
from jax.experimental.pallas import tpu as pltpu
from jax.sharding import PartitionSpec as P

HEAD_DIM = 72

MESH = pl.DeviceIdType.MESH
NB=4
def place():
    dp = lax.axis_index("dp"); band = lax.axis_index("band")
    return dp, band
def gather_kernel(width, qp_in, inner_in, outer_in, tok_in, cot_in, mod_in,
                  qp_out, inner_out, outer_out, tok_out, cot_out, mod_out,
                  z_send, z_recv, a_send, a_recv, b_send, b_recv, c_send, c_recv,
                  t_send, t_recv, m_send, m_recv, local_sem, h_sem, bq, bi, bo, bt):
    dp, band = place()
    core = lax.rem(dp, 2); px = lax.rem(dp // 2, 2); py = lax.rem(dp // 4, 2)
    base = dp - core
    kind = py * 2 + px
    sib = dp + 1 - 2 * core
    xdp = dp + 2 - 4 * px
    ydp = dp + 4 - 8 * py
    dev = lambda d, b: {"dp": d, "band": b}
    barrier = pltpu.get_barrier_semaphore()
    peers = [dev(xdp, band), dev(ydp, band), dev(sib, band)]
    for k in range(1, NB):
        ob = lax.rem(band + k, NB)
        peers += [dev(dp, ob), dev(sib, ob)]
    for q in peers:
        pl.semaphore_signal(barrier, inc=1, device_id=q, device_id_type=MESH)
    pl.semaphore_wait(barrier, len(peers))

    def rc(src, dst, ss, rs, to):
        return pltpu.make_async_remote_copy(src_ref=src, dst_ref=dst, send_sem=ss, recv_sem=rs, device_id=to, device_id_type=MESH)
    ins = (qp_in, inner_in, outer_in); outs = (qp_out, inner_out, outer_out)
    def cols(t, n=1):
        return pl.ds(pl.multiple_of(t * width, 128), n * width)
    def unit(ph, b, t, h):
        return outs[ph].at[b, t, h] if ph == 2 else outs[ph].at[b, h, :, cols(t)]
    def own(ph):
        return ins[ph].at[kind, core] if ph == 2 else ins[ph].at[core, :, cols(kind)]
    def pair(ph, b, h, y):
        return outs[ph].at[b, pl.ds(2 * y, 2), h] if ph == 2 else outs[ph].at[b, h, :, cols(2 * y, 2)]
    def row(ph, b, h):
        return outs[ph].at[b, :, h] if ph == 2 else outs[ph].at[b, h]
    sends = []
    def go(c):
        c.start(); sends.append(c)
    slot = lax.rem(band, 2)
    def move(which, src, dst):
        for i in range(2):
            to_core = band // 2; to_band = 2 * core + i
            home = jnp.logical_and(to_core == core, to_band == band)
            @pl.when(home)
            def _():
                pltpu.make_async_copy(src.at[i], bt.at[which], h_sem.at[which]).start()
                pltpu.make_async_copy(src.at[i], bt.at[which], h_sem.at[which]).wait()
                pltpu.make_async_copy(bt.at[which], dst.at[slot], t_recv.at[which, slot]).start()
            @pl.when(jnp.logical_not(home))
            def _():
                rc(src.at[i], dst.at[slot], t_send.at[which, i], t_recv.at[which, slot], dev(base + to_core, to_band)).start()
    def move_wait(which, src, dst):
        for i in range(2):
            to_core = band // 2; to_band = 2 * core + i
            home = jnp.logical_and(to_core == core, to_band == band)
            @pl.when(jnp.logical_not(home))
            def _():
                rc(src.at[i], dst.at[slot], t_send.at[which, i], t_recv.at[which, slot], dev(base + to_core, to_band)).wait_send()
        for s in range(2):
            pltpu.make_async_copy(src.at[s], dst.at[s], t_recv.at[which, s]).wait()
    def mods():
        for i in range(2):
            for c in range(2):
                home = jnp.logical_and(c == core, 2 * core + i == band)
                @pl.when(home)
                def _():
                    pltpu.make_async_copy(mod_in.at[i], mod_out.at[band], m_recv.at[band]).start()
                @pl.when(jnp.logical_not(home))
                def _():
                    rc(mod_in.at[i], mod_out.at[band], m_send.at[i, c], m_recv.at[band], dev(base + c, 2 * core + i)).start()
    def mods_wait():
        for i in range(2):
            for c in range(2):
                home = jnp.logical_and(c == core, 2 * core + i == band)
                @pl.when(jnp.logical_not(home))
                def _():
                    rc(mod_in.at[i], mod_out.at[band], m_send.at[i, c], m_recv.at[band], dev(base + c, 2 * core + i)).wait_send()
        for b in range(NB):
            pltpu.make_async_copy(mod_in.at[0], mod_out.at[b], m_recv.at[b]).wait()
    def zstart(ph):
        for k in (1, 3, 2):
            ob = lax.rem(band + k, NB)
            go(rc(own(ph), unit(ph, band, kind, core), z_send.at[ph, k], z_recv.at[ph, k], dev(dp, ob)))
    mods()
    move(0, tok_in, tok_out)
    zstart(0)
    bounce = (bq, bi, bo)
    for ph in range(3):
        pltpu.make_async_copy(ins[ph], bounce[ph], local_sem.at[ph]).start()
    for ph in range(3):
        pltpu.make_async_copy(ins[ph], bounce[ph], local_sem.at[ph]).wait()
        pltpu.make_async_copy(bounce[ph], outs[ph].at[band], local_sem.at[ph]).start()
    steps = [(ph, k) for ph in range(3) for k in (1, 3, 2)]
    n = len(steps)
    frm = lambda k: lax.rem(band + NB - k, NB)
    other = lambda v: 1 - v
    for s in range(n + 3):
        if s < n:
            ph, k = steps[s]; b = frm(k)
            u = unit(ph, b, kind, core)
            rc(u, u, z_send.at[ph, k], z_recv.at[ph, k], dev(dp, band)).wait_recv()
            go(rc(u, u, a_send.at[s], a_recv.at[s], dev(xdp if s % 2 == 0 else ydp, band)))
            if k == 3 and ph < 2:
                zstart(ph + 1)
            if k == 2 and ph == 2:
                move(1, cot_in, cot_out)
        r = s - 1
        if 0 <= r < n:
            ph, k = steps[r]; b = frm(k)
            got = py * 2 + other(px) if r % 2 == 0 else other(py) * 2 + px
            u = unit(ph, b, got, core)
            rc(u, u, a_send.at[r], a_recv.at[r], dev(xdp, band)).wait_recv()
            if r % 2 == 0:
                v = pair(ph, b, core, py)
                go(rc(v, v, b_send.at[r, 0], b_recv.at[r, 0], dev(ydp, band)))
            else:
                for j in range(2):
                    v = unit(ph, b, j * 2 + px, core)
                    go(rc(v, v, b_send.at[r, j], b_recv.at[r, j], dev(xdp, band)))
        r = s - 2
        if 0 <= r < n:
            ph, k = steps[r]; b = frm(k)
            if r % 2 == 0:
                v = pair(ph, b, core, other(py))
                rc(v, v, b_send.at[r, 0], b_recv.at[r, 0], dev(ydp, band)).wait_recv()
            else:
                for j in range(2):
                    v = unit(ph, b, j * 2 + other(px), core)
                    rc(v, v, b_send.at[r, j], b_recv.at[r, j], dev(xdp, band)).wait_recv()
            w = row(ph, b, core)
            go(rc(w, w, c_send.at[r], c_recv.at[r], dev(sib, band)))
        r = s - 3
        if 0 <= r < n:
            ph, k = steps[r]; b = frm(k)
            w = row(ph, b, other(core))
            rc(w, w, c_send.at[r], c_recv.at[r], dev(sib, band)).wait_recv()
    for ph in range(3):
        pltpu.make_async_copy(bounce[ph], outs[ph].at[band], local_sem.at[ph]).wait()
    mods_wait()
    move_wait(0, tok_in, tok_out)
    move_wait(1, cot_in, cot_out)
    for c in sends: c.wait_send()

def gather_weights(qp, inner, outer, tok, cot, mod, width):
    half = qp.shape[0] // 2
    ff = qp.shape[1]
    bf = jnp.bfloat16
    qp = qp.reshape(2, half, ff); inner = inner.reshape(2, half, ff); outer = outer.reshape(4, 2, half, width)
    D = pltpu.SemaphoreType.DMA
    outs = pl.pallas_call(
        functools.partial(gather_kernel, width),
        out_shape=[jax.ShapeDtypeStruct((NB,) + qp.shape, bf), jax.ShapeDtypeStruct((NB,) + inner.shape, bf),
                   jax.ShapeDtypeStruct((NB,) + outer.shape, bf),
                   jax.ShapeDtypeStruct(tok.shape, bf), jax.ShapeDtypeStruct(cot.shape, bf),
                   jax.ShapeDtypeStruct((NB,) + mod.shape[1:], jnp.float32)],
        in_specs=[pl.BlockSpec(memory_space=pl.ANY)] * 6,
        out_specs=[pl.BlockSpec(memory_space=pl.ANY)] * 6,
        scratch_shapes=[D((3, 4)), D((3, 4)), D((9,)), D((9,)), D((9, 2)), D((9, 2)), D((9,)), D((9,)),
                        D((2, 2)), D((2, 2)), D((2, 2)), D((4,)), D((3,)), D((2,)),
                        pltpu.VMEM(qp.shape, bf), pltpu.VMEM(inner.shape, bf), pltpu.VMEM(outer.shape, bf),
                        pltpu.VMEM((2,) + tok.shape[1:], bf)],
        compiler_params=pltpu.CompilerParams(collective_id=0, has_side_effects=True, vmem_limit_bytes=32*2**20),
        name="gather_weights",
    )(qp, inner, outer, tok, cot, mod)
    return outs


def normalize(values):
    average = jnp.mean(values, -1, keepdims=True)
    centered = values - average
    variance = jnp.mean(centered * centered, -1, keepdims=True)
    inverse = lax.rsqrt(variance + 1e-06)
    return (centered * inverse, inverse)


def norm_back(grad_normed, normed, inverse):
    first = jnp.mean(grad_normed, -1, keepdims=True)
    second = jnp.mean(grad_normed * normed, -1, keepdims=True)
    return inverse * (grad_normed - first - normed * second)


def contract(operand, grad_rows):
    return lax.dot_general(
        operand, grad_rows, (((0, 1), (0, 1)), ((), ())), preferred_element_type=jnp.float32
    )


def split_heads(rows):
    return rows.reshape(rows.shape[0], rows.shape[1], rows.shape[2] // HEAD_DIM, HEAD_DIM)


def score_block(query_rows, key_rows, key_valid):
    scores = jnp.einsum(
        "iqhd,ikhd->ihqk",
        split_heads(query_rows),
        split_heads(key_rows),
        preferred_element_type=jnp.float32,
    )
    scores = scores * HEAD_DIM ** (-0.5)
    return jnp.where(key_valid[:, None, None, :], scores, -1e30)


def attention_forward(query_rows, key_rows, value_rows, key_valid):
    scores = score_block(query_rows, key_rows, key_valid)
    row_top = jnp.max(scores, -1, keepdims=True)
    exponent = jnp.exp(scores - row_top)
    row_total = jnp.sum(exponent, -1, keepdims=True)
    soft_weights = (exponent / row_total).astype(jnp.bfloat16)
    mixed_rows = jnp.einsum(
        "ihqk,ikhd->iqhd", soft_weights, split_heads(value_rows), preferred_element_type=jnp.float32
    )
    return (
        mixed_rows.reshape(query_rows.shape[:2] + (value_rows.shape[2],)).astype(jnp.bfloat16),
        row_top + jnp.log(row_total),
    )


def attention_backward(query_rows, key_rows, value_rows, log_total, grad_mixed, key_valid):
    soft_weights = jnp.exp(score_block(query_rows, key_rows, key_valid) - log_total)
    grad_heads = split_heads(grad_mixed)
    grad_soft = jnp.einsum(
        "iqhd,ikhd->ihqk", grad_heads, split_heads(value_rows), preferred_element_type=jnp.float32
    )
    row_inner = jnp.sum(soft_weights * grad_soft, -1, keepdims=True)
    grad_scores = (soft_weights * (grad_soft - row_inner)).astype(jnp.bfloat16)
    score_scale = HEAD_DIM ** (-0.5)
    grad_query = score_scale * jnp.einsum(
        "ihqk,ikhd->iqhd", grad_scores, split_heads(key_rows), preferred_element_type=jnp.float32
    )
    grad_key = score_scale * jnp.einsum(
        "ihqk,iqhd->ikhd", grad_scores, split_heads(query_rows), preferred_element_type=jnp.float32
    )
    grad_value = jnp.einsum(
        "ihqk,iqhd->ikhd",
        soft_weights.astype(jnp.bfloat16),
        grad_heads,
        preferred_element_type=jnp.float32,
    )
    return (
        grad_query.reshape(query_rows.shape),
        grad_key.reshape(key_rows.shape),
        grad_value.reshape(value_rows.shape),
    )


def pair_perm(dp_count, band_count):
    return [
        (dp * band_count + band, (dp ^ 1) * band_count + band)
        for dp in range(dp_count)
        for band in range(band_count)
    ]


def home_perm_back(dp_count, band_count, turn):
    pairs = []
    for dp in range(dp_count):
        for band in range(band_count):
            to_dp = dp - dp % 2 + band // 2
            to_band = 2 * (dp % 2) + (band + turn) % 2
            pairs.append((dp * band_count + band, to_dp * band_count + to_band))
    return pairs


def send_home(rows, band, perms):
    odd = lax.rem(band, 2) == 1
    first = jnp.where(odd, rows[1], rows[0])
    second = jnp.where(odd, rows[0], rows[1])
    got = [lax.ppermute(part, ("dp", "band"), perm) for part, perm in zip((first, second), perms)]
    return jnp.stack([jnp.where(odd, got[1], got[0]), jnp.where(odd, got[0], got[1])])


def position_rows(row_index, col_index, width):
    quarter = width // 4
    frequency = 10000.0 ** (-jnp.arange(quarter, dtype=jnp.float32) / quarter)
    angles = jnp.arange(128, dtype=jnp.float32)[:, None] * frequency
    table = jnp.concatenate([jnp.sin(angles), jnp.cos(angles)], -1)
    places = jnp.arange(128, dtype=jnp.int32)
    pick = lambda index: jnp.dot(
        (index[:, None] == places).astype(jnp.float32), table, precision=lax.Precision.HIGHEST
    )
    return jnp.concatenate([pick(row_index), pick(col_index)], -1)


def rows_dot(left, right):
    return lax.dot_general(left, right, (((0,), (0,)), ((), ())), preferred_element_type=jnp.float32)


def back_dot(left, right):
    return lax.dot_general(left, right, (((1,), (1,)), ((), ())), preferred_element_type=jnp.float32)


def own_piece(vector, count, band_place):
    return lax.dynamic_slice_in_dim(vector, band_place * count, count, 0)


def body(
    tokens,
    condition,
    patch_grid,
    ada_weight,
    ada_bias,
    qkv_weight,
    query_bias,
    value_bias,
    proj_weight,
    proj_bias,
    inner_weight,
    inner_bias,
    outer_weight,
    outer_bias,
    cotangent,
):
    both = ("dp", "band")
    dp_count = lax.axis_size("dp")
    band_count = lax.axis_size("band")
    images, band_slots, width = tokens.shape
    band = lax.axis_index("band")
    dp = lax.axis_index("dp")
    core = lax.rem(dp, 2)
    hidden = inner_weight.shape[1]
    part_rows = qkv_weight.shape[0]
    siblings = pair_perm(dp_count, band_count)
    homes = [home_perm_back(dp_count, band_count, turn) for turn in range(2)]

    condition_f = condition.astype(jnp.float32)
    activated = jax.nn.silu(condition_f).astype(jnp.bfloat16)
    own_activated = lax.dynamic_slice_in_dim(activated, band * part_rows, part_rows, 1)
    share = jnp.dot(own_activated, ada_weight, preferred_element_type=jnp.float32)
    share = share + lax.dynamic_update_slice_in_dim(
        jnp.zeros((ada_weight.shape[1],), jnp.float32),
        ada_bias.astype(jnp.float32),
        band * ada_bias.shape[0],
        0,
    )
    biases = jnp.concatenate([query_bias, value_bias, proj_bias, inner_bias, outer_bias])
    bias_count = biases.shape[0]
    mod_count = share.shape[1]
    note = jnp.concatenate(
        [
            share,
            jnp.broadcast_to(biases.astype(jnp.float32), (images, bias_count)),
            patch_grid.astype(jnp.float32),
        ],
        1,
    )
    note_rows = -(-note.shape[1] // 1024) * 8
    note = jnp.pad(note, ((0, 0), (0, note_rows * 128 - note.shape[1])))
    note = note.reshape(images, note_rows, 128)
    first_weight = jnp.concatenate([qkv_weight, proj_weight], 1)
    first_full, inner_full, outer_full, tokens_here, cotangent_here, notes = gather_weights(
        first_weight, inner_weight, outer_weight, tokens, cotangent, note, width
    )
    first_full = first_full.reshape(width, -1)
    inner_full = inner_full.reshape(width, hidden)
    outer_full = outer_full.reshape(hidden, width)
    qkv_full = first_full[:, : 3 * width]
    proj_full = first_full[:, 3 * width :]
    notes = notes.reshape(band_count, -1)
    modulation = jnp.sum(notes[:, :mod_count], 0)
    pieces = []
    at = mod_count
    for piece in (query_bias, value_bias, proj_bias, inner_bias, outer_bias):
        pieces.append(notes[:, at : at + piece.shape[0]].reshape(-1))
        at += piece.shape[0]
    query_bias_full, value_bias_full, proj_bias_full, inner_bias_full, outer_bias_full = pieces
    grid_rows = notes[0, at].astype(jnp.int32)
    grid_cols = notes[0, at + 1].astype(jnp.int32)

    rows = images * band_slots
    ids = core * rows + jnp.arange(rows, dtype=jnp.int32)
    within = ids % band_slots
    band_rows = grid_rows // band_count
    is_valid = within < band_rows * grid_cols
    row_index = ids // band_slots * band_rows + within // grid_cols
    col_index = within % grid_cols
    key_valid = jnp.concatenate([is_valid, is_valid])

    shift_one, scale_one, gate_one, shift_two, scale_two, gate_two = [
        modulation[index * width : (index + 1) * width] for index in range(6)
    ]
    residual = tokens_here.reshape(rows, width).astype(jnp.float32) + position_rows(
        row_index, col_index, width
    )
    normed_one, inverse_one = normalize(residual)
    attn_in = (normed_one * (1.0 + scale_one) + shift_one).astype(jnp.bfloat16)
    projected = jnp.dot(attn_in, qkv_full, preferred_element_type=jnp.float32)
    query_rows = (projected[:, :width] + query_bias_full).astype(jnp.bfloat16)
    key_value = (
        projected[:, width:] + jnp.concatenate([jnp.zeros((width,), jnp.float32), value_bias_full])
    ).astype(jnp.bfloat16)
    other_key_value = lax.ppermute(key_value, both, siblings)
    keys = jnp.concatenate([key_value[:, :width], other_key_value[:, :width]])
    values = jnp.concatenate([key_value[:, width:], other_key_value[:, width:]])
    mixed_rows, band_total = attention_forward(
        query_rows[None], keys[None], values[None], key_valid[None]
    )
    mixed_rows = mixed_rows[0]
    attended = jnp.dot(mixed_rows, proj_full, preferred_element_type=jnp.float32) + proj_bias_full
    middle = residual + gate_one * attended
    normed_two, inverse_two = normalize(middle)
    mlp_in = (normed_two * (1.0 + scale_two) + shift_two).astype(jnp.bfloat16)
    hidden_pre = jnp.dot(mlp_in, inner_full, preferred_element_type=jnp.float32) + inner_bias_full
    hidden_act = jax.nn.gelu(hidden_pre, approximate=True).astype(jnp.bfloat16)
    mlp_out = jnp.dot(hidden_act, outer_full, preferred_element_type=jnp.float32) + outer_bias_full
    block_out = (middle + gate_two * mlp_out).astype(jnp.bfloat16)
    block_home = send_home(block_out.reshape(images, band_slots, width), band, homes)

    grad_out = cotangent_here.reshape(rows, width).astype(jnp.float32) * is_valid[:, None].astype(
        jnp.float32
    )
    grad_gate_two = jnp.sum(grad_out * mlp_out, 0)
    grad_mlp = (gate_two * grad_out).astype(jnp.bfloat16)
    gelu_back = jax.vjp(partial(jax.nn.gelu, approximate=True), hidden_pre)[1]
    grad_outer = rows_dot(hidden_act, grad_mlp).astype(jnp.bfloat16)
    grad_outer_bias = jnp.sum(grad_mlp.astype(jnp.float32), 0)
    grad_hidden = back_dot(grad_mlp, outer_full)
    grad_pre = gelu_back(grad_hidden)[0].astype(jnp.bfloat16)
    grad_inner = rows_dot(mlp_in, grad_pre).astype(jnp.bfloat16)
    grad_inner_bias = jnp.sum(grad_pre.astype(jnp.float32), 0)
    grad_mlp_in = back_dot(grad_pre, inner_full)
    grad_shift_two = jnp.sum(grad_mlp_in, 0)
    grad_scale_two = jnp.sum(grad_mlp_in * normed_two, 0)
    grad_middle = grad_out + norm_back(grad_mlp_in * (1.0 + scale_two), normed_two, inverse_two)
    grad_gate_one = jnp.sum(grad_middle * attended, 0)
    grad_attended = (gate_one * grad_middle).astype(jnp.bfloat16)
    grad_proj = rows_dot(mixed_rows, grad_attended).astype(jnp.bfloat16)
    grad_proj_bias = jnp.sum(grad_attended.astype(jnp.float32), 0)
    grad_mixed = back_dot(grad_attended, proj_full).astype(jnp.bfloat16)
    band_dq, key_terms, value_terms = attention_backward(
        query_rows[None], keys[None], values[None], band_total, grad_mixed[None], key_valid[None]
    )
    terms = jnp.concatenate([key_terms[0], value_terms[0]], -1)
    other_terms = lax.ppermute(terms[rows:].astype(jnp.bfloat16), both, siblings)
    grad_key_value = (terms[:rows] + other_terms.astype(jnp.float32)).astype(jnp.bfloat16)
    grad_query = band_dq[0].astype(jnp.bfloat16)
    grad_qkv = jnp.concatenate([grad_query, grad_key_value], -1)
    grad_qkv_weight = rows_dot(attn_in, grad_qkv).astype(jnp.bfloat16)
    grad_attn_in = back_dot(grad_qkv, qkv_full)
    grad_query_bias = jnp.sum(grad_query.astype(jnp.float32), 0)
    grad_value_bias = jnp.sum(grad_key_value[:, width:].astype(jnp.float32), 0)
    grad_shift_one = jnp.sum(grad_attn_in, 0)
    grad_scale_one = jnp.sum(grad_attn_in * normed_one, 0)
    grad_tokens = grad_middle + norm_back(grad_attn_in * (1.0 + scale_one), normed_one, inverse_one)
    tokens_home = send_home(
        grad_tokens.astype(jnp.bfloat16).reshape(images, band_slots, width), band, homes
    ).astype(jnp.float32)

    part_mod = jnp.concatenate(
        [grad_shift_one, grad_scale_one, grad_gate_one, grad_shift_two, grad_scale_two, grad_gate_two]
    )
    grad_mod = (part_mod + lax.ppermute(part_mod, both, siblings)).astype(jnp.bfloat16)
    every_mod = lax.all_gather(grad_mod, both, axis=0).reshape(dp_count // 2, 2, band_count, -1)
    every_mod = every_mod[:, 0].reshape(dp_count * images, -1)
    every_activated = lax.all_gather(own_activated, "dp", axis=0, tiled=True)
    grad_ada = rows_dot(every_activated, every_mod)
    grad_ada_bias = own_piece(jnp.sum(every_mod.astype(jnp.float32), 0), ada_bias.shape[0], band)
    own_mod = lax.dynamic_slice_in_dim(every_mod, images * dp, images, 0)
    grad_act = lax.all_gather(back_dot(own_mod, ada_weight), "band", axis=1, tiled=True)
    grad_condition = jax.vjp(jax.nn.silu, condition_f)[1](grad_act)[0]

    def total(piece):
        scattered = lax.psum_scatter(piece, ("band", "dp"), scatter_dimension=0, tiled=True)
        return lax.all_gather(scattered, "dp", axis=0, tiled=True).astype(jnp.float32)

    bias_grads = lax.psum(
        jnp.concatenate(
            [grad_query_bias, grad_value_bias, grad_proj_bias, grad_inner_bias, grad_outer_bias]
        ),
        both,
    )
    bias_parts = []
    at = 0
    for piece in (query_bias, value_bias, proj_bias, inner_bias, outer_bias):
        whole = piece.shape[0] * band_count
        bias_parts.append(own_piece(bias_grads[at : at + whole], piece.shape[0], band))
        at += whole
    return (
        block_home,
        tokens_home,
        grad_condition,
        grad_ada,
        grad_ada_bias,
        total(grad_qkv_weight),
        bias_parts[0],
        bias_parts[1],
        total(grad_proj),
        bias_parts[2],
        total(grad_inner),
        bias_parts[3],
        total(grad_outer),
        bias_parts[4],
    )


def solution(mesh):
    placed = (
        P("dp", "band", None),
        P("dp", None),
        P("dp", None),
        P("band", None),
        P("band"),
        P("band", None),
        P("band"),
        P("band"),
        P("band", None),
        P("band"),
        P("band", None),
        P("band"),
        P("band", None),
        P("band"),
        P("dp", "band", None),
    )
    return jax.shard_map(
        body,
        mesh=mesh,
        in_specs=placed,
        out_specs=(
            P("dp", "band", None),
            P("dp", "band", None),
            P("dp", None),
            P("band", None),
            P("band"),
            P("band", None),
            P("band"),
            P("band"),
            P("band", None),
            P("band"),
            P("band", None),
            P("band"),
            P("band", None),
            P("band"),
        ),
        check_vma=False,
    )
```

```python
import functools
from functools import partial

import jax
import jax.numpy as jnp
from jax import lax
from jax.experimental import pallas as pl
from jax.experimental.pallas import tpu as pltpu
from jax.sharding import PartitionSpec as P

HEAD_DIM = 72

MESH = pl.DeviceIdType.MESH
NB=4
def place():
    dp = lax.axis_index("dp"); band = lax.axis_index("band")
    return dp, band
def gather_kernel(width, qp_in, inner_in, outer_in, tok_in, cot_in, mod_in,
                  qp_out, inner_out, outer_out, tok_out, cot_out, mod_out,
                  z_send, z_recv, a_send, a_recv, b_send, b_recv, c_send, c_recv,
                  t_send, t_recv, m_send, m_recv, local_sem, h_sem, bq, bi, bo, bt):
    dp, band = place()
    core = lax.rem(dp, 2); px = lax.rem(dp // 2, 2); py = lax.rem(dp // 4, 2)
    base = dp - core
    kind = py * 2 + px
    sib = dp + 1 - 2 * core
    xdp = dp + 2 - 4 * px
    ydp = dp + 4 - 8 * py
    dev = lambda d, b: {"dp": d, "band": b}
    barrier = pltpu.get_barrier_semaphore()
    peers = [dev(xdp, band), dev(ydp, band), dev(sib, band)]
    for k in range(1, NB):
        ob = lax.rem(band + k, NB)
        peers += [dev(dp, ob), dev(sib, ob)]
    for q in peers:
        pl.semaphore_signal(barrier, inc=1, device_id=q, device_id_type=MESH)
    pl.semaphore_wait(barrier, len(peers))

    def rc(src, dst, ss, rs, to):
        return pltpu.make_async_remote_copy(src_ref=src, dst_ref=dst, send_sem=ss, recv_sem=rs, device_id=to, device_id_type=MESH)
    ins = (qp_in, inner_in, outer_in); outs = (qp_out, inner_out, outer_out)
    def cols(t, n=1):
        return pl.ds(pl.multiple_of(t * width, 128), n * width)
    def unit(ph, b, t, h):
        return outs[ph].at[b, t, h] if ph == 2 else outs[ph].at[b, h, :, cols(t)]
    def own(ph):
        return ins[ph].at[kind, core] if ph == 2 else ins[ph].at[core, :, cols(kind)]
    def pair(ph, b, h, y):
        return outs[ph].at[b, pl.ds(2 * y, 2), h] if ph == 2 else outs[ph].at[b, h, :, cols(2 * y, 2)]
    def row(ph, b, h):
        return outs[ph].at[b, :, h] if ph == 2 else outs[ph].at[b, h]
    sends = []
    def go(c):
        c.start(); sends.append(c)
    slot = lax.rem(band, 2)
    def move(which, src, dst):
        for i in range(2):
            to_core = band // 2; to_band = 2 * core + i
            home = jnp.logical_and(to_core == core, to_band == band)
            @pl.when(home)
            def _():
                pltpu.make_async_copy(src.at[i], bt.at[which], h_sem.at[which]).start()
                pltpu.make_async_copy(src.at[i], bt.at[which], h_sem.at[which]).wait()
                pltpu.make_async_copy(bt.at[which], dst.at[slot], t_recv.at[which, slot]).start()
            @pl.when(jnp.logical_not(home))
            def _():
                rc(src.at[i], dst.at[slot], t_send.at[which, i], t_recv.at[which, slot], dev(base + to_core, to_band)).start()
    def move_wait(which, src, dst):
        for i in range(2):
            to_core = band // 2; to_band = 2 * core + i
            home = jnp.logical_and(to_core == core, to_band == band)
            @pl.when(jnp.logical_not(home))
            def _():
                rc(src.at[i], dst.at[slot], t_send.at[which, i], t_recv.at[which, slot], dev(base + to_core, to_band)).wait_send()
        for s in range(2):
            pltpu.make_async_copy(src.at[s], dst.at[s], t_recv.at[which, s]).wait()
    def mods():
        for i in range(2):
            for c in range(2):
                home = jnp.logical_and(c == core, 2 * core + i == band)
                @pl.when(home)
                def _():
                    pltpu.make_async_copy(mod_in.at[i], mod_out.at[band], m_recv.at[band]).start()
                @pl.when(jnp.logical_not(home))
                def _():
                    rc(mod_in.at[i], mod_out.at[band], m_send.at[i, c], m_recv.at[band], dev(base + c, 2 * core + i)).start()
    def mods_wait():
        for i in range(2):
            for c in range(2):
                home = jnp.logical_and(c == core, 2 * core + i == band)
                @pl.when(jnp.logical_not(home))
                def _():
                    rc(mod_in.at[i], mod_out.at[band], m_send.at[i, c], m_recv.at[band], dev(base + c, 2 * core + i)).wait_send()
        for b in range(NB):
            pltpu.make_async_copy(mod_in.at[0], mod_out.at[b], m_recv.at[b]).wait()
    def zstart(ph):
        for k in (1, 3, 2):
            ob = lax.rem(band + k, NB)
            go(rc(own(ph), unit(ph, band, kind, core), z_send.at[ph, k], z_recv.at[ph, k], dev(dp, ob)))
    mods()
    move(0, tok_in, tok_out)
    zstart(0)
    bounce = (bq, bi, bo)
    for ph in range(3):
        pltpu.make_async_copy(ins[ph], bounce[ph], local_sem.at[ph]).start()
    for ph in range(3):
        pltpu.make_async_copy(ins[ph], bounce[ph], local_sem.at[ph]).wait()
        pltpu.make_async_copy(bounce[ph], outs[ph].at[band], local_sem.at[ph]).start()
    steps = [(ph, k) for ph in range(3) for k in (1, 3, 2)]
    n = len(steps)
    frm = lambda k: lax.rem(band + NB - k, NB)
    other = lambda v: 1 - v
    for s in range(n + 3):
        if s < n:
            ph, k = steps[s]; b = frm(k)
            u = unit(ph, b, kind, core)
            rc(u, u, z_send.at[ph, k], z_recv.at[ph, k], dev(dp, band)).wait_recv()
            go(rc(u, u, a_send.at[s], a_recv.at[s], dev(xdp if s % 2 == 0 else ydp, band)))
            if k == 3 and ph < 2:
                zstart(ph + 1)
            if k == 2 and ph == 2:
                move(1, cot_in, cot_out)
        r = s - 1
        if 0 <= r < n:
            ph, k = steps[r]; b = frm(k)
            got = py * 2 + other(px) if r % 2 == 0 else other(py) * 2 + px
            u = unit(ph, b, got, core)
            rc(u, u, a_send.at[r], a_recv.at[r], dev(xdp, band)).wait_recv()
            if r % 2 == 0:
                v = pair(ph, b, core, py)
                go(rc(v, v, b_send.at[r, 0], b_recv.at[r, 0], dev(ydp, band)))
            else:
                for j in range(2):
                    v = unit(ph, b, j * 2 + px, core)
                    go(rc(v, v, b_send.at[r, j], b_recv.at[r, j], dev(xdp, band)))
        r = s - 2
        if 0 <= r < n:
            ph, k = steps[r]; b = frm(k)
            if r % 2 == 0:
                v = pair(ph, b, core, other(py))
                rc(v, v, b_send.at[r, 0], b_recv.at[r, 0], dev(ydp, band)).wait_recv()
            else:
                for j in range(2):
                    v = unit(ph, b, j * 2 + other(px), core)
                    rc(v, v, b_send.at[r, j], b_recv.at[r, j], dev(xdp, band)).wait_recv()
            w = row(ph, b, core)
            go(rc(w, w, c_send.at[r], c_recv.at[r], dev(sib, band)))
        r = s - 3
        if 0 <= r < n:
            ph, k = steps[r]; b = frm(k)
            w = row(ph, b, other(core))
            rc(w, w, c_send.at[r], c_recv.at[r], dev(sib, band)).wait_recv()
    for ph in range(3):
        pltpu.make_async_copy(bounce[ph], outs[ph].at[band], local_sem.at[ph]).wait()
    mods_wait()
    move_wait(0, tok_in, tok_out)
    move_wait(1, cot_in, cot_out)
    for c in sends: c.wait_send()

def gather_weights(qp, inner, outer, tok, cot, mod, width):
    half = qp.shape[0] // 2
    ff = qp.shape[1]
    bf = jnp.bfloat16
    qp = qp.reshape(2, half, ff); inner = inner.reshape(2, half, ff); outer = outer.reshape(4, 2, half, width)
    D = pltpu.SemaphoreType.DMA
    outs = pl.pallas_call(
        functools.partial(gather_kernel, width),
        out_shape=[jax.ShapeDtypeStruct((NB,) + qp.shape, bf), jax.ShapeDtypeStruct((NB,) + inner.shape, bf),
                   jax.ShapeDtypeStruct((NB,) + outer.shape, bf),
                   jax.ShapeDtypeStruct(tok.shape, bf), jax.ShapeDtypeStruct(cot.shape, bf),
                   jax.ShapeDtypeStruct((NB,) + mod.shape[1:], jnp.float32)],
        in_specs=[pl.BlockSpec(memory_space=pl.ANY)] * 6,
        out_specs=[pl.BlockSpec(memory_space=pl.ANY)] * 6,
        scratch_shapes=[D((3, 4)), D((3, 4)), D((9,)), D((9,)), D((9, 2)), D((9, 2)), D((9,)), D((9,)),
                        D((2, 2)), D((2, 2)), D((2, 2)), D((4,)), D((3,)), D((2,)),
                        pltpu.VMEM(qp.shape, bf), pltpu.VMEM(inner.shape, bf), pltpu.VMEM(outer.shape, bf),
                        pltpu.VMEM((2,) + tok.shape[1:], bf)],
        compiler_params=pltpu.CompilerParams(collective_id=0, has_side_effects=True, vmem_limit_bytes=32*2**20),
        name="gather_weights",
    )(qp, inner, outer, tok, cot, mod)
    return outs


LANES = 128
PACK_ROWS = 128


def pack_heads(source, first, heads_ref, row0, rows, tail):
    heads = heads_ref.shape[0]

    @pl.loop(0, rows // PACK_ROWS)
    def _(step):
        at = pl.multiple_of(step * PACK_ROWS, PACK_ROWS)
        block = source[pl.ds(at, PACK_ROWS), first : first + heads * HEAD_DIM]
        end = tail(at)
        for h in range(heads):
            part = block[:, h * HEAD_DIM : (h + 1) * HEAD_DIM]
            heads_ref[h, pl.ds(row0 + at, PACK_ROWS), :] = jnp.concatenate([part, end], 1)


def unpack_heads(heads_ref, row0, rows, target, first):
    heads = heads_ref.shape[0]

    @pl.loop(0, rows // PACK_ROWS)
    def _(step):
        at = pl.multiple_of(step * PACK_ROWS, PACK_ROWS)
        parts = [heads_ref[h, pl.ds(row0 + at, PACK_ROWS), :][:, :HEAD_DIM] for h in range(heads)]
        target[pl.ds(at, PACK_ROWS), first : first + heads * HEAD_DIM] = jnp.concatenate(parts, 1)


def flat_tail(value):
    def tail(at):
        lane = lax.broadcasted_iota(jnp.int32, (PACK_ROWS, LANES - HEAD_DIM), 1)
        return jnp.where(lane == 0, value, 0.0).astype(jnp.bfloat16)

    return tail


def key_tail(valid_count, band_slots):
    def tail(at):
        shape = (PACK_ROWS, LANES - HEAD_DIM)
        lane = lax.broadcasted_iota(jnp.int32, shape, 1)
        slot = lax.rem(at + lax.broadcasted_iota(jnp.int32, shape, 0), band_slots)
        return jnp.where(jnp.logical_and(lane == 0, slot >= valid_count), -1e30, 0.0).astype(jnp.bfloat16)

    return tail


def lanes_dot(left, right):
    return lax.dot_general(left, right, (((1,), (1,)), ((), ())), preferred_element_type=jnp.float32)


def rows_dot(left, right):
    return lax.dot_general(left, right, (((0,), (0,)), ((), ())), preferred_element_type=jnp.float32)


SCORE_SCALE = HEAD_DIM ** (-0.5)


def attend_kernel(band_slots, count_ref, q_ref, own_ref, far_ref, out_ref, top_ref, qh, kh, vh):
    rows, width = q_ref.shape
    heads = qh.shape[0]
    pack_heads(q_ref, 0, qh, 0, rows, flat_tail(1.0))
    for row0, ref in ((0, own_ref), (rows, far_ref)):
        pack_heads(ref, 0, kh, row0, rows, key_tail(count_ref[0], band_slots))
        pack_heads(ref, width, vh, row0, rows, flat_tail(0.0))

    @pl.loop(0, heads)
    def _(h):
        for block in range(2):
            at = pl.ds(block * rows // 2, rows // 2)
            scores = lanes_dot(kh[h], qh[h, at, :]) * SCORE_SCALE
            top = jnp.max(scores, 0, keepdims=True)
            weights = jnp.exp(scores - top)
            total = jnp.sum(weights, 0, keepdims=True)
            low = (weights * (1.0 / total)).astype(jnp.bfloat16)
            mixed = rows_dot(vh[h], low)
            qh[h, at, :] = jnp.transpose(mixed).astype(jnp.bfloat16)
            top_ref[h, :, at] = jnp.broadcast_to(top + jnp.log(total), (8, rows // 2))

    unpack_heads(qh, 0, rows, out_ref, 0)


def attend(count, query, own, far, band_slots):
    rows, width = query.shape
    heads = width // HEAD_DIM
    bf = jnp.bfloat16
    vmem = pl.BlockSpec(memory_space=pltpu.VMEM)
    return pl.pallas_call(
        partial(attend_kernel, band_slots),
        out_shape=[
            jax.ShapeDtypeStruct((rows, width), bf),
            jax.ShapeDtypeStruct((heads, 8, rows), jnp.float32),
        ],
        in_specs=[pl.BlockSpec(memory_space=pltpu.SMEM), vmem, vmem, vmem],
        out_specs=[vmem, vmem],
        scratch_shapes=[
            pltpu.VMEM((heads, rows, LANES), bf),
            pltpu.VMEM((heads, 2 * rows, LANES), bf),
            pltpu.VMEM((heads, 2 * rows, LANES), bf),
        ],
        compiler_params=pltpu.CompilerParams(vmem_limit_bytes=48 * 2**20),
        cost_estimate=pl.CostEstimate(
            flops=8 * rows * rows * width, bytes_accessed=16 * rows * width, transcendentals=2 * heads * rows * rows
        ),
        name="attend",
    )(count, query, own, far)


def attend_head(h, qh, kh, vh, gh, top_ref):
    query = qh[h]
    key = kh[h]
    grad = gh[h]
    probs = jnp.exp(lanes_dot(key, query) * SCORE_SCALE - top_ref[h, 0:1, :])
    grad_probs = lanes_dot(vh[h], grad)
    inner = jnp.sum(probs * grad_probs, 0, keepdims=True)
    grad_scores = (probs * (grad_probs - inner)).astype(jnp.bfloat16)
    vh[h] = jnp.dot(
        probs.astype(jnp.bfloat16), grad, preferred_element_type=jnp.float32
    ).astype(jnp.bfloat16)
    grad_query = rows_dot(key, grad_scores)
    kh[h] = (
        SCORE_SCALE * jnp.dot(grad_scores, query, preferred_element_type=jnp.float32)
    ).astype(jnp.bfloat16)
    qh[h] = (SCORE_SCALE * jnp.transpose(grad_query)).astype(jnp.bfloat16)


def attend_back_kernel(band_slots, count_ref, q_ref, own_ref, far_ref, grad_ref, top_ref,
                       dq_ref, down_ref, dfar_ref, qh, kh, vh, gh):
    rows, width = q_ref.shape
    heads = qh.shape[0]
    pack_heads(q_ref, 0, qh, 0, rows, flat_tail(1.0))
    pack_heads(grad_ref, 0, gh, 0, rows, flat_tail(0.0))
    for row0, ref in ((0, own_ref), (rows, far_ref)):
        pack_heads(ref, 0, kh, row0, rows, key_tail(count_ref[0], band_slots))
        pack_heads(ref, width, vh, row0, rows, flat_tail(0.0))

    @pl.loop(0, heads)
    def _(h):
        attend_head(h, qh, kh, vh, gh, top_ref)

    unpack_heads(qh, 0, rows, dq_ref, 0)
    for row0, ref in ((0, down_ref), (rows, dfar_ref)):
        unpack_heads(kh, row0, rows, ref, 0)
        unpack_heads(vh, row0, rows, ref, width)


def attend_back(count, query, own, far, grad, top, band_slots):
    rows, width = query.shape
    heads = width // HEAD_DIM
    bf = jnp.bfloat16
    vmem = pl.BlockSpec(memory_space=pltpu.VMEM)
    return pl.pallas_call(
        partial(attend_back_kernel, band_slots),
        out_shape=[
            jax.ShapeDtypeStruct((rows, width), bf),
            jax.ShapeDtypeStruct((rows, 2 * width), bf),
            jax.ShapeDtypeStruct((rows, 2 * width), bf),
        ],
        in_specs=[pl.BlockSpec(memory_space=pltpu.SMEM)] + [vmem] * 5,
        out_specs=[vmem] * 3,
        scratch_shapes=[
            pltpu.VMEM((heads, rows, LANES), bf),
            pltpu.VMEM((heads, 2 * rows, LANES), bf),
            pltpu.VMEM((heads, 2 * rows, LANES), bf),
            pltpu.VMEM((heads, rows, LANES), bf),
        ],
        compiler_params=pltpu.CompilerParams(vmem_limit_bytes=56 * 2**20),
        cost_estimate=pl.CostEstimate(
            flops=20 * rows * rows * width, bytes_accessed=32 * rows * width, transcendentals=2 * heads * rows * rows
        ),
        name="attend_back",
    )(count, query, own, far, grad, top)


def compass():
    dp = lax.axis_index("dp")
    band = lax.axis_index("band")
    core = lax.rem(dp, 2)
    px = lax.rem(dp // 2, 2)
    py = lax.rem(dp // 4, 2)
    return dict(
        dp=dp, band=band, core=core, px=px, py=py, kind=2 * py + px,
        sib=dp + 1 - 2 * core, xdp=dp + 2 - 4 * px, ydp=dp + 4 - 8 * py,
    )


def add_rows(total, term):
    rows = total.shape[0]

    @pl.loop(0, rows // 16)
    def _(step):
        at = pl.ds(pl.multiple_of(step * 16, 16), 16)
        total[at, :] = (
            total[at, :].astype(jnp.float32) + term[at, :].astype(jnp.float32)
        ).astype(jnp.bfloat16)


def reduce_barrier(me):
    barrier = pltpu.get_barrier_semaphore()
    peers = [(me["xdp"], me["band"]), (me["ydp"], me["band"]), (me["sib"], me["band"])]
    peers += [(me["dp"], lax.rem(me["band"] + k, NB)) for k in range(1, NB)]
    for dp, band in peers:
        pl.semaphore_signal(
            barrier, inc=1, device_id={"dp": dp, "band": band}, device_id_type=MESH
        )
    pl.semaphore_wait(barrier, len(peers))


REDUCE_ORDER = (1, 3, 2, 0)


def reduce_scratch(phases, half, width):
    bf = jnp.bfloat16
    n = phases * NB
    D = pltpu.SemaphoreType.DMA
    return dict(
        acc=pltpu.VMEM((n, 4, half, width), bf),
        recv_a=pltpu.VMEM((n, 4, half, width), bf),
        recv_b=pltpu.VMEM((n, 2, half, width), bf),
        recv_c=pltpu.VMEM((n, half, width), bf),
        recv_z=pltpu.VMEM((phases, NB, half, width), bf),
        a_send=D((n,)), a_recv=D((n,)), a_own=D((n,)),
        b_send=D((n, 2)), b_recv=D((n,)), c_send=D((n,)), c_recv=D((n,)),
        z_send=D((phases, NB)), z_recv=D((phases, NB)),
        d_send=D((phases, 4)), d_recv=D((phases, 4)), d_own=D((phases,)),
    )


def reduce_steps(me, phases, source, out, sc, last):
    dp, band, core, px, py, kind = (me[k] for k in ("dp", "band", "core", "px", "py", "kind"))
    here = lambda d: {"dp": d, "band": band}
    chunks = [(phase, k) for phase in range(phases) for k in REDUCE_ORDER]
    n = len(chunks)
    flip = lambda v: 1 - v
    sends = []

    def remote(src, dst, ss, rs, to):
        return pltpu.make_async_remote_copy(
            src_ref=src, dst_ref=dst, send_sem=ss, recv_sem=rs, device_id=to, device_id_type=MESH
        )

    def go(copy):
        copy.start()
        sends.append(copy)

    def start_a(s):
        phase, k = chunks[s]
        b = lax.rem(band + k, NB)
        for t in range(4):
            remote(
                source(phase, b, t, flip(core)), sc["recv_a"].at[s, t],
                sc["a_send"].at[s], sc["a_recv"].at[s], here(me["sib"]),
            ).start()
            pltpu.make_async_copy(
                source(phase, b, t, core), sc["acc"].at[s, t], sc["a_own"].at[s]
            ).start()

    def first(s, j, send):
        if s % 2 == 0:
            return 2 * j + (flip(px) if send else px)
        return 2 * (flip(py) if send else py) + j

    def second(s, send):
        if s % 2 == 0:
            return 2 * (flip(py) if send else py) + px
        return 2 * py + (flip(px) if send else px)

    def a_to_b(s):
        acc, got = sc["acc"], sc["recv_a"]
        pltpu.make_async_copy(got.at[s], acc.at[s], sc["a_own"].at[s]).wait()
        whole = remote(got.at[s], got.at[s], sc["a_send"].at[s], sc["a_recv"].at[s], here(me["sib"]))
        whole.wait_recv()
        to = here(me["xdp"] if s % 2 == 0 else me["ydp"])
        for j in range(2):
            t = first(s, j, True)
            add_rows(acc.at[s, t], got.at[s, t])
            go(remote(acc.at[s, t], sc["recv_b"].at[s, j], sc["b_send"].at[s, j], sc["b_recv"].at[s], to))
        for j in range(2):
            t = first(s, j, False)
            add_rows(acc.at[s, t], got.at[s, t])
        whole.wait_send()

    def b_to_c(s):
        acc, got = sc["acc"], sc["recv_b"]
        remote(got.at[s], got.at[s], sc["b_send"].at[s, 0], sc["b_recv"].at[s], here(me["xdp"])).wait_recv()
        to = here(me["ydp"] if s % 2 == 0 else me["xdp"])
        away = flip(py) if s % 2 == 0 else flip(px)
        stay = py if s % 2 == 0 else px
        add_rows(acc.at[s, second(s, True)], got.at[s, away])
        go(remote(acc.at[s, second(s, True)], sc["recv_c"].at[s], sc["c_send"].at[s], sc["c_recv"].at[s], to))
        add_rows(acc.at[s, kind], got.at[s, stay])

    def c_to_z(s):
        acc, got = sc["acc"], sc["recv_c"]
        phase, k = chunks[s]
        remote(got.at[s], got.at[s], sc["c_send"].at[s], sc["c_recv"].at[s], here(me["xdp"])).wait_recv()
        add_rows(acc.at[s, kind], got.at[s])
        if k != 0:
            b = lax.rem(band + k, NB)
            go(remote(
                acc.at[s, kind], sc["recv_z"].at[phase, k], sc["z_send"].at[phase, k],
                sc["z_recv"].at[phase, k], {"dp": dp, "band": b},
            ))

    def z_to_d(phase):
        s = phase * NB + NB - 1
        acc, got = sc["acc"], sc["recv_z"]
        for k in range(1, NB):
            remote(
                got.at[phase, k], got.at[phase, k], sc["z_send"].at[phase, k],
                sc["z_recv"].at[phase, k], here(dp),
            ).wait_recv()
        rows = acc.shape[2]

        @pl.loop(0, rows // 16)
        def _(step):
            at = pl.ds(pl.multiple_of(step * 16, 16), 16)
            total = acc[s, kind, at, :].astype(jnp.float32)
            for k in range(1, NB):
                total = total + got[phase, k, at, :].astype(jnp.float32)
            got[phase, 0, at, :] = total.astype(jnp.bfloat16)

        unit = out[phase].at[kind, core]
        own = pltpu.make_async_copy(got.at[phase, 0], unit, sc["d_own"].at[phase])
        own.start()
        go(remote(
            got.at[phase, 0], unit, sc["d_send"].at[phase, 0], sc["d_recv"].at[phase, 0],
            here(me["xdp"] if phase % 2 == 0 else me["ydp"]),
        ))
        own.wait()

    def d_second(phase):
        even = phase % 2 == 0
        mate = 2 * py + flip(px) if even else 2 * flip(py) + px
        unit = out[phase].at[mate, core]
        remote(unit, unit, sc["d_send"].at[phase, 0], sc["d_recv"].at[phase, 0], here(me["xdp"])).wait_recv()
        if even:
            pair = out[phase].at[pl.ds(2 * py, 2), core]
            go(remote(pair, pair, sc["d_send"].at[phase, 1], sc["d_recv"].at[phase, 1], here(me["ydp"])))
        else:
            for j in range(2):
                unit = out[phase].at[2 * j + px, core]
                go(remote(unit, unit, sc["d_send"].at[phase, 1 + j], sc["d_recv"].at[phase, 1 + j], here(me["xdp"])))

    def d_third(phase):
        if phase % 2 == 0:
            pair = out[phase].at[pl.ds(2 * flip(py), 2), core]
            remote(pair, pair, sc["d_send"].at[phase, 1], sc["d_recv"].at[phase, 1], here(me["ydp"])).wait_recv()
        else:
            for j in range(2):
                unit = out[phase].at[2 * j + flip(px), core]
                remote(unit, unit, sc["d_send"].at[phase, 1 + j], sc["d_recv"].at[phase, 1 + j], here(me["xdp"])).wait_recv()
        row = out[phase].at[:, core]
        go(remote(row, row, sc["d_send"].at[phase, 3], sc["d_recv"].at[phase, 3], here(me["sib"])))

    def d_last(phase):
        row = out[phase].at[:, flip(core)]
        remote(row, row, sc["d_send"].at[phase, 3], sc["d_recv"].at[phase, 3], here(me["sib"])).wait_recv()

    def finish():
        for copy in sends:
            copy.wait_send()

    steps = [lambda: [start_a(s) for s in range(n)]]
    late = {}
    for phase in range(phases):
        end = (phase + 1) * NB - 1
        for lag, do in ((4, z_to_d), (5, d_second), (6, d_third), (7, d_last)):
            late.setdefault(end + lag, []).append(partial(do, phase))
    for s in range(n + 8):
        batch = []
        if s < n:
            batch.append(partial(a_to_b, s))
        if 0 <= s - 1 < n:
            batch.append(partial(b_to_c, s - 1))
        if 0 <= s - 2 < n:
            batch.append(partial(c_to_z, s - 2))
        batch += late.get(s, [])
        if batch:
            steps.append(lambda batch=batch: [do() for do in batch])
    steps.append(finish)
    return steps


def reduce_kernel(counts, names, *refs):
    me = compass()
    phases = len(counts)
    grads = []
    at = 0
    for count in counts:
        grads.append(refs[at : at + count])
        at += count
    out = refs[at : at + phases]
    sc = dict(zip(names, refs[at + phases :]))

    def source(phase, b, t, h):
        if len(grads[phase]) == 1:
            return grads[phase][0].at[b, t, h]
        return grads[phase][t].at[b, h]

    reduce_barrier(me)
    for step in reduce_steps(me, phases, source, out, sc, None):
        step()


def reduce_grads(grads, collective_id):
    phases = len(grads)
    half, width = grads[0][0].shape[-2:]
    counts = tuple(len(phase) for phase in grads)
    scratch = reduce_scratch(phases, half, width)
    return pl.pallas_call(
        partial(reduce_kernel, counts, tuple(scratch)),
        out_shape=[jax.ShapeDtypeStruct((4, 2, half, width), jnp.bfloat16)] * phases,
        in_specs=[pl.BlockSpec(memory_space=pl.ANY)] * sum(counts),
        out_specs=[pl.BlockSpec(memory_space=pl.ANY)] * phases,
        scratch_shapes=list(scratch.values()),
        compiler_params=pltpu.CompilerParams(
            collective_id=collective_id, has_side_effects=True, vmem_limit_bytes=56 * 2**20
        ),
        name="reduce_grads",
    )(*[unit for phase in grads for unit in phase])


def normalize(values):
    average = jnp.mean(values, -1, keepdims=True)
    centered = values - average
    variance = jnp.mean(centered * centered, -1, keepdims=True)
    inverse = lax.rsqrt(variance + 1e-06)
    return (centered * inverse, inverse)


def norm_back(grad_normed, normed, inverse):
    first = jnp.mean(grad_normed, -1, keepdims=True)
    second = jnp.mean(grad_normed * normed, -1, keepdims=True)
    return inverse * (grad_normed - first - normed * second)


def pair_perm(dp_count, band_count):
    return [
        (dp * band_count + band, (dp ^ 1) * band_count + band)
        for dp in range(dp_count)
        for band in range(band_count)
    ]


def home_perm_back(dp_count, band_count, turn):
    pairs = []
    for dp in range(dp_count):
        for band in range(band_count):
            to_dp = dp - dp % 2 + band // 2
            to_band = 2 * (dp % 2) + (band + turn) % 2
            pairs.append((dp * band_count + band, to_dp * band_count + to_band))
    return pairs


def send_home(rows, band, perms):
    odd = lax.rem(band, 2) == 1
    first = jnp.where(odd, rows[1], rows[0])
    second = jnp.where(odd, rows[0], rows[1])
    got = [lax.ppermute(part, ("dp", "band"), perm) for part, perm in zip((first, second), perms)]
    return jnp.stack([jnp.where(odd, got[1], got[0]), jnp.where(odd, got[0], got[1])])


def position_rows(row_index, col_index, width):
    quarter = width // 4
    frequency = 10000.0 ** (-jnp.arange(quarter, dtype=jnp.float32) / quarter)
    angles = jnp.arange(128, dtype=jnp.float32)[:, None] * frequency
    table = jnp.concatenate([jnp.sin(angles), jnp.cos(angles)], -1)
    places = jnp.arange(128, dtype=jnp.int32)
    pick = lambda index: jnp.dot(
        (index[:, None] == places).astype(jnp.float32), table, precision=lax.Precision.HIGHEST
    )
    return jnp.concatenate([pick(row_index), pick(col_index)], -1)


def over_groups(piece, dp_count):
    if dp_count == 8:
        return piece
    groups = [[rank + 8 * group for group in range(dp_count // 8)] for rank in range(8)]
    return lax.psum(piece.astype(jnp.float32), "dp", axis_index_groups=groups)


def own_piece(vector, count, band_place):
    return lax.dynamic_slice_in_dim(vector, band_place * count, count, 0)


def body(
    tokens,
    condition,
    patch_grid,
    ada_weight,
    ada_bias,
    qkv_weight,
    query_bias,
    value_bias,
    proj_weight,
    proj_bias,
    inner_weight,
    inner_bias,
    outer_weight,
    outer_bias,
    cotangent,
):
    both = ("dp", "band")
    dp_count = lax.axis_size("dp")
    band_count = lax.axis_size("band")
    images, band_slots, width = tokens.shape
    band = lax.axis_index("band")
    dp = lax.axis_index("dp")
    core = lax.rem(dp, 2)
    hidden = inner_weight.shape[1]
    part_rows = qkv_weight.shape[0]
    siblings = pair_perm(dp_count, band_count)
    homes = [home_perm_back(dp_count, band_count, turn) for turn in range(2)]

    condition_f = condition.astype(jnp.float32)
    activated = jax.nn.silu(condition_f).astype(jnp.bfloat16)
    own_activated = lax.dynamic_slice_in_dim(activated, band * part_rows, part_rows, 1)
    share = jnp.dot(own_activated, ada_weight, preferred_element_type=jnp.float32)
    share = share + lax.dynamic_update_slice_in_dim(
        jnp.zeros((ada_weight.shape[1],), jnp.float32),
        ada_bias.astype(jnp.float32),
        band * ada_bias.shape[0],
        0,
    )
    biases = jnp.concatenate([query_bias, value_bias, proj_bias, inner_bias, outer_bias])
    bias_count = biases.shape[0]
    mod_count = share.shape[1]
    note = jnp.concatenate(
        [
            share,
            jnp.broadcast_to(biases.astype(jnp.float32), (images, bias_count)),
            patch_grid.astype(jnp.float32),
        ],
        1,
    )
    note_rows = -(-note.shape[1] // 1024) * 8
    note = jnp.pad(note, ((0, 0), (0, note_rows * 128 - note.shape[1])))
    note = note.reshape(images, note_rows, 128)
    first_weight = jnp.concatenate([qkv_weight, proj_weight], 1)
    first_full, inner_full, outer_full, tokens_here, cotangent_here, notes = gather_weights(
        first_weight, inner_weight, outer_weight, tokens, cotangent, note, width
    )
    first_full = first_full.reshape(width, -1)
    inner_full = inner_full.reshape(width, hidden)
    outer_full = outer_full.reshape(hidden, width)
    qkv_full = first_full[:, : 3 * width]
    proj_full = first_full[:, 3 * width :]
    notes = notes.reshape(band_count, -1)
    modulation = jnp.sum(notes[:, :mod_count], 0)
    pieces = []
    at = mod_count
    for piece in (query_bias, value_bias, proj_bias, inner_bias, outer_bias):
        pieces.append(notes[:, at : at + piece.shape[0]].reshape(-1))
        at += piece.shape[0]
    query_bias_full, value_bias_full, proj_bias_full, inner_bias_full, outer_bias_full = pieces
    grid_rows = notes[0, at].astype(jnp.int32)
    grid_cols = notes[0, at + 1].astype(jnp.int32)

    rows = images * band_slots
    ids = core * rows + jnp.arange(rows, dtype=jnp.int32)
    within = ids % band_slots
    band_rows = grid_rows // band_count
    is_valid = within < band_rows * grid_cols
    row_index = ids // band_slots * band_rows + within // grid_cols
    col_index = within % grid_cols

    shift_one, scale_one, gate_one, shift_two, scale_two, gate_two = [
        modulation[index * width : (index + 1) * width] for index in range(6)
    ]
    residual = tokens_here.reshape(rows, width).astype(jnp.float32) + position_rows(
        row_index, col_index, width
    )
    normed_one, inverse_one = normalize(residual)
    attn_in = (normed_one * (1.0 + scale_one) + shift_one).astype(jnp.bfloat16)
    projected = jnp.dot(attn_in, qkv_full, preferred_element_type=jnp.float32)
    query_rows = (projected[:, :width] + query_bias_full).astype(jnp.bfloat16)
    key_value = (
        projected[:, width:] + jnp.concatenate([jnp.zeros((width,), jnp.float32), value_bias_full])
    ).astype(jnp.bfloat16)
    other_key_value = lax.ppermute(key_value, both, siblings)
    valid_count = (band_rows * grid_cols).reshape(1)
    mixed_rows, tops = attend(valid_count, query_rows, key_value, other_key_value, band_slots)
    attended = jnp.dot(mixed_rows, proj_full, preferred_element_type=jnp.float32) + proj_bias_full
    middle = residual + gate_one * attended
    normed_two, inverse_two = normalize(middle)
    mlp_in = (normed_two * (1.0 + scale_two) + shift_two).astype(jnp.bfloat16)
    hidden_pre = jnp.dot(mlp_in, inner_full, preferred_element_type=jnp.float32) + inner_bias_full
    hidden_act = jax.nn.gelu(hidden_pre, approximate=True).astype(jnp.bfloat16)
    mlp_out = jnp.dot(hidden_act, outer_full, preferred_element_type=jnp.float32) + outer_bias_full
    block_out = (middle + gate_two * mlp_out).astype(jnp.bfloat16)
    block_home = send_home(block_out.reshape(images, band_slots, width), band, homes)

    grad_out = cotangent_here.reshape(rows, width).astype(jnp.float32) * is_valid[:, None].astype(
        jnp.float32
    )
    grad_gate_two = jnp.sum(grad_out * mlp_out, 0)
    grad_mlp = (gate_two * grad_out).astype(jnp.bfloat16)
    gelu_back = jax.vjp(partial(jax.nn.gelu, approximate=True), hidden_pre)[1]
    blocks = (band_count, 2, part_rows // 2, width)
    grad_outer = rows_dot(hidden_act, grad_mlp).astype(jnp.bfloat16).reshape(
        band_count, 4, 2, part_rows // 2, width
    )
    grad_outer_bias = jnp.sum(grad_mlp.astype(jnp.float32), 0)
    grad_hidden = lanes_dot(grad_mlp, outer_full)
    grad_pre = gelu_back(grad_hidden)[0].astype(jnp.bfloat16)
    grad_inner = [
        rows_dot(mlp_in, grad_pre[:, t * width : (t + 1) * width]).astype(jnp.bfloat16).reshape(blocks)
        for t in range(4)
    ]
    outer_sum, inner_sum = reduce_grads([[grad_outer], grad_inner], 1)
    grad_inner_bias = jnp.sum(grad_pre.astype(jnp.float32), 0)
    grad_mlp_in = lanes_dot(grad_pre, inner_full)
    grad_shift_two = jnp.sum(grad_mlp_in, 0)
    grad_scale_two = jnp.sum(grad_mlp_in * normed_two, 0)
    grad_middle = grad_out + norm_back(grad_mlp_in * (1.0 + scale_two), normed_two, inverse_two)
    grad_gate_one = jnp.sum(grad_middle * attended, 0)
    grad_attended = (gate_one * grad_middle).astype(jnp.bfloat16)
    grad_proj = rows_dot(mixed_rows, grad_attended).astype(jnp.bfloat16)
    grad_proj_bias = jnp.sum(grad_attended.astype(jnp.float32), 0)
    grad_mixed = lanes_dot(grad_attended, proj_full).astype(jnp.bfloat16)
    grad_query, own_terms, far_terms = attend_back(
        valid_count, query_rows, key_value, other_key_value, grad_mixed, tops, band_slots
    )
    other_terms = lax.ppermute(far_terms, both, siblings)
    grad_key_value = (own_terms.astype(jnp.float32) + other_terms.astype(jnp.float32)).astype(
        jnp.bfloat16
    )
    grad_qkv = jnp.concatenate([grad_query, grad_key_value], -1)
    grad_first = [
        rows_dot(attn_in, part).astype(jnp.bfloat16).reshape(blocks)
        for part in (grad_query, grad_key_value[:, :width], grad_key_value[:, width:])
    ]
    (first_sum,) = reduce_grads([grad_first + [grad_proj.reshape(blocks)]], 2)
    grad_attn_in = lanes_dot(grad_qkv, qkv_full)
    grad_query_bias = jnp.sum(grad_query.astype(jnp.float32), 0)
    grad_value_bias = jnp.sum(grad_key_value[:, width:].astype(jnp.float32), 0)
    grad_shift_one = jnp.sum(grad_attn_in, 0)
    grad_scale_one = jnp.sum(grad_attn_in * normed_one, 0)
    grad_tokens = grad_middle + norm_back(grad_attn_in * (1.0 + scale_one), normed_one, inverse_one)
    tokens_home = send_home(
        grad_tokens.astype(jnp.bfloat16).reshape(images, band_slots, width), band, homes
    ).astype(jnp.float32)

    part_mod = jnp.concatenate(
        [grad_shift_one, grad_scale_one, grad_gate_one, grad_shift_two, grad_scale_two, grad_gate_two]
    )
    grad_mod = (part_mod + lax.ppermute(part_mod, both, siblings)).astype(jnp.bfloat16)
    every_mod = lax.all_gather(grad_mod, both, axis=0).reshape(dp_count // 2, 2, band_count, -1)
    every_mod = every_mod[:, 0].reshape(dp_count * images, -1)
    every_activated = lax.all_gather(own_activated, "dp", axis=0, tiled=True)
    grad_ada = rows_dot(every_activated, every_mod)
    grad_ada_bias = own_piece(jnp.sum(every_mod.astype(jnp.float32), 0), ada_bias.shape[0], band)
    own_mod = lax.dynamic_slice_in_dim(every_mod, images * dp, images, 0)
    grad_act = lax.all_gather(lanes_dot(own_mod, ada_weight), "band", axis=1, tiled=True)
    grad_condition = jax.vjp(jax.nn.silu, condition_f)[1](grad_act)[0]

    def side_by_side(units):
        return jnp.concatenate([unit.reshape(part_rows, width) for unit in units], 1).astype(jnp.float32)

    first_sum, inner_sum, outer_sum = [
        over_groups(piece, dp_count) for piece in (first_sum, inner_sum, outer_sum)
    ]
    weight_sums = dict(
        qkv=side_by_side([first_sum[t] for t in range(3)]),
        proj=first_sum[3].reshape(part_rows, width).astype(jnp.float32),
        inner=side_by_side([inner_sum[t] for t in range(4)]),
        outer=outer_sum.reshape(4 * part_rows, width).astype(jnp.float32),
    )
    bias_grads = lax.psum(
        jnp.concatenate(
            [grad_query_bias, grad_value_bias, grad_proj_bias, grad_inner_bias, grad_outer_bias]
        ),
        both,
    )
    bias_parts = []
    at = 0
    for piece in (query_bias, value_bias, proj_bias, inner_bias, outer_bias):
        whole = piece.shape[0] * band_count
        bias_parts.append(own_piece(bias_grads[at : at + whole], piece.shape[0], band))
        at += whole
    return (
        block_home,
        tokens_home,
        grad_condition,
        grad_ada,
        grad_ada_bias,
        weight_sums["qkv"],
        bias_parts[0],
        bias_parts[1],
        weight_sums["proj"],
        bias_parts[2],
        weight_sums["inner"],
        bias_parts[3],
        weight_sums["outer"],
        bias_parts[4],
    )


def solution(mesh):
    placed = (
        P("dp", "band", None),
        P("dp", None),
        P("dp", None),
        P("band", None),
        P("band"),
        P("band", None),
        P("band"),
        P("band"),
        P("band", None),
        P("band"),
        P("band", None),
        P("band"),
        P("band", None),
        P("band"),
        P("dp", "band", None),
    )
    return jax.shard_map(
        body,
        mesh=mesh,
        in_specs=placed,
        out_specs=(
            P("dp", "band", None),
            P("dp", "band", None),
            P("dp", None),
            P("band", None),
            P("band"),
            P("band", None),
            P("band"),
            P("band"),
            P("band", None),
            P("band"),
            P("band", None),
            P("band"),
            P("band", None),
            P("band"),
        ),
        check_vma=False,
    )
```

```python
import functools
from functools import partial

import jax
import jax.numpy as jnp
from jax import lax
from jax.experimental import pallas as pl
from jax.experimental.pallas import tpu as pltpu
from jax.sharding import PartitionSpec as P

HEAD_DIM = 72

MESH = pl.DeviceIdType.MESH
NB=4
def place():
    dp = lax.axis_index("dp"); band = lax.axis_index("band")
    return dp, band
def gather_kernel(width, qp_in, inner_in, outer_in, tok_in, cot_in, mod_in,
                  qp_out, inner_out, outer_out, tok_out, cot_out, mod_out,
                  z_send, z_recv, a_send, a_recv, b_send, b_recv, c_send, c_recv,
                  t_send, t_recv, m_send, m_recv, local_sem, h_sem, bq, bi, bo, bt):
    dp, band = place()
    core = lax.rem(dp, 2); px = lax.rem(dp // 2, 2); py = lax.rem(dp // 4, 2)
    base = dp - core
    kind = py * 2 + px
    sib = dp + 1 - 2 * core
    xdp = dp + 2 - 4 * px
    ydp = dp + 4 - 8 * py
    dev = lambda d, b: {"dp": d, "band": b}
    barrier = pltpu.get_barrier_semaphore()
    peers = [dev(xdp, band), dev(ydp, band), dev(sib, band)]
    for k in range(1, NB):
        ob = lax.rem(band + k, NB)
        peers += [dev(dp, ob), dev(sib, ob)]
    for q in peers:
        pl.semaphore_signal(barrier, inc=1, device_id=q, device_id_type=MESH)
    pl.semaphore_wait(barrier, len(peers))

    def rc(src, dst, ss, rs, to):
        return pltpu.make_async_remote_copy(src_ref=src, dst_ref=dst, send_sem=ss, recv_sem=rs, device_id=to, device_id_type=MESH)
    ins = (qp_in, inner_in, outer_in); outs = (qp_out, inner_out, outer_out)
    def cols(t, n=1):
        return pl.ds(pl.multiple_of(t * width, 128), n * width)
    def unit(ph, b, t, h):
        return outs[ph].at[b, t, h] if ph == 2 else outs[ph].at[b, h, :, cols(t)]
    def own(ph):
        return ins[ph].at[kind, core] if ph == 2 else ins[ph].at[core, :, cols(kind)]
    def pair(ph, b, h, y):
        return outs[ph].at[b, pl.ds(2 * y, 2), h] if ph == 2 else outs[ph].at[b, h, :, cols(2 * y, 2)]
    def row(ph, b, h):
        return outs[ph].at[b, :, h] if ph == 2 else outs[ph].at[b, h]
    sends = []
    def go(c):
        c.start(); sends.append(c)
    slot = lax.rem(band, 2)
    def move(which, src, dst):
        for i in range(2):
            to_core = band // 2; to_band = 2 * core + i
            home = jnp.logical_and(to_core == core, to_band == band)
            @pl.when(home)
            def _():
                pltpu.make_async_copy(src.at[i], bt.at[which], h_sem.at[which]).start()
                pltpu.make_async_copy(src.at[i], bt.at[which], h_sem.at[which]).wait()
                pltpu.make_async_copy(bt.at[which], dst.at[slot], t_recv.at[which, slot]).start()
            @pl.when(jnp.logical_not(home))
            def _():
                rc(src.at[i], dst.at[slot], t_send.at[which, i], t_recv.at[which, slot], dev(base + to_core, to_band)).start()
    def move_wait(which, src, dst):
        for i in range(2):
            to_core = band // 2; to_band = 2 * core + i
            home = jnp.logical_and(to_core == core, to_band == band)
            @pl.when(jnp.logical_not(home))
            def _():
                rc(src.at[i], dst.at[slot], t_send.at[which, i], t_recv.at[which, slot], dev(base + to_core, to_band)).wait_send()
        for s in range(2):
            pltpu.make_async_copy(src.at[s], dst.at[s], t_recv.at[which, s]).wait()
    def mods():
        for i in range(2):
            for c in range(2):
                home = jnp.logical_and(c == core, 2 * core + i == band)
                @pl.when(home)
                def _():
                    pltpu.make_async_copy(mod_in.at[i], mod_out.at[band], m_recv.at[band]).start()
                @pl.when(jnp.logical_not(home))
                def _():
                    rc(mod_in.at[i], mod_out.at[band], m_send.at[i, c], m_recv.at[band], dev(base + c, 2 * core + i)).start()
    def mods_wait():
        for i in range(2):
            for c in range(2):
                home = jnp.logical_and(c == core, 2 * core + i == band)
                @pl.when(jnp.logical_not(home))
                def _():
                    rc(mod_in.at[i], mod_out.at[band], m_send.at[i, c], m_recv.at[band], dev(base + c, 2 * core + i)).wait_send()
        for b in range(NB):
            pltpu.make_async_copy(mod_in.at[0], mod_out.at[b], m_recv.at[b]).wait()
    def zstart(ph):
        for k in (1, 3, 2):
            ob = lax.rem(band + k, NB)
            go(rc(own(ph), unit(ph, band, kind, core), z_send.at[ph, k], z_recv.at[ph, k], dev(dp, ob)))
    mods()
    move(0, tok_in, tok_out)
    zstart(0)
    bounce = (bq, bi, bo)
    for ph in range(3):
        pltpu.make_async_copy(ins[ph], bounce[ph], local_sem.at[ph]).start()
    for ph in range(3):
        pltpu.make_async_copy(ins[ph], bounce[ph], local_sem.at[ph]).wait()
        pltpu.make_async_copy(bounce[ph], outs[ph].at[band], local_sem.at[ph]).start()
    steps = [(ph, k) for ph in range(3) for k in (1, 3, 2)]
    n = len(steps)
    frm = lambda k: lax.rem(band + NB - k, NB)
    other = lambda v: 1 - v
    for s in range(n + 3):
        if s < n:
            ph, k = steps[s]; b = frm(k)
            u = unit(ph, b, kind, core)
            rc(u, u, z_send.at[ph, k], z_recv.at[ph, k], dev(dp, band)).wait_recv()
            go(rc(u, u, a_send.at[s], a_recv.at[s], dev(xdp if s % 2 == 0 else ydp, band)))
            if k == 3 and ph < 2:
                zstart(ph + 1)
            if k == 2 and ph == 2:
                move(1, cot_in, cot_out)
        r = s - 1
        if 0 <= r < n:
            ph, k = steps[r]; b = frm(k)
            got = py * 2 + other(px) if r % 2 == 0 else other(py) * 2 + px
            u = unit(ph, b, got, core)
            rc(u, u, a_send.at[r], a_recv.at[r], dev(xdp, band)).wait_recv()
            if r % 2 == 0:
                v = pair(ph, b, core, py)
                go(rc(v, v, b_send.at[r, 0], b_recv.at[r, 0], dev(ydp, band)))
            else:
                for j in range(2):
                    v = unit(ph, b, j * 2 + px, core)
                    go(rc(v, v, b_send.at[r, j], b_recv.at[r, j], dev(xdp, band)))
        r = s - 2
        if 0 <= r < n:
            ph, k = steps[r]; b = frm(k)
            if r % 2 == 0:
                v = pair(ph, b, core, other(py))
                rc(v, v, b_send.at[r, 0], b_recv.at[r, 0], dev(ydp, band)).wait_recv()
            else:
                for j in range(2):
                    v = unit(ph, b, j * 2 + other(px), core)
                    rc(v, v, b_send.at[r, j], b_recv.at[r, j], dev(xdp, band)).wait_recv()
            w = row(ph, b, core)
            go(rc(w, w, c_send.at[r], c_recv.at[r], dev(sib, band)))
        r = s - 3
        if 0 <= r < n:
            ph, k = steps[r]; b = frm(k)
            w = row(ph, b, other(core))
            rc(w, w, c_send.at[r], c_recv.at[r], dev(sib, band)).wait_recv()
    for ph in range(3):
        pltpu.make_async_copy(bounce[ph], outs[ph].at[band], local_sem.at[ph]).wait()
    mods_wait()
    move_wait(0, tok_in, tok_out)
    move_wait(1, cot_in, cot_out)
    for c in sends: c.wait_send()

def gather_weights(qp, inner, outer, tok, cot, mod, width):
    half = qp.shape[0] // 2
    ff = qp.shape[1]
    bf = jnp.bfloat16
    qp = qp.reshape(2, half, ff); inner = inner.reshape(2, half, ff); outer = outer.reshape(4, 2, half, width)
    D = pltpu.SemaphoreType.DMA
    outs = pl.pallas_call(
        functools.partial(gather_kernel, width),
        out_shape=[jax.ShapeDtypeStruct((NB,) + qp.shape, bf), jax.ShapeDtypeStruct((NB,) + inner.shape, bf),
                   jax.ShapeDtypeStruct((NB,) + outer.shape, bf),
                   jax.ShapeDtypeStruct(tok.shape, bf), jax.ShapeDtypeStruct(cot.shape, bf),
                   jax.ShapeDtypeStruct((NB,) + mod.shape[1:], jnp.float32)],
        in_specs=[pl.BlockSpec(memory_space=pl.ANY)] * 6,
        out_specs=[pl.BlockSpec(memory_space=pl.ANY)] * 6,
        scratch_shapes=[D((3, 4)), D((3, 4)), D((9,)), D((9,)), D((9, 2)), D((9, 2)), D((9,)), D((9,)),
                        D((2, 2)), D((2, 2)), D((2, 2)), D((4,)), D((3,)), D((2,)),
                        pltpu.VMEM(qp.shape, bf), pltpu.VMEM(inner.shape, bf), pltpu.VMEM(outer.shape, bf),
                        pltpu.VMEM((2,) + tok.shape[1:], bf)],
        compiler_params=pltpu.CompilerParams(collective_id=0, has_side_effects=True, vmem_limit_bytes=32*2**20),
        name="gather_weights",
    )(qp, inner, outer, tok, cot, mod)
    return outs


LANES = 128
PACK_ROWS = 128


def pack_heads(source, first, heads_ref, row0, rows, tail):
    heads = heads_ref.shape[0]

    @pl.loop(0, rows // PACK_ROWS)
    def _(step):
        at = pl.multiple_of(step * PACK_ROWS, PACK_ROWS)
        block = source[pl.ds(at, PACK_ROWS), first : first + heads * HEAD_DIM]
        end = tail(at)
        for h in range(heads):
            part = block[:, h * HEAD_DIM : (h + 1) * HEAD_DIM]
            heads_ref[h, pl.ds(row0 + at, PACK_ROWS), :] = jnp.concatenate([part, end], 1)


def unpack_heads(heads_ref, row0, rows, target, first):
    heads = heads_ref.shape[0]

    @pl.loop(0, rows // PACK_ROWS)
    def _(step):
        at = pl.multiple_of(step * PACK_ROWS, PACK_ROWS)
        parts = [heads_ref[h, pl.ds(row0 + at, PACK_ROWS), :][:, :HEAD_DIM] for h in range(heads)]
        target[pl.ds(at, PACK_ROWS), first : first + heads * HEAD_DIM] = jnp.concatenate(parts, 1)


def flat_tail(value):
    def tail(at):
        lane = lax.broadcasted_iota(jnp.int32, (PACK_ROWS, LANES - HEAD_DIM), 1)
        return jnp.where(lane == 0, value, 0.0).astype(jnp.bfloat16)

    return tail


def key_tail(valid_count, band_slots):
    def tail(at):
        shape = (PACK_ROWS, LANES - HEAD_DIM)
        lane = lax.broadcasted_iota(jnp.int32, shape, 1)
        slot = lax.rem(at + lax.broadcasted_iota(jnp.int32, shape, 0), band_slots)
        return jnp.where(jnp.logical_and(lane == 0, slot >= valid_count), -1e30, 0.0).astype(jnp.bfloat16)

    return tail


def lanes_dot(left, right):
    return lax.dot_general(left, right, (((1,), (1,)), ((), ())), preferred_element_type=jnp.float32)


def rows_dot(left, right):
    return lax.dot_general(left, right, (((0,), (0,)), ((), ())), preferred_element_type=jnp.float32)


SCORE_SCALE = HEAD_DIM ** (-0.5)


def attend_kernel(band_slots, count_ref, q_ref, own_ref, far_ref, out_ref, top_ref, qh, kh, vh):
    rows, width = q_ref.shape
    heads = qh.shape[0]
    pack_heads(q_ref, 0, qh, 0, rows, flat_tail(1.0))
    for row0, ref in ((0, own_ref), (rows, far_ref)):
        pack_heads(ref, 0, kh, row0, rows, key_tail(count_ref[0], band_slots))
        pack_heads(ref, width, vh, row0, rows, flat_tail(0.0))

    @pl.loop(0, heads)
    def _(h):
        for block in range(2):
            at = pl.ds(block * rows // 2, rows // 2)
            scores = lanes_dot(kh[h], qh[h, at, :]) * SCORE_SCALE
            top = jnp.max(scores, 0, keepdims=True)
            weights = jnp.exp(scores - top)
            total = jnp.sum(weights, 0, keepdims=True)
            low = (weights * (1.0 / total)).astype(jnp.bfloat16)
            mixed = rows_dot(vh[h], low)
            qh[h, at, :] = jnp.transpose(mixed).astype(jnp.bfloat16)
            top_ref[h, :, at] = jnp.broadcast_to(top + jnp.log(total), (8, rows // 2))

    unpack_heads(qh, 0, rows, out_ref, 0)


def attend(count, query, own, far, band_slots):
    rows, width = query.shape
    heads = width // HEAD_DIM
    bf = jnp.bfloat16
    vmem = pl.BlockSpec(memory_space=pltpu.VMEM)
    return pl.pallas_call(
        partial(attend_kernel, band_slots),
        out_shape=[
            jax.ShapeDtypeStruct((rows, width), bf),
            jax.ShapeDtypeStruct((heads, 8, rows), jnp.float32),
        ],
        in_specs=[pl.BlockSpec(memory_space=pltpu.SMEM), vmem, vmem, vmem],
        out_specs=[vmem, vmem],
        scratch_shapes=[
            pltpu.VMEM((heads, rows, LANES), bf),
            pltpu.VMEM((heads, 2 * rows, LANES), bf),
            pltpu.VMEM((heads, 2 * rows, LANES), bf),
        ],
        compiler_params=pltpu.CompilerParams(vmem_limit_bytes=48 * 2**20),
        cost_estimate=pl.CostEstimate(
            flops=8 * rows * rows * width, bytes_accessed=16 * rows * width, transcendentals=2 * heads * rows * rows
        ),
        name="attend",
    )(count, query, own, far)


def attend_head(h, qh, kh, vh, gh, top_ref):
    query = qh[h]
    key = kh[h]
    grad = gh[h]
    probs = jnp.exp(lanes_dot(key, query) * SCORE_SCALE - top_ref[h, 0:1, :])
    grad_probs = lanes_dot(vh[h], grad)
    inner = jnp.sum(probs * grad_probs, 0, keepdims=True)
    grad_scores = (probs * (grad_probs - inner)).astype(jnp.bfloat16)
    vh[h] = jnp.dot(
        probs.astype(jnp.bfloat16), grad, preferred_element_type=jnp.float32
    ).astype(jnp.bfloat16)
    grad_query = rows_dot(key, grad_scores)
    kh[h] = (
        SCORE_SCALE * jnp.dot(grad_scores, query, preferred_element_type=jnp.float32)
    ).astype(jnp.bfloat16)
    qh[h] = (SCORE_SCALE * jnp.transpose(grad_query)).astype(jnp.bfloat16)


def compass():
    dp = lax.axis_index("dp")
    band = lax.axis_index("band")
    core = lax.rem(dp, 2)
    px = lax.rem(dp // 2, 2)
    py = lax.rem(dp // 4, 2)
    return dict(
        dp=dp, band=band, core=core, px=px, py=py, kind=2 * py + px,
        sib=dp + 1 - 2 * core, xdp=dp + 2 - 4 * px, ydp=dp + 4 - 8 * py,
    )


def add_rows(total, term):
    rows = total.shape[0]

    @pl.loop(0, rows // 16)
    def _(step):
        at = pl.ds(pl.multiple_of(step * 16, 16), 16)
        total[at, :] = (
            total[at, :].astype(jnp.float32) + term[at, :].astype(jnp.float32)
        ).astype(jnp.bfloat16)


def reduce_barrier(me):
    barrier = pltpu.get_barrier_semaphore()
    peers = [(me["xdp"], me["band"]), (me["ydp"], me["band"]), (me["sib"], me["band"])]
    peers += [(me["dp"], lax.rem(me["band"] + k, NB)) for k in range(1, NB)]
    for dp, band in peers:
        pl.semaphore_signal(
            barrier, inc=1, device_id={"dp": dp, "band": band}, device_id_type=MESH
        )
    pl.semaphore_wait(barrier, len(peers))


def run_all(batch):
    for do in batch:
        do()


REDUCE_ORDER = (1, 3, 2, 0)


def reduce_scratch(phases, half, width):
    bf = jnp.bfloat16
    n = phases * NB
    D = pltpu.SemaphoreType.DMA
    return dict(
        acc=pltpu.VMEM((n, 4, half, width), bf),
        recv_a=pltpu.VMEM((n, 4, half, width), bf),
        recv_b=pltpu.VMEM((n, 2, half, width), bf),
        recv_c=pltpu.VMEM((n, half, width), bf),
        recv_z=pltpu.VMEM((phases, NB, half, width), bf),
        a_send=D((n,)), a_recv=D((n,)), a_own=D((n,)),
        b_send=D((n, 2)), b_recv=D((n,)), c_send=D((n,)), c_recv=D((n,)),
        z_send=D((phases, NB)), z_recv=D((phases, NB)),
        d_send=D((phases, 4)), d_recv=D((phases, 4)), d_own=D((phases,)),
    )


def reduce_steps(me, phases, source, out, sc, beside=()):
    dp, band, core, px, py, kind = (me[k] for k in ("dp", "band", "core", "px", "py", "kind"))
    here = lambda d: {"dp": d, "band": band}
    chunks = [(phase, k) for phase in range(phases) for k in REDUCE_ORDER]
    n = len(chunks)
    flip = lambda v: 1 - v
    sends = []

    def remote(src, dst, ss, rs, to):
        return pltpu.make_async_remote_copy(
            src_ref=src, dst_ref=dst, send_sem=ss, recv_sem=rs, device_id=to, device_id_type=MESH
        )

    def go(make):
        make().start()
        sends.append(make)

    def start_a(s):
        phase, k = chunks[s]
        b = lax.rem(band + k, NB)
        for t in range(4):
            remote(
                source(phase, b, t, flip(core)), sc["recv_a"].at[s, t],
                sc["a_send"].at[s], sc["a_recv"].at[s], here(me["sib"]),
            ).start()
            pltpu.make_async_copy(
                source(phase, b, t, core), sc["acc"].at[s, t], sc["a_own"].at[s]
            ).start()

    def first(s, j, send):
        if s % 2 == 0:
            return 2 * j + (flip(px) if send else px)
        return 2 * (flip(py) if send else py) + j

    def second(s, send):
        if s % 2 == 0:
            return 2 * (flip(py) if send else py) + px
        return 2 * py + (flip(px) if send else px)

    def send_b(s, j):
        return remote(
            sc["acc"].at[s, first(s, j, True)], sc["recv_b"].at[s, j], sc["b_send"].at[s, j],
            sc["b_recv"].at[s], here(me["xdp"] if s % 2 == 0 else me["ydp"]),
        )

    def send_c(s):
        return remote(
            sc["acc"].at[s, second(s, True)], sc["recv_c"].at[s], sc["c_send"].at[s],
            sc["c_recv"].at[s], here(me["ydp"] if s % 2 == 0 else me["xdp"]),
        )

    def send_z(s):
        phase, k = chunks[s]
        return remote(
            sc["acc"].at[s, kind], sc["recv_z"].at[phase, k], sc["z_send"].at[phase, k],
            sc["z_recv"].at[phase, k], {"dp": dp, "band": lax.rem(band + k, NB)},
        )

    def send_d(phase, slot):
        ss, rs = sc["d_send"].at[phase, slot], sc["d_recv"].at[phase, slot]
        even = phase % 2 == 0
        if slot == 0:
            unit = out[phase].at[kind, core]
            return remote(sc["recv_z"].at[phase, 0], unit, ss, rs, here(me["xdp"] if even else me["ydp"]))
        if slot == 3:
            row = out[phase].at[:, core]
            return remote(row, row, ss, rs, here(me["sib"]))
        if even:
            pair = out[phase].at[pl.ds(2 * py, 2), core]
            return remote(pair, pair, ss, rs, here(me["ydp"]))
        unit = out[phase].at[2 * (slot - 1) + px, core]
        return remote(unit, unit, ss, rs, here(me["xdp"]))

    def a_to_b(s):
        acc, got = sc["acc"], sc["recv_a"]
        pltpu.make_async_copy(got.at[s], acc.at[s], sc["a_own"].at[s]).wait()
        whole = remote(got.at[s], got.at[s], sc["a_send"].at[s], sc["a_recv"].at[s], here(me["sib"]))
        whole.wait_recv()
        for j in range(2):
            t = first(s, j, True)
            add_rows(acc.at[s, t], got.at[s, t])
            go(partial(send_b, s, j))
        for j in range(2):
            t = first(s, j, False)
            add_rows(acc.at[s, t], got.at[s, t])
        whole.wait_send()

    def b_to_c(s):
        acc, got = sc["acc"], sc["recv_b"]
        remote(got.at[s], got.at[s], sc["b_send"].at[s, 0], sc["b_recv"].at[s], here(me["xdp"])).wait_recv()
        away = flip(py) if s % 2 == 0 else flip(px)
        stay = py if s % 2 == 0 else px
        add_rows(acc.at[s, second(s, True)], got.at[s, away])
        go(partial(send_c, s))
        add_rows(acc.at[s, kind], got.at[s, stay])

    def c_to_z(s):
        acc, got = sc["acc"], sc["recv_c"]
        phase, k = chunks[s]
        remote(got.at[s], got.at[s], sc["c_send"].at[s], sc["c_recv"].at[s], here(me["xdp"])).wait_recv()
        add_rows(acc.at[s, kind], got.at[s])
        if k != 0:
            go(partial(send_z, s))

    def z_to_d(phase):
        s = phase * NB + NB - 1
        acc, got = sc["acc"], sc["recv_z"]
        for k in range(1, NB):
            remote(
                got.at[phase, k], got.at[phase, k], sc["z_send"].at[phase, k],
                sc["z_recv"].at[phase, k], here(dp),
            ).wait_recv()
        rows = acc.shape[2]

        @pl.loop(0, rows // 16)
        def _(step):
            at = pl.ds(pl.multiple_of(step * 16, 16), 16)
            total = acc[s, kind, at, :].astype(jnp.float32)
            for k in range(1, NB):
                total = total + got[phase, k, at, :].astype(jnp.float32)
            got[phase, 0, at, :] = total.astype(jnp.bfloat16)

        unit = out[phase].at[kind, core]
        own = pltpu.make_async_copy(got.at[phase, 0], unit, sc["d_own"].at[phase])
        own.start()
        go(partial(send_d, phase, 0))
        own.wait()

    def d_second(phase):
        even = phase % 2 == 0
        mate = 2 * py + flip(px) if even else 2 * flip(py) + px
        unit = out[phase].at[mate, core]
        remote(unit, unit, sc["d_send"].at[phase, 0], sc["d_recv"].at[phase, 0], here(me["xdp"])).wait_recv()
        for slot in (1,) if even else (1, 2):
            go(partial(send_d, phase, slot))

    def d_third(phase):
        if phase % 2 == 0:
            pair = out[phase].at[pl.ds(2 * flip(py), 2), core]
            remote(pair, pair, sc["d_send"].at[phase, 1], sc["d_recv"].at[phase, 1], here(me["ydp"])).wait_recv()
        else:
            for j in range(2):
                unit = out[phase].at[2 * j + flip(px), core]
                remote(unit, unit, sc["d_send"].at[phase, 1 + j], sc["d_recv"].at[phase, 1 + j], here(me["xdp"])).wait_recv()
        go(partial(send_d, phase, 3))

    def d_last(phase):
        row = out[phase].at[:, flip(core)]
        remote(row, row, sc["d_send"].at[phase, 3], sc["d_recv"].at[phase, 3], here(me["sib"])).wait_recv()

    def finish():
        for make in sends:
            make().wait_send()

    steps = [partial(run_all, [partial(start_a, s) for s in range(n)])]
    late = {}
    for phase in range(phases):
        end = (phase + 1) * NB - 1
        for lag, do in ((4, z_to_d), (5, d_second), (6, d_third), (7, d_last)):
            late.setdefault(end + lag, []).append(partial(do, phase))
    for s in range(n + 8):
        batch = []
        if s < n:
            batch.append(partial(a_to_b, s))
        if 0 <= s - 1 < n:
            batch.append(partial(b_to_c, s - 1))
        if 0 <= s - 2 < n:
            batch.append(partial(c_to_z, s - 2))
        if s < len(beside):
            batch.append(beside[s])
        batch += late.get(s, [])
        if batch:
            steps.append(partial(run_all, batch))
    steps.append(finish)
    return steps


def reduce_sources(counts, refs):
    grads = []
    at = 0
    for count in counts:
        grads.append(refs[at : at + count])
        at += count

    def source(phase, b, t, h):
        if len(grads[phase]) == 1:
            return grads[phase][0].at[b, t, h]
        return grads[phase][t].at[b, h]

    return source


def small_scratch(mod_rows, bias_rows, cond_rows, cond_cols):
    D = pltpu.SemaphoreType.DMA
    f32 = jnp.float32
    return dict(
        s_core=pltpu.VMEM((mod_rows + bias_rows, 128), f32),
        s_every=pltpu.VMEM((NB, 4, mod_rows, 128), jnp.bfloat16),
        s_bias=pltpu.VMEM((3, bias_rows, 128), f32),
        s_got=pltpu.VMEM((2 + NB, bias_rows, 128), f32),
        s_flat=pltpu.VMEM((8, mod_rows, 128), f32),
        s_cond=pltpu.VMEM((NB, cond_rows, cond_cols), f32),
        s_send=D((8,)), s_recv=D((8,)), sz_send=D((2, NB)), sz_recv=D((2, NB)),
        sc_send=D((NB,)), sc_recv=D((NB,)),
    )


def small_steps(me, mods, images, small_ref, ada_ref, every_ref, bias_ref, cond_ref, sc):
    dp, band, core, px, py, kind = (me[k] for k in ("dp", "band", "core", "px", "py", "kind"))
    here = lambda d: {"dp": d, "band": band}
    every, bias, got, cond = sc["s_every"], sc["s_bias"], sc["s_got"], sc["s_cond"]
    mod_rows = every.shape[2]
    flip = lambda v: 1 - v

    def remote(src, dst, ss, rs, to):
        return pltpu.make_async_remote_copy(
            src_ref=src, dst_ref=dst, send_sem=ss, recv_sem=rs, device_id=to, device_id_type=MESH
        )

    def plain(index, src, dst, to):
        return remote(src, dst, sc["s_send"].at[index], sc["s_recv"].at[index], to)

    def core_copy():
        return plain(0, small_ref, sc["s_core"], here(me["sib"]))

    def x_copies(mine):
        unit = every.at[band, kind if mine else 2 * py + flip(px)]
        return [
            plain(1, unit, unit, here(me["xdp"])),
            plain(2, bias.at[0], got.at[0], here(me["xdp"])),
        ]

    def y_copies(mine):
        pair = every.at[band, pl.ds(2 * (py if mine else flip(py)), 2)]
        return [
            plain(3, pair, pair, here(me["ydp"])),
            plain(4, bias.at[1], got.at[1], here(me["ydp"])),
        ]

    def z_copies(k, mine):
        to = {"dp": dp, "band": lax.rem(band + k, NB)}
        block = every.at[band if mine else lax.rem(band + NB - k, NB)]
        return [
            remote(block, block, sc["sz_send"].at[0, k], sc["sz_recv"].at[0, k], to),
            remote(bias.at[2], got.at[2 + k], sc["sz_send"].at[1, k], sc["sz_recv"].at[1, k], to),
        ]

    def cond_copy(k, mine):
        to = {"dp": dp, "band": lax.rem(band + k, NB)}
        block = cond.at[band if mine else lax.rem(band + NB - k, NB)]
        return remote(block, block, sc["sc_send"].at[k], sc["sc_recv"].at[k], to)

    def begin():
        core_copy().start()

    def cores():
        core_copy().wait()
        total = small_ref[...] + sc["s_core"][...]
        every[band, kind] = total[:mod_rows].astype(jnp.bfloat16)
        bias[0] = total[mod_rows:]
        for copy in x_copies(True):
            copy.start()

    def over_x():
        for copy in x_copies(True):
            copy.wait_send()
        for copy in x_copies(False):
            copy.wait_recv()
        bias[1] = bias[0] + got[0]
        for copy in y_copies(True):
            copy.start()

    def over_y():
        for copy in y_copies(True):
            copy.wait_send()
        for copy in y_copies(False):
            copy.wait_recv()
        bias[2] = bias[1] + got[1]
        for k in range(1, NB):
            for copy in z_copies(k, True):
                copy.start()

    def over_z():
        for k in range(1, NB):
            for copy in z_copies(k, True):
                copy.wait_send()
            for copy in z_copies(k, False):
                copy.wait_recv()
        bias_ref[...] = bias[2] + got[3] + got[4] + got[5]
        every_ref[...] = every[...]
        flat = sc["s_flat"]
        for i in range(images):
            flat[i] = every[images * core + i, kind].astype(jnp.float32)
        parts = mods // 128
        lead = flat.shape[0]
        total = jnp.zeros((lead, ada_ref.shape[0]), jnp.float32)
        for r in range(parts):
            left = jnp.concatenate(
                [flat[i, r : r + 1, :] for i in range(images)]
                + [jnp.zeros((lead - images, 128), jnp.float32)]
            ).astype(jnp.bfloat16)
            total = total + lanes_dot(left, ada_ref[:, r * 128 : (r + 1) * 128])
        pad = cond.shape[2] - total.shape[1]
        cond[band] = jnp.concatenate([total, jnp.zeros((lead, pad), jnp.float32)], 1)
        for k in range(1, NB):
            cond_copy(k, True).start()

    def conditions():
        for k in range(1, NB):
            cond_copy(k, True).wait_send()
            cond_copy(k, False).wait_recv()
        cond_ref[...] = cond[...]

    return [begin, cores, over_x, over_y, over_z, conditions]


def reduce_last_kernel(counts, mods, images, names, *refs):
    me = compass()
    phases = len(counts)
    at = sum(counts)
    source = reduce_sources(counts, refs)
    small_ref, ada_ref = refs[at : at + 2]
    out = refs[at + 2 : at + 2 + phases]
    every_ref, bias_ref, cond_ref = refs[at + 2 + phases : at + 5 + phases]
    sc = dict(zip(names, refs[at + 5 + phases :]))
    reduce_barrier(me)
    small = small_steps(me, mods, images, small_ref, ada_ref, every_ref, bias_ref, cond_ref, sc)
    small[0]()
    for step in reduce_steps(me, phases, source, out, sc, small[1:]):
        step()


def reduce_last(grads, mod_part, bias_part, ada_weight, images, collective_id):
    phases = len(grads)
    half, width = grads[0][0].shape[-2:]
    counts = tuple(len(phase) for phase in grads)
    mod_rows, bias_rows = mod_part.shape[0], bias_part.shape[0]
    cond_cols = -(-ada_weight.shape[0] // 128) * 128
    scratch = dict(**reduce_scratch(phases, half, width), **small_scratch(mod_rows, bias_rows, 8, cond_cols))
    any_, vmem = pl.BlockSpec(memory_space=pl.ANY), pl.BlockSpec(memory_space=pltpu.VMEM)
    outs = pl.pallas_call(
        partial(reduce_last_kernel, counts, ada_weight.shape[1], images, tuple(scratch)),
        out_shape=[jax.ShapeDtypeStruct((4, 2, half, width), jnp.bfloat16)] * phases
        + [
            jax.ShapeDtypeStruct((NB, 4, mod_rows, 128), jnp.bfloat16),
            jax.ShapeDtypeStruct((bias_rows, 128), jnp.float32),
            jax.ShapeDtypeStruct((NB, 8, cond_cols), jnp.float32),
        ],
        in_specs=[any_] * sum(counts) + [vmem] * 2,
        out_specs=[any_] * phases + [vmem] * 3,
        scratch_shapes=list(scratch.values()),
        compiler_params=pltpu.CompilerParams(
            collective_id=collective_id, has_side_effects=True, vmem_limit_bytes=56 * 2**20
        ),
        name="reduce_last",
    )(*[unit for phase in grads for unit in phase], jnp.concatenate([mod_part, bias_part]), ada_weight)
    return outs[:phases], outs[phases], outs[phases + 1], outs[phases + 2]


def reduce_attend_kernel(counts, band_slots, names, *refs):
    me = compass()
    phases = len(counts)
    at = sum(counts)
    source = reduce_sources(counts, refs)
    count_ref, q_ref, own_ref, far_ref, grad_ref, top_ref = refs[at : at + 6]
    at += 6
    out = refs[at : at + phases]
    dq_ref, down_ref, dfar_ref = refs[at + phases : at + phases + 3]
    sc = dict(zip(names, refs[at + phases + 3 :]))
    qh, kh, vh, gh, stage, stage_sem = (sc[k] for k in ("qh", "kh", "vh", "gh", "stage", "stage_sem"))
    rows, width = q_ref.shape
    heads = qh.shape[0]
    reduce_barrier(me)
    steps = reduce_steps(me, phases, source, out, sc)
    steps[0]()
    keys, plain, ones = key_tail(count_ref[0], band_slots), flat_tail(0.0), flat_tail(1.0)
    loads = [(q_ref, 0, qh, 0, ones), (grad_ref, 0, gh, 0, plain)]
    for row0, ref in ((0, own_ref), (rows, far_ref)):
        loads += [(ref, 0, kh, row0, keys), (ref, width, vh, row0, plain)]

    def load(i):
        ref, column = loads[i][:2]
        return pltpu.make_async_copy(ref.at[:, pl.ds(column, width)], stage.at[i % 2], stage_sem.at[i % 2])

    load(0).start()
    for i, (ref, column, heads_ref, row0, tail) in enumerate(loads):
        if i + 1 < len(loads):
            load(i + 1).start()
        load(i).wait()
        pack_heads(stage.at[i % 2], 0, heads_ref, row0, rows, tail)
    rest = steps[1:]

    @pl.loop(0, heads)
    def _(h):
        attend_head(h, qh, kh, vh, gh, top_ref)
        for i, step in enumerate(rest[:heads]):
            pl.when(h == i)(step)

    stores = [(qh, 0, dq_ref, 0)]
    for row0, ref in ((0, down_ref), (rows, dfar_ref)):
        stores += [(kh, row0, ref, 0), (vh, row0, ref, width)]

    def store(i):
        ref, column = stores[i][2:]
        return pltpu.make_async_copy(stage.at[i % 2], ref.at[:, pl.ds(column, width)], stage_sem.at[i % 2])

    for i, (heads_ref, row0, ref, column) in enumerate(stores):
        if i >= 2:
            store(i - 2).wait()
        unpack_heads(heads_ref, row0, rows, stage.at[i % 2], 0)
        store(i).start()
    for i in (len(stores) - 2, len(stores) - 1):
        store(i).wait()
    for step in rest[heads:]:
        step()


def reduce_attend(grads, count, query, own, far, grad, top, band_slots, collective_id):
    phases = len(grads)
    half, width = grads[0][0].shape[-2:]
    counts = tuple(len(phase) for phase in grads)
    rows = query.shape[0]
    heads = width // HEAD_DIM
    bf = jnp.bfloat16
    scratch = reduce_scratch(phases, half, width)
    scratch.update(
        qh=pltpu.VMEM((heads, rows, LANES), bf),
        kh=pltpu.VMEM((heads, 2 * rows, LANES), bf),
        vh=pltpu.VMEM((heads, 2 * rows, LANES), bf),
        gh=pltpu.VMEM((heads, rows, LANES), bf),
        stage=pltpu.VMEM((2, rows, width), bf),
        stage_sem=pltpu.SemaphoreType.DMA((2,)),
    )
    any_, vmem = pl.BlockSpec(memory_space=pl.ANY), pl.BlockSpec(memory_space=pltpu.VMEM)
    smem = pl.BlockSpec(memory_space=pltpu.SMEM)
    outs = pl.pallas_call(
        partial(reduce_attend_kernel, counts, band_slots, tuple(scratch)),
        out_shape=[jax.ShapeDtypeStruct((4, 2, half, width), bf)] * phases
        + [
            jax.ShapeDtypeStruct((rows, width), bf),
            jax.ShapeDtypeStruct((rows, 2 * width), bf),
            jax.ShapeDtypeStruct((rows, 2 * width), bf),
        ],
        in_specs=[any_] * sum(counts) + [smem] + [any_] * 4 + [vmem],
        out_specs=[any_] * (phases + 3),
        scratch_shapes=list(scratch.values()),
        compiler_params=pltpu.CompilerParams(
            collective_id=collective_id, has_side_effects=True, vmem_limit_bytes=60 * 2**20
        ),
        name="reduce_attend",
    )(*[unit for phase in grads for unit in phase], count, query, own, far, grad, top)
    return outs[:phases], outs[phases], outs[phases + 1], outs[phases + 2]


def normalize(values):
    average = jnp.mean(values, -1, keepdims=True)
    centered = values - average
    variance = jnp.mean(centered * centered, -1, keepdims=True)
    inverse = lax.rsqrt(variance + 1e-06)
    return (centered * inverse, inverse)


def norm_back(grad_normed, normed, inverse):
    first = jnp.mean(grad_normed, -1, keepdims=True)
    second = jnp.mean(grad_normed * normed, -1, keepdims=True)
    return inverse * (grad_normed - first - normed * second)


def pair_perm(dp_count, band_count):
    return [
        (dp * band_count + band, (dp ^ 1) * band_count + band)
        for dp in range(dp_count)
        for band in range(band_count)
    ]


def home_perm_back(dp_count, band_count, turn):
    pairs = []
    for dp in range(dp_count):
        for band in range(band_count):
            to_dp = dp - dp % 2 + band // 2
            to_band = 2 * (dp % 2) + (band + turn) % 2
            pairs.append((dp * band_count + band, to_dp * band_count + to_band))
    return pairs


def send_home(rows, band, perms):
    odd = lax.rem(band, 2) == 1
    first = jnp.where(odd, rows[1], rows[0])
    second = jnp.where(odd, rows[0], rows[1])
    got = [lax.ppermute(part, ("dp", "band"), perm) for part, perm in zip((first, second), perms)]
    return jnp.stack([jnp.where(odd, got[1], got[0]), jnp.where(odd, got[0], got[1])])


def position_rows(row_index, col_index, width):
    quarter = width // 4
    frequency = 10000.0 ** (-jnp.arange(quarter, dtype=jnp.float32) / quarter)
    angles = jnp.arange(128, dtype=jnp.float32)[:, None] * frequency
    table = jnp.concatenate([jnp.sin(angles), jnp.cos(angles)], -1)
    places = jnp.arange(128, dtype=jnp.int32)
    pick = lambda index: jnp.dot(
        (index[:, None] == places).astype(jnp.float32), table, precision=lax.Precision.HIGHEST
    )
    return jnp.concatenate([pick(row_index), pick(col_index)], -1)


def over_groups(piece, dp_count):
    if dp_count == 8:
        return piece
    groups = [[rank + 8 * group for group in range(dp_count // 8)] for rank in range(8)]
    return lax.psum(piece.astype(jnp.float32), "dp", axis_index_groups=groups)


def every_group(piece, dp_count):
    if dp_count == 8:
        return piece[None]
    groups = [[rank + 8 * group for group in range(dp_count // 8)] for rank in range(8)]
    return lax.all_gather(piece, "dp", axis_index_groups=groups)


def own_piece(vector, count, band_place):
    return lax.dynamic_slice_in_dim(vector, band_place * count, count, 0)


def body(
    tokens,
    condition,
    patch_grid,
    ada_weight,
    ada_bias,
    qkv_weight,
    query_bias,
    value_bias,
    proj_weight,
    proj_bias,
    inner_weight,
    inner_bias,
    outer_weight,
    outer_bias,
    cotangent,
):
    both = ("dp", "band")
    dp_count = lax.axis_size("dp")
    band_count = lax.axis_size("band")
    images, band_slots, width = tokens.shape
    band = lax.axis_index("band")
    dp = lax.axis_index("dp")
    core = lax.rem(dp, 2)
    hidden = inner_weight.shape[1]
    part_rows = qkv_weight.shape[0]
    siblings = pair_perm(dp_count, band_count)
    homes = [home_perm_back(dp_count, band_count, turn) for turn in range(2)]

    condition_f = condition.astype(jnp.float32)
    activated = jax.nn.silu(condition_f).astype(jnp.bfloat16)
    own_activated = lax.dynamic_slice_in_dim(activated, band * part_rows, part_rows, 1)
    share = jnp.dot(own_activated, ada_weight, preferred_element_type=jnp.float32)
    share = share + lax.dynamic_update_slice_in_dim(
        jnp.zeros((ada_weight.shape[1],), jnp.float32),
        ada_bias.astype(jnp.float32),
        band * ada_bias.shape[0],
        0,
    )
    biases = jnp.concatenate([query_bias, value_bias, proj_bias, inner_bias, outer_bias])
    bias_count = biases.shape[0]
    mod_count = share.shape[1]
    note = jnp.concatenate(
        [
            share,
            jnp.broadcast_to(biases.astype(jnp.float32), (images, bias_count)),
            condition_f,
            patch_grid.astype(jnp.float32),
        ],
        1,
    )
    note_rows = -(-note.shape[1] // 1024) * 8
    note = jnp.pad(note, ((0, 0), (0, note_rows * 128 - note.shape[1])))
    note = note.reshape(images, note_rows, 128)
    first_weight = jnp.concatenate([qkv_weight, proj_weight], 1)
    first_full, inner_full, outer_full, tokens_here, cotangent_here, notes = gather_weights(
        first_weight, inner_weight, outer_weight, tokens, cotangent, note, width
    )
    first_full = first_full.reshape(width, -1)
    inner_full = inner_full.reshape(width, hidden)
    outer_full = outer_full.reshape(hidden, width)
    qkv_full = first_full[:, : 3 * width]
    proj_full = first_full[:, 3 * width :]
    notes = notes.reshape(band_count, -1)
    modulation = jnp.sum(notes[:, :mod_count], 0)
    pieces = []
    at = mod_count
    for piece in (query_bias, value_bias, proj_bias, inner_bias, outer_bias):
        pieces.append(notes[:, at : at + piece.shape[0]].reshape(-1))
        at += piece.shape[0]
    query_bias_full, value_bias_full, proj_bias_full, inner_bias_full, outer_bias_full = pieces
    condition_here = notes[0, at : at + width]
    at += width
    grid_rows = notes[0, at].astype(jnp.int32)
    grid_cols = notes[0, at + 1].astype(jnp.int32)

    rows = images * band_slots
    ids = core * rows + jnp.arange(rows, dtype=jnp.int32)
    within = ids % band_slots
    band_rows = grid_rows // band_count
    is_valid = within < band_rows * grid_cols
    row_index = ids // band_slots * band_rows + within // grid_cols
    col_index = within % grid_cols

    shift_one, scale_one, gate_one, shift_two, scale_two, gate_two = [
        modulation[index * width : (index + 1) * width] for index in range(6)
    ]
    residual = tokens_here.reshape(rows, width).astype(jnp.float32) + position_rows(
        row_index, col_index, width
    )
    normed_one, inverse_one = normalize(residual)
    attn_in = (normed_one * (1.0 + scale_one) + shift_one).astype(jnp.bfloat16)
    projected = jnp.dot(attn_in, qkv_full, preferred_element_type=jnp.float32)
    query_rows = (projected[:, :width] + query_bias_full).astype(jnp.bfloat16)
    key_value = (
        projected[:, width:] + jnp.concatenate([jnp.zeros((width,), jnp.float32), value_bias_full])
    ).astype(jnp.bfloat16)
    other_key_value = lax.ppermute(key_value, both, siblings)
    valid_count = (band_rows * grid_cols).reshape(1)
    mixed_rows, tops = attend(valid_count, query_rows, key_value, other_key_value, band_slots)
    attended = jnp.dot(mixed_rows, proj_full, preferred_element_type=jnp.float32) + proj_bias_full
    middle = residual + gate_one * attended
    normed_two, inverse_two = normalize(middle)
    mlp_in = (normed_two * (1.0 + scale_two) + shift_two).astype(jnp.bfloat16)
    hidden_pre = jnp.dot(mlp_in, inner_full, preferred_element_type=jnp.float32) + inner_bias_full
    hidden_act = jax.nn.gelu(hidden_pre, approximate=True).astype(jnp.bfloat16)
    mlp_out = jnp.dot(hidden_act, outer_full, preferred_element_type=jnp.float32) + outer_bias_full
    block_out = (middle + gate_two * mlp_out).astype(jnp.bfloat16)
    block_home = send_home(block_out.reshape(images, band_slots, width), band, homes)

    grad_out = cotangent_here.reshape(rows, width).astype(jnp.float32) * is_valid[:, None].astype(
        jnp.float32
    )
    grad_gate_two = jnp.sum(grad_out * mlp_out, 0)
    grad_mlp = (gate_two * grad_out).astype(jnp.bfloat16)
    gelu_back = jax.vjp(partial(jax.nn.gelu, approximate=True), hidden_pre)[1]
    blocks = (band_count, 2, part_rows // 2, width)
    grad_outer = rows_dot(hidden_act, grad_mlp).astype(jnp.bfloat16).reshape(
        band_count, 4, 2, part_rows // 2, width
    )
    grad_outer_bias = jnp.sum(grad_mlp.astype(jnp.float32), 0)
    grad_hidden = lanes_dot(grad_mlp, outer_full)
    grad_pre = gelu_back(grad_hidden)[0].astype(jnp.bfloat16)
    grad_inner = [
        rows_dot(mlp_in, grad_pre[:, t * width : (t + 1) * width]).astype(jnp.bfloat16).reshape(blocks)
        for t in range(4)
    ]
    grad_inner_bias = jnp.sum(grad_pre.astype(jnp.float32), 0)
    grad_mlp_in = lanes_dot(grad_pre, inner_full)
    grad_shift_two = jnp.sum(grad_mlp_in, 0)
    grad_scale_two = jnp.sum(grad_mlp_in * normed_two, 0)
    grad_middle = grad_out + norm_back(grad_mlp_in * (1.0 + scale_two), normed_two, inverse_two)
    grad_gate_one = jnp.sum(grad_middle * attended, 0)
    grad_attended = (gate_one * grad_middle).astype(jnp.bfloat16)
    grad_proj = rows_dot(mixed_rows, grad_attended).astype(jnp.bfloat16)
    grad_proj_bias = jnp.sum(grad_attended.astype(jnp.float32), 0)
    grad_mixed = lanes_dot(grad_attended, proj_full).astype(jnp.bfloat16)
    (outer_sum, inner_sum), grad_query, own_terms, far_terms = reduce_attend(
        [[grad_outer], grad_inner], valid_count, query_rows, key_value, other_key_value, grad_mixed, tops,
        band_slots, 1,
    )
    other_terms = lax.ppermute(far_terms, both, siblings)
    grad_key_value = (own_terms.astype(jnp.float32) + other_terms.astype(jnp.float32)).astype(
        jnp.bfloat16
    )
    grad_qkv = jnp.concatenate([grad_query, grad_key_value], -1)
    grad_first = [
        rows_dot(attn_in, part).astype(jnp.bfloat16).reshape(blocks)
        for part in (grad_query, grad_key_value[:, :width], grad_key_value[:, width:])
    ]
    grad_attn_in = lanes_dot(grad_qkv, qkv_full)
    grad_query_bias = jnp.sum(grad_query.astype(jnp.float32), 0)
    grad_value_bias = jnp.sum(grad_key_value[:, width:].astype(jnp.float32), 0)
    grad_shift_one = jnp.sum(grad_attn_in, 0)
    grad_scale_one = jnp.sum(grad_attn_in * normed_one, 0)
    grad_tokens = grad_middle + norm_back(grad_attn_in * (1.0 + scale_one), normed_one, inverse_one)
    tokens_home = send_home(
        grad_tokens.astype(jnp.bfloat16).reshape(images, band_slots, width), band, homes
    ).astype(jnp.float32)

    part_mod = jnp.concatenate(
        [grad_shift_one, grad_scale_one, grad_gate_one, grad_shift_two, grad_scale_two, grad_gate_two]
    )
    part_mod = jnp.concatenate([part_mod, 0.5 * condition_here]).reshape(-1, 128)
    part_mod = jnp.pad(part_mod, ((0, -part_mod.shape[0] % 16), (0, 0)))
    part_bias = jnp.concatenate(
        [grad_query_bias, grad_value_bias, grad_proj_bias, grad_inner_bias, grad_outer_bias]
    ).reshape(-1, 128)
    (first_sum,), every, bias_grads, grad_act = reduce_last(
        [grad_first + [grad_proj.reshape(blocks)]], part_mod, part_bias, ada_weight, images, 2
    )
    every = every_group(every, dp_count)
    bias_grads = over_groups(bias_grads, dp_count).reshape(-1)
    every = jnp.swapaxes(every, 1, 2).reshape(dp_count * images, -1)
    every_mod = every[:, :mod_count]
    every_condition = every[:, mod_count : mod_count + width]
    every_activated = jax.nn.silu(every_condition.astype(jnp.float32)).astype(jnp.bfloat16)
    every_activated = lax.dynamic_slice_in_dim(every_activated, band * part_rows, part_rows, 1)
    grad_ada = rows_dot(every_activated, every_mod)
    grad_ada_bias = own_piece(jnp.sum(every_mod.astype(jnp.float32), 0), ada_bias.shape[0], band)
    grad_act = jnp.swapaxes(grad_act[:, :images, :part_rows], 0, 1).reshape(images, width)
    grad_condition = jax.vjp(jax.nn.silu, condition_f)[1](grad_act)[0]

    def side_by_side(units):
        return jnp.concatenate([unit.reshape(part_rows, width) for unit in units], 1).astype(jnp.float32)

    first_sum, inner_sum, outer_sum = [
        over_groups(piece, dp_count) for piece in (first_sum, inner_sum, outer_sum)
    ]
    weight_sums = dict(
        qkv=side_by_side([first_sum[t] for t in range(3)]),
        proj=first_sum[3].reshape(part_rows, width).astype(jnp.float32),
        inner=side_by_side([inner_sum[t] for t in range(4)]),
        outer=outer_sum.reshape(4 * part_rows, width).astype(jnp.float32),
    )
    bias_parts = []
    at = 0
    for piece in (query_bias, value_bias, proj_bias, inner_bias, outer_bias):
        whole = piece.shape[0] * band_count
        bias_parts.append(own_piece(bias_grads[at : at + whole], piece.shape[0], band))
        at += whole
    return (
        block_home,
        tokens_home,
        grad_condition,
        grad_ada,
        grad_ada_bias,
        weight_sums["qkv"],
        bias_parts[0],
        bias_parts[1],
        weight_sums["proj"],
        bias_parts[2],
        weight_sums["inner"],
        bias_parts[3],
        weight_sums["outer"],
        bias_parts[4],
    )


def solution(mesh):
    placed = (
        P("dp", "band", None),
        P("dp", None),
        P("dp", None),
        P("band", None),
        P("band"),
        P("band", None),
        P("band"),
        P("band"),
        P("band", None),
        P("band"),
        P("band", None),
        P("band"),
        P("band", None),
        P("band"),
        P("dp", "band", None),
    )
    return jax.shard_map(
        body,
        mesh=mesh,
        in_specs=placed,
        out_specs=(
            P("dp", "band", None),
            P("dp", "band", None),
            P("dp", None),
            P("band", None),
            P("band"),
            P("band", None),
            P("band"),
            P("band"),
            P("band", None),
            P("band"),
            P("band", None),
            P("band"),
            P("band", None),
            P("band"),
        ),
        check_vma=False,
    )
```

```python
import functools
from functools import partial

import jax
import jax.numpy as jnp
from jax import lax
from jax.experimental import pallas as pl
from jax.experimental.pallas import tpu as pltpu
from jax.sharding import PartitionSpec as P

HEAD_DIM = 72


MESH = pl.DeviceIdType.MESH
NB = 4


def normalize(values):
    average = jnp.mean(values, -1, keepdims=True)
    centered = values - average
    variance = jnp.mean(centered * centered, -1, keepdims=True)
    inverse = lax.rsqrt(variance + 1e-06)
    return (centered * inverse, inverse)


def norm_back(grad_normed, normed, inverse):
    first = jnp.mean(grad_normed, -1, keepdims=True)
    second = jnp.mean(grad_normed * normed, -1, keepdims=True)
    return inverse * (grad_normed - first - normed * second)


LANES = 128
PACK_ROWS = 128


def pack_heads(source, first, heads_ref, row0, rows, tail):
    heads = heads_ref.shape[0]

    @pl.loop(0, rows // PACK_ROWS)
    def _(step):
        at = pl.multiple_of(step * PACK_ROWS, PACK_ROWS)
        block = source[pl.ds(at, PACK_ROWS), first : first + heads * HEAD_DIM]
        end = tail(at)
        for h in range(heads):
            part = block[:, h * HEAD_DIM : (h + 1) * HEAD_DIM]
            heads_ref[h, pl.ds(row0 + at, PACK_ROWS), :] = jnp.concatenate([part, end], 1)


def unpack_heads(heads_ref, row0, rows, target, first):
    heads = heads_ref.shape[0]

    @pl.loop(0, rows // PACK_ROWS)
    def _(step):
        at = pl.multiple_of(step * PACK_ROWS, PACK_ROWS)
        parts = [heads_ref[h, pl.ds(row0 + at, PACK_ROWS), :][:, :HEAD_DIM] for h in range(heads)]
        target[pl.ds(at, PACK_ROWS), first : first + heads * HEAD_DIM] = jnp.concatenate(parts, 1)


def flat_tail(value):
    def tail(at):
        lane = lax.broadcasted_iota(jnp.int32, (PACK_ROWS, LANES - HEAD_DIM), 1)
        return jnp.where(lane == 0, value, 0.0).astype(jnp.bfloat16)

    return tail


def key_tail(valid_count, band_slots):
    def tail(at):
        shape = (PACK_ROWS, LANES - HEAD_DIM)
        lane = lax.broadcasted_iota(jnp.int32, shape, 1)
        slot = lax.rem(at + lax.broadcasted_iota(jnp.int32, shape, 0), band_slots)
        return jnp.where(jnp.logical_and(lane == 0, slot >= valid_count), -1e30, 0.0).astype(jnp.bfloat16)

    return tail


def lanes_dot(left, right):
    return lax.dot_general(left, right, (((1,), (1,)), ((), ())), preferred_element_type=jnp.float32)


def rows_dot(left, right):
    return lax.dot_general(left, right, (((0,), (0,)), ((), ())), preferred_element_type=jnp.float32)


SCORE_SCALE = HEAD_DIM ** (-0.5)


def attend_block(h, qh, kh, vh, top_ref):
    rows = qh.shape[1]
    for block in range(2):
        at = pl.ds(block * rows // 2, rows // 2)
        scores = lanes_dot(kh[h], qh[h, at, :]) * SCORE_SCALE
        top = jnp.max(scores, 0, keepdims=True)
        weights = jnp.exp(scores - top)
        total = jnp.sum(weights, 0, keepdims=True)
        low = (weights * (1.0 / total)).astype(jnp.bfloat16)
        mixed = rows_dot(vh[h], low)
        qh[h, at, :] = jnp.transpose(mixed).astype(jnp.bfloat16)
        top_ref[h, :, at] = jnp.broadcast_to(top + jnp.log(total), (8, rows // 2))


def attend_head(h, qh, kh, vh, gh, top_ref):
    query = qh[h]
    key = kh[h]
    grad = gh[h]
    probs = jnp.exp(lanes_dot(key, query) * SCORE_SCALE - top_ref[h, 0:1, :])
    grad_probs = lanes_dot(vh[h], grad)
    inner = jnp.sum(probs * grad_probs, 0, keepdims=True)
    grad_scores = (probs * (grad_probs - inner)).astype(jnp.bfloat16)
    vh[h] = jnp.dot(
        probs.astype(jnp.bfloat16), grad, preferred_element_type=jnp.float32
    ).astype(jnp.bfloat16)
    grad_query = rows_dot(key, grad_scores)
    kh[h] = (
        SCORE_SCALE * jnp.dot(grad_scores, query, preferred_element_type=jnp.float32)
    ).astype(jnp.bfloat16)
    qh[h] = (SCORE_SCALE * jnp.transpose(grad_query)).astype(jnp.bfloat16)


def compass():
    dp = lax.axis_index("dp")
    band = lax.axis_index("band")
    core = lax.rem(dp, 2)
    px = lax.rem(dp // 2, 2)
    py = lax.rem(dp // 4, 2)
    return dict(
        dp=dp, band=band, core=core, px=px, py=py, kind=2 * py + px,
        sib=dp + 1 - 2 * core, xdp=dp + 2 - 4 * px, ydp=dp + 4 - 8 * py,
    )


def add_rows(total, term):
    rows = total.shape[0]

    @pl.loop(0, rows // 16)
    def _(step):
        at = pl.ds(pl.multiple_of(step * 16, 16), 16)
        total[at, :] = (
            total[at, :].astype(jnp.float32) + term[at, :].astype(jnp.float32)
        ).astype(jnp.bfloat16)


def reduce_barrier(me):
    barrier = pltpu.get_barrier_semaphore()
    peers = [(me["xdp"], me["band"]), (me["ydp"], me["band"]), (me["sib"], me["band"])]
    peers += [(me["dp"], lax.rem(me["band"] + k, NB)) for k in range(1, NB)]
    for dp, band in peers:
        pl.semaphore_signal(
            barrier, inc=1, device_id={"dp": dp, "band": band}, device_id_type=MESH
        )
    pl.semaphore_wait(barrier, len(peers))


def run_all(batch):
    for do in batch:
        do()


REDUCE_ORDER = (1, 3, 2, 0)


def reduce_scratch(phases, half, width):
    bf = jnp.bfloat16
    n = phases * NB
    D = pltpu.SemaphoreType.DMA
    return dict(
        acc=pltpu.VMEM((n, 4, half, width), bf),
        recv_a=pltpu.VMEM((n, 4, half, width), bf),
        recv_b=pltpu.VMEM((n, 2, half, width), bf),
        recv_c=pltpu.VMEM((n, half, width), bf),
        recv_z=pltpu.VMEM((phases, NB, half, width), bf),
        a_send=D((n,)), a_recv=D((n,)), a_own=D((n,)),
        b_send=D((n, 2)), b_recv=D((n,)), c_send=D((n,)), c_recv=D((n,)),
        z_send=D((phases, NB)), z_recv=D((phases, NB)),
        d_send=D((phases, 4)), d_recv=D((phases, 4)), d_own=D((phases,)),
    )


def reduce_steps(me, phases, source, out, sc, beside=()):
    dp, band, core, px, py, kind = (me[k] for k in ("dp", "band", "core", "px", "py", "kind"))
    here = lambda d: {"dp": d, "band": band}
    chunks = [(phase, k) for phase in range(phases) for k in REDUCE_ORDER]
    n = len(chunks)
    flip = lambda v: 1 - v
    sends = []

    def remote(src, dst, ss, rs, to):
        return pltpu.make_async_remote_copy(
            src_ref=src, dst_ref=dst, send_sem=ss, recv_sem=rs, device_id=to, device_id_type=MESH
        )

    def go(make):
        make().start()
        sends.append(make)

    def start_a(s):
        phase, k = chunks[s]
        b = lax.rem(band + k, NB)
        for t in range(4):
            remote(
                source(phase, b, t, flip(core)), sc["recv_a"].at[s, t],
                sc["a_send"].at[s], sc["a_recv"].at[s], here(me["sib"]),
            ).start()
            pltpu.make_async_copy(
                source(phase, b, t, core), sc["acc"].at[s, t], sc["a_own"].at[s]
            ).start()

    def first(s, j, send):
        if s % 2 == 0:
            return 2 * j + (flip(px) if send else px)
        return 2 * (flip(py) if send else py) + j

    def second(s, send):
        if s % 2 == 0:
            return 2 * (flip(py) if send else py) + px
        return 2 * py + (flip(px) if send else px)

    def send_b(s, j):
        return remote(
            sc["acc"].at[s, first(s, j, True)], sc["recv_b"].at[s, j], sc["b_send"].at[s, j],
            sc["b_recv"].at[s], here(me["xdp"] if s % 2 == 0 else me["ydp"]),
        )

    def send_c(s):
        return remote(
            sc["acc"].at[s, second(s, True)], sc["recv_c"].at[s], sc["c_send"].at[s],
            sc["c_recv"].at[s], here(me["ydp"] if s % 2 == 0 else me["xdp"]),
        )

    def send_z(s):
        phase, k = chunks[s]
        return remote(
            sc["acc"].at[s, kind], sc["recv_z"].at[phase, k], sc["z_send"].at[phase, k],
            sc["z_recv"].at[phase, k], {"dp": dp, "band": lax.rem(band + k, NB)},
        )

    def send_d(phase, slot):
        ss, rs = sc["d_send"].at[phase, slot], sc["d_recv"].at[phase, slot]
        even = phase % 2 == 0
        if slot == 0:
            unit = out[phase].at[kind, core]
            return remote(sc["recv_z"].at[phase, 0], unit, ss, rs, here(me["xdp"] if even else me["ydp"]))
        if slot == 3:
            row = out[phase].at[:, core]
            return remote(row, row, ss, rs, here(me["sib"]))
        if even:
            pair = out[phase].at[pl.ds(2 * py, 2), core]
            return remote(pair, pair, ss, rs, here(me["ydp"]))
        unit = out[phase].at[2 * (slot - 1) + px, core]
        return remote(unit, unit, ss, rs, here(me["xdp"]))

    def a_to_b(s):
        acc, got = sc["acc"], sc["recv_a"]
        pltpu.make_async_copy(got.at[s], acc.at[s], sc["a_own"].at[s]).wait()
        whole = remote(got.at[s], got.at[s], sc["a_send"].at[s], sc["a_recv"].at[s], here(me["sib"]))
        whole.wait_recv()
        for j in range(2):
            t = first(s, j, True)
            add_rows(acc.at[s, t], got.at[s, t])
            go(partial(send_b, s, j))
        for j in range(2):
            t = first(s, j, False)
            add_rows(acc.at[s, t], got.at[s, t])
        whole.wait_send()

    def b_to_c(s):
        acc, got = sc["acc"], sc["recv_b"]
        remote(got.at[s], got.at[s], sc["b_send"].at[s, 0], sc["b_recv"].at[s], here(me["xdp"])).wait_recv()
        away = flip(py) if s % 2 == 0 else flip(px)
        stay = py if s % 2 == 0 else px
        add_rows(acc.at[s, second(s, True)], got.at[s, away])
        go(partial(send_c, s))
        add_rows(acc.at[s, kind], got.at[s, stay])

    def c_to_z(s):
        acc, got = sc["acc"], sc["recv_c"]
        phase, k = chunks[s]
        remote(got.at[s], got.at[s], sc["c_send"].at[s], sc["c_recv"].at[s], here(me["xdp"])).wait_recv()
        add_rows(acc.at[s, kind], got.at[s])
        if k != 0:
            go(partial(send_z, s))

    def z_to_d(phase):
        s = phase * NB + NB - 1
        acc, got = sc["acc"], sc["recv_z"]
        for k in range(1, NB):
            remote(
                got.at[phase, k], got.at[phase, k], sc["z_send"].at[phase, k],
                sc["z_recv"].at[phase, k], here(dp),
            ).wait_recv()
        rows = acc.shape[2]

        @pl.loop(0, rows // 16)
        def _(step):
            at = pl.ds(pl.multiple_of(step * 16, 16), 16)
            total = acc[s, kind, at, :].astype(jnp.float32)
            for k in range(1, NB):
                total = total + got[phase, k, at, :].astype(jnp.float32)
            got[phase, 0, at, :] = total.astype(jnp.bfloat16)

        unit = out[phase].at[kind, core]
        own = pltpu.make_async_copy(got.at[phase, 0], unit, sc["d_own"].at[phase])
        own.start()
        go(partial(send_d, phase, 0))
        own.wait()

    def d_second(phase):
        even = phase % 2 == 0
        mate = 2 * py + flip(px) if even else 2 * flip(py) + px
        unit = out[phase].at[mate, core]
        remote(unit, unit, sc["d_send"].at[phase, 0], sc["d_recv"].at[phase, 0], here(me["xdp"])).wait_recv()
        for slot in (1,) if even else (1, 2):
            go(partial(send_d, phase, slot))

    def d_third(phase):
        if phase % 2 == 0:
            pair = out[phase].at[pl.ds(2 * flip(py), 2), core]
            remote(pair, pair, sc["d_send"].at[phase, 1], sc["d_recv"].at[phase, 1], here(me["ydp"])).wait_recv()
        else:
            for j in range(2):
                unit = out[phase].at[2 * j + flip(px), core]
                remote(unit, unit, sc["d_send"].at[phase, 1 + j], sc["d_recv"].at[phase, 1 + j], here(me["xdp"])).wait_recv()
        go(partial(send_d, phase, 3))

    def d_last(phase):
        row = out[phase].at[:, flip(core)]
        remote(row, row, sc["d_send"].at[phase, 3], sc["d_recv"].at[phase, 3], here(me["sib"])).wait_recv()

    def finish():
        for make in sends:
            make().wait_send()

    steps = [partial(run_all, [partial(start_a, s) for s in range(n)])]
    late = {}
    for phase in range(phases):
        end = (phase + 1) * NB - 1
        for lag, do in ((4, z_to_d), (5, d_second), (6, d_third), (7, d_last)):
            late.setdefault(end + lag, []).append(partial(do, phase))
    for s in range(n + 8):
        batch = []
        if s < n:
            batch.append(partial(a_to_b, s))
        if 0 <= s - 1 < n:
            batch.append(partial(b_to_c, s - 1))
        if 0 <= s - 2 < n:
            batch.append(partial(c_to_z, s - 2))
        if s < len(beside):
            batch.append(beside[s])
        batch += late.get(s, [])
        if batch:
            steps.append(partial(run_all, batch))
    steps.append(finish)
    return steps


def reduce_sources(counts, refs):
    grads = []
    at = 0
    for count in counts:
        grads.append(refs[at : at + count])
        at += count

    def source(phase, b, t, h):
        if len(grads[phase]) == 1:
            return grads[phase][0].at[b, t, h]
        return grads[phase][t].at[b, h]

    return source


def small_scratch(mod_rows, bias_rows, cond_rows, cond_cols):
    D = pltpu.SemaphoreType.DMA
    f32 = jnp.float32
    return dict(
        s_core=pltpu.VMEM((mod_rows + bias_rows, 128), f32),
        s_every=pltpu.VMEM((NB, 4, mod_rows, 128), jnp.bfloat16),
        s_bias=pltpu.VMEM((3, bias_rows, 128), f32),
        s_got=pltpu.VMEM((2 + NB, bias_rows, 128), f32),
        s_flat=pltpu.VMEM((8, mod_rows, 128), f32),
        s_cond=pltpu.VMEM((NB, cond_rows, cond_cols), f32),
        s_send=D((8,)), s_recv=D((8,)), sz_send=D((2, NB)), sz_recv=D((2, NB)),
        sc_send=D((NB,)), sc_recv=D((NB,)),
    )


def small_steps(me, mods, images, small_ref, ada_ref, every_ref, bias_ref, cond_ref, sc):
    dp, band, core, px, py, kind = (me[k] for k in ("dp", "band", "core", "px", "py", "kind"))
    here = lambda d: {"dp": d, "band": band}
    every, bias, got, cond = sc["s_every"], sc["s_bias"], sc["s_got"], sc["s_cond"]
    mod_rows = every.shape[2]
    flip = lambda v: 1 - v

    def remote(src, dst, ss, rs, to):
        return pltpu.make_async_remote_copy(
            src_ref=src, dst_ref=dst, send_sem=ss, recv_sem=rs, device_id=to, device_id_type=MESH
        )

    def plain(index, src, dst, to):
        return remote(src, dst, sc["s_send"].at[index], sc["s_recv"].at[index], to)

    def core_copy():
        return plain(0, small_ref, sc["s_core"], here(me["sib"]))

    def x_copies(mine):
        unit = every.at[band, kind if mine else 2 * py + flip(px)]
        return [
            plain(1, unit, unit, here(me["xdp"])),
            plain(2, bias.at[0], got.at[0], here(me["xdp"])),
        ]

    def y_copies(mine):
        pair = every.at[band, pl.ds(2 * (py if mine else flip(py)), 2)]
        return [
            plain(3, pair, pair, here(me["ydp"])),
            plain(4, bias.at[1], got.at[1], here(me["ydp"])),
        ]

    def z_copies(k, mine):
        to = {"dp": dp, "band": lax.rem(band + k, NB)}
        block = every.at[band if mine else lax.rem(band + NB - k, NB)]
        return [
            remote(block, block, sc["sz_send"].at[0, k], sc["sz_recv"].at[0, k], to),
            remote(bias.at[2], got.at[2 + k], sc["sz_send"].at[1, k], sc["sz_recv"].at[1, k], to),
        ]

    def cond_copy(k, mine):
        to = {"dp": dp, "band": lax.rem(band + k, NB)}
        block = cond.at[band if mine else lax.rem(band + NB - k, NB)]
        return remote(block, block, sc["sc_send"].at[k], sc["sc_recv"].at[k], to)

    def begin():
        core_copy().start()

    def cores():
        core_copy().wait()
        total = small_ref[...] + sc["s_core"][...]
        every[band, kind] = total[:mod_rows].astype(jnp.bfloat16)
        bias[0] = total[mod_rows:]
        for copy in x_copies(True):
            copy.start()

    def over_x():
        for copy in x_copies(True):
            copy.wait_send()
        for copy in x_copies(False):
            copy.wait_recv()
        bias[1] = bias[0] + got[0]
        for copy in y_copies(True):
            copy.start()

    def over_y():
        for copy in y_copies(True):
            copy.wait_send()
        for copy in y_copies(False):
            copy.wait_recv()
        bias[2] = bias[1] + got[1]
        for k in range(1, NB):
            for copy in z_copies(k, True):
                copy.start()

    def over_z():
        for k in range(1, NB):
            for copy in z_copies(k, True):
                copy.wait_send()
            for copy in z_copies(k, False):
                copy.wait_recv()
        bias_ref[...] = bias[2] + got[3] + got[4] + got[5]
        every_ref[...] = every[...]
        flat = sc["s_flat"]
        for i in range(images):
            flat[i] = every[images * core + i, kind].astype(jnp.float32)
        parts = mods // 128
        lead = flat.shape[0]
        total = jnp.zeros((lead, ada_ref.shape[0]), jnp.float32)
        for r in range(parts):
            left = jnp.concatenate(
                [flat[i, r : r + 1, :] for i in range(images)]
                + [jnp.zeros((lead - images, 128), jnp.float32)]
            ).astype(jnp.bfloat16)
            total = total + lanes_dot(left, ada_ref[:, r * 128 : (r + 1) * 128])
        pad = cond.shape[2] - total.shape[1]
        cond[band] = jnp.concatenate([total, jnp.zeros((lead, pad), jnp.float32)], 1)
        for k in range(1, NB):
            cond_copy(k, True).start()

    def conditions():
        for k in range(1, NB):
            cond_copy(k, True).wait_send()
            cond_copy(k, False).wait_recv()
        cond_ref[...] = cond[...]

    return [begin, cores, over_x, over_y, over_z, conditions]


def reduce_last_kernel(counts, mods, images, names, *refs):
    me = compass()
    phases = len(counts)
    at = sum(counts)
    source = reduce_sources(counts, refs)
    small_ref, ada_ref = refs[at : at + 2]
    out = refs[at + 2 : at + 2 + phases]
    every_ref, bias_ref, cond_ref = refs[at + 2 + phases : at + 5 + phases]
    sc = dict(zip(names, refs[at + 5 + phases :]))
    reduce_barrier(me)
    small = small_steps(me, mods, images, small_ref, ada_ref, every_ref, bias_ref, cond_ref, sc)
    small[0]()
    for step in reduce_steps(me, phases, source, out, sc, small[1:]):
        step()


def reduce_last(grads, mod_part, bias_part, ada_weight, images, collective_id):
    phases = len(grads)
    half, width = grads[0][0].shape[-2:]
    counts = tuple(len(phase) for phase in grads)
    mod_rows, bias_rows = mod_part.shape[0], bias_part.shape[0]
    cond_cols = -(-ada_weight.shape[0] // 128) * 128
    scratch = dict(**reduce_scratch(phases, half, width), **small_scratch(mod_rows, bias_rows, 8, cond_cols))
    any_, vmem = pl.BlockSpec(memory_space=pl.ANY), pl.BlockSpec(memory_space=pltpu.VMEM)
    outs = pl.pallas_call(
        partial(reduce_last_kernel, counts, ada_weight.shape[1], images, tuple(scratch)),
        out_shape=[jax.ShapeDtypeStruct((4, 2, half, width), jnp.bfloat16)] * phases
        + [
            jax.ShapeDtypeStruct((NB, 4, mod_rows, 128), jnp.bfloat16),
            jax.ShapeDtypeStruct((bias_rows, 128), jnp.float32),
            jax.ShapeDtypeStruct((NB, 8, cond_cols), jnp.float32),
        ],
        in_specs=[any_] * sum(counts) + [vmem] * 2,
        out_specs=[any_] * phases + [vmem] * 3,
        scratch_shapes=list(scratch.values()),
        compiler_params=pltpu.CompilerParams(
            collective_id=collective_id, has_side_effects=True, vmem_limit_bytes=56 * 2**20
        ),
        name="reduce_last",
    )(*[unit for phase in grads for unit in phase], jnp.concatenate([mod_part, bias_part]), ada_weight)
    return outs[:phases], outs[phases], outs[phases + 1], outs[phases + 2]


def reduce_attend_kernel(counts, band_slots, names, *refs):
    me = compass()
    phases = len(counts)
    at = sum(counts)
    source = reduce_sources(counts, refs)
    count_ref, q_ref, own_ref, far_ref, grad_ref, top_ref = refs[at : at + 6]
    at += 6
    out = refs[at : at + phases]
    dq_ref, down_ref, dfar_ref = refs[at + phases : at + phases + 3]
    sc = dict(zip(names, refs[at + phases + 3 :]))
    qh, kh, vh, gh, stage, stage_sem = (sc[k] for k in ("qh", "kh", "vh", "gh", "stage", "stage_sem"))
    rows, width = q_ref.shape
    heads = qh.shape[0]
    reduce_barrier(me)
    steps = reduce_steps(me, phases, source, out, sc)
    steps[0]()
    keys, plain, ones = key_tail(count_ref[0], band_slots), flat_tail(0.0), flat_tail(1.0)
    loads = [(q_ref, 0, qh, 0, ones), (grad_ref, 0, gh, 0, plain)]
    for row0, ref in ((0, own_ref), (rows, far_ref)):
        loads += [(ref, 0, kh, row0, keys), (ref, width, vh, row0, plain)]

    def load(i):
        ref, column = loads[i][:2]
        return pltpu.make_async_copy(ref.at[:, pl.ds(column, width)], stage.at[i % 2], stage_sem.at[i % 2])

    load(0).start()
    for i, (ref, column, heads_ref, row0, tail) in enumerate(loads):
        if i + 1 < len(loads):
            load(i + 1).start()
        load(i).wait()
        pack_heads(stage.at[i % 2], 0, heads_ref, row0, rows, tail)
    rest = steps[1:]

    @pl.loop(0, heads)
    def _(h):
        attend_head(h, qh, kh, vh, gh, top_ref)
        for i, step in enumerate(rest[:heads]):
            pl.when(h == i)(step)

    stores = [(qh, 0, dq_ref, 0)]
    for row0, ref in ((0, down_ref), (rows, dfar_ref)):
        stores += [(kh, row0, ref, 0), (vh, row0, ref, width)]

    def store(i):
        ref, column = stores[i][2:]
        return pltpu.make_async_copy(stage.at[i % 2], ref.at[:, pl.ds(column, width)], stage_sem.at[i % 2])

    for i, (heads_ref, row0, ref, column) in enumerate(stores):
        if i >= 2:
            store(i - 2).wait()
        unpack_heads(heads_ref, row0, rows, stage.at[i % 2], 0)
        store(i).start()
    for i in (len(stores) - 2, len(stores) - 1):
        store(i).wait()
    for step in rest[heads:]:
        step()


def reduce_attend(grads, count, query, own, far, grad, top, band_slots, collective_id):
    phases = len(grads)
    half, width = grads[0][0].shape[-2:]
    counts = tuple(len(phase) for phase in grads)
    rows = query.shape[0]
    heads = width // HEAD_DIM
    bf = jnp.bfloat16
    scratch = reduce_scratch(phases, half, width)
    scratch.update(
        qh=pltpu.VMEM((heads, rows, LANES), bf),
        kh=pltpu.VMEM((heads, 2 * rows, LANES), bf),
        vh=pltpu.VMEM((heads, 2 * rows, LANES), bf),
        gh=pltpu.VMEM((heads, rows, LANES), bf),
        stage=pltpu.VMEM((2, rows, width), bf),
        stage_sem=pltpu.SemaphoreType.DMA((2,)),
    )
    any_, vmem = pl.BlockSpec(memory_space=pl.ANY), pl.BlockSpec(memory_space=pltpu.VMEM)
    smem = pl.BlockSpec(memory_space=pltpu.SMEM)
    outs = pl.pallas_call(
        partial(reduce_attend_kernel, counts, band_slots, tuple(scratch)),
        out_shape=[jax.ShapeDtypeStruct((4, 2, half, width), bf)] * phases
        + [
            jax.ShapeDtypeStruct((rows, width), bf),
            jax.ShapeDtypeStruct((rows, 2 * width), bf),
            jax.ShapeDtypeStruct((rows, 2 * width), bf),
        ],
        in_specs=[any_] * sum(counts) + [smem] + [any_] * 4 + [vmem],
        out_specs=[any_] * (phases + 3),
        scratch_shapes=list(scratch.values()),
        compiler_params=pltpu.CompilerParams(
            collective_id=collective_id, has_side_effects=True, vmem_limit_bytes=60 * 2**20
        ),
        name="reduce_attend",
    )(*[unit for phase in grads for unit in phase], count, query, own, far, grad, top)
    return outs[:phases], outs[phases], outs[phases + 1], outs[phases + 2]


GATHER_ORDER = (1, 3, 2)
MOD_BLOCKS = 6
BLOCK = 128


def forward_scratch(half, ff, width, rows, note_rows, images):
    bf, f32 = jnp.bfloat16, jnp.float32
    D = pltpu.SemaphoreType.DMA
    heads = width // HEAD_DIM
    V = pltpu.VMEM
    return dict(
        qp=V((NB, 2, half, ff), bf), bounce_i=V((2, half, ff), bf), bounce_o=V((4, 2, half, width), bf),
        bounce_t=V((rows // images, width), bf), tok=V((images, rows // images, width), bf),
        notes=V((NB, note_rows, 128), f32), vec=V((16, width), f32),
        residual=V((rows, width), f32), attn_in=V((rows, width), bf), query=V((rows, width), bf),
        own=V((rows, 2 * width), bf), far=V((rows, 2 * width), bf), mixed=V((rows, width), bf),
        attended=V((rows, width), f32), mlp_in=V((rows, width), bf), tops=V((heads, 8, rows), f32),
        qh=V((heads, rows, LANES), bf), kh=V((heads, 2 * rows, LANES), bf), vh=V((heads, 2 * rows, LANES), bf),
        z_send=D((3, NB)), z_recv=D((3, NB)), a_send=D((9,)), a_recv=D((9,)), b_send=D((9, 2)), b_recv=D((9, 2)),
        c_send=D((9,)), c_recv=D((9,)), t_send=D((2, 2)), t_recv=D((2, 2)), m_send=D((2, 2)), m_recv=D((NB,)),
        local=D((4,)), kv_send=D((1,)), kv_recv=D((1,)), done=D((12,)),
    )


def gather_steps(me, width, ins, outs, tok_in, tok_out, cot_in, cot_out, note_in, note_out, sc):
    dp, band, core, px, py, kind = (me[k] for k in ("dp", "band", "core", "px", "py", "kind"))
    base = dp - core
    dev = lambda d, b: {"dp": d, "band": b}
    here = lambda d: dev(d, band)
    flip = lambda v: 1 - v
    order = [(ph, k) for ph in range(3) for k in GATHER_ORDER]
    sends = []

    def remote(src, dst, ss, rs, to):
        return pltpu.make_async_remote_copy(
            src_ref=src, dst_ref=dst, send_sem=ss, recv_sem=rs, device_id=to, device_id_type=MESH
        )

    def go(make):
        make().start()
        sends.append(make)

    def cols(t, n=1):
        return pl.ds(pl.multiple_of(t * width, 128), n * width)

    def unit(ph, b, t, h):
        return outs[ph].at[b, t, h] if ph == 2 else outs[ph].at[b, h, :, cols(t)]

    def pair(ph, b, h, y):
        return outs[ph].at[b, pl.ds(2 * y, 2), h] if ph == 2 else outs[ph].at[b, h, :, cols(2 * y, 2)]

    def row(ph, b, h):
        return outs[ph].at[b, :, h] if ph == 2 else outs[ph].at[b, h]

    def came(k):
        return lax.rem(band + NB - k, NB)

    def send_z(ph, k):
        src = ins[ph].at[kind, core] if ph == 2 else ins[ph].at[core, :, cols(kind)]
        return remote(
            src, unit(ph, band, kind, core), sc["z_send"].at[ph, k], sc["z_recv"].at[ph, k],
            dev(dp, lax.rem(band + k, NB)),
        )

    def send_a(s):
        ph, k = order[s]
        u = unit(ph, came(k), kind, core)
        return remote(u, u, sc["a_send"].at[s], sc["a_recv"].at[s], here(me["xdp"] if s % 2 == 0 else me["ydp"]))

    def b_copy(s, j, mine):
        ph, k = order[s]
        if s % 2 == 0:
            u = pair(ph, came(k), core, py if mine else flip(py))
            to = me["ydp"]
        else:
            u = unit(ph, came(k), 2 * j + (px if mine else flip(px)), core)
            to = me["xdp"]
        return remote(u, u, sc["b_send"].at[s, j], sc["b_recv"].at[s, j], here(to))

    def c_copy(s, mine):
        ph, k = order[s]
        u = row(ph, came(k), core if mine else flip(core))
        return remote(u, u, sc["c_send"].at[s], sc["c_recv"].at[s], here(me["sib"]))

    def z_start(ph):
        for k in GATHER_ORDER:
            go(partial(send_z, ph, k))

    def z_wait(s):
        ph, k = order[s]
        u = unit(ph, came(k), kind, core)
        remote(u, u, sc["z_send"].at[ph, k], sc["z_recv"].at[ph, k], here(dp)).wait_recv()
        go(partial(send_a, s))
        if k == GATHER_ORDER[1] and ph < 2:
            z_start(ph + 1)
        if k == GATHER_ORDER[2] and ph == 2:
            move(1, cot_in, cot_out, sc["bounce_t"])

    def a_wait(s):
        ph, k = order[s]
        got = 2 * py + flip(px) if s % 2 == 0 else 2 * flip(py) + px
        u = unit(ph, came(k), got, core)
        remote(u, u, sc["a_send"].at[s], sc["a_recv"].at[s], here(me["xdp"])).wait_recv()
        for j in range(1 if s % 2 == 0 else 2):
            go(partial(b_copy, s, j, True))

    def b_wait(s):
        for j in range(1 if s % 2 == 0 else 2):
            b_copy(s, j, False).wait_recv()
        go(partial(c_copy, s, True))

    def c_wait(s):
        c_copy(s, False).wait_recv()

    slot = lax.rem(band, 2)

    def image_copy(which, src, dst, i):
        to = dev(base + band // 2, 2 * core + i)
        return remote(src.at[i], dst.at[slot], sc["t_send"].at[which, i], sc["t_recv"].at[which, slot], to)

    def at_home(i):
        return jnp.logical_and(band // 2 == core, 2 * core + i == band)

    def move(which, src, dst, bounce=None):
        for i in range(2):

            @pl.when(at_home(i))
            def _():
                if bounce is None:
                    pltpu.make_async_copy(src.at[i], dst.at[slot], sc["t_recv"].at[which, slot]).start()
                else:
                    inward = pltpu.make_async_copy(src.at[i], bounce, sc["local"].at[3])
                    inward.start()
                    inward.wait()
                    pltpu.make_async_copy(bounce, dst.at[slot], sc["t_recv"].at[which, slot]).start()

            @pl.when(jnp.logical_not(at_home(i)))
            def _():
                image_copy(which, src, dst, i).start()

    def move_wait(which, src, dst):
        for i in range(2):

            @pl.when(jnp.logical_not(at_home(i)))
            def _():
                image_copy(which, src, dst, i).wait_send()

        for s in range(2):
            pltpu.make_async_copy(dst.at[s], dst.at[s], sc["t_recv"].at[which, s]).wait()

    def note_copy(i, c):
        return remote(
            note_in.at[i], note_out.at[band], sc["m_send"].at[i, c], sc["m_recv"].at[band],
            dev(base + c, 2 * core + i),
        )

    def note_home(i, c):
        return jnp.logical_and(c == core, 2 * core + i == band)

    def begin():
        for i in range(2):
            for c in range(2):

                @pl.when(note_home(i, c))
                def _():
                    pltpu.make_async_copy(note_in.at[i], note_out.at[band], sc["m_recv"].at[band]).start()

                @pl.when(jnp.logical_not(note_home(i, c)))
                def _():
                    note_copy(i, c).start()

        move(0, tok_in, tok_out)
        z_start(0)
        for ph, dst in enumerate((outs[0].at[band], sc["bounce_i"], sc["bounce_o"])):
            pltpu.make_async_copy(ins[ph], dst, sc["local"].at[ph]).start()

    def arrived():
        for i in range(2):
            for c in range(2):

                @pl.when(jnp.logical_not(note_home(i, c)))
                def _():
                    note_copy(i, c).wait_send()

        for b in range(NB):
            pltpu.make_async_copy(note_in.at[0], note_out.at[b], sc["m_recv"].at[b]).wait()
        move_wait(0, tok_in, tok_out)

    def place():
        for ph, dst in ((1, sc["bounce_i"]), (2, sc["bounce_o"])):
            pltpu.make_async_copy(ins[ph], dst, sc["local"].at[ph]).wait()
            pltpu.make_async_copy(dst, outs[ph].at[band], sc["local"].at[ph]).start()

    def first_here():
        pltpu.make_async_copy(ins[0], outs[0].at[band], sc["local"].at[0]).wait()

    def finish():
        for ph, src in ((1, sc["bounce_i"]), (2, sc["bounce_o"])):
            pltpu.make_async_copy(src, outs[ph].at[band], sc["local"].at[ph]).wait()
        move_wait(1, cot_in, cot_out)
        for make in sends:
            make().wait_send()

    return dict(
        begin=begin, arrived=arrived, place=place, first_here=first_here, finish=finish,
        z=z_wait, a=a_wait, b=b_wait, c=c_wait,
    )


def forward_kernel(names, band_slots, *refs):
    me = compass()
    qp_in, inner_in, outer_in, tok_in, cot_in, note_in, table_ref = refs[:7]
    (qp_out, inner_out, outer_out, cot_out, vec_out, residual_out, attn_out, query_out, own_out, far_out,
     tops_out, mixed_out, attended_out, mlp_out) = refs[7:21]
    sc = dict(zip(names, refs[21:]))
    rows, width = sc["residual"].shape
    heads = width // HEAD_DIM
    core = me["core"]
    qp, tok, notes, vec = sc["qp"], sc["tok"], sc["notes"], sc["vec"]

    barrier = pltpu.get_barrier_semaphore()
    peers = [(me["xdp"], me["band"]), (me["ydp"], me["band"]), (me["sib"], me["band"])]
    for k in range(1, NB):
        other = lax.rem(me["band"] + k, NB)
        peers += [(me["dp"], other), (me["sib"], other)]
    for d, b in peers:
        pl.semaphore_signal(barrier, inc=1, device_id={"dp": d, "band": b}, device_id_type=MESH)
    pl.semaphore_wait(barrier, len(peers))

    g = gather_steps(
        me, width, (qp_in, inner_in, outer_in), (qp, inner_out, outer_out), tok_in, tok, cot_in, cot_out,
        note_in, notes, sc,
    )
    saves = []

    def save(src, dst):
        copy = pltpu.make_async_copy(src, dst, sc["done"].at[len(saves)])
        copy.start()
        saves.append(copy)

    def run(text):
        for word in text.split():
            g[word[0]](int(word[1:]))

    g["begin"]()
    g["place"]()
    g["arrived"]()
    spread_notes(notes, vec, width)
    grid_rows = notes[0, 63:64, 0:1]
    grid_cols = notes[0, 63:64, 1:2]
    band_rows = jnp.floor(grid_rows * 0.25)
    valid_count = (band_rows * grid_cols).astype(jnp.int32)
    lane = lax.broadcasted_iota(jnp.int32, (1, width), 1)
    vec[15:16, :] = jnp.where(lane == 0, band_rows * grid_cols, 0.0)
    save(vec, vec_out)

    @pl.loop(0, rows // BLOCK)
    def _(step):
        at = pl.multiple_of(step * BLOCK, BLOCK)
        sub = pl.ds(at, BLOCK)
        per_image = band_slots // BLOCK
        within = (
            lax.rem(step, per_image) * BLOCK + lax.broadcasted_iota(jnp.int32, (BLOCK, 1), 0)
        ).astype(jnp.float32)
        down = jnp.floor((within + 0.5) / grid_cols)
        place = (2 * core + step // per_image).astype(jnp.float32)
        picks = []
        for index in (place * band_rows + down, within - down * grid_cols):
            lanes = lax.broadcasted_iota(jnp.int32, (BLOCK, 128), 1).astype(jnp.float32)
            pick = jnp.where(lanes == index, 1.0, 0.0).astype(jnp.bfloat16)
            part = [jnp.dot(pick, table_ref[i], preferred_element_type=jnp.float32) for i in range(3)]
            picks.append(part[0] + (part[1] + part[2]))
        token = tok[step // per_image, pl.ds(lax.rem(step, per_image) * BLOCK, BLOCK), :]
        residual = token.astype(jnp.float32) + jnp.concatenate(picks, 1)
        sc["residual"][sub, :] = residual
        normed = normalize(residual)[0]
        sc["attn_in"][sub, :] = (normed * (1.0 + vec[1:2, :]) + vec[0:1, :]).astype(jnp.bfloat16)

    save(sc["residual"], residual_out)
    save(sc["attn_in"], attn_out)
    run("z0 z1 a0 z2 a1 b0 a2 b1 c0 b2 c1")
    g["first_here"]()
    run("z3 c2")
    save(qp, qp_out)
    tile = width // 3
    full = NB * 2 * qp.shape[2]

    def product(left_ref, first, step):
        at = pl.ds(pl.multiple_of(first + step * tile, 128), tile)
        return jnp.dot(
            left_ref[...], qp[:, :, :, at].reshape(full, tile), preferred_element_type=jnp.float32
        )

    def here(step):
        return pl.ds(pl.multiple_of(step * tile, 128), tile)

    @pl.loop(0, 3)
    def _(step):
        sc["own"][:, here(step)] = product(sc["attn_in"], width, step).astype(jnp.bfloat16)

    run("z4 a3")

    @pl.loop(0, 3)
    def _(step):
        value = product(sc["attn_in"], 2 * width, step) + vec[7:8, here(step)]
        sc["own"][:, here(step + 3)] = value.astype(jnp.bfloat16)

    swap = pltpu.make_async_remote_copy(
        src_ref=sc["own"], dst_ref=sc["far"], send_sem=sc["kv_send"].at[0], recv_sem=sc["kv_recv"].at[0],
        device_id={"dp": me["sib"], "band": me["band"]}, device_id_type=MESH,
    )
    swap.start()
    run("z5 a4 b3")

    @pl.loop(0, 3)
    def _(step):
        value = product(sc["attn_in"], 0, step) + vec[6:7, here(step)]
        sc["query"][:, here(step)] = value.astype(jnp.bfloat16)

    save(sc["query"], query_out)
    save(sc["own"], own_out)
    qh, kh, vh = sc["qh"], sc["kh"], sc["vh"]
    keys, plain = key_tail(valid_count, band_slots), flat_tail(0.0)
    pack_heads(sc["query"], 0, qh, 0, rows, flat_tail(1.0))
    pack_heads(sc["own"], 0, kh, 0, rows, keys)
    pack_heads(sc["own"], width, vh, 0, rows, plain)
    swap.wait()
    save(sc["far"], far_out)
    pack_heads(sc["far"], 0, kh, rows, rows, keys)
    pack_heads(sc["far"], width, vh, rows, rows, plain)
    beside = ["z6 a5 b4 c3", "", "z7 a6 b5 c4", "", "", "z8 a7 b6 c5", "", "", "a8 b7 c6", "", "", "b8 c7", "", "", "c8"]

    @pl.loop(0, heads)
    def _(h):
        attend_block(h, qh, kh, vh, sc["tops"])
        for i, text in enumerate(beside):
            if text:
                pl.when(h == i)(partial(run, text))

    unpack_heads(qh, 0, rows, sc["mixed"], 0)
    save(sc["tops"], tops_out)
    save(sc["mixed"], mixed_out)

    @pl.loop(0, 3)
    def _(step):
        sc["attended"][:, here(step)] = product(sc["mixed"], 3 * width, step) + vec[8:9, here(step)]

    save(sc["attended"], attended_out)

    @pl.loop(0, rows // BLOCK)
    def _(step):
        sub = pl.ds(pl.multiple_of(step * BLOCK, BLOCK), BLOCK)
        middle = sc["residual"][sub, :] + vec[2:3, :] * sc["attended"][sub, :]
        normed = normalize(middle)[0]
        sc["mlp_in"][sub, :] = (normed * (1.0 + vec[4:5, :]) + vec[3:4, :]).astype(jnp.bfloat16)

    save(sc["mlp_in"], mlp_out)
    g["finish"]()
    for copy in saves:
        copy.wait()


NOTE_COND, NOTE_GRID, NOTE_BIAS = 54, 63, 64


def spread_notes(notes, vec, width):
    lines = width // 128
    share = notes.shape[0]
    total = notes[0, 0:NOTE_GRID, :] + 0.0
    for b in range(1, share):
        total = total + notes[b, 0:NOTE_GRID, :]

    def flat(block, first):
        return jnp.concatenate([block[first + i : first + i + 1, :] for i in range(lines)], 1)

    for index in range(MOD_BLOCKS):
        vec[index : index + 1, :] = flat(total, index * lines)
    small = width // share
    for index in range(4):
        parts = []
        for b in range(share):
            first = NOTE_BIAS + 3 * index
            for i in range(3):
                parts.append(notes[b, first + i : first + i + 1, : min(128, small - 128 * i)])
        vec[6 + index : 7 + index, :] = jnp.concatenate(parts, 1)
    for b in range(share):
        block = notes[b, NOTE_BIAS + 12 : NOTE_BIAS + 12 + lines, :]
        vec[10 + b : 11 + b, :] = flat(block, 0)
    vec[14:15, :] = flat(notes[0, NOTE_COND : NOTE_COND + lines, :], 0)


def forward_block(qp, inner, outer, tok, cot, note, table):
    half, ff = qp.shape[0] // 2, qp.shape[1]
    images, band_slots, width = tok.shape
    rows = images * band_slots
    heads = width // HEAD_DIM
    bf, f32 = jnp.bfloat16, jnp.float32
    S = jax.ShapeDtypeStruct
    qp, inner = qp.reshape(2, half, ff), inner.reshape(2, half, ff)
    outer = outer.reshape(4, 2, half, width)
    scratch = forward_scratch(half, ff, width, rows, note.shape[1], images)
    any_ = pl.BlockSpec(memory_space=pl.ANY)
    return pl.pallas_call(
        partial(forward_kernel, tuple(scratch), band_slots),
        out_shape=[
            S((NB, 2, half, ff), bf), S((NB, 2, half, ff), bf), S((NB, 4, 2, half, width), bf), S(cot.shape, bf),
            S((16, width), f32), S((rows, width), f32), S((rows, width), bf), S((rows, width), bf),
            S((rows, 2 * width), bf), S((rows, 2 * width), bf), S((heads, 8, rows), f32), S((rows, width), bf),
            S((rows, width), f32), S((rows, width), bf),
        ],
        in_specs=[any_] * 6 + [pl.BlockSpec(memory_space=pltpu.VMEM)],
        out_specs=[any_] * 14,
        scratch_shapes=list(scratch.values()),
        compiler_params=pltpu.CompilerParams(
            collective_id=0, has_side_effects=True, vmem_limit_bytes=60 * 2**20
        ),
        name="forward_block",
    )(qp, inner, outer, tok, cot, note, table)


def pair_perm(dp_count, band_count):
    return [
        (dp * band_count + band, (dp ^ 1) * band_count + band)
        for dp in range(dp_count)
        for band in range(band_count)
    ]


def home_perm_back(dp_count, band_count, turn):
    pairs = []
    for dp in range(dp_count):
        for band in range(band_count):
            to_dp = dp - dp % 2 + band // 2
            to_band = 2 * (dp % 2) + (band + turn) % 2
            pairs.append((dp * band_count + band, to_dp * band_count + to_band))
    return pairs


def send_home(rows, band, perms):
    odd = lax.rem(band, 2) == 1
    first = jnp.where(odd, rows[1], rows[0])
    second = jnp.where(odd, rows[0], rows[1])
    got = [lax.ppermute(part, ("dp", "band"), perm) for part, perm in zip((first, second), perms)]
    return jnp.stack([jnp.where(odd, got[1], got[0]), jnp.where(odd, got[0], got[1])])


def position_parts(width):
    quarter = width // 4
    frequency = 10000.0 ** (-jnp.arange(quarter, dtype=jnp.float32) / quarter)
    angles = jnp.arange(128, dtype=jnp.float32)[:, None] * frequency
    left = jnp.concatenate([jnp.sin(angles), jnp.cos(angles)], -1)
    parts = []
    for _ in range(3):
        part = lax.reduce_precision(left, 8, 7)
        parts.append(part.astype(jnp.bfloat16))
        left = left - part
    return jnp.stack(parts)


def over_groups(piece, dp_count):
    if dp_count == 8:
        return piece
    groups = [[rank + 8 * group for group in range(dp_count // 8)] for rank in range(8)]
    return lax.psum(piece.astype(jnp.float32), "dp", axis_index_groups=groups)


def every_group(piece, dp_count):
    if dp_count == 8:
        return piece[None]
    groups = [[rank + 8 * group for group in range(dp_count // 8)] for rank in range(8)]
    return lax.all_gather(piece, "dp", axis_index_groups=groups)


def own_piece(vector, count, band_place):
    return lax.dynamic_slice_in_dim(vector, band_place * count, count, 0)


def body(
    tokens,
    condition,
    patch_grid,
    ada_weight,
    ada_bias,
    qkv_weight,
    query_bias,
    value_bias,
    proj_weight,
    proj_bias,
    inner_weight,
    inner_bias,
    outer_weight,
    outer_bias,
    cotangent,
):
    both = ("dp", "band")
    dp_count = lax.axis_size("dp")
    band_count = lax.axis_size("band")
    images, band_slots, width = tokens.shape
    band = lax.axis_index("band")
    dp = lax.axis_index("dp")
    core = lax.rem(dp, 2)
    hidden = inner_weight.shape[1]
    part_rows = qkv_weight.shape[0]
    siblings = pair_perm(dp_count, band_count)
    homes = [home_perm_back(dp_count, band_count, turn) for turn in range(2)]

    condition_f = condition.astype(jnp.float32)
    activated = jax.nn.silu(condition_f).astype(jnp.bfloat16)
    own_activated = lax.dynamic_slice_in_dim(activated, band * part_rows, part_rows, 1)
    share = jnp.dot(own_activated, ada_weight, preferred_element_type=jnp.float32)
    share = share + lax.dynamic_update_slice_in_dim(
        jnp.zeros((ada_weight.shape[1],), jnp.float32),
        ada_bias.astype(jnp.float32),
        band * ada_bias.shape[0],
        0,
    )
    mod_count = share.shape[1]
    lines = lambda vector: jnp.pad(
        vector.astype(jnp.float32), [(0, 0)] * (vector.ndim - 1) + [(0, -vector.shape[-1] % 128)]
    )
    spread = lambda vector: jnp.broadcast_to(lines(vector), (images, -(-vector.shape[0] // 128) * 128))
    note = jnp.concatenate(
        [share, condition_f, lines(patch_grid)]
        + [spread(bias) for bias in (query_bias, value_bias, proj_bias, outer_bias, inner_bias)],
        1,
    )
    note = jnp.pad(note, ((0, 0), (0, -note.shape[1] % 1024))).reshape(images, -1, 128)
    first_weight = jnp.concatenate([qkv_weight, proj_weight], 1)
    (first_full, inner_full, outer_full, cotangent_here, vectors, residual, attn_in, query_rows, key_value,
     other_key_value, tops, mixed_rows, attended, mlp_in) = forward_block(
        first_weight, inner_weight, outer_weight, tokens, cotangent, note, position_parts(width)
    )
    first_full = first_full.reshape(width, -1)
    inner_full = inner_full.reshape(width, hidden)
    outer_full = outer_full.reshape(hidden, width)
    qkv_full = first_full[:, : 3 * width]
    proj_full = first_full[:, 3 * width :]
    scale_one, gate_one = vectors[1], vectors[2]
    scale_two, gate_two = vectors[4], vectors[5]
    outer_bias_full = vectors[9]
    inner_bias_full = vectors[10:14].reshape(-1)
    condition_here = vectors[14]
    valid_count = vectors[15, :1].astype(jnp.int32)
    rows = images * band_slots
    is_valid = jnp.arange(rows, dtype=jnp.int32) % band_slots < valid_count
    normed_one, inverse_one = normalize(residual)
    middle = residual + gate_one * attended
    normed_two, inverse_two = normalize(middle)
    hidden_pre = jnp.dot(mlp_in, inner_full, preferred_element_type=jnp.float32) + inner_bias_full
    hidden_act = jax.nn.gelu(hidden_pre, approximate=True).astype(jnp.bfloat16)
    mlp_out = jnp.dot(hidden_act, outer_full, preferred_element_type=jnp.float32) + outer_bias_full
    block_out = (middle + gate_two * mlp_out).astype(jnp.bfloat16)
    block_home = send_home(block_out.reshape(images, band_slots, width), band, homes)

    grad_out = cotangent_here.reshape(rows, width).astype(jnp.float32) * is_valid[:, None].astype(
        jnp.float32
    )
    grad_gate_two = jnp.sum(grad_out * mlp_out, 0)
    grad_mlp = (gate_two * grad_out).astype(jnp.bfloat16)
    gelu_back = jax.vjp(partial(jax.nn.gelu, approximate=True), hidden_pre)[1]
    blocks = (band_count, 2, part_rows // 2, width)
    grad_outer = rows_dot(hidden_act, grad_mlp).astype(jnp.bfloat16).reshape(
        band_count, 4, 2, part_rows // 2, width
    )
    grad_outer_bias = jnp.sum(grad_mlp.astype(jnp.float32), 0)
    grad_hidden = lanes_dot(grad_mlp, outer_full)
    grad_pre = gelu_back(grad_hidden)[0].astype(jnp.bfloat16)
    grad_inner = [
        rows_dot(mlp_in, grad_pre[:, t * width : (t + 1) * width]).astype(jnp.bfloat16).reshape(blocks)
        for t in range(4)
    ]
    grad_inner_bias = jnp.sum(grad_pre.astype(jnp.float32), 0)
    grad_mlp_in = lanes_dot(grad_pre, inner_full)
    grad_shift_two = jnp.sum(grad_mlp_in, 0)
    grad_scale_two = jnp.sum(grad_mlp_in * normed_two, 0)
    grad_middle = grad_out + norm_back(grad_mlp_in * (1.0 + scale_two), normed_two, inverse_two)
    grad_gate_one = jnp.sum(grad_middle * attended, 0)
    grad_attended = (gate_one * grad_middle).astype(jnp.bfloat16)
    grad_proj = rows_dot(mixed_rows, grad_attended).astype(jnp.bfloat16)
    grad_proj_bias = jnp.sum(grad_attended.astype(jnp.float32), 0)
    grad_mixed = lanes_dot(grad_attended, proj_full).astype(jnp.bfloat16)
    (outer_sum, inner_sum), grad_query, own_terms, far_terms = reduce_attend(
        [[grad_outer], grad_inner], valid_count, query_rows, key_value, other_key_value, grad_mixed, tops,
        band_slots, 1,
    )
    other_terms = lax.ppermute(far_terms, both, siblings)
    grad_key_value = (own_terms.astype(jnp.float32) + other_terms.astype(jnp.float32)).astype(
        jnp.bfloat16
    )
    grad_qkv = jnp.concatenate([grad_query, grad_key_value], -1)
    grad_first = [
        rows_dot(attn_in, part).astype(jnp.bfloat16).reshape(blocks)
        for part in (grad_query, grad_key_value[:, :width], grad_key_value[:, width:])
    ]
    grad_attn_in = lanes_dot(grad_qkv, qkv_full)
    grad_query_bias = jnp.sum(grad_query.astype(jnp.float32), 0)
    grad_value_bias = jnp.sum(grad_key_value[:, width:].astype(jnp.float32), 0)
    grad_shift_one = jnp.sum(grad_attn_in, 0)
    grad_scale_one = jnp.sum(grad_attn_in * normed_one, 0)
    grad_tokens = grad_middle + norm_back(grad_attn_in * (1.0 + scale_one), normed_one, inverse_one)
    tokens_home = send_home(
        grad_tokens.astype(jnp.bfloat16).reshape(images, band_slots, width), band, homes
    ).astype(jnp.float32)

    part_mod = jnp.concatenate(
        [grad_shift_one, grad_scale_one, grad_gate_one, grad_shift_two, grad_scale_two, grad_gate_two]
    )
    part_mod = jnp.concatenate([part_mod, 0.5 * condition_here]).reshape(-1, 128)
    part_mod = jnp.pad(part_mod, ((0, -part_mod.shape[0] % 16), (0, 0)))
    part_bias = jnp.concatenate(
        [grad_query_bias, grad_value_bias, grad_proj_bias, grad_inner_bias, grad_outer_bias]
    ).reshape(-1, 128)
    (first_sum,), every, bias_grads, grad_act = reduce_last(
        [grad_first + [grad_proj.reshape(blocks)]], part_mod, part_bias, ada_weight, images, 2
    )
    every = every_group(every, dp_count)
    bias_grads = over_groups(bias_grads, dp_count).reshape(-1)
    every = jnp.swapaxes(every, 1, 2).reshape(dp_count * images, -1)
    every_mod = every[:, :mod_count]
    every_condition = every[:, mod_count : mod_count + width]
    every_activated = jax.nn.silu(every_condition.astype(jnp.float32)).astype(jnp.bfloat16)
    every_activated = lax.dynamic_slice_in_dim(every_activated, band * part_rows, part_rows, 1)
    grad_ada = rows_dot(every_activated, every_mod)
    grad_ada_bias = own_piece(jnp.sum(every_mod.astype(jnp.float32), 0), ada_bias.shape[0], band)
    grad_act = jnp.swapaxes(grad_act[:, :images, :part_rows], 0, 1).reshape(images, width)
    grad_condition = jax.vjp(jax.nn.silu, condition_f)[1](grad_act)[0]

    def side_by_side(units):
        return jnp.concatenate([unit.reshape(part_rows, width) for unit in units], 1).astype(jnp.float32)

    first_sum, inner_sum, outer_sum = [
        over_groups(piece, dp_count) for piece in (first_sum, inner_sum, outer_sum)
    ]
    weight_sums = dict(
        qkv=side_by_side([first_sum[t] for t in range(3)]),
        proj=first_sum[3].reshape(part_rows, width).astype(jnp.float32),
        inner=side_by_side([inner_sum[t] for t in range(4)]),
        outer=outer_sum.reshape(4 * part_rows, width).astype(jnp.float32),
    )
    bias_parts = []
    at = 0
    for piece in (query_bias, value_bias, proj_bias, inner_bias, outer_bias):
        whole = piece.shape[0] * band_count
        bias_parts.append(own_piece(bias_grads[at : at + whole], piece.shape[0], band))
        at += whole
    return (
        block_home,
        tokens_home,
        grad_condition,
        grad_ada,
        grad_ada_bias,
        weight_sums["qkv"],
        bias_parts[0],
        bias_parts[1],
        weight_sums["proj"],
        bias_parts[2],
        weight_sums["inner"],
        bias_parts[3],
        weight_sums["outer"],
        bias_parts[4],
    )


def solution(mesh):
    placed = (
        P("dp", "band", None),
        P("dp", None),
        P("dp", None),
        P("band", None),
        P("band"),
        P("band", None),
        P("band"),
        P("band"),
        P("band", None),
        P("band"),
        P("band", None),
        P("band"),
        P("band", None),
        P("band"),
        P("dp", "band", None),
    )
    return jax.shard_map(
        body,
        mesh=mesh,
        in_specs=placed,
        out_specs=(
            P("dp", "band", None),
            P("dp", "band", None),
            P("dp", None),
            P("band", None),
            P("band"),
            P("band", None),
            P("band"),
            P("band"),
            P("band", None),
            P("band"),
            P("band", None),
            P("band"),
            P("band", None),
            P("band"),
        ),
        check_vma=False,
    )
```

```python
from functools import partial
from types import SimpleNamespace

import jax
import jax.numpy as jnp
from jax import lax
from jax.experimental import pallas as pl
from jax.experimental.pallas import tpu as pltpu
from jax.sharding import PartitionSpec as P

HEAD_DIM = 72


MESH = pl.DeviceIdType.MESH
NB = 4


def device(dp, band):
    return {"dp": dp, "band": band}


def normalize(values):
    average = jnp.mean(values, -1, keepdims=True)
    centered = values - average
    variance = jnp.mean(centered * centered, -1, keepdims=True)
    inverse = lax.rsqrt(variance + 1e-06)
    return (centered * inverse, inverse)


def norm_back(grad_normed, normed, inverse):
    first = jnp.mean(grad_normed, -1, keepdims=True)
    second = jnp.mean(grad_normed * normed, -1, keepdims=True)
    return inverse * (grad_normed - first - normed * second)


LANES = 128
PACK_ROWS = 128


def pack_heads(source, first, heads_ref, row0, rows, tail):
    heads = heads_ref.shape[0]

    @pl.loop(0, rows // PACK_ROWS)
    def _(step):
        at = pl.multiple_of(step * PACK_ROWS, PACK_ROWS)
        block = source[pl.ds(at, PACK_ROWS), first : first + heads * HEAD_DIM]
        end = tail(at)
        for h in range(heads):
            part = block[:, h * HEAD_DIM : (h + 1) * HEAD_DIM]
            heads_ref[h, pl.ds(row0 + at, PACK_ROWS), :] = jnp.concatenate([part, end], 1)


def unpack_heads(heads_ref, row0, rows, target, first):
    heads = heads_ref.shape[0]

    @pl.loop(0, rows // PACK_ROWS)
    def _(step):
        at = pl.multiple_of(step * PACK_ROWS, PACK_ROWS)
        parts = [heads_ref[h, pl.ds(row0 + at, PACK_ROWS), :][:, :HEAD_DIM] for h in range(heads)]
        target[pl.ds(at, PACK_ROWS), first : first + heads * HEAD_DIM] = jnp.concatenate(parts, 1)


def flat_tail(value):
    def tail(at):
        lane = lax.broadcasted_iota(jnp.int32, (PACK_ROWS, LANES - HEAD_DIM), 1)
        return jnp.where(lane == 0, value, 0.0).astype(jnp.bfloat16)

    return tail


def key_tail(valid_count, band_slots):
    def tail(at):
        shape = (PACK_ROWS, LANES - HEAD_DIM)
        lane = lax.broadcasted_iota(jnp.int32, shape, 1)
        slot = lax.rem(at + lax.broadcasted_iota(jnp.int32, shape, 0), band_slots)
        return jnp.where(jnp.logical_and(lane == 0, slot >= valid_count), -1e30, 0.0).astype(jnp.bfloat16)

    return tail


def lanes_dot(left, right):
    return lax.dot_general(left, right, (((1,), (1,)), ((), ())), preferred_element_type=jnp.float32)


def rows_dot(left, right):
    return lax.dot_general(left, right, (((0,), (0,)), ((), ())), preferred_element_type=jnp.float32)


SCORE_SCALE = HEAD_DIM ** (-0.5)


def attend_block(h, qh, kh, vh, top_ref):
    rows = qh.shape[1]
    for block in range(2):
        at = pl.ds(block * rows // 2, rows // 2)
        scores = lanes_dot(kh[h], qh[h, at, :]) * SCORE_SCALE
        top = jnp.max(scores, 0, keepdims=True)
        weights = jnp.exp(scores - top)
        total = jnp.sum(weights, 0, keepdims=True)
        low = (weights * (1.0 / total)).astype(jnp.bfloat16)
        mixed = rows_dot(vh[h], low)
        qh[h, at, :] = jnp.transpose(mixed).astype(jnp.bfloat16)
        top_ref[h, :, at] = jnp.broadcast_to(top + jnp.log(total), (8, rows // 2))


def attend_head(h, qh, kh, vh, gh, top_ref):
    query = qh[h]
    key = kh[h]
    grad = gh[h]
    probs = jnp.exp(lanes_dot(key, query) * SCORE_SCALE - top_ref[h, 0:1, :])
    grad_probs = lanes_dot(vh[h], grad)
    inner = jnp.sum(probs * grad_probs, 0, keepdims=True)
    grad_scores = (probs * (grad_probs - inner)).astype(jnp.bfloat16)
    vh[h] = jnp.dot(
        probs.astype(jnp.bfloat16), grad, preferred_element_type=jnp.float32
    ).astype(jnp.bfloat16)
    grad_query = rows_dot(key, grad_scores)
    kh[h] = (
        SCORE_SCALE * jnp.dot(grad_scores, query, preferred_element_type=jnp.float32)
    ).astype(jnp.bfloat16)
    qh[h] = (SCORE_SCALE * jnp.transpose(grad_query)).astype(jnp.bfloat16)


def compass():
    dp = lax.axis_index("dp")
    band = lax.axis_index("band")
    core = lax.rem(dp, 2)
    px = lax.rem(dp // 2, 2)
    py = lax.rem(dp // 4, 2)
    return SimpleNamespace(
        dp=dp, band=band, core=core, px=px, py=py, kind=2 * py + px,
        sib=dp + 1 - 2 * core, xdp=dp + 2 - 4 * px, ydp=dp + 4 - 8 * py,
    )


def add_rows(total, term):
    rows = total.shape[0]

    @pl.loop(0, rows // 16)
    def _(step):
        at = pl.ds(pl.multiple_of(step * 16, 16), 16)
        total[at, :] = (
            total[at, :].astype(jnp.float32) + term[at, :].astype(jnp.float32)
        ).astype(jnp.bfloat16)


def run_all(batch):
    for do in batch:
        do()


REDUCE_ORDER = (1, 3, 2, 0)


def reduce_scratch(phases, half, width):
    bf = jnp.bfloat16
    n = phases * NB
    D = pltpu.SemaphoreType.DMA
    return dict(
        acc=pltpu.VMEM((n, 4, half, width), bf),
        recv_a=pltpu.VMEM((n, 4, half, width), bf),
        recv_b=pltpu.VMEM((n, 2, half, width), bf),
        recv_c=pltpu.VMEM((n, half, width), bf),
        recv_z=pltpu.VMEM((phases, NB, half, width), bf),
        a_send=D((n,)), a_recv=D((n,)), a_own=D((n,)),
        b_send=D((n, 2)), b_recv=D((n,)), c_send=D((n,)), c_recv=D((n,)),
        z_send=D((phases, NB)), z_recv=D((phases, NB)),
        d_send=D((phases, 4)), d_recv=D((phases, 4)), d_own=D((phases,)),
    )


def reduce_steps(me, phases, source, out, sc, beside=()):
    dp, band, core, px, py, kind = me.dp, me.band, me.core, me.px, me.py, me.kind
    here = lambda d: device(d, band)
    chunks = [(phase, k) for phase in range(phases) for k in REDUCE_ORDER]
    n = len(chunks)
    flip = lambda v: 1 - v
    sends = []

    def remote(src, dst, ss, rs, to):
        return pltpu.make_async_remote_copy(
            src_ref=src, dst_ref=dst, send_sem=ss, recv_sem=rs, device_id=to, device_id_type=MESH
        )

    def go(make):
        make().start()
        sends.append(make)

    def start_a(s):
        phase, k = chunks[s]
        b = lax.rem(band + k, NB)
        for t in range(4):
            remote(
                source(phase, b, t, flip(core)), sc.recv_a.at[s, t],
                sc.a_send.at[s], sc.a_recv.at[s], here(me.sib),
            ).start()
            pltpu.make_async_copy(
                source(phase, b, t, core), sc.acc.at[s, t], sc.a_own.at[s]
            ).start()

    def first(s, j, send):
        if s % 2 == 0:
            return 2 * j + (flip(px) if send else px)
        return 2 * (flip(py) if send else py) + j

    def second(s, send):
        if s % 2 == 0:
            return 2 * (flip(py) if send else py) + px
        return 2 * py + (flip(px) if send else px)

    def send_b(s, j):
        return remote(
            sc.acc.at[s, first(s, j, True)], sc.recv_b.at[s, j], sc.b_send.at[s, j],
            sc.b_recv.at[s], here(me.xdp if s % 2 == 0 else me.ydp),
        )

    def send_c(s):
        return remote(
            sc.acc.at[s, second(s, True)], sc.recv_c.at[s], sc.c_send.at[s],
            sc.c_recv.at[s], here(me.ydp if s % 2 == 0 else me.xdp),
        )

    def send_z(s):
        phase, k = chunks[s]
        return remote(
            sc.acc.at[s, kind], sc.recv_z.at[phase, k], sc.z_send.at[phase, k],
            sc.z_recv.at[phase, k], device(dp, lax.rem(band + k, NB)),
        )

    def send_d(phase, slot):
        ss, rs = sc.d_send.at[phase, slot], sc.d_recv.at[phase, slot]
        even = phase % 2 == 0
        if slot == 0:
            unit = out[phase].at[kind, core]
            return remote(sc.recv_z.at[phase, 0], unit, ss, rs, here(me.xdp if even else me.ydp))
        if slot == 3:
            row = out[phase].at[:, core]
            return remote(row, row, ss, rs, here(me.sib))
        if even:
            pair = out[phase].at[pl.ds(2 * py, 2), core]
            return remote(pair, pair, ss, rs, here(me.ydp))
        unit = out[phase].at[2 * (slot - 1) + px, core]
        return remote(unit, unit, ss, rs, here(me.xdp))

    def a_to_b(s):
        acc, got = sc.acc, sc.recv_a
        pltpu.make_async_copy(got.at[s], acc.at[s], sc.a_own.at[s]).wait()
        whole = remote(got.at[s], got.at[s], sc.a_send.at[s], sc.a_recv.at[s], here(me.sib))
        whole.wait_recv()
        for j in range(2):
            t = first(s, j, True)
            add_rows(acc.at[s, t], got.at[s, t])
            go(partial(send_b, s, j))
        for j in range(2):
            t = first(s, j, False)
            add_rows(acc.at[s, t], got.at[s, t])
        whole.wait_send()

    def b_to_c(s):
        acc, got = sc.acc, sc.recv_b
        remote(got.at[s], got.at[s], sc.b_send.at[s, 0], sc.b_recv.at[s], here(me.xdp)).wait_recv()
        away = flip(py) if s % 2 == 0 else flip(px)
        stay = py if s % 2 == 0 else px
        add_rows(acc.at[s, second(s, True)], got.at[s, away])
        go(partial(send_c, s))
        add_rows(acc.at[s, kind], got.at[s, stay])

    def c_to_z(s):
        acc, got = sc.acc, sc.recv_c
        phase, k = chunks[s]
        remote(got.at[s], got.at[s], sc.c_send.at[s], sc.c_recv.at[s], here(me.xdp)).wait_recv()
        add_rows(acc.at[s, kind], got.at[s])
        if k != 0:
            go(partial(send_z, s))

    def z_to_d(phase):
        s = phase * NB + NB - 1
        acc, got = sc.acc, sc.recv_z
        for k in range(1, NB):
            remote(
                got.at[phase, k], got.at[phase, k], sc.z_send.at[phase, k],
                sc.z_recv.at[phase, k], here(dp),
            ).wait_recv()
        rows = acc.shape[2]

        @pl.loop(0, rows // 16)
        def _(step):
            at = pl.ds(pl.multiple_of(step * 16, 16), 16)
            total = acc[s, kind, at, :].astype(jnp.float32)
            for k in range(1, NB):
                total = total + got[phase, k, at, :].astype(jnp.float32)
            got[phase, 0, at, :] = total.astype(jnp.bfloat16)

        unit = out[phase].at[kind, core]
        own = pltpu.make_async_copy(got.at[phase, 0], unit, sc.d_own.at[phase])
        own.start()
        go(partial(send_d, phase, 0))
        own.wait()

    def d_second(phase):
        even = phase % 2 == 0
        mate = 2 * py + flip(px) if even else 2 * flip(py) + px
        unit = out[phase].at[mate, core]
        remote(unit, unit, sc.d_send.at[phase, 0], sc.d_recv.at[phase, 0], here(me.xdp)).wait_recv()
        for slot in (1,) if even else (1, 2):
            go(partial(send_d, phase, slot))

    def d_third(phase):
        if phase % 2 == 0:
            pair = out[phase].at[pl.ds(2 * flip(py), 2), core]
            remote(pair, pair, sc.d_send.at[phase, 1], sc.d_recv.at[phase, 1], here(me.ydp)).wait_recv()
        else:
            for j in range(2):
                unit = out[phase].at[2 * j + flip(px), core]
                remote(unit, unit, sc.d_send.at[phase, 1 + j], sc.d_recv.at[phase, 1 + j], here(me.xdp)).wait_recv()
        go(partial(send_d, phase, 3))

    def d_last(phase):
        row = out[phase].at[:, flip(core)]
        remote(row, row, sc.d_send.at[phase, 3], sc.d_recv.at[phase, 3], here(me.sib)).wait_recv()

    def finish():
        for make in sends:
            make().wait_send()

    table = {-1: [partial(start_a, s) for s in range(n)]}

    def put(at, do):
        table.setdefault(at, []).append(do)

    for at, do in enumerate(beside):
        put(at, do)
    for s in range(n):
        put(s + 3, partial(b_to_c, s))
        put(s + 5, partial(c_to_z, s))
        put(s, partial(a_to_b, s))
    for phase in range(phases):
        end = (phase + 1) * NB - 1 + 5
        for lag, do in ((2, z_to_d), (3, d_second), (4, d_third), (5, d_last)):
            put(end + lag, partial(do, phase))
    steps = [partial(run_all, table[at]) for at in sorted(table)]
    steps.append(finish)
    return steps


def home_scratch():
    D = pltpu.SemaphoreType.DMA
    return dict(home_send=D((2,)), home_recv=D((2,)))


def home_steps(me, rows_ref, home_ref, sc):
    band, core = me.band, me.core
    slot = lax.rem(band, 2)

    def stays(s):
        return jnp.logical_and(band // 2 == core, 2 * core + s == band)

    def copy(s):
        to = device(me.dp - core + band // 2, 2 * core + s)
        return pltpu.make_async_remote_copy(
            src_ref=rows_ref.at[s], dst_ref=home_ref.at[slot], send_sem=sc.home_send.at[s],
            recv_sem=sc.home_recv.at[slot], device_id=to, device_id_type=MESH,
        )

    def begin():
        for s in range(2):
            pl.when(stays(s))(
                lambda: pltpu.make_async_copy(
                    rows_ref.at[s], home_ref.at[slot], sc.home_recv.at[slot]
                ).start()
            )
            pl.when(jnp.logical_not(stays(s)))(lambda: copy(s).start())

    def finish():
        for s in range(2):
            pl.when(jnp.logical_not(stays(s)))(lambda: copy(s).wait_send())
        for i in range(2):
            pltpu.make_async_copy(rows_ref.at[i], home_ref.at[i], sc.home_recv.at[i]).wait()

    return begin, finish


def group_barrier(me):
    barrier = pltpu.get_barrier_semaphore()
    peers = [(me.xdp, me.band), (me.ydp, me.band), (me.sib, me.band)]
    for k in range(1, NB):
        other = lax.rem(me.band + k, NB)
        peers += [(me.dp, other), (me.sib, other)]
    for dp, band in peers:
        pl.semaphore_signal(
            barrier, inc=1, device_id=device(dp, band), device_id_type=MESH
        )
    pl.semaphore_wait(barrier, len(peers))


def reduce_sources(counts, refs):
    grads = []
    at = 0
    for count in counts:
        grads.append(refs[at : at + count])
        at += count

    def source(phase, b, t, h):
        if len(grads[phase]) == 1:
            return grads[phase][0].at[b, t, h]
        return grads[phase][t].at[b, h]

    return source


def small_scratch(mod_rows, bias_rows, cond_rows, cond_cols):
    D = pltpu.SemaphoreType.DMA
    f32 = jnp.float32
    return dict(
        s_core=pltpu.VMEM((mod_rows + bias_rows, 128), f32),
        s_every=pltpu.VMEM((NB, 4, mod_rows, 128), jnp.bfloat16),
        s_bias=pltpu.VMEM((3, bias_rows, 128), f32),
        s_got=pltpu.VMEM((2 + NB, bias_rows, 128), f32),
        s_flat=pltpu.VMEM((8, mod_rows, 128), f32),
        s_cond=pltpu.VMEM((NB, cond_rows, cond_cols), f32),
        s_send=D((8,)), s_recv=D((8,)), sz_send=D((2, NB)), sz_recv=D((2, NB)),
        sc_send=D((NB,)), sc_recv=D((NB,)),
    )


def small_steps(me, mods, images, small_ref, ada_ref, every_ref, bias_ref, cond_ref, sc):
    dp, band, core, px, py, kind = me.dp, me.band, me.core, me.px, me.py, me.kind
    here = lambda d: device(d, band)
    every, bias, got, cond = sc.s_every, sc.s_bias, sc.s_got, sc.s_cond
    mod_rows = every.shape[2]
    flip = lambda v: 1 - v

    def remote(src, dst, ss, rs, to):
        return pltpu.make_async_remote_copy(
            src_ref=src, dst_ref=dst, send_sem=ss, recv_sem=rs, device_id=to, device_id_type=MESH
        )

    def plain(index, src, dst, to):
        return remote(src, dst, sc.s_send.at[index], sc.s_recv.at[index], to)

    def core_copy():
        return plain(0, small_ref, sc.s_core, here(me.sib))

    def x_copies(mine):
        unit = every.at[band, kind if mine else 2 * py + flip(px)]
        return [
            plain(1, unit, unit, here(me.xdp)),
            plain(2, bias.at[0], got.at[0], here(me.xdp)),
        ]

    def y_copies(mine):
        pair = every.at[band, pl.ds(2 * (py if mine else flip(py)), 2)]
        return [
            plain(3, pair, pair, here(me.ydp)),
            plain(4, bias.at[1], got.at[1], here(me.ydp)),
        ]

    def z_copies(k, mine):
        to = device(dp, lax.rem(band + k, NB))
        block = every.at[band if mine else lax.rem(band + NB - k, NB)]
        return [
            remote(block, block, sc.sz_send.at[0, k], sc.sz_recv.at[0, k], to),
            remote(bias.at[2], got.at[2 + k], sc.sz_send.at[1, k], sc.sz_recv.at[1, k], to),
        ]

    def cond_copy(k, mine):
        to = device(dp, lax.rem(band + k, NB))
        block = cond.at[band if mine else lax.rem(band + NB - k, NB)]
        return remote(block, block, sc.sc_send.at[k], sc.sc_recv.at[k], to)

    def begin():
        core_copy().start()

    def cores():
        core_copy().wait()
        total = small_ref[...] + sc.s_core[...]
        every[band, kind] = total[:mod_rows].astype(jnp.bfloat16)
        bias[0] = total[mod_rows:]
        for copy in x_copies(True):
            copy.start()

    def over_x():
        for copy in x_copies(True):
            copy.wait_send()
        for copy in x_copies(False):
            copy.wait_recv()
        bias[1] = bias[0] + got[0]
        for copy in y_copies(True):
            copy.start()

    def over_y():
        for copy in y_copies(True):
            copy.wait_send()
        for copy in y_copies(False):
            copy.wait_recv()
        bias[2] = bias[1] + got[1]
        for k in range(1, NB):
            for copy in z_copies(k, True):
                copy.start()

    def over_z():
        for k in range(1, NB):
            for copy in z_copies(k, True):
                copy.wait_send()
            for copy in z_copies(k, False):
                copy.wait_recv()
        bias_ref[...] = bias[2] + got[3] + got[4] + got[5]
        every_ref[...] = every[...]
        flat = sc.s_flat
        for i in range(images):
            flat[i] = every[images * core + i, kind].astype(jnp.float32)
        parts = mods // 128
        lead = flat.shape[0]
        total = jnp.zeros((lead, ada_ref.shape[0]), jnp.float32)
        for r in range(parts):
            left = jnp.concatenate(
                [flat[i, r : r + 1, :] for i in range(images)]
                + [jnp.zeros((lead - images, 128), jnp.float32)]
            ).astype(jnp.bfloat16)
            total = total + lanes_dot(left, ada_ref[:, r * 128 : (r + 1) * 128])
        pad = cond.shape[2] - total.shape[1]
        cond[band] = jnp.concatenate([total, jnp.zeros((lead, pad), jnp.float32)], 1)
        for k in range(1, NB):
            cond_copy(k, True).start()

    def conditions():
        for k in range(1, NB):
            cond_copy(k, True).wait_send()
            cond_copy(k, False).wait_recv()
        cond_ref[...] = cond[...]

    return [begin, cores, over_x, over_y, over_z, conditions]


def reduce_last_kernel(counts, mods, images, names, *refs):
    me = compass()
    phases = len(counts)
    at = sum(counts)
    source = reduce_sources(counts, refs)
    rows_ref, small_ref, ada_ref = refs[at : at + 3]
    at += 3
    out = refs[at : at + phases]
    home_ref, every_ref, bias_ref, cond_ref = refs[at + phases : at + 4 + phases]
    sc = SimpleNamespace(**dict(zip(names, refs[at + 4 + phases :])))
    group_barrier(me)
    small = small_steps(me, mods, images, small_ref, ada_ref, every_ref, bias_ref, cond_ref, sc)
    small[0]()
    depart, settle = home_steps(me, rows_ref, home_ref, sc)
    depart()
    for step in reduce_steps(me, phases, source, out, sc, small[1:]):
        step()
    settle()


def reduce_last(grads, rows, mod_part, bias_part, ada_weight, images, collective_id):
    phases = len(grads)
    half, width = grads[0][0].shape[-2:]
    counts = tuple(len(phase) for phase in grads)
    mod_rows, bias_rows = mod_part.shape[0], bias_part.shape[0]
    cond_cols = -(-ada_weight.shape[0] // 128) * 128
    scratch = dict(
        **reduce_scratch(phases, half, width), **small_scratch(mod_rows, bias_rows, 8, cond_cols), **home_scratch()
    )
    any_, vmem = pl.BlockSpec(memory_space=pl.ANY), pl.BlockSpec(memory_space=pltpu.VMEM)
    outs = pl.pallas_call(
        partial(reduce_last_kernel, counts, ada_weight.shape[1], images, tuple(scratch)),
        out_shape=[jax.ShapeDtypeStruct((4, 2, half, width), jnp.bfloat16)] * phases
        + [
            jax.ShapeDtypeStruct(rows.shape, rows.dtype),
            jax.ShapeDtypeStruct((NB, 4, mod_rows, 128), jnp.bfloat16),
            jax.ShapeDtypeStruct((bias_rows, 128), jnp.float32),
            jax.ShapeDtypeStruct((NB, 8, cond_cols), jnp.float32),
        ],
        in_specs=[any_] * (sum(counts) + 1) + [vmem] * 2,
        out_specs=[any_] * (phases + 1) + [vmem] * 3,
        scratch_shapes=list(scratch.values()),
        compiler_params=pltpu.CompilerParams(
            collective_id=collective_id, has_side_effects=True, vmem_limit_bytes=56 * 2**20
        ),
        name="reduce_last",
    )(*[unit for phase in grads for unit in phase], rows, jnp.concatenate([mod_part, bias_part]), ada_weight)
    return outs[:phases], *outs[phases:]


def reduce_attend_kernel(counts, band_slots, names, *refs):
    me = compass()
    phases = len(counts)
    at = sum(counts)
    source = reduce_sources(counts, refs)
    rows_ref, count_ref, q_ref, own_ref, far_ref, grad_ref, top_ref = refs[at : at + 7]
    at += 7
    out = refs[at : at + phases]
    home_ref, dq_ref, down_ref, dfar_ref = refs[at + phases : at + phases + 4]
    sc = SimpleNamespace(**dict(zip(names, refs[at + phases + 4 :])))
    qh, kh, vh, gh, stage, stage_sem = sc.qh, sc.kh, sc.vh, sc.gh, sc.stage, sc.stage_sem
    rows, width = q_ref.shape
    heads = qh.shape[0]
    group_barrier(me)
    steps = reduce_steps(me, phases, source, out, sc)
    depart, settle = home_steps(me, rows_ref, home_ref, sc)
    steps[0]()
    depart()
    keys, plain, ones = key_tail(count_ref[0], band_slots), flat_tail(0.0), flat_tail(1.0)
    loads = [(q_ref, 0, qh, 0, ones), (grad_ref, 0, gh, 0, plain)]
    for row0, ref in ((0, own_ref), (rows, far_ref)):
        loads += [(ref, 0, kh, row0, keys), (ref, width, vh, row0, plain)]

    def load(i):
        ref, column = loads[i][:2]
        return pltpu.make_async_copy(ref.at[:, pl.ds(column, width)], stage.at[i % 2], stage_sem.at[i % 2])

    load(0).start()
    for step in steps[1:4]:
        step()
    for i, (ref, column, heads_ref, row0, tail) in enumerate(loads):
        if i + 1 < len(loads):
            load(i + 1).start()
        load(i).wait()
        pack_heads(stage.at[i % 2], 0, heads_ref, row0, rows, tail)
    rest = steps[4:]
    inside = heads // 2

    @pl.loop(0, heads)
    def _(h):
        attend_head(h, qh, kh, vh, gh, top_ref)
        for i, step in enumerate(rest[:inside]):
            pl.when(h == 2 * i)(step)

    stores = [(qh, 0, dq_ref, 0)]
    for row0, ref in ((0, down_ref), (rows, dfar_ref)):
        stores += [(kh, row0, ref, 0), (vh, row0, ref, width)]

    def store(i):
        ref, column = stores[i][2:]
        return pltpu.make_async_copy(stage.at[i % 2], ref.at[:, pl.ds(column, width)], stage_sem.at[i % 2])

    for i, (heads_ref, row0, ref, column) in enumerate(stores):
        if i >= 2:
            store(i - 2).wait()
        unpack_heads(heads_ref, row0, rows, stage.at[i % 2], 0)
        store(i).start()
    for i in (len(stores) - 2, len(stores) - 1):
        store(i).wait()
    for step in rest[inside:]:
        step()
    settle()


def reduce_attend(grads, rows_out, count, query, own, far, grad, top, band_slots, collective_id):
    phases = len(grads)
    half, width = grads[0][0].shape[-2:]
    counts = tuple(len(phase) for phase in grads)
    rows = query.shape[0]
    heads = width // HEAD_DIM
    bf = jnp.bfloat16
    scratch = reduce_scratch(phases, half, width)
    scratch.update(
        qh=pltpu.VMEM((heads, rows, LANES), bf),
        kh=pltpu.VMEM((heads, 2 * rows, LANES), bf),
        vh=pltpu.VMEM((heads, 2 * rows, LANES), bf),
        gh=pltpu.VMEM((heads, rows, LANES), bf),
        stage=pltpu.VMEM((2, rows, width), bf),
        stage_sem=pltpu.SemaphoreType.DMA((2,)),
        **home_scratch(),
    )
    any_, vmem = pl.BlockSpec(memory_space=pl.ANY), pl.BlockSpec(memory_space=pltpu.VMEM)
    smem = pl.BlockSpec(memory_space=pltpu.SMEM)
    outs = pl.pallas_call(
        partial(reduce_attend_kernel, counts, band_slots, tuple(scratch)),
        out_shape=[jax.ShapeDtypeStruct((4, 2, half, width), bf)] * phases
        + [
            jax.ShapeDtypeStruct(rows_out.shape, bf),
            jax.ShapeDtypeStruct((rows, width), bf),
            jax.ShapeDtypeStruct((rows, 2 * width), bf),
            jax.ShapeDtypeStruct((rows, 2 * width), bf),
        ],
        in_specs=[any_] * (sum(counts) + 1) + [smem] + [any_] * 4 + [vmem],
        out_specs=[any_] * (phases + 4),
        scratch_shapes=list(scratch.values()),
        compiler_params=pltpu.CompilerParams(
            collective_id=collective_id, has_side_effects=True, vmem_limit_bytes=60 * 2**20
        ),
        name="reduce_attend",
    )(*[unit for phase in grads for unit in phase], rows_out, count, query, own, far, grad, top)
    return outs[:phases], *outs[phases:]


MOD_BLOCKS = 6
BLOCK = 128


def forward_scratch(half, ff, width, rows, note_rows, images):
    bf, f32 = jnp.bfloat16, jnp.float32
    D = pltpu.SemaphoreType.DMA
    heads = width // HEAD_DIM
    V = pltpu.VMEM
    return dict(
        qp=V((NB, 2, half, ff), bf), bounce_i=V((2, half, ff), bf), bounce_o=V((4, 2, half, width), bf),
        bounce_t=V((rows // images, width), bf), tok=V((images, rows // images, width), bf),
        notes=V((NB, note_rows, 128), f32), vec=V((16, width), f32),
        residual=V((rows, width), f32), attn_in=V((rows, width), bf), query=V((rows, width), bf),
        own=V((rows, 2 * width), bf), far=V((rows, 2 * width), bf), mixed=V((rows, width), bf),
        attended=V((rows, width), f32), mlp_in=V((rows, width), bf), tops=V((heads, 8, rows), f32),
        qh=V((heads, rows, LANES), bf), kh=V((heads, 2 * rows, LANES), bf), vh=V((heads, 2 * rows, LANES), bf),
        z_send=D((3, 2)), z_recv=D((3, NB)), f_send=D((3, NB)), a_send=D((9,)), a_recv=D((9,)), b_send=D((9, 2)), b_recv=D((9, 2)),
        c_send=D((9,)), c_recv=D((9,)), t_send=D((2, 2)), t_recv=D((2, 2)), m_send=D((2, 2)), m_recv=D((NB,)),
        local=D((4,)), kv_send=D((1,)), kv_recv=D((1,)), done=D((12,)),
    )


def gather_steps(me, width, ins, outs, tok_in, tok_out, cot_in, cot_out, note_in, note_out, sc):
    dp, band, core, px, py, kind = me.dp, me.band, me.core, me.px, me.py, me.kind
    base = dp - core
    dev = lambda d, b: device(d, b)
    here = lambda d: dev(d, band)
    flip = lambda v: 1 - v
    low = band < 2
    bands = (band + 1 - 2 * lax.rem(band, 2), jnp.where(low, 2, 1), jnp.where(low, 3, 0))
    order = [(ph, b) for ph in range(3) for b in bands]
    inside = jnp.logical_or(band == 1, band == 2)
    sends = []

    def remote(src, dst, ss, rs, to):
        return pltpu.make_async_remote_copy(
            src_ref=src, dst_ref=dst, send_sem=ss, recv_sem=rs, device_id=to, device_id_type=MESH
        )

    def go(make):
        make().start()
        sends.append(make)

    def cols(t, n=1):
        return pl.ds(pl.multiple_of(t * width, 128), n * width)

    def unit(ph, b, t, h):
        return outs[ph].at[b, t, h] if ph == 2 else outs[ph].at[b, h, :, cols(t)]

    def pair(ph, b, h, y):
        return outs[ph].at[b, pl.ds(2 * y, 2), h] if ph == 2 else outs[ph].at[b, h, :, cols(2 * y, 2)]

    def row(ph, b, h):
        return outs[ph].at[b, :, h] if ph == 2 else outs[ph].at[b, h]

    def own_z(ph, up):
        src = ins[ph].at[kind, core] if ph == 2 else ins[ph].at[core, :, cols(kind)]
        return remote(
            src, unit(ph, band, kind, core), sc.z_send.at[ph, up], sc.z_recv.at[ph, band],
            dev(dp, band - 1 + 2 * up),
        )

    def pass_z(s):
        ph, b = order[s]
        u = unit(ph, b, kind, core)
        return remote(
            u, u, sc.f_send.at[ph, b], sc.z_recv.at[ph, b], dev(dp, jnp.where(b < band, band + 1, band - 1))
        )

    def send_a(s):
        ph, b = order[s]
        u = unit(ph, b, kind, core)
        return remote(u, u, sc.a_send.at[s], sc.a_recv.at[s], here(me.xdp if s % 2 == 0 else me.ydp))

    def b_copy(s, j, mine):
        ph, b = order[s]
        if s % 2 == 0:
            u = pair(ph, b, core, py if mine else flip(py))
            to = me.ydp
        else:
            u = unit(ph, b, 2 * j + (px if mine else flip(px)), core)
            to = me.xdp
        return remote(u, u, sc.b_send.at[s, j], sc.b_recv.at[s, j], here(to))

    def c_copy(s, mine):
        ph, b = order[s]
        u = row(ph, b, core if mine else flip(core))
        return remote(u, u, sc.c_send.at[s], sc.c_recv.at[s], here(me.sib))

    def z_start(ph):
        pl.when(band < NB - 1)(lambda: own_z(ph, 1).start())
        pl.when(band > 0)(lambda: own_z(ph, 0).start())

    def z_wait(s):
        ph, b = order[s]
        u = unit(ph, b, kind, core)
        remote(u, u, sc.a_send.at[s], sc.z_recv.at[ph, b], here(dp)).wait_recv()
        pl.when(inside)(lambda: pass_z(s).start())
        go(partial(send_a, s))

    def a_wait(s):
        ph, b = order[s]
        got = 2 * py + flip(px) if s % 2 == 0 else 2 * flip(py) + px
        u = unit(ph, b, got, core)
        remote(u, u, sc.a_send.at[s], sc.a_recv.at[s], here(me.xdp)).wait_recv()
        for j in range(1 if s % 2 == 0 else 2):
            go(partial(b_copy, s, j, True))

    def b_wait(s):
        for j in range(1 if s % 2 == 0 else 2):
            b_copy(s, j, False).wait_recv()
        go(partial(c_copy, s, True))

    def c_wait(s):
        c_copy(s, False).wait_recv()

    slot = lax.rem(band, 2)

    def image_copy(which, src, dst, i):
        to = dev(base + band // 2, 2 * core + i)
        return remote(src.at[i], dst.at[slot], sc.t_send.at[which, i], sc.t_recv.at[which, slot], to)

    def at_home(i):
        return jnp.logical_and(band // 2 == core, 2 * core + i == band)

    def move(which, src, dst, bounce=None):
        for i in range(2):

            @pl.when(at_home(i))
            def _():
                if bounce is None:
                    pltpu.make_async_copy(src.at[i], dst.at[slot], sc.t_recv.at[which, slot]).start()
                else:
                    inward = pltpu.make_async_copy(src.at[i], bounce, sc.local.at[3])
                    inward.start()
                    inward.wait()
                    pltpu.make_async_copy(bounce, dst.at[slot], sc.t_recv.at[which, slot]).start()

            @pl.when(jnp.logical_not(at_home(i)))
            def _():
                image_copy(which, src, dst, i).start()

    def move_wait(which, src, dst):
        for i in range(2):

            @pl.when(jnp.logical_not(at_home(i)))
            def _():
                image_copy(which, src, dst, i).wait_send()

        for s in range(2):
            pltpu.make_async_copy(dst.at[s], dst.at[s], sc.t_recv.at[which, s]).wait()

    def note_copy(i, c):
        return remote(
            note_in.at[i], note_out.at[band], sc.m_send.at[i, c], sc.m_recv.at[band],
            dev(base + c, 2 * core + i),
        )

    def note_home(i, c):
        return jnp.logical_and(c == core, 2 * core + i == band)

    def begin():
        for i in range(2):
            for c in range(2):

                @pl.when(note_home(i, c))
                def _():
                    pltpu.make_async_copy(note_in.at[i], note_out.at[band], sc.m_recv.at[band]).start()

                @pl.when(jnp.logical_not(note_home(i, c)))
                def _():
                    note_copy(i, c).start()

        z_start(0)
        for ph, dst in enumerate((outs[0].at[band], sc.bounce_i, sc.bounce_o)):
            pltpu.make_async_copy(ins[ph], dst, sc.local.at[ph]).start()

    def arrived():
        for i in range(2):
            for c in range(2):

                @pl.when(jnp.logical_not(note_home(i, c)))
                def _():
                    note_copy(i, c).wait_send()

        for b in range(NB):
            pltpu.make_async_copy(note_in.at[0], note_out.at[b], sc.m_recv.at[b]).wait()
        move_wait(0, tok_in, tok_out)

    def place():
        for ph, dst in ((1, sc.bounce_i), (2, sc.bounce_o)):
            pltpu.make_async_copy(ins[ph], dst, sc.local.at[ph]).wait()
            pltpu.make_async_copy(dst, outs[ph].at[band], sc.local.at[ph]).start()

    def first_here():
        pltpu.make_async_copy(ins[0], outs[0].at[band], sc.local.at[0]).wait()

    def finish():
        for ph, src in ((1, sc.bounce_i), (2, sc.bounce_o)):
            pltpu.make_async_copy(src, outs[ph].at[band], sc.local.at[ph]).wait()
        move_wait(1, cot_in, cot_out)
        for ph in range(3):
            pl.when(band < NB - 1)(lambda: own_z(ph, 1).wait_send())
            pl.when(band > 0)(lambda: own_z(ph, 0).wait_send())
        for s in range(len(order)):
            pl.when(inside)(lambda: pass_z(s).wait_send())
        for make in sends:
            make().wait_send()

    def images(which):
        if which == 0:
            move(0, tok_in, tok_out)
        else:
            move(1, cot_in, cot_out, sc.bounce_t)

    return SimpleNamespace(
        i=images, s=z_start,
        begin=begin, arrived=arrived, place=place, first_here=first_here, finish=finish,
        z=z_wait, a=a_wait, b=b_wait, c=c_wait,
    )


def forward_kernel(names, band_slots, *refs):
    me = compass()
    qp_in, inner_in, outer_in, tok_in, cot_in, note_in, table_ref = refs[:7]
    (qp_out, inner_out, outer_out, cot_out, vec_out, residual_out, attn_out, query_out, own_out, far_out,
     tops_out, mixed_out, attended_out, mlp_out) = refs[7:21]
    sc = SimpleNamespace(**dict(zip(names, refs[21:])))
    rows, width = sc.residual.shape
    heads = width // HEAD_DIM
    core = me.core
    qp, tok, notes, vec = sc.qp, sc.tok, sc.notes, sc.vec

    group_barrier(me)
    g = gather_steps(
        me, width, (qp_in, inner_in, outer_in), (qp, inner_out, outer_out), tok_in, tok, cot_in, cot_out,
        note_in, notes, sc,
    )
    saves = []

    def save(src, dst):
        copy = pltpu.make_async_copy(src, dst, sc.done.at[len(saves)])
        copy.start()
        saves.append(copy)

    def run(*words):
        for do, index in words:
            do(index)

    g.begin()
    g.place()
    run((g.z, 0), (g.z, 1), (g.i, 0), (g.a, 0), (g.a, 1), (g.z, 2), (g.s, 1), (g.b, 0), (g.b, 1), (g.a, 2), (g.c, 0), (g.c, 1), (g.z, 3), (g.z, 4), (g.b, 2))
    g.arrived()
    spread_notes(notes, vec, width)
    grid_rows = notes[0, 63:64, 0:1]
    grid_cols = notes[0, 63:64, 1:2]
    band_rows = jnp.floor(grid_rows * 0.25)
    valid_count = (band_rows * grid_cols).astype(jnp.int32)
    lane = lax.broadcasted_iota(jnp.int32, (1, width), 1)
    vec[15:16, :] = jnp.where(lane == 0, band_rows * grid_cols, 0.0)
    save(vec, vec_out)

    @pl.loop(0, rows // BLOCK)
    def _(step):
        at = pl.multiple_of(step * BLOCK, BLOCK)
        sub = pl.ds(at, BLOCK)
        per_image = band_slots // BLOCK
        within = (
            lax.rem(step, per_image) * BLOCK + lax.broadcasted_iota(jnp.int32, (BLOCK, 1), 0)
        ).astype(jnp.float32)
        down = jnp.floor((within + 0.5) / grid_cols)
        place = (2 * core + step // per_image).astype(jnp.float32)
        picks = []
        for index in (place * band_rows + down, within - down * grid_cols):
            lanes = lax.broadcasted_iota(jnp.int32, (BLOCK, 128), 1).astype(jnp.float32)
            pick = jnp.where(lanes == index, 1.0, 0.0).astype(jnp.bfloat16)
            part = [jnp.dot(pick, table_ref[i], preferred_element_type=jnp.float32) for i in range(3)]
            picks.append(part[0] + (part[1] + part[2]))
        token = tok[step // per_image, pl.ds(lax.rem(step, per_image) * BLOCK, BLOCK), :]
        residual = token.astype(jnp.float32) + jnp.concatenate(picks, 1)
        sc.residual[sub, :] = residual
        normed = normalize(residual)[0]
        sc.attn_in[sub, :] = (normed * (1.0 + vec[1:2, :]) + vec[0:1, :]).astype(jnp.bfloat16)

    save(sc.residual, residual_out)
    save(sc.attn_in, attn_out)
    g.first_here()
    run((g.c, 2))
    save(qp, qp_out)
    tile = width // 3
    full = NB * 2 * qp.shape[2]

    def product(left_ref, first, step):
        at = pl.ds(pl.multiple_of(first + step * tile, 128), tile)
        return jnp.dot(
            left_ref[...], qp[:, :, :, at].reshape(full, tile), preferred_element_type=jnp.float32
        )

    def here(step):
        return pl.ds(pl.multiple_of(step * tile, 128), tile)

    @pl.loop(0, 3)
    def _(step):
        sc.own[:, here(step)] = product(sc.attn_in, width, step).astype(jnp.bfloat16)

    run((g.a, 3), (g.z, 5), (g.s, 2))

    @pl.loop(0, 3)
    def _(step):
        value = product(sc.attn_in, 2 * width, step) + vec[7:8, here(step)]
        sc.own[:, here(step + 3)] = value.astype(jnp.bfloat16)

    swap = pltpu.make_async_remote_copy(
        src_ref=sc.own, dst_ref=sc.far, send_sem=sc.kv_send.at[0], recv_sem=sc.kv_recv.at[0],
        device_id=device(me.sib, me.band), device_id_type=MESH,
    )
    swap.start()
    run((g.a, 4), (g.b, 3))

    @pl.loop(0, 3)
    def _(step):
        value = product(sc.attn_in, 0, step) + vec[6:7, here(step)]
        sc.query[:, here(step)] = value.astype(jnp.bfloat16)

    save(sc.query, query_out)
    save(sc.own, own_out)
    run((g.a, 5), (g.b, 4), (g.c, 3), (g.z, 6))
    qh, kh, vh = sc.qh, sc.kh, sc.vh
    keys, plain = key_tail(valid_count, band_slots), flat_tail(0.0)
    pack_heads(sc.query, 0, qh, 0, rows, flat_tail(1.0))
    pack_heads(sc.own, 0, kh, 0, rows, keys)
    pack_heads(sc.own, width, vh, 0, rows, plain)
    swap.wait()
    save(sc.far, far_out)
    pack_heads(sc.far, 0, kh, rows, rows, keys)
    pack_heads(sc.far, width, vh, rows, rows, plain)
    beside = {
        0: ((g.z, 7), (g.b, 5), (g.c, 4)), 2: ((g.a, 6), (g.z, 8), (g.i, 1)), 4: ((g.a, 7), (g.b, 6), (g.c, 5)), 7: ((g.a, 8), (g.b, 7), (g.c, 6)), 10: ((g.b, 8), (g.c, 7)),
        13: ((g.c, 8),),
    }

    @pl.loop(0, heads)
    def _(h):
        attend_block(h, qh, kh, vh, sc.tops)
        for i, words in beside.items():
            pl.when(h == i)(partial(run, *words))

    unpack_heads(qh, 0, rows, sc.mixed, 0)
    save(sc.tops, tops_out)
    save(sc.mixed, mixed_out)

    @pl.loop(0, 3)
    def _(step):
        sc.attended[:, here(step)] = product(sc.mixed, 3 * width, step) + vec[8:9, here(step)]

    save(sc.attended, attended_out)

    @pl.loop(0, rows // BLOCK)
    def _(step):
        sub = pl.ds(pl.multiple_of(step * BLOCK, BLOCK), BLOCK)
        middle = sc.residual[sub, :] + vec[2:3, :] * sc.attended[sub, :]
        normed = normalize(middle)[0]
        sc.mlp_in[sub, :] = (normed * (1.0 + vec[4:5, :]) + vec[3:4, :]).astype(jnp.bfloat16)

    save(sc.mlp_in, mlp_out)
    g.finish()
    for copy in saves:
        copy.wait()


NOTE_COND, NOTE_GRID, NOTE_BIAS = 54, 63, 64


def spread_notes(notes, vec, width):
    lines = width // 128
    share = notes.shape[0]
    total = notes[0, 0:NOTE_GRID, :] + 0.0
    for b in range(1, share):
        total = total + notes[b, 0:NOTE_GRID, :]

    def flat(block, first):
        return jnp.concatenate([block[first + i : first + i + 1, :] for i in range(lines)], 1)

    for index in range(MOD_BLOCKS):
        vec[index : index + 1, :] = flat(total, index * lines)
    small = width // share
    for index in range(4):
        parts = []
        for b in range(share):
            first = NOTE_BIAS + 3 * index
            for i in range(3):
                parts.append(notes[b, first + i : first + i + 1, : min(128, small - 128 * i)])
        vec[6 + index : 7 + index, :] = jnp.concatenate(parts, 1)
    for b in range(share):
        block = notes[b, NOTE_BIAS + 12 : NOTE_BIAS + 12 + lines, :]
        vec[10 + b : 11 + b, :] = flat(block, 0)
    vec[14:15, :] = flat(notes[0, NOTE_COND : NOTE_COND + lines, :], 0)


def forward_block(qp, inner, outer, tok, cot, note, table):
    half, ff = qp.shape[0] // 2, qp.shape[1]
    images, band_slots, width = tok.shape
    rows = images * band_slots
    heads = width // HEAD_DIM
    bf, f32 = jnp.bfloat16, jnp.float32
    S = jax.ShapeDtypeStruct
    qp, inner = qp.reshape(2, half, ff), inner.reshape(2, half, ff)
    outer = outer.reshape(4, 2, half, width)
    scratch = forward_scratch(half, ff, width, rows, note.shape[1], images)
    any_ = pl.BlockSpec(memory_space=pl.ANY)
    return pl.pallas_call(
        partial(forward_kernel, tuple(scratch), band_slots),
        out_shape=[
            S((NB, 2, half, ff), bf), S((NB, 2, half, ff), bf), S((NB, 4, 2, half, width), bf), S(cot.shape, bf),
            S((16, width), f32), S((rows, width), f32), S((rows, width), bf), S((rows, width), bf),
            S((rows, 2 * width), bf), S((rows, 2 * width), bf), S((heads, 8, rows), f32), S((rows, width), bf),
            S((rows, width), f32), S((rows, width), bf),
        ],
        in_specs=[any_] * 6 + [pl.BlockSpec(memory_space=pltpu.VMEM)],
        out_specs=[any_] * 14,
        scratch_shapes=list(scratch.values()),
        compiler_params=pltpu.CompilerParams(
            collective_id=0, has_side_effects=True, vmem_limit_bytes=60 * 2**20
        ),
        name="forward_block",
    )(qp, inner, outer, tok, cot, note, table)


def pair_perm(dp_count, band_count):
    return [
        (dp * band_count + band, (dp ^ 1) * band_count + band)
        for dp in range(dp_count)
        for band in range(band_count)
    ]


def position_parts(width):
    quarter = width // 4
    frequency = 10000.0 ** (-jnp.arange(quarter, dtype=jnp.float32) / quarter)
    angles = jnp.arange(128, dtype=jnp.float32)[:, None] * frequency
    left = jnp.concatenate([jnp.sin(angles), jnp.cos(angles)], -1)
    parts = []
    for _ in range(3):
        part = lax.reduce_precision(left, 8, 7)
        parts.append(part.astype(jnp.bfloat16))
        left = left - part
    return jnp.stack(parts)


def over_groups(piece, dp_count):
    if dp_count == 8:
        return piece
    groups = [[rank + 8 * group for group in range(dp_count // 8)] for rank in range(8)]
    return lax.psum(piece.astype(jnp.float32), "dp", axis_index_groups=groups)


def every_group(piece, dp_count):
    if dp_count == 8:
        return piece[None]
    groups = [[rank + 8 * group for group in range(dp_count // 8)] for rank in range(8)]
    return lax.all_gather(piece, "dp", axis_index_groups=groups)


def own_piece(vector, count, band_place):
    return lax.dynamic_slice_in_dim(vector, band_place * count, count, 0)


def body(
    tokens,
    condition,
    patch_grid,
    ada_weight,
    ada_bias,
    qkv_weight,
    query_bias,
    value_bias,
    proj_weight,
    proj_bias,
    inner_weight,
    inner_bias,
    outer_weight,
    outer_bias,
    cotangent,
):
    both = ("dp", "band")
    dp_count = lax.axis_size("dp")
    band_count = lax.axis_size("band")
    images, band_slots, width = tokens.shape
    band = lax.axis_index("band")
    dp = lax.axis_index("dp")
    core = lax.rem(dp, 2)
    hidden = inner_weight.shape[1]
    part_rows = qkv_weight.shape[0]
    siblings = pair_perm(dp_count, band_count)

    condition_f = condition.astype(jnp.float32)
    activated = jax.nn.silu(condition_f).astype(jnp.bfloat16)
    own_activated = lax.dynamic_slice_in_dim(activated, band * part_rows, part_rows, 1)
    share = jnp.dot(own_activated, ada_weight, preferred_element_type=jnp.float32)
    share = share + lax.dynamic_update_slice_in_dim(
        jnp.zeros((ada_weight.shape[1],), jnp.float32),
        ada_bias.astype(jnp.float32),
        band * ada_bias.shape[0],
        0,
    )
    mod_count = share.shape[1]
    lines = lambda vector: jnp.pad(
        vector.astype(jnp.float32), [(0, 0)] * (vector.ndim - 1) + [(0, -vector.shape[-1] % 128)]
    )
    spread = lambda vector: jnp.broadcast_to(lines(vector), (images, -(-vector.shape[0] // 128) * 128))
    note = jnp.concatenate(
        [share, condition_f, lines(patch_grid)]
        + [spread(bias) for bias in (query_bias, value_bias, proj_bias, outer_bias, inner_bias)],
        1,
    )
    note = jnp.pad(note, ((0, 0), (0, -note.shape[1] % 1024))).reshape(images, -1, 128)
    first_weight = jnp.concatenate([qkv_weight, proj_weight], 1)
    (first_full, inner_full, outer_full, cotangent_here, vectors, residual, attn_in, query_rows, key_value,
     other_key_value, tops, mixed_rows, attended, mlp_in) = forward_block(
        first_weight, inner_weight, outer_weight, tokens, cotangent, note, position_parts(width)
    )
    first_full = first_full.reshape(width, -1)
    inner_full = inner_full.reshape(width, hidden)
    outer_full = outer_full.reshape(hidden, width)
    qkv_full = first_full[:, : 3 * width]
    proj_full = first_full[:, 3 * width :]
    scale_one, gate_one = vectors[1], vectors[2]
    scale_two, gate_two = vectors[4], vectors[5]
    outer_bias_full = vectors[9]
    inner_bias_full = vectors[10:14].reshape(-1)
    condition_here = vectors[14]
    valid_count = vectors[15, :1].astype(jnp.int32)
    rows = images * band_slots
    is_valid = jnp.arange(rows, dtype=jnp.int32) % band_slots < valid_count
    normed_one, inverse_one = normalize(residual)
    middle = residual + gate_one * attended
    normed_two, inverse_two = normalize(middle)
    hidden_pre = jnp.dot(mlp_in, inner_full, preferred_element_type=jnp.float32) + inner_bias_full
    hidden_act = jax.nn.gelu(hidden_pre, approximate=True).astype(jnp.bfloat16)
    mlp_out = jnp.dot(hidden_act, outer_full, preferred_element_type=jnp.float32) + outer_bias_full
    block_out = (middle + gate_two * mlp_out).astype(jnp.bfloat16)

    grad_out = cotangent_here.reshape(rows, width).astype(jnp.float32) * is_valid[:, None].astype(
        jnp.float32
    )
    grad_gate_two = jnp.sum(grad_out * mlp_out, 0)
    grad_mlp = (gate_two * grad_out).astype(jnp.bfloat16)
    gelu_back = jax.vjp(partial(jax.nn.gelu, approximate=True), hidden_pre)[1]
    blocks = (band_count, 2, part_rows // 2, width)
    grad_outer = rows_dot(hidden_act, grad_mlp).astype(jnp.bfloat16).reshape(
        band_count, 4, 2, part_rows // 2, width
    )
    grad_outer_bias = jnp.sum(grad_mlp.astype(jnp.float32), 0)
    grad_hidden = lanes_dot(grad_mlp, outer_full)
    grad_pre = gelu_back(grad_hidden)[0].astype(jnp.bfloat16)
    grad_inner = [
        rows_dot(mlp_in, grad_pre[:, t * width : (t + 1) * width]).astype(jnp.bfloat16).reshape(blocks)
        for t in range(4)
    ]
    grad_inner_bias = jnp.sum(grad_pre.astype(jnp.float32), 0)
    grad_mlp_in = lanes_dot(grad_pre, inner_full)
    grad_shift_two = jnp.sum(grad_mlp_in, 0)
    grad_scale_two = jnp.sum(grad_mlp_in * normed_two, 0)
    grad_middle = grad_out + norm_back(grad_mlp_in * (1.0 + scale_two), normed_two, inverse_two)
    grad_gate_one = jnp.sum(grad_middle * attended, 0)
    grad_attended = (gate_one * grad_middle).astype(jnp.bfloat16)
    grad_proj = rows_dot(mixed_rows, grad_attended).astype(jnp.bfloat16)
    grad_proj_bias = jnp.sum(grad_attended.astype(jnp.float32), 0)
    grad_mixed = lanes_dot(grad_attended, proj_full).astype(jnp.bfloat16)
    (outer_sum, inner_sum), block_home, grad_query, own_terms, far_terms = reduce_attend(
        [[grad_outer], grad_inner], block_out.reshape(images, band_slots, width), valid_count, query_rows, key_value, other_key_value, grad_mixed, tops,
        band_slots, 1,
    )
    other_terms = lax.ppermute(far_terms, both, siblings)
    grad_key_value = (own_terms.astype(jnp.float32) + other_terms.astype(jnp.float32)).astype(
        jnp.bfloat16
    )
    grad_qkv = jnp.concatenate([grad_query, grad_key_value], -1)
    grad_first = [
        rows_dot(attn_in, part).astype(jnp.bfloat16).reshape(blocks)
        for part in (grad_query, grad_key_value[:, :width], grad_key_value[:, width:])
    ]
    grad_attn_in = lanes_dot(grad_qkv, qkv_full)
    grad_query_bias = jnp.sum(grad_query.astype(jnp.float32), 0)
    grad_value_bias = jnp.sum(grad_key_value[:, width:].astype(jnp.float32), 0)
    grad_shift_one = jnp.sum(grad_attn_in, 0)
    grad_scale_one = jnp.sum(grad_attn_in * normed_one, 0)
    grad_tokens = grad_middle + norm_back(grad_attn_in * (1.0 + scale_one), normed_one, inverse_one)
    part_mod = jnp.concatenate(
        [grad_shift_one, grad_scale_one, grad_gate_one, grad_shift_two, grad_scale_two, grad_gate_two]
    )
    part_mod = jnp.concatenate([part_mod, 0.5 * condition_here]).reshape(-1, 128)
    part_mod = jnp.pad(part_mod, ((0, -part_mod.shape[0] % 16), (0, 0)))
    part_bias = jnp.concatenate(
        [grad_query_bias, grad_value_bias, grad_proj_bias, grad_inner_bias, grad_outer_bias]
    ).reshape(-1, 128)
    (first_sum,), tokens_home, every, bias_grads, grad_act = reduce_last(
        [grad_first + [grad_proj.reshape(blocks)]],
        grad_tokens.astype(jnp.bfloat16).reshape(images, band_slots, width), part_mod, part_bias, ada_weight, images, 2
    )
    tokens_home = tokens_home.astype(jnp.float32)
    every = every_group(every, dp_count)
    bias_grads = over_groups(bias_grads, dp_count).reshape(-1)
    every = jnp.swapaxes(every, 1, 2).reshape(dp_count * images, -1)
    every_mod = every[:, :mod_count]
    every_condition = every[:, mod_count : mod_count + width]
    every_activated = jax.nn.silu(every_condition.astype(jnp.float32)).astype(jnp.bfloat16)
    every_activated = lax.dynamic_slice_in_dim(every_activated, band * part_rows, part_rows, 1)
    grad_ada = rows_dot(every_activated, every_mod)
    grad_ada_bias = own_piece(jnp.sum(every_mod.astype(jnp.float32), 0), ada_bias.shape[0], band)
    grad_act = jnp.swapaxes(grad_act[:, :images, :part_rows], 0, 1).reshape(images, width)
    grad_condition = jax.vjp(jax.nn.silu, condition_f)[1](grad_act)[0]

    def side_by_side(units):
        return jnp.concatenate([unit.reshape(part_rows, width) for unit in units], 1).astype(jnp.float32)

    first_sum, inner_sum, outer_sum = [
        over_groups(piece, dp_count) for piece in (first_sum, inner_sum, outer_sum)
    ]
    qkv_sum = side_by_side([first_sum[t] for t in range(3)])
    proj_sum = first_sum[3].reshape(part_rows, width).astype(jnp.float32)
    inner_sum = side_by_side([inner_sum[t] for t in range(4)])
    outer_sum = outer_sum.reshape(4 * part_rows, width).astype(jnp.float32)
    bias_parts = []
    at = 0
    for piece in (query_bias, value_bias, proj_bias, inner_bias, outer_bias):
        whole = piece.shape[0] * band_count
        bias_parts.append(own_piece(bias_grads[at : at + whole], piece.shape[0], band))
        at += whole
    return (
        block_home,
        tokens_home,
        grad_condition,
        grad_ada,
        grad_ada_bias,
        qkv_sum,
        bias_parts[0],
        bias_parts[1],
        proj_sum,
        bias_parts[2],
        inner_sum,
        bias_parts[3],
        outer_sum,
        bias_parts[4],
    )


def solution(mesh):
    placed = (
        P("dp", "band", None),
        P("dp", None),
        P("dp", None),
        P("band", None),
        P("band"),
        P("band", None),
        P("band"),
        P("band"),
        P("band", None),
        P("band"),
        P("band", None),
        P("band"),
        P("band", None),
        P("band"),
        P("dp", "band", None),
    )
    return jax.shard_map(
        body,
        mesh=mesh,
        in_specs=placed,
        out_specs=(
            P("dp", "band", None),
            P("dp", "band", None),
            P("dp", None),
            P("band", None),
            P("band"),
            P("band", None),
            P("band"),
            P("band"),
            P("band", None),
            P("band"),
            P("band", None),
            P("band"),
            P("band", None),
            P("band"),
        ),
        check_vma=False,
    )
```

```python
from functools import partial
from types import SimpleNamespace

import jax
import jax.numpy as jnp
from jax import lax
from jax.experimental import pallas as pl
from jax.experimental.pallas import tpu as pltpu
from jax.sharding import PartitionSpec as P

HEAD_DIM = 72


MESH = pl.DeviceIdType.MESH
NB = 4


def device(dp, band):
    return {"dp": dp, "band": band}


def normalize(values):
    average = jnp.mean(values, -1, keepdims=True)
    centered = values - average
    variance = jnp.mean(centered * centered, -1, keepdims=True)
    inverse = lax.rsqrt(variance + 1e-06)
    return (centered * inverse, inverse)


def norm_back(grad_normed, normed, inverse):
    first = jnp.mean(grad_normed, -1, keepdims=True)
    second = jnp.mean(grad_normed * normed, -1, keepdims=True)
    return inverse * (grad_normed - first - normed * second)


LANES = 128
PACK_ROWS = 128


def pack_heads(source, first, heads_ref, row0, rows, tail):
    heads = heads_ref.shape[0]

    @pl.loop(0, rows // PACK_ROWS)
    def _(step):
        at = pl.multiple_of(step * PACK_ROWS, PACK_ROWS)
        block = source[pl.ds(at, PACK_ROWS), first : first + heads * HEAD_DIM]
        end = tail(at)
        for h in range(heads):
            part = block[:, h * HEAD_DIM : (h + 1) * HEAD_DIM]
            heads_ref[h, pl.ds(row0 + at, PACK_ROWS), :] = jnp.concatenate([part, end], 1)


def unpack_heads(heads_ref, row0, rows, target, first):
    heads = heads_ref.shape[0]

    @pl.loop(0, rows // PACK_ROWS)
    def _(step):
        at = pl.multiple_of(step * PACK_ROWS, PACK_ROWS)
        parts = [heads_ref[h, pl.ds(row0 + at, PACK_ROWS), :][:, :HEAD_DIM] for h in range(heads)]
        target[pl.ds(at, PACK_ROWS), first : first + heads * HEAD_DIM] = jnp.concatenate(parts, 1)


def flat_tail(value):
    def tail(at):
        lane = lax.broadcasted_iota(jnp.int32, (PACK_ROWS, LANES - HEAD_DIM), 1)
        return jnp.where(lane == 0, value, 0.0).astype(jnp.bfloat16)

    return tail


def key_tail(valid_count, band_slots):
    def tail(at):
        shape = (PACK_ROWS, LANES - HEAD_DIM)
        lane = lax.broadcasted_iota(jnp.int32, shape, 1)
        slot = lax.rem(at + lax.broadcasted_iota(jnp.int32, shape, 0), band_slots)
        return jnp.where(jnp.logical_and(lane == 0, slot >= valid_count), -1e30, 0.0).astype(jnp.bfloat16)

    return tail


def lanes_dot(left, right):
    return lax.dot_general(left, right, (((1,), (1,)), ((), ())), preferred_element_type=jnp.float32)


def rows_dot(left, right):
    return lax.dot_general(left, right, (((0,), (0,)), ((), ())), preferred_element_type=jnp.float32)


SCORE_SCALE = HEAD_DIM ** (-0.5)


def attend_block(h, qh, kh, vh, top_ref):
    rows = qh.shape[1]
    for block in range(2):
        at = pl.ds(block * rows // 2, rows // 2)
        scores = lanes_dot(kh[h], qh[h, at, :]) * SCORE_SCALE
        top = jnp.max(scores, 0, keepdims=True)
        weights = jnp.exp(scores - top)
        total = jnp.sum(weights, 0, keepdims=True)
        low = (weights * (1.0 / total)).astype(jnp.bfloat16)
        mixed = rows_dot(vh[h], low)
        qh[h, at, :] = jnp.transpose(mixed).astype(jnp.bfloat16)
        top_ref[h, :, at] = jnp.broadcast_to(top + jnp.log(total), (8, rows // 2))


def attend_head(h, qh, kh, vh, gh, top_ref):
    query = qh[h]
    key = kh[h]
    grad = gh[h]
    probs = jnp.exp(lanes_dot(key, query) * SCORE_SCALE - top_ref[h, 0:1, :])
    grad_probs = lanes_dot(vh[h], grad)
    inner = jnp.sum(probs * grad_probs, 0, keepdims=True)
    grad_scores = (probs * (grad_probs - inner)).astype(jnp.bfloat16)
    vh[h] = jnp.dot(
        probs.astype(jnp.bfloat16), grad, preferred_element_type=jnp.float32
    ).astype(jnp.bfloat16)
    grad_query = rows_dot(key, grad_scores)
    kh[h] = (
        SCORE_SCALE * jnp.dot(grad_scores, query, preferred_element_type=jnp.float32)
    ).astype(jnp.bfloat16)
    qh[h] = (SCORE_SCALE * jnp.transpose(grad_query)).astype(jnp.bfloat16)


def compass():
    dp = lax.axis_index("dp")
    band = lax.axis_index("band")
    core = lax.rem(dp, 2)
    px = lax.rem(dp // 2, 2)
    py = lax.rem(dp // 4, 2)
    return SimpleNamespace(
        dp=dp, band=band, core=core, px=px, py=py, kind=2 * py + px,
        sib=dp + 1 - 2 * core, xdp=dp + 2 - 4 * px, ydp=dp + 4 - 8 * py,
    )


def add_rows(total, term):
    rows = total.shape[0]

    @pl.loop(0, rows // 16)
    def _(step):
        at = pl.ds(pl.multiple_of(step * 16, 16), 16)
        total[at, :] = (
            total[at, :].astype(jnp.float32) + term[at, :].astype(jnp.float32)
        ).astype(jnp.bfloat16)


def run_all(batch):
    for do in batch:
        do()


REDUCE_ORDER = (1, 3, 2, 0)


FRONT, BACK = 1, 2


def reduce_scratch(plan, half, width):
    bf = jnp.bfloat16
    n = NB * sum(1 for todo in plan if todo & FRONT)
    m = len(plan)
    D = pltpu.SemaphoreType.DMA
    scratch = dict(
        recv_z=pltpu.VMEM((m, NB, half, width), bf), z_send=D((m, NB)), z_recv=D((m, NB)),
        d_send=D((m, 6)), d_recv=D((m, 6)), d_own=D((m,)), part_sem=D((m,)),
    )
    if n:
        scratch.update(
            acc=pltpu.VMEM((n, 4, half, width), bf), recv_a=pltpu.VMEM((n, 4, half, width), bf),
            recv_b=pltpu.VMEM((n, 2, half, width), bf), recv_c=pltpu.VMEM((n, half, width), bf),
            a_send=D((n,)), a_recv=D((n,)), a_own=D((n,)),
            b_send=D((n, 2, 2)), b_recv=D((n, 2, 2)), c_send=D((n, 2)), c_recv=D((n, 2)),
        )
    return scratch


def reduce_steps(me, plan, source, out, parts_in, parts_out, sc, beside=(), ahead=3):
    dp, band, core, px, py, kind = me.dp, me.band, me.core, me.px, me.py, me.kind
    here = lambda d: device(d, band)
    fronts = [phase for phase, todo in enumerate(plan) if todo & FRONT]
    backs = [phase for phase, todo in enumerate(plan) if todo & BACK]
    chunks = [(phase, k) for phase in fronts for k in REDUCE_ORDER]
    n = len(chunks)
    flip = lambda v: 1 - v
    sends = []
    rows = sc.recv_z.shape[2]
    cut = rows // 32 * 16
    spans = (pl.ds(0, cut), pl.ds(cut, rows - cut))

    def remote(src, dst, ss, rs, to):
        return pltpu.make_async_remote_copy(
            src_ref=src, dst_ref=dst, send_sem=ss, recv_sem=rs, device_id=to, device_id_type=MESH
        )

    def go(make):
        make().start()
        sends.append(make)

    def target(k):
        return device(dp, lax.rem(band + k, NB))

    def start_a(s):
        phase, k = chunks[s]
        b = lax.rem(band + k, NB)
        for t in range(4):
            remote(
                source(phase, b, t, flip(core)), sc.recv_a.at[s, t], sc.a_send.at[s], sc.a_recv.at[s],
                here(me.sib),
            ).start()
            pltpu.make_async_copy(source(phase, b, t, core), sc.acc.at[s, t], sc.a_own.at[s]).start()

    def first(half, j, send):
        if half == 0:
            return 2 * j + (flip(px) if send else px)
        return 2 * (flip(py) if send else py) + j

    def second(half, send):
        if half == 0:
            return 2 * (flip(py) if send else py) + px
        return 2 * py + (flip(px) if send else px)

    def near(half):
        return here(me.xdp if half == 0 else me.ydp)

    def send_b(s, half, j):
        return remote(
            sc.acc.at[s, first(half, j, True), spans[half]], sc.recv_b.at[s, j, spans[half]],
            sc.b_send.at[s, half, j], sc.b_recv.at[s, half, j], near(half),
        )

    def send_c(s, half):
        return remote(
            sc.acc.at[s, second(half, True), spans[half]], sc.recv_c.at[s, spans[half]],
            sc.c_send.at[s, half], sc.c_recv.at[s, half], near(1 - half),
        )

    def send_z(phase, k, src):
        return remote(src, sc.recv_z.at[phase, k], sc.z_send.at[phase, k], sc.z_recv.at[phase, k], target(k))

    def unit_z(s):
        phase, k = chunks[s]
        return send_z(phase, k, sc.acc.at[s, kind])

    def part_load(phase):
        return pltpu.make_async_copy(parts_in[phase], sc.recv_z.at[phase, 0], sc.part_sem.at[phase])

    def part_store(phase):
        return pltpu.make_async_copy(sc.recv_z.at[phase, 0], parts_out[phase], sc.part_sem.at[phase])

    def d_copy(phase, half, slot, mine):
        ss, rs = sc.d_send.at[phase, 3 * half + slot], sc.d_recv.at[phase, 3 * half + slot]
        span = spans[half]
        if slot == 0:
            src = sc.recv_z.at[phase, 0, span]
            return remote(src, out[phase].at[kind, core, span], ss, rs, near(half))
        j = slot - 1
        t = 2 * (py if mine else flip(py)) + j if half == 0 else 2 * j + (px if mine else flip(px))
        unit = out[phase].at[t, core, span]
        return remote(unit, unit, ss, rs, near(1 - half))

    def d_cross(phase, mine):
        row = out[phase].at[:, core if mine else flip(core)]
        return remote(row, row, sc.z_send.at[phase, 0], sc.z_recv.at[phase, 0], here(me.sib))

    def a_to_b(s):
        acc, got = sc.acc, sc.recv_a
        pltpu.make_async_copy(got.at[s], acc.at[s], sc.a_own.at[s]).wait()
        whole = remote(got.at[s], got.at[s], sc.a_send.at[s], sc.a_recv.at[s], here(me.sib))
        whole.wait_recv()
        for j in range(2):
            for half in range(2):
                t = first(half, j, True)
                add_rows(acc.at[s, t, spans[half]], got.at[s, t, spans[half]])
                go(partial(send_b, s, half, j))
        for j in range(2):
            for half in range(2):
                t = first(half, j, False)
                add_rows(acc.at[s, t, spans[half]], got.at[s, t, spans[half]])
        whole.wait_send()

    def b_to_c(s):
        acc, got = sc.acc, sc.recv_b
        for half in range(2):
            for j in range(2):
                send_b(s, half, j).wait_recv()
            away = flip(py) if half == 0 else flip(px)
            t = second(half, True)
            add_rows(acc.at[s, t, spans[half]], got.at[s, away, spans[half]])
            go(partial(send_c, s, half))
        for half in range(2):
            stay = py if half == 0 else px
            add_rows(acc.at[s, kind, spans[half]], got.at[s, stay, spans[half]])

    def c_to_z(s):
        phase, k = chunks[s]
        for half in range(2):
            send_c(s, half).wait_recv()
            add_rows(sc.acc.at[s, kind, spans[half]], sc.recv_c.at[s, spans[half]])
        if k != 0:
            go(partial(unit_z, s))

    def z_sum(phase):
        got = sc.recv_z
        for k in range(1, NB):
            remote(
                got.at[phase, k], got.at[phase, k], sc.z_send.at[phase, k], sc.z_recv.at[phase, k], here(dp)
            ).wait_recv()
        s = NB * fronts.index(phase) + NB - 1

        @pl.loop(0, rows // 16)
        def _(step):
            at = pl.ds(pl.multiple_of(step * 16, 16), 16)
            total = sc.acc[s, kind, at, :].astype(jnp.float32)
            for k in range(1, NB):
                total = total + got[phase, k, at, :].astype(jnp.float32)
            got[phase, 0, at, :] = total.astype(jnp.bfloat16)

        if not plan[phase] & BACK:
            part_store(phase).start()

    def d_first(phase):
        if not plan[phase] & FRONT:
            part_load(phase).wait()
        own_copy = pltpu.make_async_copy(sc.recv_z.at[phase, 0], out[phase].at[kind, core], sc.d_own.at[phase])
        own_copy.start()
        for half in range(2):
            go(partial(d_copy, phase, half, 0, True))
        own_copy.wait()

    def d_second(phase):
        for half in range(2):
            d_copy(phase, half, 0, False).wait_recv()
            for slot in (1, 2):
                go(partial(d_copy, phase, half, slot, True))

    def d_third(phase):
        for half in range(2):
            for slot in (1, 2):
                d_copy(phase, half, slot, False).wait_recv()
        go(partial(d_cross, phase, True))

    def d_last(phase):
        d_cross(phase, False).wait_recv()

    def finish():
        for phase in fronts:
            if not plan[phase] & BACK:
                part_store(phase).wait()
        for make in sends:
            make().wait_send()

    table = {-1: [partial(start_a, s) for s in range(n)]}

    def put(at, do):
        table.setdefault(at, []).append(do)

    for phase in backs:
        if not plan[phase] & FRONT:
            put(-1, lambda phase=phase: part_load(phase).start())
    for at, do in enumerate(beside):
        put(at, do)
    for s in range(n):
        put(s + ahead, partial(b_to_c, s))
        put(s + ahead + 1, partial(c_to_z, s))
        put(s, partial(a_to_b, s))
    for phase, todo in enumerate(plan):
        end = 0
        if todo & FRONT:
            end = NB * fronts.index(phase) + NB + ahead + 1
            put(end, partial(z_sum, phase))
        if todo & BACK:
            for lag, do in ((0, d_first), (1, d_second), (2, d_third), (4, d_last)):
                put(end + lag, partial(do, phase))
    steps = [partial(run_all, table[at]) for at in sorted(table)]
    steps.append(finish)
    return steps


def home_scratch():
    D = pltpu.SemaphoreType.DMA
    return dict(home_send=D((2,)), home_recv=D((2,)))


def home_steps(me, rows_ref, home_ref, sc):
    band, core = me.band, me.core
    slot = lax.rem(band, 2)

    def stays(s):
        return jnp.logical_and(band // 2 == core, 2 * core + s == band)

    def copy(s):
        to = device(me.dp - core + band // 2, 2 * core + s)
        return pltpu.make_async_remote_copy(
            src_ref=rows_ref.at[s], dst_ref=home_ref.at[slot], send_sem=sc.home_send.at[s],
            recv_sem=sc.home_recv.at[slot], device_id=to, device_id_type=MESH,
        )

    def begin():
        for s in range(2):
            pl.when(stays(s))(
                lambda: pltpu.make_async_copy(
                    rows_ref.at[s], home_ref.at[slot], sc.home_recv.at[slot]
                ).start()
            )
            pl.when(jnp.logical_not(stays(s)))(lambda: copy(s).start())

    def finish():
        for s in range(2):
            pl.when(jnp.logical_not(stays(s)))(lambda: copy(s).wait_send())
        for i in range(2):
            pltpu.make_async_copy(rows_ref.at[i], home_ref.at[i], sc.home_recv.at[i]).wait()

    return begin, finish


def group_barrier(me):
    barrier = pltpu.get_barrier_semaphore()
    peers = [(me.xdp, me.band), (me.ydp, me.band), (me.sib, me.band)]
    for k in range(1, NB):
        other = lax.rem(me.band + k, NB)
        peers += [(me.dp, other), (me.sib, other)]
    for dp, band in peers:
        pl.semaphore_signal(
            barrier, inc=1, device_id=device(dp, band), device_id_type=MESH
        )
    pl.semaphore_wait(barrier, len(peers))


def reduce_refs(plan, counts, refs):
    take = iter(refs)
    grads = [[next(take) for _ in range(count)] for count in counts]

    def source(phase, b, t, h):
        if len(grads[phase]) == 1:
            return grads[phase][0].at[b, t, h]
        return grads[phase][t].at[b, h]

    return source, [next(take) if todo == BACK else None for todo in plan]


def reduce_outs(plan, refs):
    take = iter(refs)
    out = [next(take) if todo & BACK else None for todo in plan]
    return out, [next(take) if todo == FRONT else None for todo in plan]


def reduce_shapes(plan, half, width):
    bf = jnp.bfloat16
    shapes = [jax.ShapeDtypeStruct((4, 2, half, width), bf) for todo in plan if todo & BACK]
    return shapes + [jax.ShapeDtypeStruct((half, width), bf) for todo in plan if todo == FRONT]


def small_scratch(mod_rows, bias_rows, cond_rows, cond_cols):
    D = pltpu.SemaphoreType.DMA
    f32 = jnp.float32
    return dict(
        s_core=pltpu.VMEM((mod_rows + bias_rows, 128), f32),
        s_every=pltpu.VMEM((NB, 4, mod_rows, 128), jnp.bfloat16),
        s_bias=pltpu.VMEM((3, bias_rows, 128), f32),
        s_got=pltpu.VMEM((2 + NB, bias_rows, 128), f32),
        s_flat=pltpu.VMEM((8, mod_rows, 128), f32),
        s_cond=pltpu.VMEM((NB, cond_rows, cond_cols), f32),
        s_send=D((8,)), s_recv=D((8,)), sz_send=D((2, NB)), sz_recv=D((2, NB)),
        sc_send=D((NB,)), sc_recv=D((NB,)),
    )


def small_steps(me, mods, images, small_ref, ada_ref, every_ref, bias_ref, cond_ref, sc):
    dp, band, core, px, py, kind = me.dp, me.band, me.core, me.px, me.py, me.kind
    here = lambda d: device(d, band)
    every, bias, got, cond = sc.s_every, sc.s_bias, sc.s_got, sc.s_cond
    mod_rows = every.shape[2]
    flip = lambda v: 1 - v

    def remote(src, dst, ss, rs, to):
        return pltpu.make_async_remote_copy(
            src_ref=src, dst_ref=dst, send_sem=ss, recv_sem=rs, device_id=to, device_id_type=MESH
        )

    def plain(index, src, dst, to):
        return remote(src, dst, sc.s_send.at[index], sc.s_recv.at[index], to)

    def core_copy():
        return plain(0, small_ref, sc.s_core, here(me.sib))

    def x_copies(mine):
        unit = every.at[band, kind if mine else 2 * py + flip(px)]
        return [
            plain(1, unit, unit, here(me.xdp)),
            plain(2, bias.at[0], got.at[0], here(me.xdp)),
        ]

    def y_copies(mine):
        pair = every.at[band, pl.ds(2 * (py if mine else flip(py)), 2)]
        return [
            plain(3, pair, pair, here(me.ydp)),
            plain(4, bias.at[1], got.at[1], here(me.ydp)),
        ]

    def z_copies(k, mine):
        to = device(dp, lax.rem(band + k, NB))
        block = every.at[band if mine else lax.rem(band + NB - k, NB)]
        return [
            remote(block, block, sc.sz_send.at[0, k], sc.sz_recv.at[0, k], to),
            remote(bias.at[2], got.at[2 + k], sc.sz_send.at[1, k], sc.sz_recv.at[1, k], to),
        ]

    def cond_copy(k, mine):
        to = device(dp, lax.rem(band + k, NB))
        block = cond.at[band if mine else lax.rem(band + NB - k, NB)]
        return remote(block, block, sc.sc_send.at[k], sc.sc_recv.at[k], to)

    def begin():
        core_copy().start()

    def cores():
        core_copy().wait()
        total = small_ref[...] + sc.s_core[...]
        every[band, kind] = total[:mod_rows].astype(jnp.bfloat16)
        bias[0] = total[mod_rows:]
        for copy in x_copies(True):
            copy.start()

    def over_x():
        for copy in x_copies(True):
            copy.wait_send()
        for copy in x_copies(False):
            copy.wait_recv()
        bias[1] = bias[0] + got[0]
        for copy in y_copies(True):
            copy.start()

    def over_y():
        for copy in y_copies(True):
            copy.wait_send()
        for copy in y_copies(False):
            copy.wait_recv()
        bias[2] = bias[1] + got[1]
        for k in range(1, NB):
            for copy in z_copies(k, True):
                copy.start()

    def over_z():
        for k in range(1, NB):
            for copy in z_copies(k, True):
                copy.wait_send()
            for copy in z_copies(k, False):
                copy.wait_recv()
        bias_ref[...] = bias[2] + got[3] + got[4] + got[5]
        every_ref[...] = every[...]
        flat = sc.s_flat
        for i in range(images):
            flat[i] = every[images * core + i, kind].astype(jnp.float32)
        parts = mods // 128
        lead = flat.shape[0]
        total = jnp.zeros((lead, ada_ref.shape[0]), jnp.float32)
        for r in range(parts):
            left = jnp.concatenate(
                [flat[i, r : r + 1, :] for i in range(images)]
                + [jnp.zeros((lead - images, 128), jnp.float32)]
            ).astype(jnp.bfloat16)
            total = total + lanes_dot(left, ada_ref[:, r * 128 : (r + 1) * 128])
        pad = cond.shape[2] - total.shape[1]
        cond[band] = jnp.concatenate([total, jnp.zeros((lead, pad), jnp.float32)], 1)
        for k in range(1, NB):
            cond_copy(k, True).start()

    def conditions():
        for k in range(1, NB):
            cond_copy(k, True).wait_send()
            cond_copy(k, False).wait_recv()
        cond_ref[...] = cond[...]

    return [begin, cores, over_x, over_y, over_z, conditions]


def reduce_last_kernel(plan, counts, mods, images, names, *refs):
    me = compass()
    at = sum(counts) + sum(1 for todo in plan if todo == BACK)
    source, parts = reduce_refs(plan, counts, refs)
    rows_ref, small_ref, ada_ref = refs[at : at + 3]
    at += 3
    out, given = reduce_outs(plan, refs[at:])
    at += len(plan)
    home_ref, every_ref, bias_ref, cond_ref = refs[at : at + 4]
    sc = SimpleNamespace(**dict(zip(names, refs[at + 4 :])))
    group_barrier(me)
    small = small_steps(me, mods, images, small_ref, ada_ref, every_ref, bias_ref, cond_ref, sc)
    small[0]()
    depart, settle = home_steps(me, rows_ref, home_ref, sc)
    steps = reduce_steps(me, plan, source, out, parts, given, sc, small[1:], 2)
    steps[0]()
    depart()
    for step in steps[1:]:
        step()
    settle()


def reduce_last(grads, parts, rows, mod_part, bias_part, ada_weight, images, collective_id):
    plan, counts = (BACK, FRONT | BACK), (0, len(grads))
    half, width = grads[0].shape[-2:]
    mod_rows, bias_rows = mod_part.shape[0], bias_part.shape[0]
    cond_cols = -(-ada_weight.shape[0] // 128) * 128
    scratch = dict(
        **reduce_scratch(plan, half, width), **small_scratch(mod_rows, bias_rows, 8, cond_cols), **home_scratch()
    )
    any_, vmem = pl.BlockSpec(memory_space=pl.ANY), pl.BlockSpec(memory_space=pltpu.VMEM)
    return pl.pallas_call(
        partial(reduce_last_kernel, plan, counts, ada_weight.shape[1], images, tuple(scratch)),
        out_shape=reduce_shapes(plan, half, width)
        + [
            jax.ShapeDtypeStruct(rows.shape, rows.dtype),
            jax.ShapeDtypeStruct((NB, 4, mod_rows, 128), jnp.bfloat16),
            jax.ShapeDtypeStruct((bias_rows, 128), jnp.float32),
            jax.ShapeDtypeStruct((NB, 8, cond_cols), jnp.float32),
        ],
        in_specs=[any_] * (len(grads) + 2) + [vmem] * 2,
        out_specs=[any_] * 3 + [vmem] * 3,
        scratch_shapes=list(scratch.values()),
        compiler_params=pltpu.CompilerParams(
            collective_id=collective_id, has_side_effects=True, vmem_limit_bytes=56 * 2**20
        ),
        name="reduce_last",
    )(*grads, parts, rows, jnp.concatenate([mod_part, bias_part]), ada_weight)


def reduce_attend_kernel(plan, counts, band_slots, names, *refs):
    me = compass()
    at = sum(counts) + sum(1 for todo in plan if todo == BACK)
    source, parts = reduce_refs(plan, counts, refs)
    rows_ref, count_ref, q_ref, own_ref, far_ref, grad_ref, top_ref = refs[at : at + 7]
    at += 7
    out, given = reduce_outs(plan, refs[at:])
    at += len(plan)
    home_ref, dq_ref, down_ref, dfar_ref = refs[at : at + 4]
    sc = SimpleNamespace(**dict(zip(names, refs[at + 4 :])))
    qh, kh, vh, gh, stage, stage_sem = sc.qh, sc.kh, sc.vh, sc.gh, sc.stage, sc.stage_sem
    rows, width = q_ref.shape
    heads = qh.shape[0]
    group_barrier(me)
    steps = reduce_steps(me, plan, source, out, parts, given, sc)
    depart, settle = home_steps(me, rows_ref, home_ref, sc)
    steps[0]()
    depart()
    keys, plain, ones = key_tail(count_ref[0], band_slots), flat_tail(0.0), flat_tail(1.0)
    loads = [(q_ref, 0, qh, 0, ones), (grad_ref, 0, gh, 0, plain)]
    for row0, ref in ((0, own_ref), (rows, far_ref)):
        loads += [(ref, 0, kh, row0, keys), (ref, width, vh, row0, plain)]

    def load(i):
        ref, column = loads[i][:2]
        return pltpu.make_async_copy(ref.at[:, pl.ds(column, width)], stage.at[i % 2], stage_sem.at[i % 2])

    load(0).start()
    for step in steps[1:4]:
        step()
    for i, (ref, column, heads_ref, row0, tail) in enumerate(loads):
        if i + 1 < len(loads):
            load(i + 1).start()
        load(i).wait()
        pack_heads(stage.at[i % 2], 0, heads_ref, row0, rows, tail)
    rest = steps[4:]
    inside = heads // 2

    @pl.loop(0, heads)
    def _(h):
        attend_head(h, qh, kh, vh, gh, top_ref)
        for i, step in enumerate(rest[:inside]):
            pl.when(h == 2 * i)(step)

    stores = [(qh, 0, dq_ref, 0)]
    for row0, ref in ((0, down_ref), (rows, dfar_ref)):
        stores += [(kh, row0, ref, 0), (vh, row0, ref, width)]

    def store(i):
        ref, column = stores[i][2:]
        return pltpu.make_async_copy(stage.at[i % 2], ref.at[:, pl.ds(column, width)], stage_sem.at[i % 2])

    for i, (heads_ref, row0, ref, column) in enumerate(stores):
        if i >= 2:
            store(i - 2).wait()
        unpack_heads(heads_ref, row0, rows, stage.at[i % 2], 0)
        store(i).start()
    for i in (len(stores) - 2, len(stores) - 1):
        store(i).wait()
    for step in rest[inside:]:
        step()
    settle()


def reduce_attend(plan, grads, parts, rows_out, count, query, own, far, grad, top, band_slots, collective_id):
    half, width = grads[-1][0].shape[-2:]
    counts = tuple(len(phase) for phase in grads)
    rows = query.shape[0]
    heads = width // HEAD_DIM
    bf = jnp.bfloat16
    scratch = reduce_scratch(plan, half, width)
    scratch.update(
        qh=pltpu.VMEM((heads, rows, LANES), bf),
        kh=pltpu.VMEM((heads, 2 * rows, LANES), bf),
        vh=pltpu.VMEM((heads, 2 * rows, LANES), bf),
        gh=pltpu.VMEM((heads, rows, LANES), bf),
        stage=pltpu.VMEM((2, rows, width), bf),
        stage_sem=pltpu.SemaphoreType.DMA((2,)),
        **home_scratch(),
    )
    any_, vmem = pl.BlockSpec(memory_space=pl.ANY), pl.BlockSpec(memory_space=pltpu.VMEM)
    smem = pl.BlockSpec(memory_space=pltpu.SMEM)
    units = [unit for phase in grads for unit in phase]
    return pl.pallas_call(
        partial(reduce_attend_kernel, plan, counts, band_slots, tuple(scratch)),
        out_shape=reduce_shapes(plan, half, width)
        + [
            jax.ShapeDtypeStruct(rows_out.shape, bf),
            jax.ShapeDtypeStruct((rows, width), bf),
            jax.ShapeDtypeStruct((rows, 2 * width), bf),
            jax.ShapeDtypeStruct((rows, 2 * width), bf),
        ],
        in_specs=[any_] * (len(units) + len(parts) + 1) + [smem] + [any_] * 4 + [vmem],
        out_specs=[any_] * (len(plan) + 4),
        scratch_shapes=list(scratch.values()),
        compiler_params=pltpu.CompilerParams(
            collective_id=collective_id, has_side_effects=True, vmem_limit_bytes=60 * 2**20
        ),
        name="reduce_attend",
    )(*units, *parts, rows_out, count, query, own, far, grad, top)


MOD_BLOCKS = 6
BLOCK = 128


def forward_scratch(half, ff, width, rows, note_rows, images):
    bf, f32 = jnp.bfloat16, jnp.float32
    D = pltpu.SemaphoreType.DMA
    heads = width // HEAD_DIM
    V = pltpu.VMEM
    return dict(
        qp=V((NB, 2, half, ff), bf), bounce_i=V((2, half, ff), bf), bounce_o=V((4, 2, half, width), bf),
        bounce_t=V((rows // images, width), bf), tok=V((images, rows // images, width), bf),
        notes=V((NB, note_rows, 128), f32), vec=V((16, width), f32),
        residual=V((rows, width), f32), attn_in=V((rows, width), bf), query=V((rows, width), bf),
        own=V((rows, 2 * width), bf), far=V((rows, 2 * width), bf), mixed=V((rows, width), bf),
        attended=V((rows, width), f32), mlp_in=V((rows, width), bf), tops=V((heads, 8, rows), f32),
        qh=V((heads, rows, LANES), bf), kh=V((heads, 2 * rows, LANES), bf), vh=V((heads, 2 * rows, LANES), bf),
        z_send=D((3, 2)), z_recv=D((3, NB)), f_send=D((3, NB)), a_send=D((9,)), a_recv=D((9,)), b_send=D((9, 2)), b_recv=D((9, 2)),
        c_send=D((9,)), c_recv=D((9,)), t_send=D((2, 2)), t_recv=D((2, 2)), m_send=D((2, 2)), m_recv=D((NB,)),
        local=D((4,)), kv_send=D((1,)), kv_recv=D((1,)), done=D((12,)),
    )


def gather_steps(me, width, ins, outs, tok_in, tok_out, cot_in, cot_out, note_in, note_out, sc):
    dp, band, core, px, py, kind = me.dp, me.band, me.core, me.px, me.py, me.kind
    base = dp - core
    dev = lambda d, b: device(d, b)
    here = lambda d: dev(d, band)
    flip = lambda v: 1 - v
    low = band < 2
    bands = (band + 1 - 2 * lax.rem(band, 2), jnp.where(low, 2, 1), jnp.where(low, 3, 0))
    order = [(ph, b) for ph in range(3) for b in bands]
    inside = jnp.logical_or(band == 1, band == 2)
    sends = []

    def remote(src, dst, ss, rs, to):
        return pltpu.make_async_remote_copy(
            src_ref=src, dst_ref=dst, send_sem=ss, recv_sem=rs, device_id=to, device_id_type=MESH
        )

    def go(make):
        make().start()
        sends.append(make)

    def cols(t, n=1):
        return pl.ds(pl.multiple_of(t * width, 128), n * width)

    def unit(ph, b, t, h):
        return outs[ph].at[b, t, h] if ph == 2 else outs[ph].at[b, h, :, cols(t)]

    def pair(ph, b, h, y):
        return outs[ph].at[b, pl.ds(2 * y, 2), h] if ph == 2 else outs[ph].at[b, h, :, cols(2 * y, 2)]

    def row(ph, b, h):
        return outs[ph].at[b, :, h] if ph == 2 else outs[ph].at[b, h]

    def own_z(ph, up):
        src = ins[ph].at[kind, core] if ph == 2 else ins[ph].at[core, :, cols(kind)]
        return remote(
            src, unit(ph, band, kind, core), sc.z_send.at[ph, up], sc.z_recv.at[ph, band],
            dev(dp, band - 1 + 2 * up),
        )

    def pass_z(s):
        ph, b = order[s]
        u = unit(ph, b, kind, core)
        return remote(
            u, u, sc.f_send.at[ph, b], sc.z_recv.at[ph, b], dev(dp, jnp.where(b < band, band + 1, band - 1))
        )

    def send_a(s):
        ph, b = order[s]
        u = unit(ph, b, kind, core)
        return remote(u, u, sc.a_send.at[s], sc.a_recv.at[s], here(me.xdp if s % 2 == 0 else me.ydp))

    def b_copy(s, j, mine):
        ph, b = order[s]
        if s % 2 == 0:
            u = pair(ph, b, core, py if mine else flip(py))
            to = me.ydp
        else:
            u = unit(ph, b, 2 * j + (px if mine else flip(px)), core)
            to = me.xdp
        return remote(u, u, sc.b_send.at[s, j], sc.b_recv.at[s, j], here(to))

    def c_copy(s, mine):
        ph, b = order[s]
        u = row(ph, b, core if mine else flip(core))
        return remote(u, u, sc.c_send.at[s], sc.c_recv.at[s], here(me.sib))

    def z_start(ph):
        pl.when(band < NB - 1)(lambda: own_z(ph, 1).start())
        pl.when(band > 0)(lambda: own_z(ph, 0).start())

    def z_wait(s):
        ph, b = order[s]
        u = unit(ph, b, kind, core)
        remote(u, u, sc.a_send.at[s], sc.z_recv.at[ph, b], here(dp)).wait_recv()
        pl.when(inside)(lambda: pass_z(s).start())
        go(partial(send_a, s))

    def a_wait(s):
        ph, b = order[s]
        got = 2 * py + flip(px) if s % 2 == 0 else 2 * flip(py) + px
        u = unit(ph, b, got, core)
        remote(u, u, sc.a_send.at[s], sc.a_recv.at[s], here(me.xdp)).wait_recv()
        for j in range(1 if s % 2 == 0 else 2):
            go(partial(b_copy, s, j, True))

    def b_wait(s):
        for j in range(1 if s % 2 == 0 else 2):
            b_copy(s, j, False).wait_recv()
        go(partial(c_copy, s, True))

    def c_wait(s):
        c_copy(s, False).wait_recv()

    slot = lax.rem(band, 2)

    def image_copy(which, src, dst, i):
        to = dev(base + band // 2, 2 * core + i)
        return remote(src.at[i], dst.at[slot], sc.t_send.at[which, i], sc.t_recv.at[which, slot], to)

    def at_home(i):
        return jnp.logical_and(band // 2 == core, 2 * core + i == band)

    def move(which, src, dst, bounce=None):
        for i in range(2):

            @pl.when(at_home(i))
            def _():
                if bounce is None:
                    pltpu.make_async_copy(src.at[i], dst.at[slot], sc.t_recv.at[which, slot]).start()
                else:
                    inward = pltpu.make_async_copy(src.at[i], bounce, sc.local.at[3])
                    inward.start()
                    inward.wait()
                    pltpu.make_async_copy(bounce, dst.at[slot], sc.t_recv.at[which, slot]).start()

            @pl.when(jnp.logical_not(at_home(i)))
            def _():
                image_copy(which, src, dst, i).start()

    def move_wait(which, src, dst):
        for i in range(2):

            @pl.when(jnp.logical_not(at_home(i)))
            def _():
                image_copy(which, src, dst, i).wait_send()

        for s in range(2):
            pltpu.make_async_copy(dst.at[s], dst.at[s], sc.t_recv.at[which, s]).wait()

    def note_copy(i, c):
        return remote(
            note_in.at[i], note_out.at[band], sc.m_send.at[i, c], sc.m_recv.at[band],
            dev(base + c, 2 * core + i),
        )

    def note_home(i, c):
        return jnp.logical_and(c == core, 2 * core + i == band)

    def begin():
        for i in range(2):
            for c in range(2):

                @pl.when(note_home(i, c))
                def _():
                    pltpu.make_async_copy(note_in.at[i], note_out.at[band], sc.m_recv.at[band]).start()

                @pl.when(jnp.logical_not(note_home(i, c)))
                def _():
                    note_copy(i, c).start()

        z_start(0)
        for ph, dst in enumerate((outs[0].at[band], sc.bounce_i, sc.bounce_o)):
            pltpu.make_async_copy(ins[ph], dst, sc.local.at[ph]).start()

    def arrived():
        for i in range(2):
            for c in range(2):

                @pl.when(jnp.logical_not(note_home(i, c)))
                def _():
                    note_copy(i, c).wait_send()

        for b in range(NB):
            pltpu.make_async_copy(note_in.at[0], note_out.at[b], sc.m_recv.at[b]).wait()
        move_wait(0, tok_in, tok_out)

    def place():
        for ph, dst in ((1, sc.bounce_i), (2, sc.bounce_o)):
            pltpu.make_async_copy(ins[ph], dst, sc.local.at[ph]).wait()
            pltpu.make_async_copy(dst, outs[ph].at[band], sc.local.at[ph]).start()

    def first_here():
        pltpu.make_async_copy(ins[0], outs[0].at[band], sc.local.at[0]).wait()

    def finish():
        for ph, src in ((1, sc.bounce_i), (2, sc.bounce_o)):
            pltpu.make_async_copy(src, outs[ph].at[band], sc.local.at[ph]).wait()
        move_wait(1, cot_in, cot_out)
        for ph in range(3):
            pl.when(band < NB - 1)(lambda: own_z(ph, 1).wait_send())
            pl.when(band > 0)(lambda: own_z(ph, 0).wait_send())
        for s in range(len(order)):
            pl.when(inside)(lambda: pass_z(s).wait_send())
        for make in sends:
            make().wait_send()

    def images(which):
        if which == 0:
            move(0, tok_in, tok_out)
        else:
            move(1, cot_in, cot_out, sc.bounce_t)

    return SimpleNamespace(
        i=images, s=z_start,
        begin=begin, arrived=arrived, place=place, first_here=first_here, finish=finish,
        z=z_wait, a=a_wait, b=b_wait, c=c_wait,
    )


def forward_kernel(names, band_slots, *refs):
    me = compass()
    qp_in, inner_in, outer_in, tok_in, cot_in, note_in, table_ref = refs[:7]
    (qp_out, inner_out, outer_out, cot_out, vec_out, residual_out, attn_out, query_out, own_out, far_out,
     tops_out, mixed_out, attended_out, mlp_out) = refs[7:21]
    sc = SimpleNamespace(**dict(zip(names, refs[21:])))
    rows, width = sc.residual.shape
    heads = width // HEAD_DIM
    core = me.core
    qp, tok, notes, vec = sc.qp, sc.tok, sc.notes, sc.vec

    group_barrier(me)
    g = gather_steps(
        me, width, (qp_in, inner_in, outer_in), (qp, inner_out, outer_out), tok_in, tok, cot_in, cot_out,
        note_in, notes, sc,
    )
    saves = []

    def save(src, dst):
        copy = pltpu.make_async_copy(src, dst, sc.done.at[len(saves)])
        copy.start()
        saves.append(copy)

    def run(*words):
        for do, index in words:
            do(index)

    g.begin()
    g.place()
    run((g.z, 0), (g.z, 1), (g.i, 0), (g.a, 0), (g.a, 1), (g.z, 2), (g.s, 1), (g.b, 0), (g.b, 1), (g.a, 2), (g.c, 0), (g.c, 1), (g.z, 3), (g.z, 4), (g.b, 2))
    g.arrived()
    spread_notes(notes, vec, width)
    grid_rows = notes[0, 63:64, 0:1]
    grid_cols = notes[0, 63:64, 1:2]
    band_rows = jnp.floor(grid_rows * 0.25)
    valid_count = (band_rows * grid_cols).astype(jnp.int32)
    lane = lax.broadcasted_iota(jnp.int32, (1, width), 1)
    vec[15:16, :] = jnp.where(lane == 0, band_rows * grid_cols, 0.0)
    save(vec, vec_out)

    @pl.loop(0, rows // BLOCK)
    def _(step):
        at = pl.multiple_of(step * BLOCK, BLOCK)
        sub = pl.ds(at, BLOCK)
        per_image = band_slots // BLOCK
        within = (
            lax.rem(step, per_image) * BLOCK + lax.broadcasted_iota(jnp.int32, (BLOCK, 1), 0)
        ).astype(jnp.float32)
        down = jnp.floor((within + 0.5) / grid_cols)
        place = (2 * core + step // per_image).astype(jnp.float32)
        picks = []
        for index in (place * band_rows + down, within - down * grid_cols):
            lanes = lax.broadcasted_iota(jnp.int32, (BLOCK, 128), 1).astype(jnp.float32)
            pick = jnp.where(lanes == index, 1.0, 0.0).astype(jnp.bfloat16)
            part = [jnp.dot(pick, table_ref[i], preferred_element_type=jnp.float32) for i in range(3)]
            picks.append(part[0] + (part[1] + part[2]))
        token = tok[step // per_image, pl.ds(lax.rem(step, per_image) * BLOCK, BLOCK), :]
        residual = token.astype(jnp.float32) + jnp.concatenate(picks, 1)
        sc.residual[sub, :] = residual
        normed = normalize(residual)[0]
        sc.attn_in[sub, :] = (normed * (1.0 + vec[1:2, :]) + vec[0:1, :]).astype(jnp.bfloat16)

    save(sc.residual, residual_out)
    save(sc.attn_in, attn_out)
    g.first_here()
    run((g.c, 2))
    save(qp, qp_out)
    tile = width // 3
    full = NB * 2 * qp.shape[2]

    def product(left_ref, first, step):
        at = pl.ds(pl.multiple_of(first + step * tile, 128), tile)
        return jnp.dot(
            left_ref[...], qp[:, :, :, at].reshape(full, tile), preferred_element_type=jnp.float32
        )

    def here(step):
        return pl.ds(pl.multiple_of(step * tile, 128), tile)

    @pl.loop(0, 3)
    def _(step):
        sc.own[:, here(step)] = product(sc.attn_in, width, step).astype(jnp.bfloat16)

    run((g.a, 3), (g.z, 5), (g.s, 2))

    @pl.loop(0, 3)
    def _(step):
        value = product(sc.attn_in, 2 * width, step) + vec[7:8, here(step)]
        sc.own[:, here(step + 3)] = value.astype(jnp.bfloat16)

    swap = pltpu.make_async_remote_copy(
        src_ref=sc.own, dst_ref=sc.far, send_sem=sc.kv_send.at[0], recv_sem=sc.kv_recv.at[0],
        device_id=device(me.sib, me.band), device_id_type=MESH,
    )
    swap.start()
    run((g.a, 4), (g.b, 3))

    @pl.loop(0, 3)
    def _(step):
        value = product(sc.attn_in, 0, step) + vec[6:7, here(step)]
        sc.query[:, here(step)] = value.astype(jnp.bfloat16)

    save(sc.query, query_out)
    save(sc.own, own_out)
    run((g.a, 5), (g.b, 4), (g.c, 3), (g.z, 6))
    qh, kh, vh = sc.qh, sc.kh, sc.vh
    keys, plain = key_tail(valid_count, band_slots), flat_tail(0.0)
    pack_heads(sc.query, 0, qh, 0, rows, flat_tail(1.0))
    pack_heads(sc.own, 0, kh, 0, rows, keys)
    pack_heads(sc.own, width, vh, 0, rows, plain)
    swap.wait()
    save(sc.far, far_out)
    pack_heads(sc.far, 0, kh, rows, rows, keys)
    pack_heads(sc.far, width, vh, rows, rows, plain)
    beside = {
        0: ((g.z, 7), (g.b, 5), (g.c, 4)), 2: ((g.a, 6), (g.z, 8), (g.i, 1)), 4: ((g.a, 7), (g.b, 6), (g.c, 5)), 7: ((g.a, 8), (g.b, 7), (g.c, 6)), 10: ((g.b, 8), (g.c, 7)),
        13: ((g.c, 8),),
    }

    @pl.loop(0, heads)
    def _(h):
        attend_block(h, qh, kh, vh, sc.tops)
        for i, words in beside.items():
            pl.when(h == i)(partial(run, *words))

    unpack_heads(qh, 0, rows, sc.mixed, 0)
    save(sc.tops, tops_out)
    save(sc.mixed, mixed_out)

    @pl.loop(0, 3)
    def _(step):
        sc.attended[:, here(step)] = product(sc.mixed, 3 * width, step) + vec[8:9, here(step)]

    save(sc.attended, attended_out)

    @pl.loop(0, rows // BLOCK)
    def _(step):
        sub = pl.ds(pl.multiple_of(step * BLOCK, BLOCK), BLOCK)
        middle = sc.residual[sub, :] + vec[2:3, :] * sc.attended[sub, :]
        normed = normalize(middle)[0]
        sc.mlp_in[sub, :] = (normed * (1.0 + vec[4:5, :]) + vec[3:4, :]).astype(jnp.bfloat16)

    save(sc.mlp_in, mlp_out)
    g.finish()
    for copy in saves:
        copy.wait()


NOTE_COND, NOTE_GRID, NOTE_BIAS = 54, 63, 64


def spread_notes(notes, vec, width):
    lines = width // 128
    share = notes.shape[0]
    total = notes[0, 0:NOTE_GRID, :] + 0.0
    for b in range(1, share):
        total = total + notes[b, 0:NOTE_GRID, :]

    def flat(block, first):
        return jnp.concatenate([block[first + i : first + i + 1, :] for i in range(lines)], 1)

    for index in range(MOD_BLOCKS):
        vec[index : index + 1, :] = flat(total, index * lines)
    small = width // share
    for index in range(4):
        parts = []
        for b in range(share):
            first = NOTE_BIAS + 3 * index
            for i in range(3):
                parts.append(notes[b, first + i : first + i + 1, : min(128, small - 128 * i)])
        vec[6 + index : 7 + index, :] = jnp.concatenate(parts, 1)
    for b in range(share):
        block = notes[b, NOTE_BIAS + 12 : NOTE_BIAS + 12 + lines, :]
        vec[10 + b : 11 + b, :] = flat(block, 0)
    vec[14:15, :] = flat(notes[0, NOTE_COND : NOTE_COND + lines, :], 0)


def forward_block(qp, inner, outer, tok, cot, note, table):
    half, ff = qp.shape[0] // 2, qp.shape[1]
    images, band_slots, width = tok.shape
    rows = images * band_slots
    heads = width // HEAD_DIM
    bf, f32 = jnp.bfloat16, jnp.float32
    S = jax.ShapeDtypeStruct
    qp, inner = qp.reshape(2, half, ff), inner.reshape(2, half, ff)
    outer = outer.reshape(4, 2, half, width)
    scratch = forward_scratch(half, ff, width, rows, note.shape[1], images)
    any_ = pl.BlockSpec(memory_space=pl.ANY)
    return pl.pallas_call(
        partial(forward_kernel, tuple(scratch), band_slots),
        out_shape=[
            S((NB, 2, half, ff), bf), S((NB, 2, half, ff), bf), S((NB, 4, 2, half, width), bf), S(cot.shape, bf),
            S((16, width), f32), S((rows, width), f32), S((rows, width), bf), S((rows, width), bf),
            S((rows, 2 * width), bf), S((rows, 2 * width), bf), S((heads, 8, rows), f32), S((rows, width), bf),
            S((rows, width), f32), S((rows, width), bf),
        ],
        in_specs=[any_] * 6 + [pl.BlockSpec(memory_space=pltpu.VMEM)],
        out_specs=[any_] * 14,
        scratch_shapes=list(scratch.values()),
        compiler_params=pltpu.CompilerParams(
            collective_id=0, has_side_effects=True, vmem_limit_bytes=60 * 2**20
        ),
        name="forward_block",
    )(qp, inner, outer, tok, cot, note, table)


def pair_perm(dp_count, band_count):
    return [
        (dp * band_count + band, (dp ^ 1) * band_count + band)
        for dp in range(dp_count)
        for band in range(band_count)
    ]


def position_parts(width):
    quarter = width // 4
    frequency = 10000.0 ** (-jnp.arange(quarter, dtype=jnp.float32) / quarter)
    angles = jnp.arange(128, dtype=jnp.float32)[:, None] * frequency
    left = jnp.concatenate([jnp.sin(angles), jnp.cos(angles)], -1)
    parts = []
    for _ in range(3):
        part = lax.reduce_precision(left, 8, 7)
        parts.append(part.astype(jnp.bfloat16))
        left = left - part
    return jnp.stack(parts)


def over_groups(piece, dp_count):
    if dp_count == 8:
        return piece
    groups = [[rank + 8 * group for group in range(dp_count // 8)] for rank in range(8)]
    return lax.psum(piece.astype(jnp.float32), "dp", axis_index_groups=groups)


def every_group(piece, dp_count):
    if dp_count == 8:
        return piece[None]
    groups = [[rank + 8 * group for group in range(dp_count // 8)] for rank in range(8)]
    return lax.all_gather(piece, "dp", axis_index_groups=groups)


def own_piece(vector, count, band_place):
    return lax.dynamic_slice_in_dim(vector, band_place * count, count, 0)


def body(
    tokens,
    condition,
    patch_grid,
    ada_weight,
    ada_bias,
    qkv_weight,
    query_bias,
    value_bias,
    proj_weight,
    proj_bias,
    inner_weight,
    inner_bias,
    outer_weight,
    outer_bias,
    cotangent,
):
    both = ("dp", "band")
    dp_count = lax.axis_size("dp")
    band_count = lax.axis_size("band")
    images, band_slots, width = tokens.shape
    band = lax.axis_index("band")
    dp = lax.axis_index("dp")
    core = lax.rem(dp, 2)
    hidden = inner_weight.shape[1]
    part_rows = qkv_weight.shape[0]
    siblings = pair_perm(dp_count, band_count)

    condition_f = condition.astype(jnp.float32)
    activated = jax.nn.silu(condition_f).astype(jnp.bfloat16)
    own_activated = lax.dynamic_slice_in_dim(activated, band * part_rows, part_rows, 1)
    share = jnp.dot(own_activated, ada_weight, preferred_element_type=jnp.float32)
    share = share + lax.dynamic_update_slice_in_dim(
        jnp.zeros((ada_weight.shape[1],), jnp.float32),
        ada_bias.astype(jnp.float32),
        band * ada_bias.shape[0],
        0,
    )
    mod_count = share.shape[1]
    lines = lambda vector: jnp.pad(
        vector.astype(jnp.float32), [(0, 0)] * (vector.ndim - 1) + [(0, -vector.shape[-1] % 128)]
    )
    spread = lambda vector: jnp.broadcast_to(lines(vector), (images, -(-vector.shape[0] // 128) * 128))
    note = jnp.concatenate(
        [share, condition_f, lines(patch_grid)]
        + [spread(bias) for bias in (query_bias, value_bias, proj_bias, outer_bias, inner_bias)],
        1,
    )
    note = jnp.pad(note, ((0, 0), (0, -note.shape[1] % 1024))).reshape(images, -1, 128)
    first_weight = jnp.concatenate([qkv_weight, proj_weight], 1)
    (first_full, inner_full, outer_full, cotangent_here, vectors, residual, attn_in, query_rows, key_value,
     other_key_value, tops, mixed_rows, attended, mlp_in) = forward_block(
        first_weight, inner_weight, outer_weight, tokens, cotangent, note, position_parts(width)
    )
    first_full = first_full.reshape(width, -1)
    inner_full = inner_full.reshape(width, hidden)
    outer_full = outer_full.reshape(hidden, width)
    qkv_full = first_full[:, : 3 * width]
    proj_full = first_full[:, 3 * width :]
    scale_one, gate_one = vectors[1], vectors[2]
    scale_two, gate_two = vectors[4], vectors[5]
    outer_bias_full = vectors[9]
    inner_bias_full = vectors[10:14].reshape(-1)
    condition_here = vectors[14]
    valid_count = vectors[15, :1].astype(jnp.int32)
    rows = images * band_slots
    is_valid = jnp.arange(rows, dtype=jnp.int32) % band_slots < valid_count
    normed_one, inverse_one = normalize(residual)
    middle = residual + gate_one * attended
    normed_two, inverse_two = normalize(middle)
    hidden_pre = jnp.dot(mlp_in, inner_full, preferred_element_type=jnp.float32) + inner_bias_full
    hidden_act = jax.nn.gelu(hidden_pre, approximate=True).astype(jnp.bfloat16)
    mlp_out = jnp.dot(hidden_act, outer_full, preferred_element_type=jnp.float32) + outer_bias_full
    block_out = (middle + gate_two * mlp_out).astype(jnp.bfloat16)

    grad_out = cotangent_here.reshape(rows, width).astype(jnp.float32) * is_valid[:, None].astype(
        jnp.float32
    )
    grad_gate_two = jnp.sum(grad_out * mlp_out, 0)
    grad_mlp = (gate_two * grad_out).astype(jnp.bfloat16)
    gelu_back = jax.vjp(partial(jax.nn.gelu, approximate=True), hidden_pre)[1]
    blocks = (band_count, 2, part_rows // 2, width)
    grad_outer = rows_dot(hidden_act, grad_mlp).astype(jnp.bfloat16).reshape(
        band_count, 4, 2, part_rows // 2, width
    )
    grad_outer_bias = jnp.sum(grad_mlp.astype(jnp.float32), 0)
    grad_hidden = lanes_dot(grad_mlp, outer_full)
    grad_pre = gelu_back(grad_hidden)[0].astype(jnp.bfloat16)
    grad_inner = [
        rows_dot(mlp_in, grad_pre[:, t * width : (t + 1) * width]).astype(jnp.bfloat16).reshape(blocks)
        for t in range(4)
    ]
    grad_inner_bias = jnp.sum(grad_pre.astype(jnp.float32), 0)
    grad_mlp_in = lanes_dot(grad_pre, inner_full)
    grad_shift_two = jnp.sum(grad_mlp_in, 0)
    grad_scale_two = jnp.sum(grad_mlp_in * normed_two, 0)
    grad_middle = grad_out + norm_back(grad_mlp_in * (1.0 + scale_two), normed_two, inverse_two)
    grad_gate_one = jnp.sum(grad_middle * attended, 0)
    grad_attended = (gate_one * grad_middle).astype(jnp.bfloat16)
    grad_proj = rows_dot(mixed_rows, grad_attended).astype(jnp.bfloat16)
    grad_proj_bias = jnp.sum(grad_attended.astype(jnp.float32), 0)
    grad_mixed = lanes_dot(grad_attended, proj_full).astype(jnp.bfloat16)
    outer_sum, inner_part, block_home, grad_query, own_terms, far_terms = reduce_attend(
        (FRONT | BACK, FRONT), [[grad_outer], grad_inner], [], block_out.reshape(images, band_slots, width), valid_count, query_rows, key_value, other_key_value, grad_mixed, tops,
        band_slots, 1,
    )
    other_terms = lax.ppermute(far_terms, both, siblings)
    grad_key_value = (own_terms.astype(jnp.float32) + other_terms.astype(jnp.float32)).astype(
        jnp.bfloat16
    )
    grad_qkv = jnp.concatenate([grad_query, grad_key_value], -1)
    grad_first = [
        rows_dot(attn_in, part).astype(jnp.bfloat16).reshape(blocks)
        for part in (grad_query, grad_key_value[:, :width], grad_key_value[:, width:])
    ]
    grad_attn_in = lanes_dot(grad_qkv, qkv_full)
    grad_query_bias = jnp.sum(grad_query.astype(jnp.float32), 0)
    grad_value_bias = jnp.sum(grad_key_value[:, width:].astype(jnp.float32), 0)
    grad_shift_one = jnp.sum(grad_attn_in, 0)
    grad_scale_one = jnp.sum(grad_attn_in * normed_one, 0)
    grad_tokens = grad_middle + norm_back(grad_attn_in * (1.0 + scale_one), normed_one, inverse_one)
    part_mod = jnp.concatenate(
        [grad_shift_one, grad_scale_one, grad_gate_one, grad_shift_two, grad_scale_two, grad_gate_two]
    )
    part_mod = jnp.concatenate([part_mod, 0.5 * condition_here]).reshape(-1, 128)
    part_mod = jnp.pad(part_mod, ((0, -part_mod.shape[0] % 16), (0, 0)))
    part_bias = jnp.concatenate(
        [grad_query_bias, grad_value_bias, grad_proj_bias, grad_inner_bias, grad_outer_bias]
    ).reshape(-1, 128)
    inner_sum, first_sum, tokens_home, every, bias_grads, grad_act = reduce_last(
        grad_first + [grad_proj.reshape(blocks)], inner_part, grad_tokens.astype(jnp.bfloat16).reshape(images, band_slots, width), part_mod, part_bias, ada_weight, images, 2
    )
    tokens_home = tokens_home.astype(jnp.float32)
    every = every_group(every, dp_count)
    bias_grads = over_groups(bias_grads, dp_count).reshape(-1)
    every = jnp.swapaxes(every, 1, 2).reshape(dp_count * images, -1)
    every_mod = every[:, :mod_count]
    every_condition = every[:, mod_count : mod_count + width]
    every_activated = jax.nn.silu(every_condition.astype(jnp.float32)).astype(jnp.bfloat16)
    every_activated = lax.dynamic_slice_in_dim(every_activated, band * part_rows, part_rows, 1)
    grad_ada = rows_dot(every_activated, every_mod)
    grad_ada_bias = own_piece(jnp.sum(every_mod.astype(jnp.float32), 0), ada_bias.shape[0], band)
    grad_act = jnp.swapaxes(grad_act[:, :images, :part_rows], 0, 1).reshape(images, width)
    grad_condition = jax.vjp(jax.nn.silu, condition_f)[1](grad_act)[0]

    def side_by_side(units):
        return jnp.concatenate([unit.reshape(part_rows, width) for unit in units], 1).astype(jnp.float32)

    first_sum, inner_sum, outer_sum = [
        over_groups(piece, dp_count) for piece in (first_sum, inner_sum, outer_sum)
    ]
    qkv_sum = side_by_side([first_sum[t] for t in range(3)])
    proj_sum = first_sum[3].reshape(part_rows, width).astype(jnp.float32)
    inner_sum = side_by_side([inner_sum[t] for t in range(4)])
    outer_sum = outer_sum.reshape(4 * part_rows, width).astype(jnp.float32)
    bias_parts = []
    at = 0
    for piece in (query_bias, value_bias, proj_bias, inner_bias, outer_bias):
        whole = piece.shape[0] * band_count
        bias_parts.append(own_piece(bias_grads[at : at + whole], piece.shape[0], band))
        at += whole
    return (
        block_home,
        tokens_home,
        grad_condition,
        grad_ada,
        grad_ada_bias,
        qkv_sum,
        bias_parts[0],
        bias_parts[1],
        proj_sum,
        bias_parts[2],
        inner_sum,
        bias_parts[3],
        outer_sum,
        bias_parts[4],
    )


def solution(mesh):
    placed = (
        P("dp", "band", None),
        P("dp", None),
        P("dp", None),
        P("band", None),
        P("band"),
        P("band", None),
        P("band"),
        P("band"),
        P("band", None),
        P("band"),
        P("band", None),
        P("band"),
        P("band", None),
        P("band"),
        P("dp", "band", None),
    )
    return jax.shard_map(
        body,
        mesh=mesh,
        in_specs=placed,
        out_specs=(
            P("dp", "band", None),
            P("dp", "band", None),
            P("dp", None),
            P("band", None),
            P("band"),
            P("band", None),
            P("band"),
            P("band"),
            P("band", None),
            P("band"),
            P("band", None),
            P("band"),
            P("band", None),
            P("band"),
        ),
        check_vma=False,
    )
```

```python
from functools import partial
from types import SimpleNamespace

import jax
import jax.numpy as jnp
from jax import lax
from jax.experimental import pallas as pl
from jax.experimental.pallas import tpu as pltpu
from jax.sharding import PartitionSpec as P

HEAD_DIM = 72


MESH = pl.DeviceIdType.MESH
NB = 4


def device(dp, band):
    return {"dp": dp, "band": band}


def normalize(values):
    average = jnp.mean(values, -1, keepdims=True)
    centered = values - average
    variance = jnp.mean(centered * centered, -1, keepdims=True)
    inverse = lax.rsqrt(variance + 1e-06)
    return (centered * inverse, inverse)


def norm_back(grad_normed, normed, inverse):
    first = jnp.mean(grad_normed, -1, keepdims=True)
    second = jnp.mean(grad_normed * normed, -1, keepdims=True)
    return inverse * (grad_normed - first - normed * second)


LANES = 128
PACK_ROWS = 128


def pack_heads(source, first, heads_ref, row0, rows, tail):
    heads = heads_ref.shape[0]

    @pl.loop(0, rows // PACK_ROWS)
    def _(step):
        at = pl.multiple_of(step * PACK_ROWS, PACK_ROWS)
        block = source[pl.ds(at, PACK_ROWS), first : first + heads * HEAD_DIM]
        end = tail(at)
        for h in range(heads):
            part = block[:, h * HEAD_DIM : (h + 1) * HEAD_DIM]
            heads_ref[h, pl.ds(row0 + at, PACK_ROWS), :] = jnp.concatenate([part, end], 1)


def unpack_heads(heads_ref, row0, rows, target, first):
    heads = heads_ref.shape[0]

    @pl.loop(0, rows // PACK_ROWS)
    def _(step):
        at = pl.multiple_of(step * PACK_ROWS, PACK_ROWS)
        parts = [heads_ref[h, pl.ds(row0 + at, PACK_ROWS), :][:, :HEAD_DIM] for h in range(heads)]
        target[pl.ds(at, PACK_ROWS), first : first + heads * HEAD_DIM] = jnp.concatenate(parts, 1)


def flat_tail(value):
    def tail(at):
        lane = lax.broadcasted_iota(jnp.int32, (PACK_ROWS, LANES - HEAD_DIM), 1)
        return jnp.where(lane == 0, value, 0.0).astype(jnp.bfloat16)

    return tail


def key_tail(valid_count, band_slots):
    def tail(at):
        shape = (PACK_ROWS, LANES - HEAD_DIM)
        lane = lax.broadcasted_iota(jnp.int32, shape, 1)
        slot = lax.rem(at + lax.broadcasted_iota(jnp.int32, shape, 0), band_slots)
        return jnp.where(jnp.logical_and(lane == 0, slot >= valid_count), -1e30, 0.0).astype(jnp.bfloat16)

    return tail


def lanes_dot(left, right):
    return lax.dot_general(left, right, (((1,), (1,)), ((), ())), preferred_element_type=jnp.float32)


def rows_dot(left, right):
    return lax.dot_general(left, right, (((0,), (0,)), ((), ())), preferred_element_type=jnp.float32)


SCORE_SCALE = HEAD_DIM ** (-0.5)


def attend_block(h, qh, kh, vh, top_ref):
    rows = qh.shape[1]
    for block in range(2):
        at = pl.ds(block * rows // 2, rows // 2)
        scores = lanes_dot(kh[h], qh[h, at, :]) * SCORE_SCALE
        top = jnp.max(scores, 0, keepdims=True)
        weights = jnp.exp(scores - top)
        total = jnp.sum(weights, 0, keepdims=True)
        low = (weights * (1.0 / total)).astype(jnp.bfloat16)
        mixed = rows_dot(vh[h], low)
        qh[h, at, :] = jnp.transpose(mixed).astype(jnp.bfloat16)
        top_ref[h, :, at] = jnp.broadcast_to(top + jnp.log(total), (8, rows // 2))


def attend_head(h, qh, kh, vh, gh, top_ref):
    query = qh[h]
    key = kh[h]
    grad = gh[h]
    probs = jnp.exp(lanes_dot(key, query) * SCORE_SCALE - top_ref[h, 0:1, :])
    grad_probs = lanes_dot(vh[h], grad)
    inner = jnp.sum(probs * grad_probs, 0, keepdims=True)
    grad_scores = (probs * (grad_probs - inner)).astype(jnp.bfloat16)
    vh[h] = jnp.dot(
        probs.astype(jnp.bfloat16), grad, preferred_element_type=jnp.float32
    ).astype(jnp.bfloat16)
    grad_query = rows_dot(key, grad_scores)
    kh[h] = (
        SCORE_SCALE * jnp.dot(grad_scores, query, preferred_element_type=jnp.float32)
    ).astype(jnp.bfloat16)
    qh[h] = (SCORE_SCALE * jnp.transpose(grad_query)).astype(jnp.bfloat16)


def compass():
    dp = lax.axis_index("dp")
    band = lax.axis_index("band")
    core = lax.rem(dp, 2)
    px = lax.rem(dp // 2, 2)
    py = lax.rem(dp // 4, 2)
    return SimpleNamespace(
        dp=dp, band=band, core=core, px=px, py=py, kind=2 * py + px,
        sib=dp + 1 - 2 * core, xdp=dp + 2 - 4 * px, ydp=dp + 4 - 8 * py,
    )


def add_rows(total, term):
    rows = total.shape[0]

    @pl.loop(0, rows // 16)
    def _(step):
        at = pl.ds(pl.multiple_of(step * 16, 16), 16)
        total[at, :] = (
            total[at, :].astype(jnp.float32) + term[at, :].astype(jnp.float32)
        ).astype(jnp.bfloat16)


def run_all(batch):
    for do in batch:
        do()


REDUCE_ORDER = (1, 3, 2, 0)


FRONT, BACK = 1, 2


def reduce_scratch(plan, half, width):
    bf = jnp.bfloat16
    n = NB * sum(1 for todo in plan if todo & FRONT)
    m = len(plan)
    D = pltpu.SemaphoreType.DMA
    scratch = dict(
        recv_z=pltpu.VMEM((m, NB, half, width), bf), z_send=D((m, NB)), z_recv=D((m, NB)),
        d_send=D((m, 6)), d_recv=D((m, 6)), d_own=D((m,)), part_sem=D((m,)),
    )
    if n:
        scratch.update(
            acc=pltpu.VMEM((n, 4, half, width), bf), recv_a=pltpu.VMEM((n, 4, half, width), bf),
            recv_b=pltpu.VMEM((n, 2, half, width), bf), recv_c=pltpu.VMEM((n, half, width), bf),
            a_send=D((n,)), a_recv=D((n,)), a_own=D((n,)),
            b_send=D((n, 2, 2)), b_recv=D((n, 2, 2)), c_send=D((n, 2)), c_recv=D((n, 2)),
        )
    return scratch


def reduce_steps(me, plan, source, out, parts_in, parts_out, sc, beside=(), ahead=3):
    dp, band, core, px, py, kind = me.dp, me.band, me.core, me.px, me.py, me.kind
    here = lambda d: device(d, band)
    fronts = [phase for phase, todo in enumerate(plan) if todo & FRONT]
    backs = [phase for phase, todo in enumerate(plan) if todo & BACK]
    chunks = [(phase, k) for phase in fronts for k in REDUCE_ORDER]
    n = len(chunks)
    flip = lambda v: 1 - v
    sends = []
    rows = sc.recv_z.shape[2]
    cut = rows // 32 * 16
    spans = (pl.ds(0, cut), pl.ds(cut, rows - cut))

    def remote(src, dst, ss, rs, to):
        return pltpu.make_async_remote_copy(
            src_ref=src, dst_ref=dst, send_sem=ss, recv_sem=rs, device_id=to, device_id_type=MESH
        )

    def go(make):
        make().start()
        sends.append(make)

    def target(k):
        return device(dp, lax.rem(band + k, NB))

    def start_a(s):
        phase, k = chunks[s]
        b = lax.rem(band + k, NB)
        for t in range(4):
            remote(
                source(phase, b, t, flip(core)), sc.recv_a.at[s, t], sc.a_send.at[s], sc.a_recv.at[s],
                here(me.sib),
            ).start()
            pltpu.make_async_copy(source(phase, b, t, core), sc.acc.at[s, t], sc.a_own.at[s]).start()

    def first(half, j, send):
        if half == 0:
            return 2 * j + (flip(px) if send else px)
        return 2 * (flip(py) if send else py) + j

    def second(half, send):
        if half == 0:
            return 2 * (flip(py) if send else py) + px
        return 2 * py + (flip(px) if send else px)

    def near(half):
        return here(me.xdp if half == 0 else me.ydp)

    def send_b(s, half, j):
        return remote(
            sc.acc.at[s, first(half, j, True), spans[half]], sc.recv_b.at[s, j, spans[half]],
            sc.b_send.at[s, half, j], sc.b_recv.at[s, half, j], near(half),
        )

    def send_c(s, half):
        return remote(
            sc.acc.at[s, second(half, True), spans[half]], sc.recv_c.at[s, spans[half]],
            sc.c_send.at[s, half], sc.c_recv.at[s, half], near(1 - half),
        )

    def send_z(phase, k, src):
        return remote(src, sc.recv_z.at[phase, k], sc.z_send.at[phase, k], sc.z_recv.at[phase, k], target(k))

    def unit_z(s):
        phase, k = chunks[s]
        return send_z(phase, k, sc.acc.at[s, kind])

    def part_load(phase):
        return pltpu.make_async_copy(parts_in[phase], sc.recv_z.at[phase, 0], sc.part_sem.at[phase])

    def part_store(phase):
        return pltpu.make_async_copy(sc.recv_z.at[phase, 0], parts_out[phase], sc.part_sem.at[phase])

    def d_copy(phase, half, slot, mine):
        ss, rs = sc.d_send.at[phase, 3 * half + slot], sc.d_recv.at[phase, 3 * half + slot]
        span = spans[half]
        if slot == 0:
            src = sc.recv_z.at[phase, 0, span]
            return remote(src, out[phase].at[kind, core, span], ss, rs, near(half))
        j = slot - 1
        t = 2 * (py if mine else flip(py)) + j if half == 0 else 2 * j + (px if mine else flip(px))
        unit = out[phase].at[t, core, span]
        return remote(unit, unit, ss, rs, near(1 - half))

    def d_cross(phase, mine):
        row = out[phase].at[:, core if mine else flip(core)]
        return remote(row, row, sc.z_send.at[phase, 0], sc.z_recv.at[phase, 0], here(me.sib))

    def a_to_b(s):
        acc, got = sc.acc, sc.recv_a
        pltpu.make_async_copy(got.at[s], acc.at[s], sc.a_own.at[s]).wait()
        whole = remote(got.at[s], got.at[s], sc.a_send.at[s], sc.a_recv.at[s], here(me.sib))
        whole.wait_recv()
        for j in range(2):
            for half in range(2):
                t = first(half, j, True)
                add_rows(acc.at[s, t, spans[half]], got.at[s, t, spans[half]])
                go(partial(send_b, s, half, j))
        for j in range(2):
            for half in range(2):
                t = first(half, j, False)
                add_rows(acc.at[s, t, spans[half]], got.at[s, t, spans[half]])
        whole.wait_send()

    def b_to_c(s):
        acc, got = sc.acc, sc.recv_b
        for half in range(2):
            for j in range(2):
                send_b(s, half, j).wait_recv()
            away = flip(py) if half == 0 else flip(px)
            t = second(half, True)
            add_rows(acc.at[s, t, spans[half]], got.at[s, away, spans[half]])
            go(partial(send_c, s, half))
        for half in range(2):
            stay = py if half == 0 else px
            add_rows(acc.at[s, kind, spans[half]], got.at[s, stay, spans[half]])

    def c_to_z(s):
        phase, k = chunks[s]
        for half in range(2):
            send_c(s, half).wait_recv()
            add_rows(sc.acc.at[s, kind, spans[half]], sc.recv_c.at[s, spans[half]])
        if k != 0:
            go(partial(unit_z, s))

    def z_sum(phase):
        got = sc.recv_z
        for k in range(1, NB):
            remote(
                got.at[phase, k], got.at[phase, k], sc.z_send.at[phase, k], sc.z_recv.at[phase, k], here(dp)
            ).wait_recv()
        s = NB * fronts.index(phase) + NB - 1

        @pl.loop(0, rows // 16)
        def _(step):
            at = pl.ds(pl.multiple_of(step * 16, 16), 16)
            total = sc.acc[s, kind, at, :].astype(jnp.float32)
            for k in range(1, NB):
                total = total + got[phase, k, at, :].astype(jnp.float32)
            got[phase, 0, at, :] = total.astype(jnp.bfloat16)

        if not plan[phase] & BACK:
            part_store(phase).start()

    def d_first(phase):
        if not plan[phase] & FRONT:
            part_load(phase).wait()
        own_copy = pltpu.make_async_copy(sc.recv_z.at[phase, 0], out[phase].at[kind, core], sc.d_own.at[phase])
        own_copy.start()
        for half in range(2):
            go(partial(d_copy, phase, half, 0, True))
        own_copy.wait()

    def d_second(phase):
        for half in range(2):
            d_copy(phase, half, 0, False).wait_recv()
            for slot in (1, 2):
                go(partial(d_copy, phase, half, slot, True))

    def d_third(phase):
        for half in range(2):
            for slot in (1, 2):
                d_copy(phase, half, slot, False).wait_recv()
        go(partial(d_cross, phase, True))

    def d_last(phase):
        d_cross(phase, False).wait_recv()

    def finish():
        for phase in fronts:
            if not plan[phase] & BACK:
                part_store(phase).wait()
        for make in sends:
            make().wait_send()

    table = {-1: [partial(start_a, s) for s in range(n)]}

    def put(at, do):
        table.setdefault(at, []).append(do)

    for phase in backs:
        if not plan[phase] & FRONT:
            put(-1, lambda phase=phase: part_load(phase).start())
    for at, do in enumerate(beside):
        put(at, do)
    for s in range(n):
        put(s + ahead, partial(b_to_c, s))
        put(s + ahead + 1, partial(c_to_z, s))
        put(s, partial(a_to_b, s))
    for phase, todo in enumerate(plan):
        end = 0
        if todo & FRONT:
            end = NB * fronts.index(phase) + NB + ahead + 1
            put(end, partial(z_sum, phase))
        if todo & BACK:
            for lag, do in ((0, d_first), (1, d_second), (2, d_third), (4, d_last)):
                put(end + lag, partial(do, phase))
    steps = [partial(run_all, table[at]) for at in sorted(table)]
    steps.append(finish)
    return steps


def home_scratch():
    D = pltpu.SemaphoreType.DMA
    return dict(home_send=D((2,)), home_recv=D((2,)))


def home_steps(me, rows_ref, home_ref, sc):
    band, core = me.band, me.core
    slot = lax.rem(band, 2)

    def stays(s):
        return jnp.logical_and(band // 2 == core, 2 * core + s == band)

    def copy(s):
        to = device(me.dp - core + band // 2, 2 * core + s)
        return pltpu.make_async_remote_copy(
            src_ref=rows_ref.at[s], dst_ref=home_ref.at[slot], send_sem=sc.home_send.at[s],
            recv_sem=sc.home_recv.at[slot], device_id=to, device_id_type=MESH,
        )

    def begin():
        for s in range(2):
            pl.when(stays(s))(
                lambda: pltpu.make_async_copy(
                    rows_ref.at[s], home_ref.at[slot], sc.home_recv.at[slot]
                ).start()
            )
            pl.when(jnp.logical_not(stays(s)))(lambda: copy(s).start())

    def finish():
        for s in range(2):
            pl.when(jnp.logical_not(stays(s)))(lambda: copy(s).wait_send())
        for i in range(2):
            pltpu.make_async_copy(rows_ref.at[i], home_ref.at[i], sc.home_recv.at[i]).wait()

    return begin, finish


def group_barrier(me):
    barrier = pltpu.get_barrier_semaphore()
    peers = [(me.xdp, me.band), (me.ydp, me.band), (me.sib, me.band)]
    for k in range(1, NB):
        other = lax.rem(me.band + k, NB)
        peers += [(me.dp, other), (me.sib, other)]
    for dp, band in peers:
        pl.semaphore_signal(
            barrier, inc=1, device_id=device(dp, band), device_id_type=MESH
        )
    pl.semaphore_wait(barrier, len(peers))


def reduce_refs(plan, counts, refs):
    take = iter(refs)
    grads = [[next(take) for _ in range(count)] for count in counts]

    def source(phase, b, t, h):
        if len(grads[phase]) > 1:
            return grads[phase][t].at[b, h]
        whole = grads[phase][0]
        if len(whole.shape) == 5:
            return whole.at[b, t, h]
        span = whole.shape[3] // 4
        return whole.at[b, h, :, pl.ds(pl.multiple_of(t * span, 128), span)]

    return source, [next(take) if todo == BACK else None for todo in plan]


def reduce_outs(plan, refs):
    take = iter(refs)
    out = [next(take) if todo & BACK else None for todo in plan]
    return out, [next(take) if todo == FRONT else None for todo in plan]


def reduce_shapes(plan, half, width):
    bf = jnp.bfloat16
    shapes = [jax.ShapeDtypeStruct((4, 2, half, width), bf) for todo in plan if todo & BACK]
    return shapes + [jax.ShapeDtypeStruct((half, width), bf) for todo in plan if todo == FRONT]


def small_scratch(mod_rows, bias_rows, cond_rows, cond_cols):
    D = pltpu.SemaphoreType.DMA
    f32 = jnp.float32
    return dict(
        s_core=pltpu.VMEM((mod_rows + bias_rows, 128), f32),
        s_every=pltpu.VMEM((NB, 4, mod_rows, 128), jnp.bfloat16),
        s_bias=pltpu.VMEM((3, bias_rows, 128), f32),
        s_got=pltpu.VMEM((2 + NB, bias_rows, 128), f32),
        s_flat=pltpu.VMEM((8, mod_rows, 128), f32),
        s_cond=pltpu.VMEM((NB, cond_rows, cond_cols), f32),
        s_send=D((8,)), s_recv=D((8,)), sz_send=D((2, NB)), sz_recv=D((2, NB)),
        sc_send=D((NB,)), sc_recv=D((NB,)),
    )


def small_steps(me, mods, images, small_ref, ada_ref, every_ref, bias_ref, cond_ref, sc):
    dp, band, core, px, py, kind = me.dp, me.band, me.core, me.px, me.py, me.kind
    here = lambda d: device(d, band)
    every, bias, got, cond = sc.s_every, sc.s_bias, sc.s_got, sc.s_cond
    mod_rows = every.shape[2]
    flip = lambda v: 1 - v

    def remote(src, dst, ss, rs, to):
        return pltpu.make_async_remote_copy(
            src_ref=src, dst_ref=dst, send_sem=ss, recv_sem=rs, device_id=to, device_id_type=MESH
        )

    def plain(index, src, dst, to):
        return remote(src, dst, sc.s_send.at[index], sc.s_recv.at[index], to)

    def core_copy():
        return plain(0, small_ref, sc.s_core, here(me.sib))

    def x_copies(mine):
        unit = every.at[band, kind if mine else 2 * py + flip(px)]
        return [
            plain(1, unit, unit, here(me.xdp)),
            plain(2, bias.at[0], got.at[0], here(me.xdp)),
        ]

    def y_copies(mine):
        pair = every.at[band, pl.ds(2 * (py if mine else flip(py)), 2)]
        return [
            plain(3, pair, pair, here(me.ydp)),
            plain(4, bias.at[1], got.at[1], here(me.ydp)),
        ]

    def z_copies(k, mine):
        to = device(dp, lax.rem(band + k, NB))
        block = every.at[band if mine else lax.rem(band + NB - k, NB)]
        return [
            remote(block, block, sc.sz_send.at[0, k], sc.sz_recv.at[0, k], to),
            remote(bias.at[2], got.at[2 + k], sc.sz_send.at[1, k], sc.sz_recv.at[1, k], to),
        ]

    def cond_copy(k, mine):
        to = device(dp, lax.rem(band + k, NB))
        block = cond.at[band if mine else lax.rem(band + NB - k, NB)]
        return remote(block, block, sc.sc_send.at[k], sc.sc_recv.at[k], to)

    def begin():
        core_copy().start()

    def cores():
        core_copy().wait()
        total = small_ref[...] + sc.s_core[...]
        every[band, kind] = total[:mod_rows].astype(jnp.bfloat16)
        bias[0] = total[mod_rows:]
        for copy in x_copies(True):
            copy.start()

    def over_x():
        for copy in x_copies(True):
            copy.wait_send()
        for copy in x_copies(False):
            copy.wait_recv()
        bias[1] = bias[0] + got[0]
        for copy in y_copies(True):
            copy.start()

    def over_y():
        for copy in y_copies(True):
            copy.wait_send()
        for copy in y_copies(False):
            copy.wait_recv()
        bias[2] = bias[1] + got[1]
        for k in range(1, NB):
            for copy in z_copies(k, True):
                copy.start()

    def over_z():
        for k in range(1, NB):
            for copy in z_copies(k, True):
                copy.wait_send()
            for copy in z_copies(k, False):
                copy.wait_recv()
        bias_ref[...] = bias[2] + got[3] + got[4] + got[5]
        every_ref[...] = every[...]
        flat = sc.s_flat
        for i in range(images):
            flat[i] = every[images * core + i, kind].astype(jnp.float32)
        parts = mods // 128
        lead = flat.shape[0]
        total = jnp.zeros((lead, ada_ref.shape[0]), jnp.float32)
        for r in range(parts):
            left = jnp.concatenate(
                [flat[i, r : r + 1, :] for i in range(images)]
                + [jnp.zeros((lead - images, 128), jnp.float32)]
            ).astype(jnp.bfloat16)
            total = total + lanes_dot(left, ada_ref[:, r * 128 : (r + 1) * 128])
        pad = cond.shape[2] - total.shape[1]
        cond[band] = jnp.concatenate([total, jnp.zeros((lead, pad), jnp.float32)], 1)
        for k in range(1, NB):
            cond_copy(k, True).start()

    def conditions():
        for k in range(1, NB):
            cond_copy(k, True).wait_send()
            cond_copy(k, False).wait_recv()
        cond_ref[...] = cond[...]

    return [begin, cores, over_x, over_y, over_z, conditions]


def reduce_last_kernel(plan, counts, mods, images, names, *refs):
    me = compass()
    at = sum(counts) + sum(1 for todo in plan if todo == BACK)
    source, parts = reduce_refs(plan, counts, refs)
    rows_ref, small_ref, ada_ref = refs[at : at + 3]
    at += 3
    out, given = reduce_outs(plan, refs[at:])
    at += len(plan)
    home_ref, every_ref, bias_ref, cond_ref = refs[at : at + 4]
    sc = SimpleNamespace(**dict(zip(names, refs[at + 4 :])))
    group_barrier(me)
    small = small_steps(me, mods, images, small_ref, ada_ref, every_ref, bias_ref, cond_ref, sc)
    small[0]()
    depart, settle = home_steps(me, rows_ref, home_ref, sc)
    steps = reduce_steps(me, plan, source, out, parts, given, sc, small[1:], 2)
    steps[0]()
    depart()
    for step in steps[1:]:
        step()
    settle()


def reduce_last(grads, parts, rows, mod_part, bias_part, ada_weight, images, collective_id):
    plan, counts = (BACK, FRONT | BACK), (0, len(grads))
    half, width = grads[0].shape[-2:]
    mod_rows, bias_rows = mod_part.shape[0], bias_part.shape[0]
    cond_cols = -(-ada_weight.shape[0] // 128) * 128
    scratch = dict(
        **reduce_scratch(plan, half, width), **small_scratch(mod_rows, bias_rows, 8, cond_cols), **home_scratch()
    )
    any_, vmem = pl.BlockSpec(memory_space=pl.ANY), pl.BlockSpec(memory_space=pltpu.VMEM)
    return pl.pallas_call(
        partial(reduce_last_kernel, plan, counts, ada_weight.shape[1], images, tuple(scratch)),
        out_shape=reduce_shapes(plan, half, width)
        + [
            jax.ShapeDtypeStruct(rows.shape, rows.dtype),
            jax.ShapeDtypeStruct((NB, 4, mod_rows, 128), jnp.bfloat16),
            jax.ShapeDtypeStruct((bias_rows, 128), jnp.float32),
            jax.ShapeDtypeStruct((NB, 8, cond_cols), jnp.float32),
        ],
        in_specs=[any_] * (len(grads) + 2) + [vmem] * 2,
        out_specs=[any_] * 3 + [vmem] * 3,
        scratch_shapes=list(scratch.values()),
        compiler_params=pltpu.CompilerParams(
            collective_id=collective_id, has_side_effects=True, vmem_limit_bytes=56 * 2**20
        ),
        name="reduce_last",
    )(*grads, parts, rows, jnp.concatenate([mod_part, bias_part]), ada_weight)


def reduce_attend_kernel(plan, counts, band_slots, names, *refs):
    me = compass()
    at = sum(counts) + sum(1 for todo in plan if todo == BACK)
    source, parts = reduce_refs(plan, counts, refs)
    rows_ref, count_ref, q_ref, own_ref, far_ref, grad_ref, top_ref = refs[at : at + 7]
    at += 7
    out, given = reduce_outs(plan, refs[at:])
    at += len(plan)
    home_ref, dq_ref, down_ref, dfar_ref = refs[at : at + 4]
    sc = SimpleNamespace(**dict(zip(names, refs[at + 4 :])))
    qh, kh, vh, gh, stage, stage_sem = sc.qh, sc.kh, sc.vh, sc.gh, sc.stage, sc.stage_sem
    rows, width = q_ref.shape
    heads = qh.shape[0]
    group_barrier(me)
    steps = reduce_steps(me, plan, source, out, parts, given, sc)
    depart, settle = home_steps(me, rows_ref, home_ref, sc)
    steps[0]()
    depart()
    keys, plain, ones = key_tail(count_ref[0], band_slots), flat_tail(0.0), flat_tail(1.0)
    loads = [(q_ref, 0, qh, 0, ones), (grad_ref, 0, gh, 0, plain)]
    for row0, ref in ((0, own_ref), (rows, far_ref)):
        loads += [(ref, 0, kh, row0, keys), (ref, width, vh, row0, plain)]

    def load(i):
        ref, column = loads[i][:2]
        return pltpu.make_async_copy(ref.at[:, pl.ds(column, width)], stage.at[i % 2], stage_sem.at[i % 2])

    load(0).start()
    for step in steps[1:4]:
        step()
    for i, (ref, column, heads_ref, row0, tail) in enumerate(loads):
        if i + 1 < len(loads):
            load(i + 1).start()
        load(i).wait()
        pack_heads(stage.at[i % 2], 0, heads_ref, row0, rows, tail)
    rest = steps[4:]
    inside = heads // 2

    @pl.loop(0, heads)
    def _(h):
        attend_head(h, qh, kh, vh, gh, top_ref)
        for i, step in enumerate(rest[:inside]):
            pl.when(h == 2 * i)(step)

    stores = [(qh, 0, dq_ref, 0)]
    for row0, ref in ((0, down_ref), (rows, dfar_ref)):
        stores += [(kh, row0, ref, 0), (vh, row0, ref, width)]

    def store(i):
        ref, column = stores[i][2:]
        return pltpu.make_async_copy(stage.at[i % 2], ref.at[:, pl.ds(column, width)], stage_sem.at[i % 2])

    for i, (heads_ref, row0, ref, column) in enumerate(stores):
        if i >= 2:
            store(i - 2).wait()
        unpack_heads(heads_ref, row0, rows, stage.at[i % 2], 0)
        store(i).start()
    for i in (len(stores) - 2, len(stores) - 1):
        store(i).wait()
    for step in rest[inside:]:
        step()
    settle()


def reduce_attend(plan, grads, parts, rows_out, count, query, own, far, grad, top, band_slots, collective_id):
    half, width = grads[0][0].shape[-2:]
    counts = tuple(len(phase) for phase in grads)
    rows = query.shape[0]
    heads = width // HEAD_DIM
    bf = jnp.bfloat16
    scratch = reduce_scratch(plan, half, width)
    scratch.update(
        qh=pltpu.VMEM((heads, rows, LANES), bf),
        kh=pltpu.VMEM((heads, 2 * rows, LANES), bf),
        vh=pltpu.VMEM((heads, 2 * rows, LANES), bf),
        gh=pltpu.VMEM((heads, rows, LANES), bf),
        stage=pltpu.VMEM((2, rows, width), bf),
        stage_sem=pltpu.SemaphoreType.DMA((2,)),
        **home_scratch(),
    )
    any_, vmem = pl.BlockSpec(memory_space=pl.ANY), pl.BlockSpec(memory_space=pltpu.VMEM)
    smem = pl.BlockSpec(memory_space=pltpu.SMEM)
    units = [unit for phase in grads for unit in phase]
    return pl.pallas_call(
        partial(reduce_attend_kernel, plan, counts, band_slots, tuple(scratch)),
        out_shape=reduce_shapes(plan, half, width)
        + [
            jax.ShapeDtypeStruct(rows_out.shape, bf),
            jax.ShapeDtypeStruct((rows, width), bf),
            jax.ShapeDtypeStruct((rows, 2 * width), bf),
            jax.ShapeDtypeStruct((rows, 2 * width), bf),
        ],
        in_specs=[any_] * (len(units) + len(parts) + 1) + [smem] + [any_] * 4 + [vmem],
        out_specs=[any_] * (len(plan) + 4),
        scratch_shapes=list(scratch.values()),
        compiler_params=pltpu.CompilerParams(
            collective_id=collective_id, has_side_effects=True, vmem_limit_bytes=60 * 2**20
        ),
        name="reduce_attend",
    )(*units, *parts, rows_out, count, query, own, far, grad, top)


MOD_BLOCKS = 6
BLOCK = 128


def forward_scratch(half, ff, width, rows, note_rows, images):
    bf, f32 = jnp.bfloat16, jnp.float32
    D = pltpu.SemaphoreType.DMA
    heads = width // HEAD_DIM
    V = pltpu.VMEM
    return dict(
        qp=V((NB, 2, half, ff), bf), bounce_i=V((2, half, ff), bf), bounce_o=V((4, 2, half, width), bf),
        bounce_t=V((rows // images, width), bf), tok=V((images, rows // images, width), bf),
        notes=V((NB, note_rows, 128), f32), vec=V((16, width), f32),
        residual=V((rows, width), f32), attn_in=V((rows, width), bf), query=V((rows, width), bf),
        own=V((rows, 2 * width), bf), far=V((rows, 2 * width), bf), mixed=V((rows, width), bf),
        attended=V((rows, width), f32), mlp_in=V((rows, width), bf), tops=V((heads, 8, rows), f32),
        qh=V((heads, rows, LANES), bf), kh=V((heads, 2 * rows, LANES), bf), vh=V((heads, 2 * rows, LANES), bf),
        z_send=D((3, 2)), z_recv=D((3, NB)), f_send=D((3, NB)), a_send=D((9, 2)), a_recv=D((9, 2)), b_send=D((9, 2, 2)), b_recv=D((9, 2, 2)),
        c_send=D((9,)), c_recv=D((9,)), t_send=D((2, 2)), t_recv=D((2, 2)), m_send=D((2, 2)), m_recv=D((NB,)),
        local=D((4,)), kv_send=D((1,)), kv_recv=D((1,)), done=D((12,)),
    )


def gather_steps(me, width, ins, outs, tok_in, tok_out, cot_in, cot_out, note_in, note_out, sc):
    dp, band, core, px, py, kind = me.dp, me.band, me.core, me.px, me.py, me.kind
    base = dp - core
    dev = lambda d, b: device(d, b)
    here = lambda d: dev(d, band)
    flip = lambda v: 1 - v
    low = band < 2
    bands = (band + 1 - 2 * lax.rem(band, 2), jnp.where(low, 2, 1), jnp.where(low, 3, 0))
    order = [(ph, b) for ph in range(3) for b in bands]
    inside = jnp.logical_or(band == 1, band == 2)
    sends = []

    def remote(src, dst, ss, rs, to):
        return pltpu.make_async_remote_copy(
            src_ref=src, dst_ref=dst, send_sem=ss, recv_sem=rs, device_id=to, device_id_type=MESH
        )

    def go(make):
        for copy in make():
            copy.start()
        sends.append(make)

    size = ins[0].shape[1]
    cut = size // 32 * 16
    whole, spans = pl.ds(0, size), (pl.ds(0, cut), pl.ds(cut, size - cut))

    def cols(t, n=1):
        return pl.ds(pl.multiple_of(t * width, 128), n * width)

    def unit(ph, b, t, h, span=whole):
        return outs[ph].at[b, t, h, span] if ph == 2 else outs[ph].at[b, h, span, cols(t)]

    def pair(ph, b, h, y, span):
        return outs[ph].at[b, pl.ds(2 * y, 2), h, span] if ph == 2 else outs[ph].at[b, h, span, cols(2 * y, 2)]

    def row(ph, b, h):
        return outs[ph].at[b, :, h] if ph == 2 else outs[ph].at[b, h]

    def own_z(ph, up):
        src = ins[ph].at[kind, core] if ph == 2 else ins[ph].at[core, :, cols(kind)]
        return remote(
            src, unit(ph, band, kind, core), sc.z_send.at[ph, up], sc.z_recv.at[ph, band],
            dev(dp, band - 1 + 2 * up),
        )

    def pass_z(s):
        ph, b = order[s]
        u = unit(ph, b, kind, core)
        return remote(
            u, u, sc.f_send.at[ph, b], sc.z_recv.at[ph, b], dev(dp, jnp.where(b < band, band + 1, band - 1))
        )

    def a_copy(s, half, mine):
        ph, b = order[s]
        near = 2 * py + flip(px) if half == 0 else 2 * flip(py) + px
        u = unit(ph, b, kind if mine else near, core, spans[half])
        return remote(u, u, sc.a_send.at[s, half], sc.a_recv.at[s, half], here(me.xdp if half == 0 else me.ydp))

    def b_copies(s, half, mine):
        ph, b = order[s]
        if half == 0:
            u = pair(ph, b, core, py if mine else flip(py), spans[half])
            return [remote(u, u, sc.b_send.at[s, half, 0], sc.b_recv.at[s, half, 0], here(me.ydp))]
        copies = []
        for j in range(2):
            u = unit(ph, b, 2 * j + (px if mine else flip(px)), core, spans[half])
            copies.append(remote(u, u, sc.b_send.at[s, half, j], sc.b_recv.at[s, half, j], here(me.xdp)))
        return copies

    def c_copy(s, mine):
        ph, b = order[s]
        u = row(ph, b, core if mine else flip(core))
        return remote(u, u, sc.c_send.at[s], sc.c_recv.at[s], here(me.sib))

    def z_start(ph):
        pl.when(band < NB - 1)(lambda: own_z(ph, 1).start())
        pl.when(band > 0)(lambda: own_z(ph, 0).start())

    def z_wait(s):
        ph, b = order[s]
        u = unit(ph, b, kind, core)
        remote(u, u, sc.f_send.at[ph, b], sc.z_recv.at[ph, b], here(dp)).wait_recv()
        pl.when(inside)(lambda: pass_z(s).start())
        for half in range(2):
            go(lambda half=half: [a_copy(s, half, True)])

    def a_wait(s):
        for half in range(2):
            a_copy(s, half, False).wait_recv()
            go(partial(b_copies, s, half, True))

    def b_wait(s):
        for half in range(2):
            for copy in b_copies(s, half, False):
                copy.wait_recv()
        go(lambda: [c_copy(s, True)])

    def c_wait(s):
        c_copy(s, False).wait_recv()

    slot = lax.rem(band, 2)

    def image_copy(which, src, dst, i):
        to = dev(base + band // 2, 2 * core + i)
        return remote(src.at[i], dst.at[slot], sc.t_send.at[which, i], sc.t_recv.at[which, slot], to)

    def at_home(i):
        return jnp.logical_and(band // 2 == core, 2 * core + i == band)

    def move(which, src, dst, bounce=None):
        for i in range(2):

            @pl.when(at_home(i))
            def _():
                if bounce is None:
                    pltpu.make_async_copy(src.at[i], dst.at[slot], sc.t_recv.at[which, slot]).start()
                else:
                    inward = pltpu.make_async_copy(src.at[i], bounce, sc.local.at[3])
                    inward.start()
                    inward.wait()
                    pltpu.make_async_copy(bounce, dst.at[slot], sc.t_recv.at[which, slot]).start()

            @pl.when(jnp.logical_not(at_home(i)))
            def _():
                image_copy(which, src, dst, i).start()

    def move_wait(which, src, dst):
        for i in range(2):

            @pl.when(jnp.logical_not(at_home(i)))
            def _():
                image_copy(which, src, dst, i).wait_send()

        for s in range(2):
            pltpu.make_async_copy(dst.at[s], dst.at[s], sc.t_recv.at[which, s]).wait()

    def note_copy(i, c):
        return remote(
            note_in.at[i], note_out.at[band], sc.m_send.at[i, c], sc.m_recv.at[band],
            dev(base + c, 2 * core + i),
        )

    def note_home(i, c):
        return jnp.logical_and(c == core, 2 * core + i == band)

    def begin():
        for i in range(2):
            for c in range(2):

                @pl.when(note_home(i, c))
                def _():
                    pltpu.make_async_copy(note_in.at[i], note_out.at[band], sc.m_recv.at[band]).start()

                @pl.when(jnp.logical_not(note_home(i, c)))
                def _():
                    note_copy(i, c).start()

        z_start(0)
        for ph, dst in enumerate((outs[0].at[band], sc.bounce_i, sc.bounce_o)):
            pltpu.make_async_copy(ins[ph], dst, sc.local.at[ph]).start()

    def arrived():
        for i in range(2):
            for c in range(2):

                @pl.when(jnp.logical_not(note_home(i, c)))
                def _():
                    note_copy(i, c).wait_send()

        for b in range(NB):
            pltpu.make_async_copy(note_in.at[0], note_out.at[b], sc.m_recv.at[b]).wait()
        move_wait(0, tok_in, tok_out)

    def place():
        for ph, dst in ((1, sc.bounce_i), (2, sc.bounce_o)):
            pltpu.make_async_copy(ins[ph], dst, sc.local.at[ph]).wait()
            pltpu.make_async_copy(dst, outs[ph].at[band], sc.local.at[ph]).start()

    def first_here():
        pltpu.make_async_copy(ins[0], outs[0].at[band], sc.local.at[0]).wait()

    def finish():
        for ph, src in ((1, sc.bounce_i), (2, sc.bounce_o)):
            pltpu.make_async_copy(src, outs[ph].at[band], sc.local.at[ph]).wait()
        move_wait(1, cot_in, cot_out)
        for ph in range(3):
            pl.when(band < NB - 1)(lambda: own_z(ph, 1).wait_send())
            pl.when(band > 0)(lambda: own_z(ph, 0).wait_send())
        for s in range(len(order)):
            pl.when(inside)(lambda: pass_z(s).wait_send())
        for make in sends:
            for copy in make():
                copy.wait_send()

    def images(which):
        if which == 0:
            move(0, tok_in, tok_out)
        else:
            move(1, cot_in, cot_out, sc.bounce_t)

    return SimpleNamespace(
        i=images, s=z_start,
        begin=begin, arrived=arrived, place=place, first_here=first_here, finish=finish,
        z=z_wait, a=a_wait, b=b_wait, c=c_wait,
    )


def forward_kernel(names, band_slots, *refs):
    me = compass()
    qp_in, inner_in, outer_in, tok_in, cot_in, note_in, table_ref = refs[:7]
    (qp_out, inner_out, outer_out, cot_out, vec_out, residual_out, attn_out, query_out, own_out, far_out,
     tops_out, mixed_out, attended_out, mlp_out) = refs[7:21]
    sc = SimpleNamespace(**dict(zip(names, refs[21:])))
    rows, width = sc.residual.shape
    heads = width // HEAD_DIM
    core = me.core
    qp, tok, notes, vec = sc.qp, sc.tok, sc.notes, sc.vec

    group_barrier(me)
    g = gather_steps(
        me, width, (qp_in, inner_in, outer_in), (qp, inner_out, outer_out), tok_in, tok, cot_in, cot_out,
        note_in, notes, sc,
    )
    saves = []

    def save(src, dst):
        copy = pltpu.make_async_copy(src, dst, sc.done.at[len(saves)])
        copy.start()
        saves.append(copy)

    def run(*words):
        for do, index in words:
            do(index)

    g.begin()
    g.place()
    run((g.z, 0), (g.z, 1), (g.i, 0), (g.a, 0), (g.a, 1), (g.z, 2), (g.s, 1), (g.b, 0), (g.b, 1), (g.a, 2), (g.c, 0), (g.c, 1), (g.z, 3), (g.z, 4), (g.b, 2))
    g.arrived()
    spread_notes(notes, vec, width)
    grid_rows = notes[0, 63:64, 0:1]
    grid_cols = notes[0, 63:64, 1:2]
    band_rows = jnp.floor(grid_rows * 0.25)
    valid_count = (band_rows * grid_cols).astype(jnp.int32)
    lane = lax.broadcasted_iota(jnp.int32, (1, width), 1)
    vec[15:16, :] = jnp.where(lane == 0, band_rows * grid_cols, 0.0)
    save(vec, vec_out)

    @pl.loop(0, rows // BLOCK)
    def _(step):
        at = pl.multiple_of(step * BLOCK, BLOCK)
        sub = pl.ds(at, BLOCK)
        per_image = band_slots // BLOCK
        within = (
            lax.rem(step, per_image) * BLOCK + lax.broadcasted_iota(jnp.int32, (BLOCK, 1), 0)
        ).astype(jnp.float32)
        down = jnp.floor((within + 0.5) / grid_cols)
        place = (2 * core + step // per_image).astype(jnp.float32)
        picks = []
        for index in (place * band_rows + down, within - down * grid_cols):
            lanes = lax.broadcasted_iota(jnp.int32, (BLOCK, 128), 1).astype(jnp.float32)
            pick = jnp.where(lanes == index, 1.0, 0.0).astype(jnp.bfloat16)
            part = [jnp.dot(pick, table_ref[i], preferred_element_type=jnp.float32) for i in range(3)]
            picks.append(part[0] + (part[1] + part[2]))
        token = tok[step // per_image, pl.ds(lax.rem(step, per_image) * BLOCK, BLOCK), :]
        residual = token.astype(jnp.float32) + jnp.concatenate(picks, 1)
        sc.residual[sub, :] = residual
        normed = normalize(residual)[0]
        sc.attn_in[sub, :] = (normed * (1.0 + vec[1:2, :]) + vec[0:1, :]).astype(jnp.bfloat16)

    save(sc.residual, residual_out)
    save(sc.attn_in, attn_out)
    g.first_here()
    run((g.c, 2))
    save(qp, qp_out)
    tile = width // 3
    full = NB * 2 * qp.shape[2]

    def product(left_ref, first, step):
        at = pl.ds(pl.multiple_of(first + step * tile, 128), tile)
        return jnp.dot(
            left_ref[...], qp[:, :, :, at].reshape(full, tile), preferred_element_type=jnp.float32
        )

    def here(step):
        return pl.ds(pl.multiple_of(step * tile, 128), tile)

    @pl.loop(0, 3)
    def _(step):
        sc.own[:, here(step)] = product(sc.attn_in, width, step).astype(jnp.bfloat16)

    run((g.a, 3), (g.z, 5), (g.s, 2))

    @pl.loop(0, 3)
    def _(step):
        value = product(sc.attn_in, 2 * width, step) + vec[7:8, here(step)]
        sc.own[:, here(step + 3)] = value.astype(jnp.bfloat16)

    swap = pltpu.make_async_remote_copy(
        src_ref=sc.own, dst_ref=sc.far, send_sem=sc.kv_send.at[0], recv_sem=sc.kv_recv.at[0],
        device_id=device(me.sib, me.band), device_id_type=MESH,
    )
    swap.start()
    run((g.a, 4), (g.b, 3))

    @pl.loop(0, 3)
    def _(step):
        value = product(sc.attn_in, 0, step) + vec[6:7, here(step)]
        sc.query[:, here(step)] = value.astype(jnp.bfloat16)

    save(sc.query, query_out)
    save(sc.own, own_out)
    run((g.a, 5), (g.b, 4), (g.c, 3), (g.z, 6))
    qh, kh, vh = sc.qh, sc.kh, sc.vh
    keys, plain = key_tail(valid_count, band_slots), flat_tail(0.0)
    pack_heads(sc.query, 0, qh, 0, rows, flat_tail(1.0))
    pack_heads(sc.own, 0, kh, 0, rows, keys)
    pack_heads(sc.own, width, vh, 0, rows, plain)
    swap.wait()
    save(sc.far, far_out)
    pack_heads(sc.far, 0, kh, rows, rows, keys)
    pack_heads(sc.far, width, vh, rows, rows, plain)
    beside = {
        0: ((g.z, 7), (g.b, 5), (g.c, 4)), 2: ((g.a, 6), (g.z, 8), (g.i, 1)), 4: ((g.a, 7), (g.b, 6), (g.c, 5)), 7: ((g.a, 8), (g.b, 7), (g.c, 6)), 10: ((g.b, 8), (g.c, 7)),
        13: ((g.c, 8),),
    }

    @pl.loop(0, heads)
    def _(h):
        attend_block(h, qh, kh, vh, sc.tops)
        for i, words in beside.items():
            pl.when(h == i)(partial(run, *words))

    unpack_heads(qh, 0, rows, sc.mixed, 0)
    save(sc.tops, tops_out)
    save(sc.mixed, mixed_out)

    @pl.loop(0, 3)
    def _(step):
        sc.attended[:, here(step)] = product(sc.mixed, 3 * width, step) + vec[8:9, here(step)]

    save(sc.attended, attended_out)

    @pl.loop(0, rows // BLOCK)
    def _(step):
        sub = pl.ds(pl.multiple_of(step * BLOCK, BLOCK), BLOCK)
        middle = sc.residual[sub, :] + vec[2:3, :] * sc.attended[sub, :]
        normed = normalize(middle)[0]
        sc.mlp_in[sub, :] = (normed * (1.0 + vec[4:5, :]) + vec[3:4, :]).astype(jnp.bfloat16)

    save(sc.mlp_in, mlp_out)
    g.finish()
    for copy in saves:
        copy.wait()


NOTE_COND, NOTE_GRID, NOTE_BIAS = 54, 63, 64


def spread_notes(notes, vec, width):
    lines = width // 128
    share = notes.shape[0]
    total = notes[0, 0:NOTE_GRID, :] + 0.0
    for b in range(1, share):
        total = total + notes[b, 0:NOTE_GRID, :]

    def flat(block, first):
        return jnp.concatenate([block[first + i : first + i + 1, :] for i in range(lines)], 1)

    for index in range(MOD_BLOCKS):
        vec[index : index + 1, :] = flat(total, index * lines)
    small = width // share
    for index in range(4):
        parts = []
        for b in range(share):
            first = NOTE_BIAS + 3 * index
            for i in range(3):
                parts.append(notes[b, first + i : first + i + 1, : min(128, small - 128 * i)])
        vec[6 + index : 7 + index, :] = jnp.concatenate(parts, 1)
    for b in range(share):
        block = notes[b, NOTE_BIAS + 12 : NOTE_BIAS + 12 + lines, :]
        vec[10 + b : 11 + b, :] = flat(block, 0)
    vec[14:15, :] = flat(notes[0, NOTE_COND : NOTE_COND + lines, :], 0)


def forward_block(qp, inner, outer, tok, cot, note, table):
    half, ff = qp.shape[0] // 2, qp.shape[1]
    images, band_slots, width = tok.shape
    rows = images * band_slots
    heads = width // HEAD_DIM
    bf, f32 = jnp.bfloat16, jnp.float32
    S = jax.ShapeDtypeStruct
    qp, inner = qp.reshape(2, half, ff), inner.reshape(2, half, ff)
    outer = outer.reshape(4, 2, half, width)
    scratch = forward_scratch(half, ff, width, rows, note.shape[1], images)
    any_ = pl.BlockSpec(memory_space=pl.ANY)
    return pl.pallas_call(
        partial(forward_kernel, tuple(scratch), band_slots),
        out_shape=[
            S((NB, 2, half, ff), bf), S((NB, 2, half, ff), bf), S((NB, 4, 2, half, width), bf), S(cot.shape, bf),
            S((16, width), f32), S((rows, width), f32), S((rows, width), bf), S((rows, width), bf),
            S((rows, 2 * width), bf), S((rows, 2 * width), bf), S((heads, 8, rows), f32), S((rows, width), bf),
            S((rows, width), f32), S((rows, width), bf),
        ],
        in_specs=[any_] * 6 + [pl.BlockSpec(memory_space=pltpu.VMEM)],
        out_specs=[any_] * 14,
        scratch_shapes=list(scratch.values()),
        compiler_params=pltpu.CompilerParams(
            collective_id=0, has_side_effects=True, vmem_limit_bytes=60 * 2**20
        ),
        name="forward_block",
    )(qp, inner, outer, tok, cot, note, table)


GELU_SCALE = 0.7978845608028654


def mlp_kernel(band_slots, mlp_ref, inner_ref, outer_ref, vec_ref, bias_ref, residual_ref, attended_ref, cot_ref,
               mixed_ref, proj_ref, out_ref, middle_ref, back_ref, proj_grad_ref, outer_grad_ref, inner_grad_ref,
               bias_grad_ref, sums_ref, out_acc, back_acc, grad_mlp):
    step = pl.program_id(0)
    rows = mlp_ref.shape[0]
    low = lambda value: value.astype(jnp.bfloat16)
    line = lambda index: vec_ref[index : index + 1, :]

    def grad_out(at):
        slot = lax.rem(at + lax.broadcasted_iota(jnp.int32, (BLOCK, 1), 0), band_slots)
        valid = jnp.where(slot.astype(jnp.float32) < vec_ref[15:16, 0:1], 1.0, 0.0)
        return cot_ref[pl.ds(at, BLOCK), :].astype(jnp.float32) * valid

    def add_line(index, values):
        sums_ref[index : index + 1, :] += jnp.sum(values, 0, keepdims=True)

    @pl.when(step == 0)
    def _():
        sums_ref[...] = jnp.zeros_like(sums_ref)

        @pl.loop(0, rows // BLOCK)
        def _(block):
            at = pl.multiple_of(block * BLOCK, BLOCK)
            grad = low(line(5) * grad_out(at))
            grad_mlp[pl.ds(at, BLOCK), :] = grad
            add_line(5, grad.astype(jnp.float32))
            out_acc[pl.ds(at, BLOCK), :] = jnp.zeros((BLOCK, out_acc.shape[1]), jnp.float32)
            back_acc[pl.ds(at, BLOCK), :] = jnp.zeros((BLOCK, out_acc.shape[1]), jnp.float32)

    inner, outer, grad = inner_ref[...], outer_ref[...], grad_mlp[...]
    pre = jnp.dot(mlp_ref[...], inner, preferred_element_type=jnp.float32) + bias_ref[...]
    grad_hidden = lanes_dot(grad, outer)
    square = pre * pre
    bend = jnp.tanh(GELU_SCALE * (pre * (1.0 + 0.044715 * square)))
    rise = 0.5 * (1.0 + bend)
    hidden = low(pre * rise)
    slope = rise + (0.5 * pre) * (1.0 - bend * bend) * (GELU_SCALE * (1.0 + 0.134145 * square))
    grad_pre = low(slope * grad_hidden)
    out_acc[...] += jnp.dot(hidden, outer, preferred_element_type=jnp.float32)
    outer_grad_ref[...] = low(rows_dot(hidden, grad))
    back_acc[...] += lanes_dot(grad_pre, inner)
    inner_grad_ref[...] = low(rows_dot(mlp_ref[...], grad_pre))
    bias_grad_ref[...] = jnp.broadcast_to(
        jnp.sum(grad_pre.astype(jnp.float32), 0, keepdims=True), bias_grad_ref.shape
    )

    @pl.when(step == pl.num_programs(0) - 1)
    def _():
        @pl.loop(0, rows // BLOCK)
        def _(block):
            at = pl.multiple_of(block * BLOCK, BLOCK)
            sub = pl.ds(at, BLOCK)
            attended = attended_ref[sub, :]
            middle = residual_ref[sub, :] + line(2) * attended
            normed, inverse = normalize(middle)
            mlp_out = out_acc[sub, :] + line(9)
            out_ref[sub, :] = low(middle + line(5) * mlp_out)
            grad_block = grad_out(at)
            add_line(0, grad_block * mlp_out)
            back = back_acc[sub, :]
            add_line(1, back)
            add_line(2, back * normed)
            grad_middle = grad_block + norm_back(back * (1.0 + line(4)), normed, inverse)
            middle_ref[sub, :] = grad_middle
            add_line(3, grad_middle * attended)
            grad_attended = low(line(2) * grad_middle)
            add_line(4, grad_attended.astype(jnp.float32))
            grad_mlp[sub, :] = grad_attended

        proj_grad_ref[...] = low(rows_dot(mixed_ref[...], grad_mlp[...]))
        back_ref[...] = low(lanes_dot(grad_mlp[...], proj_ref[...]))


def feed_forward(mlp_in, inner, outer, vectors, inner_bias, residual, attended, cotangent, mixed, first, band_slots):
    rows, width = mlp_in.shape
    hidden = inner.shape[1]
    tile = 512
    bf, f32 = jnp.bfloat16, jnp.float32
    S = jax.ShapeDtypeStruct
    keep = lambda *shape: pl.BlockSpec(shape, lambda j: (0,) * len(shape))
    return pl.pallas_call(
        partial(mlp_kernel, band_slots),
        grid=(hidden // tile,),
        out_shape=[
            S((rows, width), bf), S((rows, width), f32), S((rows, width), bf), S((width, width), bf),
            S((hidden, width), bf), S((width, hidden), bf), S((8, hidden), f32), S((8, width), f32),
        ],
        in_specs=[
            keep(rows, width), pl.BlockSpec((width, tile), lambda j: (0, j)), pl.BlockSpec((tile, width), lambda j: (j, 0)),
            keep(16, width), pl.BlockSpec((1, tile), lambda j: (0, j)), keep(rows, width), keep(rows, width),
            keep(rows, width), keep(rows, width), pl.BlockSpec((width, width), lambda j: (0, 3)),
        ],
        out_specs=[
            keep(rows, width), keep(rows, width), keep(rows, width), keep(width, width),
            pl.BlockSpec((tile, width), lambda j: (j, 0)), pl.BlockSpec((width, tile), lambda j: (0, j)),
            pl.BlockSpec((8, tile), lambda j: (0, j)), keep(8, width),
        ],
        scratch_shapes=[pltpu.VMEM((rows, width), f32), pltpu.VMEM((rows, width), f32), pltpu.VMEM((rows, width), bf)],
        compiler_params=pltpu.CompilerParams(vmem_limit_bytes=60 * 2**20),
        cost_estimate=pl.CostEstimate(
            flops=12 * rows * width * hidden, bytes_accessed=8 * width * hidden + 24 * rows * width,
            transcendentals=rows * hidden,
        ),
        name="feed_forward",
    )(mlp_in, inner, outer, vectors, inner_bias, residual, attended, cotangent, mixed, first)


def pair_perm(dp_count, band_count):
    return [
        (dp * band_count + band, (dp ^ 1) * band_count + band)
        for dp in range(dp_count)
        for band in range(band_count)
    ]


def position_parts(width):
    quarter = width // 4
    frequency = 10000.0 ** (-jnp.arange(quarter, dtype=jnp.float32) / quarter)
    angles = jnp.arange(128, dtype=jnp.float32)[:, None] * frequency
    left = jnp.concatenate([jnp.sin(angles), jnp.cos(angles)], -1)
    parts = []
    for _ in range(3):
        part = lax.reduce_precision(left, 8, 7)
        parts.append(part.astype(jnp.bfloat16))
        left = left - part
    return jnp.stack(parts)


def over_groups(piece, dp_count):
    if dp_count == 8:
        return piece
    groups = [[rank + 8 * group for group in range(dp_count // 8)] for rank in range(8)]
    return lax.psum(piece.astype(jnp.float32), "dp", axis_index_groups=groups)


def every_group(piece, dp_count):
    if dp_count == 8:
        return piece[None]
    groups = [[rank + 8 * group for group in range(dp_count // 8)] for rank in range(8)]
    return lax.all_gather(piece, "dp", axis_index_groups=groups)


def own_piece(vector, count, band_place):
    return lax.dynamic_slice_in_dim(vector, band_place * count, count, 0)


def body(
    tokens,
    condition,
    patch_grid,
    ada_weight,
    ada_bias,
    qkv_weight,
    query_bias,
    value_bias,
    proj_weight,
    proj_bias,
    inner_weight,
    inner_bias,
    outer_weight,
    outer_bias,
    cotangent,
):
    both = ("dp", "band")
    dp_count = lax.axis_size("dp")
    band_count = lax.axis_size("band")
    images, band_slots, width = tokens.shape
    band = lax.axis_index("band")
    dp = lax.axis_index("dp")
    core = lax.rem(dp, 2)
    hidden = inner_weight.shape[1]
    part_rows = qkv_weight.shape[0]
    siblings = pair_perm(dp_count, band_count)

    condition_f = condition.astype(jnp.float32)
    activated = jax.nn.silu(condition_f).astype(jnp.bfloat16)
    own_activated = lax.dynamic_slice_in_dim(activated, band * part_rows, part_rows, 1)
    share = jnp.dot(own_activated, ada_weight, preferred_element_type=jnp.float32)
    share = share + lax.dynamic_update_slice_in_dim(
        jnp.zeros((ada_weight.shape[1],), jnp.float32),
        ada_bias.astype(jnp.float32),
        band * ada_bias.shape[0],
        0,
    )
    mod_count = share.shape[1]
    lines = lambda vector: jnp.pad(
        vector.astype(jnp.float32), [(0, 0)] * (vector.ndim - 1) + [(0, -vector.shape[-1] % 128)]
    )
    spread = lambda vector: jnp.broadcast_to(lines(vector), (images, -(-vector.shape[0] // 128) * 128))
    note = jnp.concatenate(
        [share, condition_f, lines(patch_grid)]
        + [spread(bias) for bias in (query_bias, value_bias, proj_bias, outer_bias, inner_bias)],
        1,
    )
    note = jnp.pad(note, ((0, 0), (0, -note.shape[1] % 1024))).reshape(images, -1, 128)
    first_weight = jnp.concatenate([qkv_weight, proj_weight], 1)
    (first_full, inner_full, outer_full, cotangent_here, vectors, residual, attn_in, query_rows, key_value,
     other_key_value, tops, mixed_rows, attended, mlp_in) = forward_block(
        first_weight, inner_weight, outer_weight, tokens, cotangent, note, position_parts(width)
    )
    first_full = first_full.reshape(width, -1)
    inner_full = inner_full.reshape(width, hidden)
    outer_full = outer_full.reshape(hidden, width)
    qkv_full = first_full[:, : 3 * width]
    proj_full = first_full[:, 3 * width :]
    scale_one, gate_one = vectors[1], vectors[2]
    condition_here = vectors[14]
    valid_count = vectors[15, :1].astype(jnp.int32)
    rows = images * band_slots
    inner_bias_row = vectors[10:14].reshape(1, -1)
    (block_out, grad_middle, grad_mixed, grad_proj, grad_outer, grad_inner, grad_inner_bias, sums) = feed_forward(
        mlp_in, inner_full, outer_full, vectors, inner_bias_row, residual, attended,
        cotangent_here.reshape(rows, width), mixed_rows, first_full, band_slots,
    )
    blocks = (band_count, 2, part_rows // 2, width)
    grad_outer = grad_outer.reshape(band_count, 4, 2, part_rows // 2, width)
    grad_inner = grad_inner.reshape(band_count, 2, part_rows // 2, hidden)
    grad_inner_bias = grad_inner_bias[0]
    grad_gate_two, grad_shift_two, grad_scale_two, grad_gate_one, grad_proj_bias, grad_outer_bias = [
        sums[index] for index in range(6)
    ]
    normed_one, inverse_one = normalize(residual)
    outer_sum, inner_part, block_home, grad_query, own_terms, far_terms = reduce_attend(
        (FRONT | BACK, FRONT), [[grad_outer], [grad_inner]], [], block_out.reshape(images, band_slots, width), valid_count, query_rows, key_value, other_key_value, grad_mixed, tops,
        band_slots, 1,
    )
    other_terms = lax.ppermute(far_terms, both, siblings)
    grad_key_value = (own_terms.astype(jnp.float32) + other_terms.astype(jnp.float32)).astype(
        jnp.bfloat16
    )
    grad_qkv = jnp.concatenate([grad_query, grad_key_value], -1)
    grad_first = [
        rows_dot(attn_in, part).astype(jnp.bfloat16).reshape(blocks)
        for part in (grad_query, grad_key_value[:, :width], grad_key_value[:, width:])
    ]
    grad_attn_in = lanes_dot(grad_qkv, qkv_full)
    grad_query_bias = jnp.sum(grad_query.astype(jnp.float32), 0)
    grad_value_bias = jnp.sum(grad_key_value[:, width:].astype(jnp.float32), 0)
    grad_shift_one = jnp.sum(grad_attn_in, 0)
    grad_scale_one = jnp.sum(grad_attn_in * normed_one, 0)
    grad_tokens = grad_middle + norm_back(grad_attn_in * (1.0 + scale_one), normed_one, inverse_one)
    part_mod = jnp.concatenate(
        [grad_shift_one, grad_scale_one, grad_gate_one, grad_shift_two, grad_scale_two, grad_gate_two]
    )
    part_mod = jnp.concatenate([part_mod, 0.5 * condition_here]).reshape(-1, 128)
    part_mod = jnp.pad(part_mod, ((0, -part_mod.shape[0] % 16), (0, 0)))
    part_bias = jnp.concatenate(
        [grad_query_bias, grad_value_bias, grad_proj_bias, grad_inner_bias, grad_outer_bias]
    ).reshape(-1, 128)
    inner_sum, first_sum, tokens_home, every, bias_grads, grad_act = reduce_last(
        grad_first + [grad_proj.reshape(blocks)], inner_part, grad_tokens.astype(jnp.bfloat16).reshape(images, band_slots, width), part_mod, part_bias, ada_weight, images, 2
    )
    tokens_home = tokens_home.astype(jnp.float32)
    every = every_group(every, dp_count)
    bias_grads = over_groups(bias_grads, dp_count).reshape(-1)
    every = jnp.swapaxes(every, 1, 2).reshape(dp_count * images, -1)
    every_mod = every[:, :mod_count]
    every_condition = every[:, mod_count : mod_count + width]
    every_activated = jax.nn.silu(every_condition.astype(jnp.float32)).astype(jnp.bfloat16)
    every_activated = lax.dynamic_slice_in_dim(every_activated, band * part_rows, part_rows, 1)
    grad_ada = rows_dot(every_activated, every_mod)
    grad_ada_bias = own_piece(jnp.sum(every_mod.astype(jnp.float32), 0), ada_bias.shape[0], band)
    grad_act = jnp.swapaxes(grad_act[:, :images, :part_rows], 0, 1).reshape(images, width)
    grad_condition = jax.vjp(jax.nn.silu, condition_f)[1](grad_act)[0]

    def side_by_side(units):
        return jnp.concatenate([unit.reshape(part_rows, width) for unit in units], 1).astype(jnp.float32)

    first_sum, inner_sum, outer_sum = [
        over_groups(piece, dp_count) for piece in (first_sum, inner_sum, outer_sum)
    ]
    qkv_sum = side_by_side([first_sum[t] for t in range(3)])
    proj_sum = first_sum[3].reshape(part_rows, width).astype(jnp.float32)
    inner_sum = side_by_side([inner_sum[t] for t in range(4)])
    outer_sum = outer_sum.reshape(4 * part_rows, width).astype(jnp.float32)
    bias_parts = []
    at = 0
    for piece in (query_bias, value_bias, proj_bias, inner_bias, outer_bias):
        whole = piece.shape[0] * band_count
        bias_parts.append(own_piece(bias_grads[at : at + whole], piece.shape[0], band))
        at += whole
    return (
        block_home,
        tokens_home,
        grad_condition,
        grad_ada,
        grad_ada_bias,
        qkv_sum,
        bias_parts[0],
        bias_parts[1],
        proj_sum,
        bias_parts[2],
        inner_sum,
        bias_parts[3],
        outer_sum,
        bias_parts[4],
    )


def solution(mesh):
    placed = (
        P("dp", "band", None),
        P("dp", None),
        P("dp", None),
        P("band", None),
        P("band"),
        P("band", None),
        P("band"),
        P("band"),
        P("band", None),
        P("band"),
        P("band", None),
        P("band"),
        P("band", None),
        P("band"),
        P("dp", "band", None),
    )
    return jax.shard_map(
        body,
        mesh=mesh,
        in_specs=placed,
        out_specs=(
            P("dp", "band", None),
            P("dp", "band", None),
            P("dp", None),
            P("band", None),
            P("band"),
            P("band", None),
            P("band"),
            P("band"),
            P("band", None),
            P("band"),
            P("band", None),
            P("band"),
            P("band", None),
            P("band"),
        ),
        check_vma=False,
    )
```

```python
from functools import partial
from types import SimpleNamespace

import jax
import jax.numpy as jnp
from jax import lax
from jax.experimental import pallas as pl
from jax.experimental.pallas import tpu as pltpu
from jax.sharding import PartitionSpec as P

HEAD_DIM = 72


MESH = pl.DeviceIdType.MESH
NB = 4


def device(dp, band):
    return {"dp": dp, "band": band}


def normalize(values):
    average = jnp.mean(values, -1, keepdims=True)
    centered = values - average
    variance = jnp.mean(centered * centered, -1, keepdims=True)
    inverse = lax.rsqrt(variance + 1e-06)
    return (centered * inverse, inverse)


def norm_back(grad_normed, normed, inverse):
    first = jnp.mean(grad_normed, -1, keepdims=True)
    second = jnp.mean(grad_normed * normed, -1, keepdims=True)
    return inverse * (grad_normed - first - normed * second)


LANES = 128
PACK_ROWS = 128


def pack_heads(source, first, heads_ref, row0, rows, tail):
    heads = heads_ref.shape[0]

    @pl.loop(0, rows // PACK_ROWS)
    def _(step):
        at = pl.multiple_of(step * PACK_ROWS, PACK_ROWS)
        block = source[pl.ds(at, PACK_ROWS), first : first + heads * HEAD_DIM]
        end = tail(at)
        for h in range(heads):
            part = block[:, h * HEAD_DIM : (h + 1) * HEAD_DIM]
            heads_ref[h, pl.ds(row0 + at, PACK_ROWS), :] = jnp.concatenate([part, end], 1)


def unpack_heads(heads_ref, row0, rows, target, first):
    heads = heads_ref.shape[0]

    @pl.loop(0, rows // PACK_ROWS)
    def _(step):
        at = pl.multiple_of(step * PACK_ROWS, PACK_ROWS)
        parts = [heads_ref[h, pl.ds(row0 + at, PACK_ROWS), :][:, :HEAD_DIM] for h in range(heads)]
        target[pl.ds(at, PACK_ROWS), first : first + heads * HEAD_DIM] = jnp.concatenate(parts, 1)


def flat_tail(value):
    def tail(at):
        lane = lax.broadcasted_iota(jnp.int32, (PACK_ROWS, LANES - HEAD_DIM), 1)
        return jnp.where(lane == 0, value, 0.0).astype(jnp.bfloat16)

    return tail


def key_tail(valid_count, band_slots):
    def tail(at):
        shape = (PACK_ROWS, LANES - HEAD_DIM)
        lane = lax.broadcasted_iota(jnp.int32, shape, 1)
        slot = lax.rem(at + lax.broadcasted_iota(jnp.int32, shape, 0), band_slots)
        return jnp.where(jnp.logical_and(lane == 0, slot >= valid_count), -1e30, 0.0).astype(jnp.bfloat16)

    return tail


def lanes_dot(left, right):
    return lax.dot_general(left, right, (((1,), (1,)), ((), ())), preferred_element_type=jnp.float32)


def rows_dot(left, right):
    return lax.dot_general(left, right, (((0,), (0,)), ((), ())), preferred_element_type=jnp.float32)


SCORE_SCALE = HEAD_DIM ** (-0.5)


def attend_block(h, qh, kh, vh, top_ref):
    rows = qh.shape[1]
    for block in range(2):
        at = pl.ds(block * rows // 2, rows // 2)
        scores = lanes_dot(kh[h], qh[h, at, :]) * SCORE_SCALE
        top = jnp.max(scores, 0, keepdims=True)
        weights = jnp.exp(scores - top)
        total = jnp.sum(weights, 0, keepdims=True)
        low = (weights * (1.0 / total)).astype(jnp.bfloat16)
        mixed = rows_dot(vh[h], low)
        qh[h, at, :] = jnp.transpose(mixed).astype(jnp.bfloat16)
        top_ref[h, :, at] = jnp.broadcast_to(top + jnp.log(total), (8, rows // 2))


def attend_head(h, qh, kh, vh, gh, top_ref):
    query = qh[h]
    key = kh[h]
    grad = gh[h]
    probs = jnp.exp(lanes_dot(key, query) * SCORE_SCALE - top_ref[h, 0:1, :])
    grad_probs = lanes_dot(vh[h], grad)
    inner = jnp.sum(probs * grad_probs, 0, keepdims=True)
    grad_scores = (probs * (grad_probs - inner)).astype(jnp.bfloat16)
    vh[h] = jnp.dot(
        probs.astype(jnp.bfloat16), grad, preferred_element_type=jnp.float32
    ).astype(jnp.bfloat16)
    grad_query = rows_dot(key, grad_scores)
    kh[h] = (
        SCORE_SCALE * jnp.dot(grad_scores, query, preferred_element_type=jnp.float32)
    ).astype(jnp.bfloat16)
    qh[h] = (SCORE_SCALE * jnp.transpose(grad_query)).astype(jnp.bfloat16)


def compass():
    dp = lax.axis_index("dp")
    band = lax.axis_index("band")
    core = lax.rem(dp, 2)
    px = lax.rem(dp // 2, 2)
    py = lax.rem(dp // 4, 2)
    return SimpleNamespace(
        dp=dp, band=band, core=core, px=px, py=py, kind=2 * py + px,
        sib=dp + 1 - 2 * core, xdp=dp + 2 - 4 * px, ydp=dp + 4 - 8 * py,
    )


def add_rows(total, term):
    rows = total.shape[0]

    @pl.loop(0, rows // 16)
    def _(step):
        at = pl.ds(pl.multiple_of(step * 16, 16), 16)
        total[at, :] = (
            total[at, :].astype(jnp.float32) + term[at, :].astype(jnp.float32)
        ).astype(jnp.bfloat16)


def run_all(batch):
    for do in batch:
        do()


REDUCE_ORDER = (1, 3, 2, 0)


FRONT, BACK = 1, 2


def reduce_scratch(plan, half, width):
    bf = jnp.bfloat16
    n = NB * sum(1 for todo in plan if todo & FRONT)
    m = len(plan)
    D = pltpu.SemaphoreType.DMA
    scratch = dict(
        recv_z=pltpu.VMEM((m, NB, half, width), bf), z_send=D((m, NB)), z_recv=D((m, NB)),
        d_send=D((m, 6)), d_recv=D((m, 6)), d_own=D((m,)), part_sem=D((m,)),
    )
    if n:
        scratch.update(
            acc=pltpu.VMEM((n, 4, half, width), bf), recv_a=pltpu.VMEM((n, 4, half, width), bf),
            recv_b=pltpu.VMEM((n, 2, half, width), bf), recv_c=pltpu.VMEM((n, half, width), bf),
            a_send=D((n,)), a_recv=D((n,)), a_own=D((n,)),
            b_send=D((n, 2, 2)), b_recv=D((n, 2, 2)), c_send=D((n, 2)), c_recv=D((n, 2)),
        )
    return scratch


def reduce_steps(me, plan, source, out, parts_in, parts_out, sc, beside=(), ahead=3, by_kind=False):
    dp, band, core, px, py, kind = me.dp, me.band, me.core, me.px, me.py, me.kind
    here = lambda d: device(d, band)
    fronts = [phase for phase, todo in enumerate(plan) if todo & FRONT]
    backs = [phase for phase, todo in enumerate(plan) if todo & BACK]
    chunks = [(phase, k) for phase in fronts for k in REDUCE_ORDER]
    n = len(chunks)
    flip = lambda v: 1 - v
    sends = []
    rows = sc.recv_z.shape[2]
    cut = rows // 32 * 16
    spans = (pl.ds(0, cut), pl.ds(cut, rows - cut))

    def remote(src, dst, ss, rs, to):
        return pltpu.make_async_remote_copy(
            src_ref=src, dst_ref=dst, send_sem=ss, recv_sem=rs, device_id=to, device_id_type=MESH
        )

    def go(make):
        make().start()
        sends.append(make)

    def target(k):
        return device(dp, lax.rem(band + k, NB))

    def start_a(s, kinds=range(4)):
        phase, k = chunks[s]
        b = lax.rem(band + k, NB)
        for t in kinds:
            remote(
                source(phase, b, t, flip(core)), sc.recv_a.at[s, t], sc.a_send.at[s], sc.a_recv.at[s],
                here(me.sib),
            ).start()
            pltpu.make_async_copy(source(phase, b, t, core), sc.acc.at[s, t], sc.a_own.at[s]).start()

    def first(half, j, send):
        if half == 0:
            return 2 * j + (flip(px) if send else px)
        return 2 * (flip(py) if send else py) + j

    def second(half, send):
        if half == 0:
            return 2 * (flip(py) if send else py) + px
        return 2 * py + (flip(px) if send else px)

    def near(half):
        return here(me.xdp if half == 0 else me.ydp)

    def send_b(s, half, j):
        return remote(
            sc.acc.at[s, first(half, j, True), spans[half]], sc.recv_b.at[s, j, spans[half]],
            sc.b_send.at[s, half, j], sc.b_recv.at[s, half, j], near(half),
        )

    def send_c(s, half):
        return remote(
            sc.acc.at[s, second(half, True), spans[half]], sc.recv_c.at[s, spans[half]],
            sc.c_send.at[s, half], sc.c_recv.at[s, half], near(1 - half),
        )

    def send_z(phase, k, src):
        return remote(src, sc.recv_z.at[phase, k], sc.z_send.at[phase, k], sc.z_recv.at[phase, k], target(k))

    def unit_z(s):
        phase, k = chunks[s]
        return send_z(phase, k, sc.acc.at[s, kind])

    def part_load(phase):
        return pltpu.make_async_copy(parts_in[phase], sc.recv_z.at[phase, 0], sc.part_sem.at[phase])

    def part_store(phase):
        return pltpu.make_async_copy(sc.recv_z.at[phase, 0], parts_out[phase], sc.part_sem.at[phase])

    def d_copy(phase, half, slot, mine):
        ss, rs = sc.d_send.at[phase, 3 * half + slot], sc.d_recv.at[phase, 3 * half + slot]
        span = spans[half]
        if slot == 0:
            src = sc.recv_z.at[phase, 0, span]
            return remote(src, out[phase].at[kind, core, span], ss, rs, near(half))
        j = slot - 1
        t = 2 * (py if mine else flip(py)) + j if half == 0 else 2 * j + (px if mine else flip(px))
        unit = out[phase].at[t, core, span]
        return remote(unit, unit, ss, rs, near(1 - half))

    def d_cross(phase, mine):
        row = out[phase].at[:, core if mine else flip(core)]
        return remote(row, row, sc.z_send.at[phase, 0], sc.z_recv.at[phase, 0], here(me.sib))

    def a_to_b(s):
        acc, got = sc.acc, sc.recv_a
        pltpu.make_async_copy(got.at[s], acc.at[s], sc.a_own.at[s]).wait()
        whole = remote(got.at[s], got.at[s], sc.a_send.at[s], sc.a_recv.at[s], here(me.sib))
        whole.wait_recv()
        for j in range(2):
            for half in range(2):
                t = first(half, j, True)
                add_rows(acc.at[s, t, spans[half]], got.at[s, t, spans[half]])
                go(partial(send_b, s, half, j))
        for j in range(2):
            for half in range(2):
                t = first(half, j, False)
                add_rows(acc.at[s, t, spans[half]], got.at[s, t, spans[half]])
        whole.wait_send()

    def b_to_c(s):
        acc, got = sc.acc, sc.recv_b
        for half in range(2):
            for j in range(2):
                send_b(s, half, j).wait_recv()
            away = flip(py) if half == 0 else flip(px)
            t = second(half, True)
            add_rows(acc.at[s, t, spans[half]], got.at[s, away, spans[half]])
            go(partial(send_c, s, half))
        for half in range(2):
            stay = py if half == 0 else px
            add_rows(acc.at[s, kind, spans[half]], got.at[s, stay, spans[half]])

    def c_to_z(s):
        phase, k = chunks[s]
        for half in range(2):
            send_c(s, half).wait_recv()
            add_rows(sc.acc.at[s, kind, spans[half]], sc.recv_c.at[s, spans[half]])
        if k != 0:
            go(partial(unit_z, s))

    def z_sum(phase):
        got = sc.recv_z
        for k in range(1, NB):
            remote(
                got.at[phase, k], got.at[phase, k], sc.z_send.at[phase, k], sc.z_recv.at[phase, k], here(dp)
            ).wait_recv()
        s = NB * fronts.index(phase) + NB - 1

        @pl.loop(0, rows // 16)
        def _(step):
            at = pl.ds(pl.multiple_of(step * 16, 16), 16)
            total = sc.acc[s, kind, at, :].astype(jnp.float32)
            for k in range(1, NB):
                total = total + got[phase, k, at, :].astype(jnp.float32)
            got[phase, 0, at, :] = total.astype(jnp.bfloat16)

        if not plan[phase] & BACK:
            part_store(phase).start()

    def d_first(phase):
        if not plan[phase] & FRONT:
            part_load(phase).wait()
        own_copy = pltpu.make_async_copy(sc.recv_z.at[phase, 0], out[phase].at[kind, core], sc.d_own.at[phase])
        own_copy.start()
        for half in range(2):
            go(partial(d_copy, phase, half, 0, True))
        own_copy.wait()

    def d_second(phase):
        for half in range(2):
            d_copy(phase, half, 0, False).wait_recv()
            for slot in (1, 2):
                go(partial(d_copy, phase, half, slot, True))

    def d_third(phase):
        for half in range(2):
            for slot in (1, 2):
                d_copy(phase, half, slot, False).wait_recv()
        go(partial(d_cross, phase, True))

    def d_last(phase):
        d_cross(phase, False).wait_recv()

    def finish():
        for phase in fronts:
            if not plan[phase] & BACK:
                part_store(phase).wait()
        for make in sends:
            make().wait_send()

    table = {-1: [] if by_kind else [partial(start_a, s) for s in range(n)]}

    def put(at, do):
        table.setdefault(at, []).append(do)

    for phase in backs:
        if not plan[phase] & FRONT:
            put(-1, lambda phase=phase: part_load(phase).start())
    for at, do in enumerate(beside):
        put(at, do)
    for s in range(n):
        put(s + ahead, partial(b_to_c, s))
        put(s + ahead + 1, partial(c_to_z, s))
        put(s, partial(a_to_b, s))
    for phase, todo in enumerate(plan):
        end = 0
        if todo & FRONT:
            end = NB * fronts.index(phase) + NB + ahead + 1
            put(end, partial(z_sum, phase))
        if todo & BACK:
            for lag, do in ((0, d_first), (1, d_second), (2, d_third), (4, d_last)):
                put(end + lag - (0 if todo & FRONT else 1), partial(do, phase))
    steps = [partial(run_all, table[at]) for at in sorted(table)]
    steps.append(finish)
    if by_kind:
        return steps, lambda kind: [start_a(s, (kind,)) for s in range(n)]
    return steps


def home_scratch():
    D = pltpu.SemaphoreType.DMA
    return dict(home_send=D((2,)), home_recv=D((2,)))


def home_steps(me, rows_ref, home_ref, sc):
    band, core = me.band, me.core
    slot = lax.rem(band, 2)

    def stays(s):
        return jnp.logical_and(band // 2 == core, 2 * core + s == band)

    def copy(s):
        to = device(me.dp - core + band // 2, 2 * core + s)
        return pltpu.make_async_remote_copy(
            src_ref=rows_ref.at[s], dst_ref=home_ref.at[slot], send_sem=sc.home_send.at[s],
            recv_sem=sc.home_recv.at[slot], device_id=to, device_id_type=MESH,
        )

    def begin():
        for s in range(2):
            pl.when(stays(s))(
                lambda: pltpu.make_async_copy(
                    rows_ref.at[s], home_ref.at[slot], sc.home_recv.at[slot]
                ).start()
            )
            pl.when(jnp.logical_not(stays(s)))(lambda: copy(s).start())

    def finish():
        for s in range(2):
            pl.when(jnp.logical_not(stays(s)))(lambda: copy(s).wait_send())
        for i in range(2):
            pltpu.make_async_copy(rows_ref.at[i], home_ref.at[i], sc.home_recv.at[i]).wait()

    return begin, finish


def group_barrier(me):
    barrier = pltpu.get_barrier_semaphore()
    peers = [(me.xdp, me.band), (me.ydp, me.band), (me.sib, me.band)]
    for k in range(1, NB):
        other = lax.rem(me.band + k, NB)
        peers += [(me.dp, other), (me.sib, other)]
    for dp, band in peers:
        pl.semaphore_signal(
            barrier, inc=1, device_id=device(dp, band), device_id_type=MESH
        )
    pl.semaphore_wait(barrier, len(peers))


def reduce_refs(plan, counts, refs):
    take = iter(refs)
    grads = [[next(take) for _ in range(count)] for count in counts]

    def source(phase, b, t, h):
        if len(grads[phase]) > 1:
            return grads[phase][t].at[b, h]
        whole = grads[phase][0]
        if len(whole.shape) == 5:
            return whole.at[b, t, h]
        span = whole.shape[3] // 4
        return whole.at[b, h, :, pl.ds(pl.multiple_of(t * span, 128), span)]

    return source, [next(take) if todo == BACK else None for todo in plan]


def reduce_outs(plan, refs):
    take = iter(refs)
    out = [next(take) if todo & BACK else None for todo in plan]
    return out, [next(take) if todo == FRONT else None for todo in plan]


def reduce_shapes(plan, half, width):
    bf = jnp.bfloat16
    shapes = [jax.ShapeDtypeStruct((4, 2, half, width), bf) for todo in plan if todo & BACK]
    return shapes + [jax.ShapeDtypeStruct((half, width), bf) for todo in plan if todo == FRONT]


def small_scratch(mod_rows, bias_rows, cond_rows, cond_cols):
    D = pltpu.SemaphoreType.DMA
    f32 = jnp.float32
    return dict(
        s_core=pltpu.VMEM((mod_rows + bias_rows, 128), f32),
        s_every=pltpu.VMEM((NB, 4, mod_rows, 128), jnp.bfloat16),
        s_bias=pltpu.VMEM((3, bias_rows, 128), f32),
        s_got=pltpu.VMEM((2 + NB, bias_rows, 128), f32),
        s_flat=pltpu.VMEM((8, mod_rows, 128), f32),
        s_cond=pltpu.VMEM((NB, cond_rows, cond_cols), f32),
        s_send=D((8,)), s_recv=D((8,)), sz_send=D((2, NB)), sz_recv=D((2, NB)),
        sc_send=D((NB,)), sc_recv=D((NB,)),
    )


def small_steps(me, mods, images, small_ref, ada_ref, every_ref, bias_ref, cond_ref, sc):
    dp, band, core, px, py, kind = me.dp, me.band, me.core, me.px, me.py, me.kind
    here = lambda d: device(d, band)
    every, bias, got, cond = sc.s_every, sc.s_bias, sc.s_got, sc.s_cond
    mod_rows = every.shape[2]
    flip = lambda v: 1 - v

    def remote(src, dst, ss, rs, to):
        return pltpu.make_async_remote_copy(
            src_ref=src, dst_ref=dst, send_sem=ss, recv_sem=rs, device_id=to, device_id_type=MESH
        )

    def plain(index, src, dst, to):
        return remote(src, dst, sc.s_send.at[index], sc.s_recv.at[index], to)

    def core_copy():
        return plain(0, small_ref, sc.s_core, here(me.sib))

    def x_copies(mine):
        unit = every.at[band, kind if mine else 2 * py + flip(px)]
        return [
            plain(1, unit, unit, here(me.xdp)),
            plain(2, bias.at[0], got.at[0], here(me.xdp)),
        ]

    def y_copies(mine):
        pair = every.at[band, pl.ds(2 * (py if mine else flip(py)), 2)]
        return [
            plain(3, pair, pair, here(me.ydp)),
            plain(4, bias.at[1], got.at[1], here(me.ydp)),
        ]

    def z_copies(k, mine):
        to = device(dp, lax.rem(band + k, NB))
        block = every.at[band if mine else lax.rem(band + NB - k, NB)]
        return [
            remote(block, block, sc.sz_send.at[0, k], sc.sz_recv.at[0, k], to),
            remote(bias.at[2], got.at[2 + k], sc.sz_send.at[1, k], sc.sz_recv.at[1, k], to),
        ]

    def cond_copy(k, mine):
        to = device(dp, lax.rem(band + k, NB))
        block = cond.at[band if mine else lax.rem(band + NB - k, NB)]
        return remote(block, block, sc.sc_send.at[k], sc.sc_recv.at[k], to)

    def begin():
        core_copy().start()

    def cores():
        core_copy().wait()
        total = small_ref[...] + sc.s_core[...]
        every[band, kind] = total[:mod_rows].astype(jnp.bfloat16)
        bias[0] = total[mod_rows:]
        for copy in x_copies(True):
            copy.start()

    def over_x():
        for copy in x_copies(True):
            copy.wait_send()
        for copy in x_copies(False):
            copy.wait_recv()
        bias[1] = bias[0] + got[0]
        for copy in y_copies(True):
            copy.start()

    def over_y():
        for copy in y_copies(True):
            copy.wait_send()
        for copy in y_copies(False):
            copy.wait_recv()
        bias[2] = bias[1] + got[1]
        for k in range(1, NB):
            for copy in z_copies(k, True):
                copy.start()

    def over_z():
        for k in range(1, NB):
            for copy in z_copies(k, True):
                copy.wait_send()
            for copy in z_copies(k, False):
                copy.wait_recv()
        bias_ref[...] = bias[2] + got[3] + got[4] + got[5]
        every_ref[...] = every[...]
        flat = sc.s_flat
        for i in range(images):
            flat[i] = every[images * core + i, kind].astype(jnp.float32)
        parts = mods // 128
        lead = flat.shape[0]
        total = jnp.zeros((lead, ada_ref.shape[0]), jnp.float32)
        for r in range(parts):
            left = jnp.concatenate(
                [flat[i, r : r + 1, :] for i in range(images)]
                + [jnp.zeros((lead - images, 128), jnp.float32)]
            ).astype(jnp.bfloat16)
            total = total + lanes_dot(left, ada_ref[:, r * 128 : (r + 1) * 128])
        pad = cond.shape[2] - total.shape[1]
        cond[band] = jnp.concatenate([total, jnp.zeros((lead, pad), jnp.float32)], 1)
        for k in range(1, NB):
            cond_copy(k, True).start()

    def conditions():
        for k in range(1, NB):
            cond_copy(k, True).wait_send()
            cond_copy(k, False).wait_recv()
        cond_ref[...] = cond[...]

    return [begin, cores, over_x, over_y, over_z, conditions]


def put_lines(ref, first, values):
    for i in range(values.shape[1] // 128):
        ref[first + i : first + i + 1, :] = values[:, i * 128 : (i + 1) * 128]


def reduce_last_kernel(plan, images, band_slots, names, *refs):
    me = compass()
    (proj_ref, part_ref, attn_hbm, query_hbm, own_hbm, other_hbm, first_hbm, residual_hbm, middle_hbm, vec_ref, sums_ref,
     inner_bias_ref, ada_ref) = refs[:13]
    inner_out, first_out, home_ref, every_ref, bias_ref, cond_ref = refs[13:19]
    sc = SimpleNamespace(**dict(zip(names, refs[19:])))
    rows, width = sc.attn.shape
    lines = width // 128
    small = sc.small
    mod_rows = sc.s_every.shape[2]

    def source(phase, b, t, h):
        return proj_ref.at[b, h] if t == 3 else sc.grads.at[t, b, h]

    loads = [
        (attn_hbm, sc.attn), (query_hbm, sc.gqkv.at[:, pl.ds(0, width)]), (own_hbm, sc.gqkv.at[:, pl.ds(width, 2 * width)]),
        (other_hbm, sc.other), (first_hbm.at[:, pl.ds(0, 3 * width)], sc.first), (residual_hbm, sc.residual),
        (middle_hbm, sc.middle),
    ]

    def load(i):
        return pltpu.make_async_copy(*loads[i], sc.load_sem.at[i])

    for i in range(len(loads)):
        load(i).start()
    group_barrier(me)
    mods = MOD_BLOCKS * width
    exchange = small_steps(me, mods, images, small, ada_ref, every_ref, bias_ref, cond_ref, sc)
    depart, settle = home_steps(me, sc.tokens, home_ref, sc)
    steps, start = reduce_steps(
        me, plan, source, (inner_out, first_out), (part_ref, None), (None, None), sc, (), 2, True
    )
    start(3)
    steps[0]()
    for i in range(4):
        load(i).wait()

    sc.sums[...] = jnp.zeros_like(sc.sums)

    def add_line(index, values):
        sc.sums[index : index + 1, :] += jnp.sum(values, 0, keepdims=True)

    @pl.loop(0, rows // BLOCK)
    def _(block):
        sub = pl.ds(pl.multiple_of(block * BLOCK, BLOCK), BLOCK)
        total = sc.gqkv[sub, width:].astype(jnp.float32) + sc.other[sub, :].astype(jnp.float32)
        total = total.astype(jnp.bfloat16)
        sc.gqkv[sub, width:] = total
        add_line(1, total[:, width:].astype(jnp.float32))
        add_line(0, sc.gqkv[sub, :width].astype(jnp.float32))

    tile = width // 3
    for t in range(3):

        @pl.loop(0, 3)
        def _(j):
            at = pl.multiple_of(t * width + j * tile, 128)
            value = rows_dot(sc.attn[...], sc.gqkv[:, pl.ds(at, tile)]).astype(jnp.bfloat16)
            to = pl.ds(pl.multiple_of(j * tile, 128), tile)
            sc.grads[t, :, :, :, to] = value.reshape(sc.grads.shape[1:4] + (tile,))

        start(t)

    load(4).wait()
    for j in range(3):
        steps[1 + j]()
        sc.back[:, j * tile : (j + 1) * tile] = lanes_dot(sc.gqkv[...], sc.first[j * tile : (j + 1) * tile, :])
    load(5).wait()
    load(6).wait()

    @pl.loop(0, rows // BLOCK)
    def _(block):
        at = pl.multiple_of(block * BLOCK, BLOCK)
        sub = pl.ds(at, BLOCK)
        normed, inverse = normalize(sc.residual[sub, :])
        back = sc.back[sub, :]
        add_line(2, back)
        add_line(3, back * normed)
        grad = sc.middle[sub, :] + norm_back(back * (1.0 + vec_ref[1:2, :]), normed, inverse)
        per_image = band_slots // BLOCK
        to = pl.ds(pl.multiple_of(lax.rem(block, per_image) * BLOCK, BLOCK), BLOCK)
        sc.tokens[block // per_image, to, :] = grad.astype(jnp.bfloat16)

    small[...] = jnp.zeros_like(small)
    kept = [sc.sums[2:3, :], sc.sums[3:4, :]] + [sums_ref[i : i + 1, :] for i in (3, 1, 2, 0)]
    for i, values in enumerate(kept + [0.5 * vec_ref[14:15, :]]):
        put_lines(small, i * lines, values)
    at = mod_rows
    for values in (sc.sums[0:1, :], sc.sums[1:2, :], sums_ref[4:5, :], inner_bias_ref[0:1, :], sums_ref[5:6, :]):
        put_lines(small, at, values)
        at += values.shape[1] // 128
    exchange[0]()
    depart()
    rest = steps[4:]
    for i in range(max(len(rest), len(exchange) - 1)):
        if i + 1 < len(exchange):
            exchange[i + 1]()
        if i < len(rest):
            rest[i]()
    settle()


def reduce_last(proj, part, attn_in, query, own, other, first, residual, middle, vectors, sums, inner_bias, ada_weight,
                images, band_slots, collective_id):
    plan = (BACK, FRONT | BACK)
    half, width = proj.shape[-2:]
    rows = attn_in.shape[0]
    bf, f32 = jnp.bfloat16, jnp.float32
    V = pltpu.VMEM
    mod_rows = -(-(MOD_BLOCKS + 1) * width // 2048) * 16
    bias_rows = (4 * width + inner_bias.shape[1]) // 128
    cond_cols = -(-ada_weight.shape[0] // 128) * 128
    scratch = dict(
        **reduce_scratch(plan, half, width), **small_scratch(mod_rows, bias_rows, 8, cond_cols), **home_scratch(),
        attn=V((rows, width), bf), gqkv=V((rows, 3 * width), bf), other=V((rows, 2 * width), bf),
        first=V((width, 3 * width), bf), residual=V((rows, width), f32), middle=V((rows, width), f32),
        grads=V((3, NB, 2, half, width), bf), back=V((rows, width), f32), sums=V((8, width), f32),
        tokens=V((images, band_slots, width), bf), small=V((mod_rows + bias_rows, 128), f32),
        load_sem=pltpu.SemaphoreType.DMA((7,)),
    )
    any_, vmem = pl.BlockSpec(memory_space=pl.ANY), pl.BlockSpec(memory_space=pltpu.VMEM)
    return pl.pallas_call(
        partial(reduce_last_kernel, plan, images, band_slots, tuple(scratch)),
        out_shape=reduce_shapes(plan, half, width)
        + [
            jax.ShapeDtypeStruct((images, band_slots, width), bf),
            jax.ShapeDtypeStruct((NB, 4, mod_rows, 128), bf),
            jax.ShapeDtypeStruct((bias_rows, 128), f32),
            jax.ShapeDtypeStruct((NB, 8, cond_cols), f32),
        ],
        in_specs=[any_] * 9 + [vmem] * 4,
        out_specs=[any_] * 3 + [vmem] * 3,
        scratch_shapes=list(scratch.values()),
        compiler_params=pltpu.CompilerParams(
            collective_id=collective_id, has_side_effects=True, vmem_limit_bytes=62 * 2**20
        ),
        name="reduce_last",
    )(proj, part, attn_in, query, own, other, first, residual, middle, vectors, sums, inner_bias, ada_weight)


def reduce_attend_kernel(plan, counts, band_slots, names, *refs):
    me = compass()
    at = sum(counts) + sum(1 for todo in plan if todo == BACK)
    source, parts = reduce_refs(plan, counts, refs)
    rows_ref, count_ref, q_ref, own_ref, far_ref, grad_ref, top_ref = refs[at : at + 7]
    at += 7
    out, given = reduce_outs(plan, refs[at:])
    at += len(plan)
    home_ref, dq_ref, down_ref, dfar_ref = refs[at : at + 4]
    sc = SimpleNamespace(**dict(zip(names, refs[at + 4 :])))
    qh, kh, vh, gh, stage, stage_sem = sc.qh, sc.kh, sc.vh, sc.gh, sc.stage, sc.stage_sem
    rows, width = q_ref.shape
    heads = qh.shape[0]
    group_barrier(me)
    steps = reduce_steps(me, plan, source, out, parts, given, sc)
    depart, settle = home_steps(me, rows_ref, home_ref, sc)
    steps[0]()
    depart()
    keys, plain, ones = key_tail(count_ref[0], band_slots), flat_tail(0.0), flat_tail(1.0)
    loads = [(q_ref, 0, qh, 0, ones), (grad_ref, 0, gh, 0, plain)]
    for row0, ref in ((0, own_ref), (rows, far_ref)):
        loads += [(ref, 0, kh, row0, keys), (ref, width, vh, row0, plain)]

    def load(i):
        ref, column = loads[i][:2]
        return pltpu.make_async_copy(ref.at[:, pl.ds(column, width)], stage.at[i % 2], stage_sem.at[i % 2])

    load(0).start()
    for step in steps[1:4]:
        step()
    for i, (ref, column, heads_ref, row0, tail) in enumerate(loads):
        if i + 1 < len(loads):
            load(i + 1).start()
        load(i).wait()
        pack_heads(stage.at[i % 2], 0, heads_ref, row0, rows, tail)
    rest = steps[4:]
    inside = heads // 2

    @pl.loop(0, heads)
    def _(h):
        attend_head(h, qh, kh, vh, gh, top_ref)
        for i, step in enumerate(rest[:inside]):
            pl.when(h == 2 * i)(step)

    stores = [(qh, 0, dq_ref, 0)]
    for row0, ref in ((0, down_ref), (rows, dfar_ref)):
        stores += [(kh, row0, ref, 0), (vh, row0, ref, width)]

    def store(i):
        ref, column = stores[i][2:]
        target = ref.at[:, pl.ds(column, width)]
        if ref is not dfar_ref:
            return pltpu.make_async_copy(stage.at[i % 2], target, stage_sem.at[i % 2])
        return pltpu.make_async_remote_copy(
            src_ref=stage.at[i % 2], dst_ref=target, send_sem=sc.far_send.at[i % 2],
            recv_sem=sc.far_recv.at[i % 2], device_id=device(me.sib, me.band), device_id_type=MESH,
        )

    for i, (heads_ref, row0, ref, column) in enumerate(stores):
        if i >= 2:
            store(i - 2).wait()
        unpack_heads(heads_ref, row0, rows, stage.at[i % 2], 0)
        store(i).start()
    for i in (len(stores) - 2, len(stores) - 1):
        store(i).wait()
    for step in rest[inside:]:
        step()
    settle()


def reduce_attend(plan, grads, parts, rows_out, count, query, own, far, grad, top, band_slots, collective_id):
    half, width = grads[0][0].shape[-2:]
    counts = tuple(len(phase) for phase in grads)
    rows = query.shape[0]
    heads = width // HEAD_DIM
    bf = jnp.bfloat16
    scratch = reduce_scratch(plan, half, width)
    scratch.update(
        qh=pltpu.VMEM((heads, rows, LANES), bf),
        kh=pltpu.VMEM((heads, 2 * rows, LANES), bf),
        vh=pltpu.VMEM((heads, 2 * rows, LANES), bf),
        gh=pltpu.VMEM((heads, rows, LANES), bf),
        stage=pltpu.VMEM((2, rows, width), bf),
        stage_sem=pltpu.SemaphoreType.DMA((2,)),
        far_send=pltpu.SemaphoreType.DMA((2,)),
        far_recv=pltpu.SemaphoreType.DMA((2,)),
        **home_scratch(),
    )
    any_, vmem = pl.BlockSpec(memory_space=pl.ANY), pl.BlockSpec(memory_space=pltpu.VMEM)
    smem = pl.BlockSpec(memory_space=pltpu.SMEM)
    units = [unit for phase in grads for unit in phase]
    return pl.pallas_call(
        partial(reduce_attend_kernel, plan, counts, band_slots, tuple(scratch)),
        out_shape=reduce_shapes(plan, half, width)
        + [
            jax.ShapeDtypeStruct(rows_out.shape, bf),
            jax.ShapeDtypeStruct((rows, width), bf),
            jax.ShapeDtypeStruct((rows, 2 * width), bf),
            jax.ShapeDtypeStruct((rows, 2 * width), bf),
        ],
        in_specs=[any_] * (len(units) + len(parts) + 1) + [smem] + [any_] * 4 + [vmem],
        out_specs=[any_] * (len(plan) + 4),
        scratch_shapes=list(scratch.values()),
        compiler_params=pltpu.CompilerParams(
            collective_id=collective_id, has_side_effects=True, vmem_limit_bytes=60 * 2**20
        ),
        name="reduce_attend",
    )(*units, *parts, rows_out, count, query, own, far, grad, top)


MOD_BLOCKS = 6
BLOCK = 128


def forward_scratch(half, ff, width, rows, note_rows, images):
    bf, f32 = jnp.bfloat16, jnp.float32
    D = pltpu.SemaphoreType.DMA
    heads = width // HEAD_DIM
    V = pltpu.VMEM
    return dict(
        qp=V((NB, 2, half, ff), bf), bounce_i=V((2, half, ff), bf), bounce_o=V((4, 2, half, width), bf),
        bounce_t=V((rows // images, width), bf), tok=V((images, rows // images, width), bf),
        notes=V((NB, note_rows, 128), f32), vec=V((16, width), f32),
        residual=V((rows, width), f32), attn_in=V((rows, width), bf), query=V((rows, width), bf),
        own=V((rows, 2 * width), bf), far=V((rows, 2 * width), bf), mixed=V((rows, width), bf),
        attended=V((rows, width), f32), mlp_in=V((rows, width), bf), tops=V((heads, 8, rows), f32),
        qh=V((heads, rows, LANES), bf), kh=V((heads, 2 * rows, LANES), bf), vh=V((heads, 2 * rows, LANES), bf),
        z_send=D((3, 2)), z_recv=D((3, NB)), f_send=D((3, NB)), a_send=D((9, 2)), a_recv=D((9, 2)), b_send=D((9, 2, 2)), b_recv=D((9, 2, 2)),
        c_send=D((9,)), c_recv=D((9,)), t_send=D((2, 2)), t_recv=D((2, 2)), m_send=D((2, 2)), m_recv=D((NB,)),
        local=D((4,)), kv_send=D((1,)), kv_recv=D((1,)), done=D((12,)),
    )


def gather_steps(me, width, ins, outs, tok_in, tok_out, cot_in, cot_out, note_in, note_out, sc):
    dp, band, core, px, py, kind = me.dp, me.band, me.core, me.px, me.py, me.kind
    base = dp - core
    dev = lambda d, b: device(d, b)
    here = lambda d: dev(d, band)
    flip = lambda v: 1 - v
    low = band < 2
    bands = (band + 1 - 2 * lax.rem(band, 2), jnp.where(low, 2, 1), jnp.where(low, 3, 0))
    order = [(ph, b) for ph in range(3) for b in bands]
    inside = jnp.logical_or(band == 1, band == 2)
    sends = []

    def remote(src, dst, ss, rs, to):
        return pltpu.make_async_remote_copy(
            src_ref=src, dst_ref=dst, send_sem=ss, recv_sem=rs, device_id=to, device_id_type=MESH
        )

    def go(make):
        for copy in make():
            copy.start()
        sends.append(make)

    size = ins[0].shape[1]
    cut = size // 32 * 16
    whole, spans = pl.ds(0, size), (pl.ds(0, cut), pl.ds(cut, size - cut))

    def cols(t, n=1):
        return pl.ds(pl.multiple_of(t * width, 128), n * width)

    def unit(ph, b, t, h, span=whole):
        return outs[ph].at[b, t, h, span] if ph == 2 else outs[ph].at[b, h, span, cols(t)]

    def pair(ph, b, h, y, span):
        return outs[ph].at[b, pl.ds(2 * y, 2), h, span] if ph == 2 else outs[ph].at[b, h, span, cols(2 * y, 2)]

    def row(ph, b, h):
        return outs[ph].at[b, :, h] if ph == 2 else outs[ph].at[b, h]

    def own_z(ph, up):
        src = ins[ph].at[kind, core] if ph == 2 else ins[ph].at[core, :, cols(kind)]
        return remote(
            src, unit(ph, band, kind, core), sc.z_send.at[ph, up], sc.z_recv.at[ph, band],
            dev(dp, band - 1 + 2 * up),
        )

    def pass_z(s):
        ph, b = order[s]
        u = unit(ph, b, kind, core)
        return remote(
            u, u, sc.f_send.at[ph, b], sc.z_recv.at[ph, b], dev(dp, jnp.where(b < band, band + 1, band - 1))
        )

    def a_copy(s, half, mine):
        ph, b = order[s]
        near = 2 * py + flip(px) if half == 0 else 2 * flip(py) + px
        u = unit(ph, b, kind if mine else near, core, spans[half])
        return remote(u, u, sc.a_send.at[s, half], sc.a_recv.at[s, half], here(me.xdp if half == 0 else me.ydp))

    def b_copies(s, half, mine):
        ph, b = order[s]
        if half == 0:
            u = pair(ph, b, core, py if mine else flip(py), spans[half])
            return [remote(u, u, sc.b_send.at[s, half, 0], sc.b_recv.at[s, half, 0], here(me.ydp))]
        copies = []
        for j in range(2):
            u = unit(ph, b, 2 * j + (px if mine else flip(px)), core, spans[half])
            copies.append(remote(u, u, sc.b_send.at[s, half, j], sc.b_recv.at[s, half, j], here(me.xdp)))
        return copies

    def c_copy(s, mine):
        ph, b = order[s]
        u = row(ph, b, core if mine else flip(core))
        return remote(u, u, sc.c_send.at[s], sc.c_recv.at[s], here(me.sib))

    def z_start(ph):
        pl.when(band < NB - 1)(lambda: own_z(ph, 1).start())
        pl.when(band > 0)(lambda: own_z(ph, 0).start())

    def z_wait(s):
        ph, b = order[s]
        u = unit(ph, b, kind, core)
        remote(u, u, sc.f_send.at[ph, b], sc.z_recv.at[ph, b], here(dp)).wait_recv()
        pl.when(inside)(lambda: pass_z(s).start())
        for half in range(2):
            go(lambda half=half: [a_copy(s, half, True)])

    def a_wait(s):
        for half in range(2):
            a_copy(s, half, False).wait_recv()
            go(partial(b_copies, s, half, True))

    def b_wait(s):
        for half in range(2):
            for copy in b_copies(s, half, False):
                copy.wait_recv()
        go(lambda: [c_copy(s, True)])

    def c_wait(s):
        c_copy(s, False).wait_recv()

    slot = lax.rem(band, 2)

    def image_copy(which, src, dst, i):
        to = dev(base + band // 2, 2 * core + i)
        return remote(src.at[i], dst.at[slot], sc.t_send.at[which, i], sc.t_recv.at[which, slot], to)

    def at_home(i):
        return jnp.logical_and(band // 2 == core, 2 * core + i == band)

    def move(which, src, dst, bounce=None):
        for i in range(2):

            @pl.when(at_home(i))
            def _():
                if bounce is None:
                    pltpu.make_async_copy(src.at[i], dst.at[slot], sc.t_recv.at[which, slot]).start()
                else:
                    inward = pltpu.make_async_copy(src.at[i], bounce, sc.local.at[3])
                    inward.start()
                    inward.wait()
                    pltpu.make_async_copy(bounce, dst.at[slot], sc.t_recv.at[which, slot]).start()

            @pl.when(jnp.logical_not(at_home(i)))
            def _():
                image_copy(which, src, dst, i).start()

    def move_wait(which, src, dst):
        for i in range(2):

            @pl.when(jnp.logical_not(at_home(i)))
            def _():
                image_copy(which, src, dst, i).wait_send()

        for s in range(2):
            pltpu.make_async_copy(dst.at[s], dst.at[s], sc.t_recv.at[which, s]).wait()

    def note_copy(i, c):
        return remote(
            note_in.at[i], note_out.at[band], sc.m_send.at[i, c], sc.m_recv.at[band],
            dev(base + c, 2 * core + i),
        )

    def note_home(i, c):
        return jnp.logical_and(c == core, 2 * core + i == band)

    def begin():
        for i in range(2):
            for c in range(2):

                @pl.when(note_home(i, c))
                def _():
                    pltpu.make_async_copy(note_in.at[i], note_out.at[band], sc.m_recv.at[band]).start()

                @pl.when(jnp.logical_not(note_home(i, c)))
                def _():
                    note_copy(i, c).start()

        z_start(0)
        for ph, dst in enumerate((outs[0].at[band], sc.bounce_i, sc.bounce_o)):
            pltpu.make_async_copy(ins[ph], dst, sc.local.at[ph]).start()

    def arrived():
        for i in range(2):
            for c in range(2):

                @pl.when(jnp.logical_not(note_home(i, c)))
                def _():
                    note_copy(i, c).wait_send()

        for b in range(NB):
            pltpu.make_async_copy(note_in.at[0], note_out.at[b], sc.m_recv.at[b]).wait()
        move_wait(0, tok_in, tok_out)

    def place():
        for ph, dst in ((1, sc.bounce_i), (2, sc.bounce_o)):
            pltpu.make_async_copy(ins[ph], dst, sc.local.at[ph]).wait()
            pltpu.make_async_copy(dst, outs[ph].at[band], sc.local.at[ph]).start()

    def first_here():
        pltpu.make_async_copy(ins[0], outs[0].at[band], sc.local.at[0]).wait()

    def finish():
        for ph, src in ((1, sc.bounce_i), (2, sc.bounce_o)):
            pltpu.make_async_copy(src, outs[ph].at[band], sc.local.at[ph]).wait()
        move_wait(1, cot_in, cot_out)
        for ph in range(3):
            pl.when(band < NB - 1)(lambda: own_z(ph, 1).wait_send())
            pl.when(band > 0)(lambda: own_z(ph, 0).wait_send())
        for s in range(len(order)):
            pl.when(inside)(lambda: pass_z(s).wait_send())
        for make in sends:
            for copy in make():
                copy.wait_send()

    def images(which):
        if which == 0:
            move(0, tok_in, tok_out)
        else:
            move(1, cot_in, cot_out, sc.bounce_t)

    return SimpleNamespace(
        i=images, s=z_start,
        begin=begin, arrived=arrived, place=place, first_here=first_here, finish=finish,
        z=z_wait, a=a_wait, b=b_wait, c=c_wait,
    )


def forward_kernel(names, band_slots, *refs):
    me = compass()
    qp_in, inner_in, outer_in, tok_in, cot_in, note_in, table_ref = refs[:7]
    (qp_out, inner_out, outer_out, cot_out, vec_out, residual_out, attn_out, query_out, own_out, far_out,
     tops_out, mixed_out, attended_out, mlp_out) = refs[7:21]
    sc = SimpleNamespace(**dict(zip(names, refs[21:])))
    rows, width = sc.residual.shape
    heads = width // HEAD_DIM
    core = me.core
    qp, tok, notes, vec = sc.qp, sc.tok, sc.notes, sc.vec

    group_barrier(me)
    g = gather_steps(
        me, width, (qp_in, inner_in, outer_in), (qp, inner_out, outer_out), tok_in, tok, cot_in, cot_out,
        note_in, notes, sc,
    )
    saves = []

    def save(src, dst):
        copy = pltpu.make_async_copy(src, dst, sc.done.at[len(saves)])
        copy.start()
        saves.append(copy)

    def run(*words):
        for do, index in words:
            do(index)

    g.begin()
    g.place()
    run((g.z, 0), (g.z, 1), (g.i, 0), (g.a, 0), (g.a, 1), (g.z, 2), (g.s, 1), (g.b, 0), (g.b, 1), (g.a, 2), (g.c, 0), (g.c, 1), (g.z, 3), (g.z, 4), (g.b, 2))
    g.arrived()
    spread_notes(notes, vec, width)
    grid_rows = notes[0, 63:64, 0:1]
    grid_cols = notes[0, 63:64, 1:2]
    band_rows = jnp.floor(grid_rows * 0.25)
    valid_count = (band_rows * grid_cols).astype(jnp.int32)
    lane = lax.broadcasted_iota(jnp.int32, (1, width), 1)
    vec[15:16, :] = jnp.where(lane == 0, band_rows * grid_cols, 0.0)
    save(vec, vec_out)

    @pl.loop(0, rows // BLOCK)
    def _(step):
        at = pl.multiple_of(step * BLOCK, BLOCK)
        sub = pl.ds(at, BLOCK)
        per_image = band_slots // BLOCK
        within = (
            lax.rem(step, per_image) * BLOCK + lax.broadcasted_iota(jnp.int32, (BLOCK, 1), 0)
        ).astype(jnp.float32)
        down = jnp.floor((within + 0.5) / grid_cols)
        place = (2 * core + step // per_image).astype(jnp.float32)
        picks = []
        for index in (place * band_rows + down, within - down * grid_cols):
            lanes = lax.broadcasted_iota(jnp.int32, (BLOCK, 128), 1).astype(jnp.float32)
            pick = jnp.where(lanes == index, 1.0, 0.0).astype(jnp.bfloat16)
            part = [jnp.dot(pick, table_ref[i], preferred_element_type=jnp.float32) for i in range(3)]
            picks.append(part[0] + (part[1] + part[2]))
        token = tok[step // per_image, pl.ds(lax.rem(step, per_image) * BLOCK, BLOCK), :]
        residual = token.astype(jnp.float32) + jnp.concatenate(picks, 1)
        sc.residual[sub, :] = residual
        normed = normalize(residual)[0]
        sc.attn_in[sub, :] = (normed * (1.0 + vec[1:2, :]) + vec[0:1, :]).astype(jnp.bfloat16)

    save(sc.residual, residual_out)
    save(sc.attn_in, attn_out)
    g.first_here()
    run((g.c, 2))
    save(qp, qp_out)
    tile = width // 3
    full = NB * 2 * qp.shape[2]

    def product(left_ref, first, step):
        at = pl.ds(pl.multiple_of(first + step * tile, 128), tile)
        return jnp.dot(
            left_ref[...], qp[:, :, :, at].reshape(full, tile), preferred_element_type=jnp.float32
        )

    def here(step):
        return pl.ds(pl.multiple_of(step * tile, 128), tile)

    @pl.loop(0, 3)
    def _(step):
        sc.own[:, here(step)] = product(sc.attn_in, width, step).astype(jnp.bfloat16)

    run((g.a, 3), (g.z, 5), (g.s, 2))

    @pl.loop(0, 3)
    def _(step):
        value = product(sc.attn_in, 2 * width, step) + vec[7:8, here(step)]
        sc.own[:, here(step + 3)] = value.astype(jnp.bfloat16)

    swap = pltpu.make_async_remote_copy(
        src_ref=sc.own, dst_ref=sc.far, send_sem=sc.kv_send.at[0], recv_sem=sc.kv_recv.at[0],
        device_id=device(me.sib, me.band), device_id_type=MESH,
    )
    swap.start()
    run((g.a, 4), (g.b, 3))

    @pl.loop(0, 3)
    def _(step):
        value = product(sc.attn_in, 0, step) + vec[6:7, here(step)]
        sc.query[:, here(step)] = value.astype(jnp.bfloat16)

    save(sc.query, query_out)
    save(sc.own, own_out)
    run((g.a, 5), (g.b, 4), (g.c, 3), (g.z, 6))
    qh, kh, vh = sc.qh, sc.kh, sc.vh
    keys, plain = key_tail(valid_count, band_slots), flat_tail(0.0)
    pack_heads(sc.query, 0, qh, 0, rows, flat_tail(1.0))
    pack_heads(sc.own, 0, kh, 0, rows, keys)
    pack_heads(sc.own, width, vh, 0, rows, plain)
    swap.wait()
    save(sc.far, far_out)
    pack_heads(sc.far, 0, kh, rows, rows, keys)
    pack_heads(sc.far, width, vh, rows, rows, plain)
    beside = {
        0: ((g.z, 7), (g.b, 5), (g.c, 4)), 2: ((g.a, 6), (g.z, 8), (g.i, 1)), 4: ((g.a, 7), (g.b, 6), (g.c, 5)), 7: ((g.a, 8), (g.b, 7), (g.c, 6)), 10: ((g.b, 8), (g.c, 7)),
        13: ((g.c, 8),),
    }

    @pl.loop(0, heads)
    def _(h):
        attend_block(h, qh, kh, vh, sc.tops)
        for i, words in beside.items():
            pl.when(h == i)(partial(run, *words))

    unpack_heads(qh, 0, rows, sc.mixed, 0)
    save(sc.tops, tops_out)
    save(sc.mixed, mixed_out)

    @pl.loop(0, 3)
    def _(step):
        sc.attended[:, here(step)] = product(sc.mixed, 3 * width, step) + vec[8:9, here(step)]

    save(sc.attended, attended_out)

    @pl.loop(0, rows // BLOCK)
    def _(step):
        sub = pl.ds(pl.multiple_of(step * BLOCK, BLOCK), BLOCK)
        middle = sc.residual[sub, :] + vec[2:3, :] * sc.attended[sub, :]
        normed = normalize(middle)[0]
        sc.mlp_in[sub, :] = (normed * (1.0 + vec[4:5, :]) + vec[3:4, :]).astype(jnp.bfloat16)

    save(sc.mlp_in, mlp_out)
    g.finish()
    for copy in saves:
        copy.wait()


NOTE_COND, NOTE_GRID, NOTE_BIAS = 54, 63, 64


def spread_notes(notes, vec, width):
    lines = width // 128
    share = notes.shape[0]
    total = notes[0, 0:NOTE_GRID, :] + 0.0
    for b in range(1, share):
        total = total + notes[b, 0:NOTE_GRID, :]

    def flat(block, first):
        return jnp.concatenate([block[first + i : first + i + 1, :] for i in range(lines)], 1)

    for index in range(MOD_BLOCKS):
        vec[index : index + 1, :] = flat(total, index * lines)
    small = width // share
    for index in range(4):
        parts = []
        for b in range(share):
            first = NOTE_BIAS + 3 * index
            for i in range(3):
                parts.append(notes[b, first + i : first + i + 1, : min(128, small - 128 * i)])
        vec[6 + index : 7 + index, :] = jnp.concatenate(parts, 1)
    for b in range(share):
        block = notes[b, NOTE_BIAS + 12 : NOTE_BIAS + 12 + lines, :]
        vec[10 + b : 11 + b, :] = flat(block, 0)
    vec[14:15, :] = flat(notes[0, NOTE_COND : NOTE_COND + lines, :], 0)


def forward_block(qp, inner, outer, tok, cot, note, table):
    half, ff = qp.shape[0] // 2, qp.shape[1]
    images, band_slots, width = tok.shape
    rows = images * band_slots
    heads = width // HEAD_DIM
    bf, f32 = jnp.bfloat16, jnp.float32
    S = jax.ShapeDtypeStruct
    qp, inner = qp.reshape(2, half, ff), inner.reshape(2, half, ff)
    outer = outer.reshape(4, 2, half, width)
    scratch = forward_scratch(half, ff, width, rows, note.shape[1], images)
    any_ = pl.BlockSpec(memory_space=pl.ANY)
    return pl.pallas_call(
        partial(forward_kernel, tuple(scratch), band_slots),
        out_shape=[
            S((NB, 2, half, ff), bf), S((NB, 2, half, ff), bf), S((NB, 4, 2, half, width), bf), S(cot.shape, bf),
            S((16, width), f32), S((rows, width), f32), S((rows, width), bf), S((rows, width), bf),
            S((rows, 2 * width), bf), S((rows, 2 * width), bf), S((heads, 8, rows), f32), S((rows, width), bf),
            S((rows, width), f32), S((rows, width), bf),
        ],
        in_specs=[any_] * 6 + [pl.BlockSpec(memory_space=pltpu.VMEM)],
        out_specs=[any_] * 14,
        scratch_shapes=list(scratch.values()),
        compiler_params=pltpu.CompilerParams(
            collective_id=0, has_side_effects=True, vmem_limit_bytes=60 * 2**20
        ),
        name="forward_block",
    )(qp, inner, outer, tok, cot, note, table)


GELU_SCALE = 0.7978845608028654


def mlp_kernel(band_slots, mlp_ref, inner_ref, outer_ref, vec_ref, bias_ref, residual_ref, attended_ref, cot_ref,
               mixed_ref, proj_ref, out_ref, middle_ref, back_ref, proj_grad_ref, outer_grad_ref, inner_grad_ref,
               bias_grad_ref, sums_ref, out_acc, back_acc, grad_mlp):
    step = pl.program_id(0)
    rows = mlp_ref.shape[0]
    low = lambda value: value.astype(jnp.bfloat16)
    line = lambda index: vec_ref[index : index + 1, :]

    def grad_out(at):
        slot = lax.rem(at + lax.broadcasted_iota(jnp.int32, (BLOCK, 1), 0), band_slots)
        valid = jnp.where(slot.astype(jnp.float32) < vec_ref[15:16, 0:1], 1.0, 0.0)
        return cot_ref[pl.ds(at, BLOCK), :].astype(jnp.float32) * valid

    def add_line(index, values):
        sums_ref[index : index + 1, :] += jnp.sum(values, 0, keepdims=True)

    @pl.when(step == 0)
    def _():
        sums_ref[...] = jnp.zeros_like(sums_ref)

        @pl.loop(0, rows // BLOCK)
        def _(block):
            at = pl.multiple_of(block * BLOCK, BLOCK)
            grad = low(line(5) * grad_out(at))
            grad_mlp[pl.ds(at, BLOCK), :] = grad
            add_line(5, grad.astype(jnp.float32))
            out_acc[pl.ds(at, BLOCK), :] = jnp.zeros((BLOCK, out_acc.shape[1]), jnp.float32)
            back_acc[pl.ds(at, BLOCK), :] = jnp.zeros((BLOCK, out_acc.shape[1]), jnp.float32)

    inner, outer, grad = inner_ref[...], outer_ref[...], grad_mlp[...]
    pre = jnp.dot(mlp_ref[...], inner, preferred_element_type=jnp.float32) + bias_ref[...]
    grad_hidden = lanes_dot(grad, outer)
    square = pre * pre
    bend = jnp.tanh(GELU_SCALE * (pre * (1.0 + 0.044715 * square)))
    rise = 0.5 * (1.0 + bend)
    hidden = low(pre * rise)
    slope = rise + (0.5 * pre) * (1.0 - bend * bend) * (GELU_SCALE * (1.0 + 0.134145 * square))
    grad_pre = low(slope * grad_hidden)
    out_acc[...] += jnp.dot(hidden, outer, preferred_element_type=jnp.float32)
    outer_grad_ref[...] = low(rows_dot(hidden, grad))
    back_acc[...] += lanes_dot(grad_pre, inner)
    inner_grad_ref[...] = low(rows_dot(mlp_ref[...], grad_pre))
    bias_grad_ref[...] = jnp.broadcast_to(
        jnp.sum(grad_pre.astype(jnp.float32), 0, keepdims=True), bias_grad_ref.shape
    )

    @pl.when(step == pl.num_programs(0) - 1)
    def _():
        @pl.loop(0, rows // BLOCK)
        def _(block):
            at = pl.multiple_of(block * BLOCK, BLOCK)
            sub = pl.ds(at, BLOCK)
            attended = attended_ref[sub, :]
            middle = residual_ref[sub, :] + line(2) * attended
            normed, inverse = normalize(middle)
            mlp_out = out_acc[sub, :] + line(9)
            out_ref[sub, :] = low(middle + line(5) * mlp_out)
            grad_block = grad_out(at)
            add_line(0, grad_block * mlp_out)
            back = back_acc[sub, :]
            add_line(1, back)
            add_line(2, back * normed)
            grad_middle = grad_block + norm_back(back * (1.0 + line(4)), normed, inverse)
            middle_ref[sub, :] = grad_middle
            add_line(3, grad_middle * attended)
            grad_attended = low(line(2) * grad_middle)
            add_line(4, grad_attended.astype(jnp.float32))
            grad_mlp[sub, :] = grad_attended

        proj_grad_ref[...] = low(rows_dot(mixed_ref[...], grad_mlp[...]))
        back_ref[...] = low(lanes_dot(grad_mlp[...], proj_ref[...]))


def feed_forward(mlp_in, inner, outer, vectors, inner_bias, residual, attended, cotangent, mixed, first, band_slots):
    rows, width = mlp_in.shape
    hidden = inner.shape[1]
    tile = 512
    bf, f32 = jnp.bfloat16, jnp.float32
    S = jax.ShapeDtypeStruct
    keep = lambda *shape: pl.BlockSpec(shape, lambda j: (0,) * len(shape))
    return pl.pallas_call(
        partial(mlp_kernel, band_slots),
        grid=(hidden // tile,),
        out_shape=[
            S((rows, width), bf), S((rows, width), f32), S((rows, width), bf), S((width, width), bf),
            S((hidden, width), bf), S((width, hidden), bf), S((8, hidden), f32), S((8, width), f32),
        ],
        in_specs=[
            keep(rows, width), pl.BlockSpec((width, tile), lambda j: (0, j)), pl.BlockSpec((tile, width), lambda j: (j, 0)),
            keep(16, width), pl.BlockSpec((1, tile), lambda j: (0, j)), keep(rows, width), keep(rows, width),
            keep(rows, width), keep(rows, width), pl.BlockSpec((width, width), lambda j: (0, 3)),
        ],
        out_specs=[
            keep(rows, width), keep(rows, width), keep(rows, width), keep(width, width),
            pl.BlockSpec((tile, width), lambda j: (j, 0)), pl.BlockSpec((width, tile), lambda j: (0, j)),
            pl.BlockSpec((8, tile), lambda j: (0, j)), keep(8, width),
        ],
        scratch_shapes=[pltpu.VMEM((rows, width), f32), pltpu.VMEM((rows, width), f32), pltpu.VMEM((rows, width), bf)],
        compiler_params=pltpu.CompilerParams(vmem_limit_bytes=60 * 2**20),
        cost_estimate=pl.CostEstimate(
            flops=12 * rows * width * hidden, bytes_accessed=8 * width * hidden + 24 * rows * width,
            transcendentals=rows * hidden,
        ),
        name="feed_forward",
    )(mlp_in, inner, outer, vectors, inner_bias, residual, attended, cotangent, mixed, first)


def position_parts(width):
    quarter = width // 4
    frequency = 10000.0 ** (-jnp.arange(quarter, dtype=jnp.float32) / quarter)
    angles = jnp.arange(128, dtype=jnp.float32)[:, None] * frequency
    left = jnp.concatenate([jnp.sin(angles), jnp.cos(angles)], -1)
    parts = []
    for _ in range(3):
        part = lax.reduce_precision(left, 8, 7)
        parts.append(part.astype(jnp.bfloat16))
        left = left - part
    return jnp.stack(parts)


def over_groups(piece, dp_count):
    if dp_count == 8:
        return piece
    groups = [[rank + 8 * group for group in range(dp_count // 8)] for rank in range(8)]
    return lax.psum(piece.astype(jnp.float32), "dp", axis_index_groups=groups)


def every_group(piece, dp_count):
    if dp_count == 8:
        return piece[None]
    groups = [[rank + 8 * group for group in range(dp_count // 8)] for rank in range(8)]
    return lax.all_gather(piece, "dp", axis_index_groups=groups)


def own_piece(vector, count, band_place):
    return lax.dynamic_slice_in_dim(vector, band_place * count, count, 0)


def body(
    tokens,
    condition,
    patch_grid,
    ada_weight,
    ada_bias,
    qkv_weight,
    query_bias,
    value_bias,
    proj_weight,
    proj_bias,
    inner_weight,
    inner_bias,
    outer_weight,
    outer_bias,
    cotangent,
):
    dp_count = lax.axis_size("dp")
    band_count = lax.axis_size("band")
    images, band_slots, width = tokens.shape
    band = lax.axis_index("band")
    dp = lax.axis_index("dp")
    core = lax.rem(dp, 2)
    hidden = inner_weight.shape[1]
    part_rows = qkv_weight.shape[0]

    condition_f = condition.astype(jnp.float32)
    activated = jax.nn.silu(condition_f).astype(jnp.bfloat16)
    own_activated = lax.dynamic_slice_in_dim(activated, band * part_rows, part_rows, 1)
    share = jnp.dot(own_activated, ada_weight, preferred_element_type=jnp.float32)
    share = share + lax.dynamic_update_slice_in_dim(
        jnp.zeros((ada_weight.shape[1],), jnp.float32),
        ada_bias.astype(jnp.float32),
        band * ada_bias.shape[0],
        0,
    )
    mod_count = share.shape[1]
    lines = lambda vector: jnp.pad(
        vector.astype(jnp.float32), [(0, 0)] * (vector.ndim - 1) + [(0, -vector.shape[-1] % 128)]
    )
    spread = lambda vector: jnp.broadcast_to(lines(vector), (images, -(-vector.shape[0] // 128) * 128))
    note = jnp.concatenate(
        [share, condition_f, lines(patch_grid)]
        + [spread(bias) for bias in (query_bias, value_bias, proj_bias, outer_bias, inner_bias)],
        1,
    )
    note = jnp.pad(note, ((0, 0), (0, -note.shape[1] % 1024))).reshape(images, -1, 128)
    first_weight = jnp.concatenate([qkv_weight, proj_weight], 1)
    (first_full, inner_full, outer_full, cotangent_here, vectors, residual, attn_in, query_rows, key_value,
     other_key_value, tops, mixed_rows, attended, mlp_in) = forward_block(
        first_weight, inner_weight, outer_weight, tokens, cotangent, note, position_parts(width)
    )
    first_full = first_full.reshape(width, -1)
    inner_full = inner_full.reshape(width, hidden)
    outer_full = outer_full.reshape(hidden, width)
    valid_count = vectors[15, :1].astype(jnp.int32)
    rows = images * band_slots
    inner_bias_row = vectors[10:14].reshape(1, -1)
    (block_out, grad_middle, grad_mixed, grad_proj, grad_outer, grad_inner, grad_inner_bias, sums) = feed_forward(
        mlp_in, inner_full, outer_full, vectors, inner_bias_row, residual, attended,
        cotangent_here.reshape(rows, width), mixed_rows, first_full, band_slots,
    )
    blocks = (band_count, 2, part_rows // 2, width)
    grad_outer = grad_outer.reshape(band_count, 4, 2, part_rows // 2, width)
    grad_inner = grad_inner.reshape(band_count, 2, part_rows // 2, hidden)
    outer_sum, inner_part, block_home, grad_query, own_terms, other_terms = reduce_attend(
        (FRONT | BACK, FRONT), [[grad_outer], [grad_inner]], [], block_out.reshape(images, band_slots, width), valid_count, query_rows, key_value, other_key_value, grad_mixed, tops,
        band_slots, 1,
    )
    inner_sum, first_sum, tokens_home, every, bias_grads, grad_act = reduce_last(
        grad_proj.reshape(blocks), inner_part, attn_in, grad_query, own_terms, other_terms, first_full, residual,
        grad_middle, vectors, sums, grad_inner_bias, ada_weight, images, band_slots, 2,
    )
    tokens_home = tokens_home.astype(jnp.float32)
    every = every_group(every, dp_count)
    bias_grads = over_groups(bias_grads, dp_count).reshape(-1)
    every = jnp.swapaxes(every, 1, 2).reshape(dp_count * images, -1)
    every_mod = every[:, :mod_count]
    every_condition = every[:, mod_count : mod_count + width]
    every_activated = jax.nn.silu(every_condition.astype(jnp.float32)).astype(jnp.bfloat16)
    every_activated = lax.dynamic_slice_in_dim(every_activated, band * part_rows, part_rows, 1)
    grad_ada = rows_dot(every_activated, every_mod)
    grad_ada_bias = own_piece(jnp.sum(every_mod.astype(jnp.float32), 0), ada_bias.shape[0], band)
    grad_act = jnp.swapaxes(grad_act[:, :images, :part_rows], 0, 1).reshape(images, width)
    grad_condition = jax.vjp(jax.nn.silu, condition_f)[1](grad_act)[0]

    def side_by_side(units):
        return jnp.concatenate([unit.reshape(part_rows, width) for unit in units], 1).astype(jnp.float32)

    first_sum, inner_sum, outer_sum = [
        over_groups(piece, dp_count) for piece in (first_sum, inner_sum, outer_sum)
    ]
    qkv_sum = side_by_side([first_sum[t] for t in range(3)])
    proj_sum = first_sum[3].reshape(part_rows, width).astype(jnp.float32)
    inner_sum = side_by_side([inner_sum[t] for t in range(4)])
    outer_sum = outer_sum.reshape(4 * part_rows, width).astype(jnp.float32)
    bias_parts = []
    at = 0
    for piece in (query_bias, value_bias, proj_bias, inner_bias, outer_bias):
        whole = piece.shape[0] * band_count
        bias_parts.append(own_piece(bias_grads[at : at + whole], piece.shape[0], band))
        at += whole
    return (
        block_home,
        tokens_home,
        grad_condition,
        grad_ada,
        grad_ada_bias,
        qkv_sum,
        bias_parts[0],
        bias_parts[1],
        proj_sum,
        bias_parts[2],
        inner_sum,
        bias_parts[3],
        outer_sum,
        bias_parts[4],
    )


def solution(mesh):
    placed = (
        P("dp", "band", None),
        P("dp", None),
        P("dp", None),
        P("band", None),
        P("band"),
        P("band", None),
        P("band"),
        P("band"),
        P("band", None),
        P("band"),
        P("band", None),
        P("band"),
        P("band", None),
        P("band"),
        P("dp", "band", None),
    )
    return jax.shard_map(
        body,
        mesh=mesh,
        in_specs=placed,
        out_specs=(
            P("dp", "band", None),
            P("dp", "band", None),
            P("dp", None),
            P("band", None),
            P("band"),
            P("band", None),
            P("band"),
            P("band"),
            P("band", None),
            P("band"),
            P("band", None),
            P("band"),
            P("band", None),
            P("band"),
        ),
        check_vma=False,
    )
```

```python
from functools import partial
from types import SimpleNamespace

import jax
import jax.numpy as jnp
from jax import lax
from jax.experimental import pallas as pl
from jax.experimental.pallas import tpu as pltpu
from jax.sharding import PartitionSpec as P

HEAD_DIM = 72


MESH = pl.DeviceIdType.MESH
NB = 4


def device(dp, band):
    return {"dp": dp, "band": band}


def normalize(values):
    average = jnp.mean(values, -1, keepdims=True)
    centered = values - average
    variance = jnp.mean(centered * centered, -1, keepdims=True)
    inverse = lax.rsqrt(variance + 1e-06)
    return (centered * inverse, inverse)


def norm_back(grad_normed, normed, inverse):
    first = jnp.mean(grad_normed, -1, keepdims=True)
    second = jnp.mean(grad_normed * normed, -1, keepdims=True)
    return inverse * (grad_normed - first - normed * second)


LANES = 128
PACK_ROWS = 128


def pack_heads(source, first, heads_ref, row0, rows, tail):
    heads = heads_ref.shape[0]

    @pl.loop(0, rows // PACK_ROWS)
    def _(step):
        at = pl.multiple_of(step * PACK_ROWS, PACK_ROWS)
        block = source[pl.ds(at, PACK_ROWS), first : first + heads * HEAD_DIM]
        end = tail(at)
        for h in range(heads):
            part = block[:, h * HEAD_DIM : (h + 1) * HEAD_DIM]
            heads_ref[h, pl.ds(row0 + at, PACK_ROWS), :] = jnp.concatenate([part, end], 1)


def unpack_heads(heads_ref, row0, rows, target, first):
    heads = heads_ref.shape[0]

    @pl.loop(0, rows // PACK_ROWS)
    def _(step):
        at = pl.multiple_of(step * PACK_ROWS, PACK_ROWS)
        parts = [heads_ref[h, pl.ds(row0 + at, PACK_ROWS), :][:, :HEAD_DIM] for h in range(heads)]
        target[pl.ds(at, PACK_ROWS), first : first + heads * HEAD_DIM] = jnp.concatenate(parts, 1)


def flat_tail(value):
    def tail(at):
        lane = lax.broadcasted_iota(jnp.int32, (PACK_ROWS, LANES - HEAD_DIM), 1)
        return jnp.where(lane == 0, value, 0.0).astype(jnp.bfloat16)

    return tail


def key_tail(valid_count, band_slots):
    def tail(at):
        shape = (PACK_ROWS, LANES - HEAD_DIM)
        lane = lax.broadcasted_iota(jnp.int32, shape, 1)
        slot = lax.rem(at + lax.broadcasted_iota(jnp.int32, shape, 0), band_slots)
        return jnp.where(jnp.logical_and(lane == 0, slot >= valid_count), -1e30, 0.0).astype(jnp.bfloat16)

    return tail


def lanes_dot(left, right):
    return lax.dot_general(left, right, (((1,), (1,)), ((), ())), preferred_element_type=jnp.float32)


def rows_dot(left, right):
    return lax.dot_general(left, right, (((0,), (0,)), ((), ())), preferred_element_type=jnp.float32)


SCORE_SCALE = HEAD_DIM ** (-0.5)


def attend_block(h, qh, kh, vh, top_ref):
    rows = qh.shape[1]
    for block in range(2):
        at = pl.ds(block * rows // 2, rows // 2)
        scores = lanes_dot(kh[h], qh[h, at, :]) * SCORE_SCALE
        top = jnp.max(scores, 0, keepdims=True)
        weights = jnp.exp(scores - top)
        total = jnp.sum(weights, 0, keepdims=True)
        low = (weights * (1.0 / total)).astype(jnp.bfloat16)
        mixed = rows_dot(vh[h], low)
        qh[h, at, :] = jnp.transpose(mixed).astype(jnp.bfloat16)
        top_ref[h, :, at] = jnp.broadcast_to(top + jnp.log(total), (8, rows // 2))


def attend_head(h, qh, kh, vh, gh, top_ref):
    query = qh[h]
    key = kh[h]
    grad = gh[h]
    probs = jnp.exp(lanes_dot(key, query) * SCORE_SCALE - top_ref[h, 0:1, :])
    grad_probs = lanes_dot(vh[h], grad)
    inner = jnp.sum(probs * grad_probs, 0, keepdims=True)
    grad_scores = (probs * (grad_probs - inner)).astype(jnp.bfloat16)
    vh[h] = jnp.dot(
        probs.astype(jnp.bfloat16), grad, preferred_element_type=jnp.float32
    ).astype(jnp.bfloat16)
    grad_query = rows_dot(key, grad_scores)
    kh[h] = (
        SCORE_SCALE * jnp.dot(grad_scores, query, preferred_element_type=jnp.float32)
    ).astype(jnp.bfloat16)
    qh[h] = (SCORE_SCALE * jnp.transpose(grad_query)).astype(jnp.bfloat16)


def compass():
    dp = lax.axis_index("dp")
    band = lax.axis_index("band")
    core = lax.rem(dp, 2)
    px = lax.rem(dp // 2, 2)
    py = lax.rem(dp // 4, 2)
    return SimpleNamespace(
        dp=dp, band=band, core=core, px=px, py=py, kind=2 * py + px,
        sib=dp + 1 - 2 * core, xdp=dp + 2 - 4 * px, ydp=dp + 4 - 8 * py,
    )


def add_rows(total, term):
    rows = total.shape[0]

    @pl.loop(0, rows // 16)
    def _(step):
        at = pl.ds(pl.multiple_of(step * 16, 16), 16)
        total[at, :] = (
            total[at, :].astype(jnp.float32) + term[at, :].astype(jnp.float32)
        ).astype(jnp.bfloat16)


def run_all(batch):
    for do in batch:
        do()


REDUCE_ORDER = (1, 3, 2, 0)


FRONT, BACK = 1, 2


def reduce_scratch(plan, half, width):
    bf = jnp.bfloat16
    n = NB * sum(1 for todo in plan if todo & FRONT)
    m = len(plan)
    D = pltpu.SemaphoreType.DMA
    scratch = dict(
        recv_z=pltpu.VMEM((m, NB, half, width), bf), z_send=D((m, NB)), z_recv=D((m, NB)),
        d_send=D((m, 6)), d_recv=D((m, 6)), d_own=D((m,)), part_sem=D((m,)),
    )
    if n:
        scratch.update(
            acc=pltpu.VMEM((n, 4, half, width), bf), recv_a=pltpu.VMEM((n, 4, half, width), bf),
            recv_b=pltpu.VMEM((n, 2, half, width), bf), recv_c=pltpu.VMEM((n, half, width), bf),
            a_send=D((n,)), a_recv=D((n,)), a_own=D((n,)),
            b_send=D((n, 2, 2)), b_recv=D((n, 2, 2)), c_send=D((n, 2)), c_recv=D((n, 2)),
        )
    return scratch


def reduce_steps(me, plan, source, out, parts_in, parts_out, sc, beside=(), ahead=3, by_kind=False):
    dp, band, core, px, py, kind = me.dp, me.band, me.core, me.px, me.py, me.kind
    here = lambda d: device(d, band)
    fronts = [phase for phase, todo in enumerate(plan) if todo & FRONT]
    backs = [phase for phase, todo in enumerate(plan) if todo & BACK]
    chunks = [(phase, k) for phase in fronts for k in REDUCE_ORDER]
    n = len(chunks)
    flip = lambda v: 1 - v
    sends = []
    rows = sc.recv_z.shape[2]
    cut = rows // 32 * 16
    spans = (pl.ds(0, cut), pl.ds(cut, rows - cut))

    def remote(src, dst, ss, rs, to):
        return pltpu.make_async_remote_copy(
            src_ref=src, dst_ref=dst, send_sem=ss, recv_sem=rs, device_id=to, device_id_type=MESH
        )

    def go(make):
        make().start()
        sends.append(make)

    def target(k):
        return device(dp, lax.rem(band + k, NB))

    def start_a(s, kinds=range(4)):
        phase, k = chunks[s]
        b = lax.rem(band + k, NB)
        for t in kinds:
            remote(
                source(phase, b, t, flip(core)), sc.recv_a.at[s, t], sc.a_send.at[s], sc.a_recv.at[s],
                here(me.sib),
            ).start()
            pltpu.make_async_copy(source(phase, b, t, core), sc.acc.at[s, t], sc.a_own.at[s]).start()

    def first(half, j, send):
        if half == 0:
            return 2 * j + (flip(px) if send else px)
        return 2 * (flip(py) if send else py) + j

    def second(half, send):
        if half == 0:
            return 2 * (flip(py) if send else py) + px
        return 2 * py + (flip(px) if send else px)

    def near(half):
        return here(me.xdp if half == 0 else me.ydp)

    def send_b(s, half, j):
        return remote(
            sc.acc.at[s, first(half, j, True), spans[half]], sc.recv_b.at[s, j, spans[half]],
            sc.b_send.at[s, half, j], sc.b_recv.at[s, half, j], near(half),
        )

    def send_c(s, half):
        return remote(
            sc.acc.at[s, second(half, True), spans[half]], sc.recv_c.at[s, spans[half]],
            sc.c_send.at[s, half], sc.c_recv.at[s, half], near(1 - half),
        )

    def send_z(phase, k, src):
        return remote(src, sc.recv_z.at[phase, k], sc.z_send.at[phase, k], sc.z_recv.at[phase, k], target(k))

    def unit_z(s):
        phase, k = chunks[s]
        return send_z(phase, k, sc.acc.at[s, kind])

    def part_load(phase):
        return pltpu.make_async_copy(parts_in[phase], sc.recv_z.at[phase, 0], sc.part_sem.at[phase])

    def part_store(phase):
        return pltpu.make_async_copy(sc.recv_z.at[phase, 0], parts_out[phase], sc.part_sem.at[phase])

    def d_copy(phase, half, slot, mine):
        ss, rs = sc.d_send.at[phase, 3 * half + slot], sc.d_recv.at[phase, 3 * half + slot]
        span = spans[half]
        if slot == 0:
            src = sc.recv_z.at[phase, 0, span]
            return remote(src, out[phase].at[kind, core, span], ss, rs, near(half))
        j = slot - 1
        t = 2 * (py if mine else flip(py)) + j if half == 0 else 2 * j + (px if mine else flip(px))
        unit = out[phase].at[t, core, span]
        return remote(unit, unit, ss, rs, near(1 - half))

    def d_cross(phase, mine):
        row = out[phase].at[:, core if mine else flip(core)]
        return remote(row, row, sc.z_send.at[phase, 0], sc.z_recv.at[phase, 0], here(me.sib))

    def a_to_b(s):
        acc, got = sc.acc, sc.recv_a
        pltpu.make_async_copy(got.at[s], acc.at[s], sc.a_own.at[s]).wait()
        whole = remote(got.at[s], got.at[s], sc.a_send.at[s], sc.a_recv.at[s], here(me.sib))
        whole.wait_recv()
        for j in range(2):
            for half in range(2):
                t = first(half, j, True)
                add_rows(acc.at[s, t, spans[half]], got.at[s, t, spans[half]])
                go(partial(send_b, s, half, j))
        for j in range(2):
            for half in range(2):
                t = first(half, j, False)
                add_rows(acc.at[s, t, spans[half]], got.at[s, t, spans[half]])
        whole.wait_send()

    def b_to_c(s):
        acc, got = sc.acc, sc.recv_b
        for half in range(2):
            for j in range(2):
                send_b(s, half, j).wait_recv()
            away = flip(py) if half == 0 else flip(px)
            t = second(half, True)
            add_rows(acc.at[s, t, spans[half]], got.at[s, away, spans[half]])
            go(partial(send_c, s, half))
        for half in range(2):
            stay = py if half == 0 else px
            add_rows(acc.at[s, kind, spans[half]], got.at[s, stay, spans[half]])

    def c_to_z(s):
        phase, k = chunks[s]
        for half in range(2):
            send_c(s, half).wait_recv()
            add_rows(sc.acc.at[s, kind, spans[half]], sc.recv_c.at[s, spans[half]])
        if k != 0:
            go(partial(unit_z, s))

    def z_sum(phase):
        got = sc.recv_z
        for k in range(1, NB):
            remote(
                got.at[phase, k], got.at[phase, k], sc.z_send.at[phase, k], sc.z_recv.at[phase, k], here(dp)
            ).wait_recv()
        s = NB * fronts.index(phase) + NB - 1

        @pl.loop(0, rows // 16)
        def _(step):
            at = pl.ds(pl.multiple_of(step * 16, 16), 16)
            total = sc.acc[s, kind, at, :].astype(jnp.float32)
            for k in range(1, NB):
                total = total + got[phase, k, at, :].astype(jnp.float32)
            got[phase, 0, at, :] = total.astype(jnp.bfloat16)

        if not plan[phase] & BACK:
            part_store(phase).start()

    def d_first(phase):
        if not plan[phase] & FRONT:
            part_load(phase).wait()
        own_copy = pltpu.make_async_copy(sc.recv_z.at[phase, 0], out[phase].at[kind, core], sc.d_own.at[phase])
        own_copy.start()
        for half in range(2):
            go(partial(d_copy, phase, half, 0, True))
        own_copy.wait()

    def d_second(phase):
        for half in range(2):
            d_copy(phase, half, 0, False).wait_recv()
            for slot in (1, 2):
                go(partial(d_copy, phase, half, slot, True))

    def d_third(phase):
        for half in range(2):
            for slot in (1, 2):
                d_copy(phase, half, slot, False).wait_recv()
        go(partial(d_cross, phase, True))

    def d_last(phase):
        d_cross(phase, False).wait_recv()

    def finish():
        for phase in fronts:
            if not plan[phase] & BACK:
                part_store(phase).wait()
        for make in sends:
            make().wait_send()

    table = {-1: [] if by_kind else [partial(start_a, s) for s in range(n)]}

    def put(at, do):
        table.setdefault(at, []).append(do)

    for phase in backs:
        if not plan[phase] & FRONT:
            put(-1, lambda phase=phase: part_load(phase).start())
    for at, do in enumerate(beside):
        put(at, do)
    for s in range(n):
        put(s + ahead, partial(b_to_c, s))
        put(s + ahead + 1, partial(c_to_z, s))
        put(s, partial(a_to_b, s))
    for phase, todo in enumerate(plan):
        end = 0
        if todo & FRONT:
            end = NB * fronts.index(phase) + NB + ahead + 1
            put(end, partial(z_sum, phase))
        if todo & BACK:
            for lag, do in ((0, d_first), (1, d_second), (2, d_third), (4, d_last)):
                put(end + lag - (0 if todo & FRONT else 1), partial(do, phase))
    steps = [partial(run_all, table[at]) for at in sorted(table)]
    steps.append(finish)
    if by_kind:
        return SimpleNamespace(
            start=lambda kind: [start_a(s, (kind,)) for s in range(n)], a=a_to_b, b=b_to_c, c=c_to_z, sum=z_sum,
            take=lambda phase: part_load(phase).start(), d1=d_first, d2=d_second, d3=d_third, d4=d_last, finish=finish,
        )
    return steps


def home_scratch():
    D = pltpu.SemaphoreType.DMA
    return dict(home_send=D((2,)), home_recv=D((2,)))


def home_steps(me, rows_ref, home_ref, sc):
    band, core = me.band, me.core
    slot = lax.rem(band, 2)

    def stays(s):
        return jnp.logical_and(band // 2 == core, 2 * core + s == band)

    def copy(s):
        to = device(me.dp - core + band // 2, 2 * core + s)
        return pltpu.make_async_remote_copy(
            src_ref=rows_ref.at[s], dst_ref=home_ref.at[slot], send_sem=sc.home_send.at[s],
            recv_sem=sc.home_recv.at[slot], device_id=to, device_id_type=MESH,
        )

    def begin():
        for s in range(2):
            pl.when(stays(s))(
                lambda: pltpu.make_async_copy(
                    rows_ref.at[s], home_ref.at[slot], sc.home_recv.at[slot]
                ).start()
            )
            pl.when(jnp.logical_not(stays(s)))(lambda: copy(s).start())

    def finish():
        for s in range(2):
            pl.when(jnp.logical_not(stays(s)))(lambda: copy(s).wait_send())
        for i in range(2):
            pltpu.make_async_copy(rows_ref.at[i], home_ref.at[i], sc.home_recv.at[i]).wait()

    return begin, finish


def group_barrier(me):
    barrier = pltpu.get_barrier_semaphore()
    peers = [(me.xdp, me.band), (me.ydp, me.band), (me.sib, me.band)]
    for k in range(1, NB):
        other = lax.rem(me.band + k, NB)
        peers += [(me.dp, other), (me.sib, other)]
    for dp, band in peers:
        pl.semaphore_signal(
            barrier, inc=1, device_id=device(dp, band), device_id_type=MESH
        )
    pl.semaphore_wait(barrier, len(peers))


def reduce_refs(plan, counts, refs):
    take = iter(refs)
    grads = [[next(take) for _ in range(count)] for count in counts]

    def source(phase, b, t, h):
        if len(grads[phase]) > 1:
            return grads[phase][t].at[b, h]
        whole = grads[phase][0]
        if len(whole.shape) == 5:
            return whole.at[b, t, h]
        span = whole.shape[3] // 4
        return whole.at[b, h, :, pl.ds(pl.multiple_of(t * span, 128), span)]

    return source, [next(take) if todo == BACK else None for todo in plan]


def reduce_outs(plan, refs):
    take = iter(refs)
    out = [next(take) if todo & BACK else None for todo in plan]
    return out, [next(take) if todo == FRONT else None for todo in plan]


def reduce_shapes(plan, half, width):
    bf = jnp.bfloat16
    shapes = [jax.ShapeDtypeStruct((4, 2, half, width), bf) for todo in plan if todo & BACK]
    return shapes + [jax.ShapeDtypeStruct((half, width), bf) for todo in plan if todo == FRONT]


def small_scratch(mod_rows, bias_rows, cond_rows, cond_cols):
    D = pltpu.SemaphoreType.DMA
    f32 = jnp.float32
    return dict(
        s_core=pltpu.VMEM((mod_rows + bias_rows, 128), f32),
        s_every=pltpu.VMEM((NB, 4, mod_rows, 128), jnp.bfloat16),
        s_bias=pltpu.VMEM((3, bias_rows, 128), f32),
        s_got=pltpu.VMEM((2 + NB, bias_rows, 128), f32),
        s_flat=pltpu.VMEM((8, mod_rows, 128), f32),
        s_cond=pltpu.VMEM((NB, cond_rows, cond_cols), f32),
        s_send=D((8,)), s_recv=D((8,)), sz_send=D((2, NB)), sz_recv=D((2, NB)),
        sc_send=D((NB,)), sc_recv=D((NB,)),
    )


def small_steps(me, mods, images, small_ref, ada_ref, every_ref, bias_ref, cond_ref, sc):
    dp, band, core, px, py, kind = me.dp, me.band, me.core, me.px, me.py, me.kind
    here = lambda d: device(d, band)
    every, bias, got, cond = sc.s_every, sc.s_bias, sc.s_got, sc.s_cond
    mod_rows = every.shape[2]
    flip = lambda v: 1 - v

    def remote(src, dst, ss, rs, to):
        return pltpu.make_async_remote_copy(
            src_ref=src, dst_ref=dst, send_sem=ss, recv_sem=rs, device_id=to, device_id_type=MESH
        )

    def plain(index, src, dst, to):
        return remote(src, dst, sc.s_send.at[index], sc.s_recv.at[index], to)

    def core_copy():
        return plain(0, small_ref, sc.s_core, here(me.sib))

    def x_copies(mine):
        unit = every.at[band, kind if mine else 2 * py + flip(px)]
        return [
            plain(1, unit, unit, here(me.xdp)),
            plain(2, bias.at[0], got.at[0], here(me.xdp)),
        ]

    def y_copies(mine):
        pair = every.at[band, pl.ds(2 * (py if mine else flip(py)), 2)]
        return [
            plain(3, pair, pair, here(me.ydp)),
            plain(4, bias.at[1], got.at[1], here(me.ydp)),
        ]

    def z_copies(k, mine):
        to = device(dp, lax.rem(band + k, NB))
        block = every.at[band if mine else lax.rem(band + NB - k, NB)]
        return [
            remote(block, block, sc.sz_send.at[0, k], sc.sz_recv.at[0, k], to),
            remote(bias.at[2], got.at[2 + k], sc.sz_send.at[1, k], sc.sz_recv.at[1, k], to),
        ]

    def cond_copy(k, mine):
        to = device(dp, lax.rem(band + k, NB))
        block = cond.at[band if mine else lax.rem(band + NB - k, NB)]
        return remote(block, block, sc.sc_send.at[k], sc.sc_recv.at[k], to)

    def begin():
        core_copy().start()

    def cores():
        core_copy().wait()
        total = small_ref[...] + sc.s_core[...]
        every[band, kind] = total[:mod_rows].astype(jnp.bfloat16)
        bias[0] = total[mod_rows:]
        for copy in x_copies(True):
            copy.start()

    def over_x():
        for copy in x_copies(True):
            copy.wait_send()
        for copy in x_copies(False):
            copy.wait_recv()
        bias[1] = bias[0] + got[0]
        for copy in y_copies(True):
            copy.start()

    def over_y():
        for copy in y_copies(True):
            copy.wait_send()
        for copy in y_copies(False):
            copy.wait_recv()
        bias[2] = bias[1] + got[1]
        for k in range(1, NB):
            for copy in z_copies(k, True):
                copy.start()

    def over_z():
        for k in range(1, NB):
            for copy in z_copies(k, True):
                copy.wait_send()
            for copy in z_copies(k, False):
                copy.wait_recv()
        bias_ref[...] = bias[2] + got[3] + got[4] + got[5]
        every_ref[...] = every[...]
        flat = sc.s_flat
        for i in range(images):
            flat[i] = every[images * core + i, kind].astype(jnp.float32)
        parts = mods // 128
        lead = flat.shape[0]
        total = jnp.zeros((lead, ada_ref.shape[0]), jnp.float32)
        for r in range(parts):
            left = jnp.concatenate(
                [flat[i, r : r + 1, :] for i in range(images)]
                + [jnp.zeros((lead - images, 128), jnp.float32)]
            ).astype(jnp.bfloat16)
            total = total + lanes_dot(left, ada_ref[:, r * 128 : (r + 1) * 128])
        pad = cond.shape[2] - total.shape[1]
        cond[band] = jnp.concatenate([total, jnp.zeros((lead, pad), jnp.float32)], 1)
        for k in range(1, NB):
            cond_copy(k, True).start()

    def conditions():
        for k in range(1, NB):
            cond_copy(k, True).wait_send()
            cond_copy(k, False).wait_recv()
        cond_ref[...] = cond[...]

    return [begin, cores, over_x, over_y, over_z, conditions]


def put_lines(ref, first, values):
    for i in range(values.shape[1] // 128):
        ref[first + i : first + i + 1, :] = values[:, i * 128 : (i + 1) * 128]


def reduce_last_kernel(plan, images, band_slots, names, *refs):
    me = compass()
    (proj_ref, part_ref, attn_hbm, query_hbm, own_hbm, other_hbm, first_hbm, residual_hbm, middle_hbm, vec_ref, sums_ref,
     inner_bias_ref, ada_ref) = refs[:13]
    inner_out, first_out, home_ref, every_ref, bias_ref, cond_ref = refs[13:19]
    sc = SimpleNamespace(**dict(zip(names, refs[19:])))
    rows, width = sc.attn.shape
    lines = width // 128
    small = sc.small
    mod_rows = sc.s_every.shape[2]

    def source(phase, b, t, h):
        return proj_ref.at[b, h] if t == 3 else sc.grads.at[t, b, h]

    loads = [
        (attn_hbm, sc.attn), (query_hbm, sc.gqkv.at[:, pl.ds(0, width)]), (own_hbm, sc.gqkv.at[:, pl.ds(width, 2 * width)]),
        (other_hbm, sc.other), (first_hbm.at[:, pl.ds(0, 3 * width)], sc.first), (residual_hbm, sc.residual),
        (middle_hbm, sc.middle),
    ]

    def load(i):
        return pltpu.make_async_copy(*loads[i], sc.load_sem.at[i])

    for i in range(len(loads)):
        load(i).start()
    group_barrier(me)
    mods = MOD_BLOCKS * width
    exchange = small_steps(me, mods, images, small, ada_ref, every_ref, bias_ref, cond_ref, sc)
    depart, settle = home_steps(me, sc.tokens, home_ref, sc)
    r = reduce_steps(me, plan, source, (inner_out, first_out), (part_ref, None), (None, None), sc, (), 2, True)

    def run(*todo):
        for do, index in todo:
            do(index)

    run((r.start, 3), (r.take, 0), (r.d1, 0))
    for i in range(4):
        load(i).wait()

    sc.sums[...] = jnp.zeros_like(sc.sums)

    def add_line(index, values):
        sc.sums[index : index + 1, :] += jnp.sum(values, 0, keepdims=True)

    @pl.loop(0, rows // BLOCK)
    def _(block):
        sub = pl.ds(pl.multiple_of(block * BLOCK, BLOCK), BLOCK)
        total = sc.gqkv[sub, width:].astype(jnp.float32) + sc.other[sub, :].astype(jnp.float32)
        total = total.astype(jnp.bfloat16)
        sc.gqkv[sub, width:] = total
        add_line(1, total[:, width:].astype(jnp.float32))
        add_line(0, sc.gqkv[sub, :width].astype(jnp.float32))

    tile = width // 3
    load(4).wait()
    between = [(), ((r.d2, 0),), ()]
    for j in range(3):
        sc.back[:, j * tile : (j + 1) * tile] = lanes_dot(sc.gqkv[...], sc.first[j * tile : (j + 1) * tile, :])
        run(*between[j])
    load(5).wait()
    load(6).wait()

    @pl.loop(0, rows // BLOCK)
    def _(block):
        at = pl.multiple_of(block * BLOCK, BLOCK)
        sub = pl.ds(at, BLOCK)
        normed, inverse = normalize(sc.residual[sub, :])
        back = sc.back[sub, :]
        add_line(2, back)
        add_line(3, back * normed)
        grad = sc.middle[sub, :] + norm_back(back * (1.0 + vec_ref[1:2, :]), normed, inverse)
        per_image = band_slots // BLOCK
        to = pl.ds(pl.multiple_of(lax.rem(block, per_image) * BLOCK, BLOCK), BLOCK)
        sc.tokens[block // per_image, to, :] = grad.astype(jnp.bfloat16)

    small[...] = jnp.zeros_like(small)
    kept = [sc.sums[2:3, :], sc.sums[3:4, :]] + [sums_ref[i : i + 1, :] for i in (3, 1, 2, 0)]
    for i, values in enumerate(kept + [0.5 * vec_ref[14:15, :]]):
        put_lines(small, i * lines, values)
    at = mod_rows
    for values in (sc.sums[0:1, :], sc.sums[1:2, :], sums_ref[4:5, :], inner_bias_ref[0:1, :], sums_ref[5:6, :]):
        put_lines(small, at, values)
        at += values.shape[1] // 128
    say = lambda i: exchange[i]()
    depart()
    run((r.d3, 0))
    for t in range(3):

        @pl.loop(0, 3)
        def _(j):
            at = pl.multiple_of(t * width + j * tile, 128)
            value = rows_dot(sc.attn[...], sc.gqkv[:, pl.ds(at, tile)]).astype(jnp.bfloat16)
            to = pl.ds(pl.multiple_of(j * tile, 128), tile)
            sc.grads[t, :, :, :, to] = value.reshape(sc.grads.shape[1:4] + (tile,))

        run((r.start, t), (say, t))

    run((r.a, 0), (r.a, 1), (say, 3), (r.b, 0), (r.a, 2), (r.b, 1), (r.c, 0), (r.a, 3), (r.b, 2), (r.c, 1), (r.b, 3), (r.c, 2))
    run((r.c, 3), (say, 4), (r.sum, 1), (r.d1, 1), (r.d2, 1), (r.d3, 1), (say, 5), (r.d4, 0), (r.d4, 1))
    settle()
    r.finish()


def reduce_last(proj, part, attn_in, query, own, other, first, residual, middle, vectors, sums, inner_bias, ada_weight,
                images, band_slots, collective_id):
    plan = (BACK, FRONT | BACK)
    half, width = proj.shape[-2:]
    rows = attn_in.shape[0]
    bf, f32 = jnp.bfloat16, jnp.float32
    V = pltpu.VMEM
    mod_rows = -(-(MOD_BLOCKS + 1) * width // 2048) * 16
    bias_rows = (4 * width + inner_bias.shape[1]) // 128
    cond_cols = -(-ada_weight.shape[0] // 128) * 128
    scratch = dict(
        **reduce_scratch(plan, half, width), **small_scratch(mod_rows, bias_rows, 8, cond_cols), **home_scratch(),
        attn=V((rows, width), bf), gqkv=V((rows, 3 * width), bf), other=V((rows, 2 * width), bf),
        first=V((width, 3 * width), bf), residual=V((rows, width), f32), middle=V((rows, width), f32),
        grads=V((3, NB, 2, half, width), bf), back=V((rows, width), f32), sums=V((8, width), f32),
        tokens=V((images, band_slots, width), bf), small=V((mod_rows + bias_rows, 128), f32),
        load_sem=pltpu.SemaphoreType.DMA((7,)),
    )
    any_, vmem = pl.BlockSpec(memory_space=pl.ANY), pl.BlockSpec(memory_space=pltpu.VMEM)
    return pl.pallas_call(
        partial(reduce_last_kernel, plan, images, band_slots, tuple(scratch)),
        out_shape=reduce_shapes(plan, half, width)
        + [
            jax.ShapeDtypeStruct((images, band_slots, width), bf),
            jax.ShapeDtypeStruct((NB, 4, mod_rows, 128), bf),
            jax.ShapeDtypeStruct((bias_rows, 128), f32),
            jax.ShapeDtypeStruct((NB, 8, cond_cols), f32),
        ],
        in_specs=[any_] * 9 + [vmem] * 4,
        out_specs=[any_] * 3 + [vmem] * 3,
        scratch_shapes=list(scratch.values()),
        compiler_params=pltpu.CompilerParams(
            collective_id=collective_id, has_side_effects=True, vmem_limit_bytes=62 * 2**20
        ),
        name="reduce_last",
    )(proj, part, attn_in, query, own, other, first, residual, middle, vectors, sums, inner_bias, ada_weight)


def reduce_attend_kernel(plan, counts, band_slots, names, *refs):
    me = compass()
    at = sum(counts) + sum(1 for todo in plan if todo == BACK)
    source, parts = reduce_refs(plan, counts, refs)
    rows_ref, count_ref, q_ref, own_ref, far_ref, grad_ref, top_ref = refs[at : at + 7]
    at += 7
    out, given = reduce_outs(plan, refs[at:])
    at += len(plan)
    home_ref, dq_ref, down_ref, dfar_ref = refs[at : at + 4]
    sc = SimpleNamespace(**dict(zip(names, refs[at + 4 :])))
    qh, kh, vh, gh, stage, stage_sem = sc.qh, sc.kh, sc.vh, sc.gh, sc.stage, sc.stage_sem
    rows, width = q_ref.shape
    heads = qh.shape[0]
    group_barrier(me)
    steps = reduce_steps(me, plan, source, out, parts, given, sc)
    depart, settle = home_steps(me, rows_ref, home_ref, sc)
    steps[0]()
    depart()
    keys, plain, ones = key_tail(count_ref[0], band_slots), flat_tail(0.0), flat_tail(1.0)
    loads = [(q_ref, 0, qh, 0, ones), (grad_ref, 0, gh, 0, plain)]
    for row0, ref in ((0, own_ref), (rows, far_ref)):
        loads += [(ref, 0, kh, row0, keys), (ref, width, vh, row0, plain)]

    def load(i):
        ref, column = loads[i][:2]
        return pltpu.make_async_copy(ref.at[:, pl.ds(column, width)], stage.at[i % 2], stage_sem.at[i % 2])

    load(0).start()
    for step in steps[1:4]:
        step()
    for i, (ref, column, heads_ref, row0, tail) in enumerate(loads):
        if i + 1 < len(loads):
            load(i + 1).start()
        load(i).wait()
        pack_heads(stage.at[i % 2], 0, heads_ref, row0, rows, tail)
    rest = steps[4:]
    inside = heads // 2

    @pl.loop(0, heads)
    def _(h):
        attend_head(h, qh, kh, vh, gh, top_ref)
        for i, step in enumerate(rest[:inside]):
            pl.when(h == 2 * i)(step)

    stores = [(qh, 0, dq_ref, 0)]
    for row0, ref in ((0, down_ref), (rows, dfar_ref)):
        stores += [(kh, row0, ref, 0), (vh, row0, ref, width)]

    def store(i):
        ref, column = stores[i][2:]
        target = ref.at[:, pl.ds(column, width)]
        if ref is not dfar_ref:
            return pltpu.make_async_copy(stage.at[i % 2], target, stage_sem.at[i % 2])
        return pltpu.make_async_remote_copy(
            src_ref=stage.at[i % 2], dst_ref=target, send_sem=sc.far_send.at[i % 2],
            recv_sem=sc.far_recv.at[i % 2], device_id=device(me.sib, me.band), device_id_type=MESH,
        )

    for i, (heads_ref, row0, ref, column) in enumerate(stores):
        if i >= 2:
            store(i - 2).wait()
        unpack_heads(heads_ref, row0, rows, stage.at[i % 2], 0)
        store(i).start()
    for i in (len(stores) - 2, len(stores) - 1):
        store(i).wait()
    for step in rest[inside:]:
        step()
    settle()


def reduce_attend(plan, grads, parts, rows_out, count, query, own, far, grad, top, band_slots, collective_id):
    half, width = grads[0][0].shape[-2:]
    counts = tuple(len(phase) for phase in grads)
    rows = query.shape[0]
    heads = width // HEAD_DIM
    bf = jnp.bfloat16
    scratch = reduce_scratch(plan, half, width)
    scratch.update(
        qh=pltpu.VMEM((heads, rows, LANES), bf),
        kh=pltpu.VMEM((heads, 2 * rows, LANES), bf),
        vh=pltpu.VMEM((heads, 2 * rows, LANES), bf),
        gh=pltpu.VMEM((heads, rows, LANES), bf),
        stage=pltpu.VMEM((2, rows, width), bf),
        stage_sem=pltpu.SemaphoreType.DMA((2,)),
        far_send=pltpu.SemaphoreType.DMA((2,)),
        far_recv=pltpu.SemaphoreType.DMA((2,)),
        **home_scratch(),
    )
    any_, vmem = pl.BlockSpec(memory_space=pl.ANY), pl.BlockSpec(memory_space=pltpu.VMEM)
    smem = pl.BlockSpec(memory_space=pltpu.SMEM)
    units = [unit for phase in grads for unit in phase]
    return pl.pallas_call(
        partial(reduce_attend_kernel, plan, counts, band_slots, tuple(scratch)),
        out_shape=reduce_shapes(plan, half, width)
        + [
            jax.ShapeDtypeStruct(rows_out.shape, bf),
            jax.ShapeDtypeStruct((rows, width), bf),
            jax.ShapeDtypeStruct((rows, 2 * width), bf),
            jax.ShapeDtypeStruct((rows, 2 * width), bf),
        ],
        in_specs=[any_] * (len(units) + len(parts) + 1) + [smem] + [any_] * 4 + [vmem],
        out_specs=[any_] * (len(plan) + 4),
        scratch_shapes=list(scratch.values()),
        compiler_params=pltpu.CompilerParams(
            collective_id=collective_id, has_side_effects=True, vmem_limit_bytes=60 * 2**20
        ),
        name="reduce_attend",
    )(*units, *parts, rows_out, count, query, own, far, grad, top)


MOD_BLOCKS = 6
BLOCK = 128


def forward_scratch(half, ff, width, rows, note_rows, images):
    bf, f32 = jnp.bfloat16, jnp.float32
    D = pltpu.SemaphoreType.DMA
    heads = width // HEAD_DIM
    V = pltpu.VMEM
    return dict(
        qp=V((NB, 2, half, ff), bf), bounce_i=V((2, half, ff), bf), bounce_o=V((4, 2, half, width), bf),
        bounce_t=V((rows // images, width), bf), tok=V((images, rows // images, width), bf),
        notes=V((NB, note_rows, 128), f32), vec=V((16, width), f32),
        residual=V((rows, width), f32), attn_in=V((rows, width), bf), query=V((rows, width), bf),
        own=V((rows, 2 * width), bf), far=V((rows, 2 * width), bf), mixed=V((rows, width), bf),
        attended=V((rows, width), f32), mlp_in=V((rows, width), bf), tops=V((heads, 8, rows), f32),
        qh=V((heads, rows, LANES), bf), kh=V((heads, 2 * rows, LANES), bf), vh=V((heads, 2 * rows, LANES), bf),
        z_send=D((3, 2)), z_recv=D((3, NB)), f_send=D((3, NB)), a_send=D((9, 2)), a_recv=D((9, 2)), b_send=D((9, 2, 2)), b_recv=D((9, 2, 2)),
        c_send=D((9,)), c_recv=D((9,)), t_send=D((2, 2)), t_recv=D((2, 2)), m_send=D((2, 2)), m_recv=D((NB,)),
        local=D((4,)), kv_send=D((1,)), kv_recv=D((1,)), done=D((12,)),
    )


def gather_steps(me, width, ins, outs, tok_in, tok_out, cot_in, cot_out, note_in, note_out, sc):
    dp, band, core, px, py, kind = me.dp, me.band, me.core, me.px, me.py, me.kind
    base = dp - core
    dev = lambda d, b: device(d, b)
    here = lambda d: dev(d, band)
    flip = lambda v: 1 - v
    low = band < 2
    bands = (band + 1 - 2 * lax.rem(band, 2), jnp.where(low, 2, 1), jnp.where(low, 3, 0))
    order = [(ph, b) for ph in range(3) for b in bands]
    inside = jnp.logical_or(band == 1, band == 2)
    sends = []

    def remote(src, dst, ss, rs, to):
        return pltpu.make_async_remote_copy(
            src_ref=src, dst_ref=dst, send_sem=ss, recv_sem=rs, device_id=to, device_id_type=MESH
        )

    def go(make):
        for copy in make():
            copy.start()
        sends.append(make)

    size = ins[0].shape[1]
    cut = size // 32 * 16
    whole, spans = pl.ds(0, size), (pl.ds(0, cut), pl.ds(cut, size - cut))

    def cols(t, n=1):
        return pl.ds(pl.multiple_of(t * width, 128), n * width)

    def unit(ph, b, t, h, span=whole):
        return outs[ph].at[b, t, h, span] if ph == 2 else outs[ph].at[b, h, span, cols(t)]

    def pair(ph, b, h, y, span):
        return outs[ph].at[b, pl.ds(2 * y, 2), h, span] if ph == 2 else outs[ph].at[b, h, span, cols(2 * y, 2)]

    def row(ph, b, h):
        return outs[ph].at[b, :, h] if ph == 2 else outs[ph].at[b, h]

    def own_z(ph, up):
        src = ins[ph].at[kind, core] if ph == 2 else ins[ph].at[core, :, cols(kind)]
        return remote(
            src, unit(ph, band, kind, core), sc.z_send.at[ph, up], sc.z_recv.at[ph, band],
            dev(dp, band - 1 + 2 * up),
        )

    def pass_z(s):
        ph, b = order[s]
        u = unit(ph, b, kind, core)
        return remote(
            u, u, sc.f_send.at[ph, b], sc.z_recv.at[ph, b], dev(dp, jnp.where(b < band, band + 1, band - 1))
        )

    def a_copy(s, half, mine):
        ph, b = order[s]
        near = 2 * py + flip(px) if half == 0 else 2 * flip(py) + px
        u = unit(ph, b, kind if mine else near, core, spans[half])
        return remote(u, u, sc.a_send.at[s, half], sc.a_recv.at[s, half], here(me.xdp if half == 0 else me.ydp))

    def b_copies(s, half, mine):
        ph, b = order[s]
        if half == 0:
            u = pair(ph, b, core, py if mine else flip(py), spans[half])
            return [remote(u, u, sc.b_send.at[s, half, 0], sc.b_recv.at[s, half, 0], here(me.ydp))]
        copies = []
        for j in range(2):
            u = unit(ph, b, 2 * j + (px if mine else flip(px)), core, spans[half])
            copies.append(remote(u, u, sc.b_send.at[s, half, j], sc.b_recv.at[s, half, j], here(me.xdp)))
        return copies

    def c_copy(s, mine):
        ph, b = order[s]
        u = row(ph, b, core if mine else flip(core))
        return remote(u, u, sc.c_send.at[s], sc.c_recv.at[s], here(me.sib))

    def z_start(ph):
        pl.when(band < NB - 1)(lambda: own_z(ph, 1).start())
        pl.when(band > 0)(lambda: own_z(ph, 0).start())

    def z_wait(s):
        ph, b = order[s]
        u = unit(ph, b, kind, core)
        remote(u, u, sc.f_send.at[ph, b], sc.z_recv.at[ph, b], here(dp)).wait_recv()
        pl.when(inside)(lambda: pass_z(s).start())
        for half in range(2):
            go(lambda half=half: [a_copy(s, half, True)])

    def a_wait(s):
        for half in range(2):
            a_copy(s, half, False).wait_recv()
            go(partial(b_copies, s, half, True))

    def b_wait(s):
        for half in range(2):
            for copy in b_copies(s, half, False):
                copy.wait_recv()
        go(lambda: [c_copy(s, True)])

    def c_wait(s):
        c_copy(s, False).wait_recv()

    slot = lax.rem(band, 2)

    def image_copy(which, src, dst, i):
        to = dev(base + band // 2, 2 * core + i)
        return remote(src.at[i], dst.at[slot], sc.t_send.at[which, i], sc.t_recv.at[which, slot], to)

    def at_home(i):
        return jnp.logical_and(band // 2 == core, 2 * core + i == band)

    def move(which, src, dst, bounce=None):
        for i in range(2):

            @pl.when(at_home(i))
            def _():
                if bounce is None:
                    pltpu.make_async_copy(src.at[i], dst.at[slot], sc.t_recv.at[which, slot]).start()
                else:
                    inward = pltpu.make_async_copy(src.at[i], bounce, sc.local.at[3])
                    inward.start()
                    inward.wait()
                    pltpu.make_async_copy(bounce, dst.at[slot], sc.t_recv.at[which, slot]).start()

            @pl.when(jnp.logical_not(at_home(i)))
            def _():
                image_copy(which, src, dst, i).start()

    def move_wait(which, src, dst):
        for i in range(2):

            @pl.when(jnp.logical_not(at_home(i)))
            def _():
                image_copy(which, src, dst, i).wait_send()

        for s in range(2):
            pltpu.make_async_copy(dst.at[s], dst.at[s], sc.t_recv.at[which, s]).wait()

    def note_copy(i, c):
        return remote(
            note_in.at[i], note_out.at[band], sc.m_send.at[i, c], sc.m_recv.at[band],
            dev(base + c, 2 * core + i),
        )

    def note_home(i, c):
        return jnp.logical_and(c == core, 2 * core + i == band)

    def begin():
        for i in range(2):
            for c in range(2):

                @pl.when(note_home(i, c))
                def _():
                    pltpu.make_async_copy(note_in.at[i], note_out.at[band], sc.m_recv.at[band]).start()

                @pl.when(jnp.logical_not(note_home(i, c)))
                def _():
                    note_copy(i, c).start()

        z_start(0)
        for ph, dst in enumerate((outs[0].at[band], sc.bounce_i, sc.bounce_o)):
            pltpu.make_async_copy(ins[ph], dst, sc.local.at[ph]).start()

    def arrived():
        for i in range(2):
            for c in range(2):

                @pl.when(jnp.logical_not(note_home(i, c)))
                def _():
                    note_copy(i, c).wait_send()

        for b in range(NB):
            pltpu.make_async_copy(note_in.at[0], note_out.at[b], sc.m_recv.at[b]).wait()
        move_wait(0, tok_in, tok_out)

    def place():
        for ph, dst in ((1, sc.bounce_i), (2, sc.bounce_o)):
            pltpu.make_async_copy(ins[ph], dst, sc.local.at[ph]).wait()
            pltpu.make_async_copy(dst, outs[ph].at[band], sc.local.at[ph]).start()

    def first_here():
        pltpu.make_async_copy(ins[0], outs[0].at[band], sc.local.at[0]).wait()

    def finish():
        for ph, src in ((1, sc.bounce_i), (2, sc.bounce_o)):
            pltpu.make_async_copy(src, outs[ph].at[band], sc.local.at[ph]).wait()
        move_wait(1, cot_in, cot_out)
        for ph in range(3):
            pl.when(band < NB - 1)(lambda: own_z(ph, 1).wait_send())
            pl.when(band > 0)(lambda: own_z(ph, 0).wait_send())
        for s in range(len(order)):
            pl.when(inside)(lambda: pass_z(s).wait_send())
        for make in sends:
            for copy in make():
                copy.wait_send()

    def images(which):
        if which == 0:
            move(0, tok_in, tok_out)
        else:
            move(1, cot_in, cot_out, sc.bounce_t)

    return SimpleNamespace(
        i=images, s=z_start,
        begin=begin, arrived=arrived, place=place, first_here=first_here, finish=finish,
        z=z_wait, a=a_wait, b=b_wait, c=c_wait,
    )


def forward_kernel(names, band_slots, *refs):
    me = compass()
    qp_in, inner_in, outer_in, tok_in, cot_in, note_in, table_ref = refs[:7]
    (qp_out, inner_out, outer_out, cot_out, vec_out, residual_out, attn_out, query_out, own_out, far_out,
     tops_out, mixed_out, attended_out, mlp_out) = refs[7:21]
    sc = SimpleNamespace(**dict(zip(names, refs[21:])))
    rows, width = sc.residual.shape
    heads = width // HEAD_DIM
    core = me.core
    qp, tok, notes, vec = sc.qp, sc.tok, sc.notes, sc.vec

    group_barrier(me)
    g = gather_steps(
        me, width, (qp_in, inner_in, outer_in), (qp, inner_out, outer_out), tok_in, tok, cot_in, cot_out,
        note_in, notes, sc,
    )
    saves = []

    def save(src, dst):
        copy = pltpu.make_async_copy(src, dst, sc.done.at[len(saves)])
        copy.start()
        saves.append(copy)

    def run(*words):
        for do, index in words:
            do(index)

    g.begin()
    g.place()
    run((g.z, 0), (g.z, 1), (g.i, 0), (g.a, 0), (g.a, 1), (g.z, 2), (g.s, 1), (g.b, 0), (g.b, 1), (g.a, 2), (g.c, 0), (g.c, 1), (g.z, 3), (g.z, 4), (g.b, 2))
    g.arrived()
    spread_notes(notes, vec, width)
    grid_rows = notes[0, 63:64, 0:1]
    grid_cols = notes[0, 63:64, 1:2]
    band_rows = jnp.floor(grid_rows * 0.25)
    valid_count = (band_rows * grid_cols).astype(jnp.int32)
    lane = lax.broadcasted_iota(jnp.int32, (1, width), 1)
    vec[15:16, :] = jnp.where(lane == 0, band_rows * grid_cols, 0.0)
    save(vec, vec_out)

    @pl.loop(0, rows // BLOCK)
    def _(step):
        at = pl.multiple_of(step * BLOCK, BLOCK)
        sub = pl.ds(at, BLOCK)
        per_image = band_slots // BLOCK
        within = (
            lax.rem(step, per_image) * BLOCK + lax.broadcasted_iota(jnp.int32, (BLOCK, 1), 0)
        ).astype(jnp.float32)
        down = jnp.floor((within + 0.5) / grid_cols)
        place = (2 * core + step // per_image).astype(jnp.float32)
        picks = []
        for index in (place * band_rows + down, within - down * grid_cols):
            lanes = lax.broadcasted_iota(jnp.int32, (BLOCK, 128), 1).astype(jnp.float32)
            pick = jnp.where(lanes == index, 1.0, 0.0).astype(jnp.bfloat16)
            part = [jnp.dot(pick, table_ref[i], preferred_element_type=jnp.float32) for i in range(3)]
            picks.append(part[0] + (part[1] + part[2]))
        token = tok[step // per_image, pl.ds(lax.rem(step, per_image) * BLOCK, BLOCK), :]
        residual = token.astype(jnp.float32) + jnp.concatenate(picks, 1)
        sc.residual[sub, :] = residual
        normed = normalize(residual)[0]
        sc.attn_in[sub, :] = (normed * (1.0 + vec[1:2, :]) + vec[0:1, :]).astype(jnp.bfloat16)

    save(sc.residual, residual_out)
    save(sc.attn_in, attn_out)
    g.first_here()
    run((g.c, 2))
    save(qp, qp_out)
    tile = width // 3
    full = NB * 2 * qp.shape[2]

    def product(left_ref, first, step):
        at = pl.ds(pl.multiple_of(first + step * tile, 128), tile)
        return jnp.dot(
            left_ref[...], qp[:, :, :, at].reshape(full, tile), preferred_element_type=jnp.float32
        )

    def here(step):
        return pl.ds(pl.multiple_of(step * tile, 128), tile)

    @pl.loop(0, 3)
    def _(step):
        sc.own[:, here(step)] = product(sc.attn_in, width, step).astype(jnp.bfloat16)

    run((g.a, 3), (g.z, 5), (g.s, 2))

    @pl.loop(0, 3)
    def _(step):
        value = product(sc.attn_in, 2 * width, step) + vec[7:8, here(step)]
        sc.own[:, here(step + 3)] = value.astype(jnp.bfloat16)

    swap = pltpu.make_async_remote_copy(
        src_ref=sc.own, dst_ref=sc.far, send_sem=sc.kv_send.at[0], recv_sem=sc.kv_recv.at[0],
        device_id=device(me.sib, me.band), device_id_type=MESH,
    )
    swap.start()
    run((g.a, 4), (g.b, 3))

    @pl.loop(0, 3)
    def _(step):
        value = product(sc.attn_in, 0, step) + vec[6:7, here(step)]
        sc.query[:, here(step)] = value.astype(jnp.bfloat16)

    save(sc.query, query_out)
    save(sc.own, own_out)
    run((g.a, 5), (g.b, 4), (g.c, 3), (g.z, 6))
    qh, kh, vh = sc.qh, sc.kh, sc.vh
    keys, plain = key_tail(valid_count, band_slots), flat_tail(0.0)
    pack_heads(sc.query, 0, qh, 0, rows, flat_tail(1.0))
    pack_heads(sc.own, 0, kh, 0, rows, keys)
    pack_heads(sc.own, width, vh, 0, rows, plain)
    swap.wait()
    save(sc.far, far_out)
    pack_heads(sc.far, 0, kh, rows, rows, keys)
    pack_heads(sc.far, width, vh, rows, rows, plain)
    beside = {
        0: ((g.z, 7), (g.b, 5), (g.c, 4)), 2: ((g.a, 6), (g.z, 8), (g.i, 1)), 4: ((g.a, 7), (g.b, 6), (g.c, 5)), 7: ((g.a, 8), (g.b, 7), (g.c, 6)), 10: ((g.b, 8), (g.c, 7)),
        13: ((g.c, 8),),
    }

    @pl.loop(0, heads)
    def _(h):
        attend_block(h, qh, kh, vh, sc.tops)
        for i, words in beside.items():
            pl.when(h == i)(partial(run, *words))

    unpack_heads(qh, 0, rows, sc.mixed, 0)
    save(sc.tops, tops_out)
    save(sc.mixed, mixed_out)

    @pl.loop(0, 3)
    def _(step):
        sc.attended[:, here(step)] = product(sc.mixed, 3 * width, step) + vec[8:9, here(step)]

    save(sc.attended, attended_out)

    @pl.loop(0, rows // BLOCK)
    def _(step):
        sub = pl.ds(pl.multiple_of(step * BLOCK, BLOCK), BLOCK)
        middle = sc.residual[sub, :] + vec[2:3, :] * sc.attended[sub, :]
        normed = normalize(middle)[0]
        sc.mlp_in[sub, :] = (normed * (1.0 + vec[4:5, :]) + vec[3:4, :]).astype(jnp.bfloat16)

    save(sc.mlp_in, mlp_out)
    g.finish()
    for copy in saves:
        copy.wait()


NOTE_COND, NOTE_GRID, NOTE_BIAS = 54, 63, 64


def spread_notes(notes, vec, width):
    lines = width // 128
    share = notes.shape[0]
    total = notes[0, 0:NOTE_GRID, :] + 0.0
    for b in range(1, share):
        total = total + notes[b, 0:NOTE_GRID, :]

    def flat(block, first):
        return jnp.concatenate([block[first + i : first + i + 1, :] for i in range(lines)], 1)

    for index in range(MOD_BLOCKS):
        vec[index : index + 1, :] = flat(total, index * lines)
    small = width // share
    for index in range(4):
        parts = []
        for b in range(share):
            first = NOTE_BIAS + 3 * index
            for i in range(3):
                parts.append(notes[b, first + i : first + i + 1, : min(128, small - 128 * i)])
        vec[6 + index : 7 + index, :] = jnp.concatenate(parts, 1)
    for b in range(share):
        block = notes[b, NOTE_BIAS + 12 : NOTE_BIAS + 12 + lines, :]
        vec[10 + b : 11 + b, :] = flat(block, 0)
    vec[14:15, :] = flat(notes[0, NOTE_COND : NOTE_COND + lines, :], 0)


def forward_block(qp, inner, outer, tok, cot, note, table):
    half, ff = qp.shape[0] // 2, qp.shape[1]
    images, band_slots, width = tok.shape
    rows = images * band_slots
    heads = width // HEAD_DIM
    bf, f32 = jnp.bfloat16, jnp.float32
    S = jax.ShapeDtypeStruct
    qp, inner = qp.reshape(2, half, ff), inner.reshape(2, half, ff)
    outer = outer.reshape(4, 2, half, width)
    scratch = forward_scratch(half, ff, width, rows, note.shape[1], images)
    any_ = pl.BlockSpec(memory_space=pl.ANY)
    return pl.pallas_call(
        partial(forward_kernel, tuple(scratch), band_slots),
        out_shape=[
            S((NB, 2, half, ff), bf), S((NB, 2, half, ff), bf), S((NB, 4, 2, half, width), bf), S(cot.shape, bf),
            S((16, width), f32), S((rows, width), f32), S((rows, width), bf), S((rows, width), bf),
            S((rows, 2 * width), bf), S((rows, 2 * width), bf), S((heads, 8, rows), f32), S((rows, width), bf),
            S((rows, width), f32), S((rows, width), bf),
        ],
        in_specs=[any_] * 6 + [pl.BlockSpec(memory_space=pltpu.VMEM)],
        out_specs=[any_] * 14,
        scratch_shapes=list(scratch.values()),
        compiler_params=pltpu.CompilerParams(
            collective_id=0, has_side_effects=True, vmem_limit_bytes=60 * 2**20
        ),
        name="forward_block",
    )(qp, inner, outer, tok, cot, note, table)


GELU_SCALE = 0.7978845608028654


def mlp_kernel(band_slots, mlp_ref, inner_ref, outer_ref, vec_ref, bias_ref, residual_ref, attended_ref, cot_ref,
               mixed_ref, proj_ref, out_ref, middle_ref, back_ref, proj_grad_ref, outer_grad_ref, inner_grad_ref,
               bias_grad_ref, sums_ref, out_acc, back_acc, grad_mlp):
    step = pl.program_id(0)
    rows = mlp_ref.shape[0]
    low = lambda value: value.astype(jnp.bfloat16)
    line = lambda index: vec_ref[index : index + 1, :]

    def grad_out(at):
        slot = lax.rem(at + lax.broadcasted_iota(jnp.int32, (BLOCK, 1), 0), band_slots)
        valid = jnp.where(slot.astype(jnp.float32) < vec_ref[15:16, 0:1], 1.0, 0.0)
        return cot_ref[pl.ds(at, BLOCK), :].astype(jnp.float32) * valid

    def add_line(index, values):
        sums_ref[index : index + 1, :] += jnp.sum(values, 0, keepdims=True)

    @pl.when(step == 0)
    def _():
        sums_ref[...] = jnp.zeros_like(sums_ref)

        @pl.loop(0, rows // BLOCK)
        def _(block):
            at = pl.multiple_of(block * BLOCK, BLOCK)
            grad = low(line(5) * grad_out(at))
            grad_mlp[pl.ds(at, BLOCK), :] = grad
            add_line(5, grad.astype(jnp.float32))
            out_acc[pl.ds(at, BLOCK), :] = jnp.zeros((BLOCK, out_acc.shape[1]), jnp.float32)
            back_acc[pl.ds(at, BLOCK), :] = jnp.zeros((BLOCK, out_acc.shape[1]), jnp.float32)

    inner, outer, grad = inner_ref[...], outer_ref[...], grad_mlp[...]
    pre = jnp.dot(mlp_ref[...], inner, preferred_element_type=jnp.float32) + bias_ref[...]
    grad_hidden = lanes_dot(grad, outer)
    square = pre * pre
    bend = jnp.tanh(GELU_SCALE * (pre * (1.0 + 0.044715 * square)))
    rise = 0.5 * (1.0 + bend)
    hidden = low(pre * rise)
    slope = rise + (0.5 * pre) * (1.0 - bend * bend) * (GELU_SCALE * (1.0 + 0.134145 * square))
    grad_pre = low(slope * grad_hidden)
    out_acc[...] += jnp.dot(hidden, outer, preferred_element_type=jnp.float32)
    outer_grad_ref[...] = low(rows_dot(hidden, grad))
    back_acc[...] += lanes_dot(grad_pre, inner)
    inner_grad_ref[...] = low(rows_dot(mlp_ref[...], grad_pre))
    bias_grad_ref[...] = jnp.broadcast_to(
        jnp.sum(grad_pre.astype(jnp.float32), 0, keepdims=True), bias_grad_ref.shape
    )

    @pl.when(step == pl.num_programs(0) - 1)
    def _():
        @pl.loop(0, rows // BLOCK)
        def _(block):
            at = pl.multiple_of(block * BLOCK, BLOCK)
            sub = pl.ds(at, BLOCK)
            attended = attended_ref[sub, :]
            middle = residual_ref[sub, :] + line(2) * attended
            normed, inverse = normalize(middle)
            mlp_out = out_acc[sub, :] + line(9)
            out_ref[sub, :] = low(middle + line(5) * mlp_out)
            grad_block = grad_out(at)
            add_line(0, grad_block * mlp_out)
            back = back_acc[sub, :]
            add_line(1, back)
            add_line(2, back * normed)
            grad_middle = grad_block + norm_back(back * (1.0 + line(4)), normed, inverse)
            middle_ref[sub, :] = grad_middle
            add_line(3, grad_middle * attended)
            grad_attended = low(line(2) * grad_middle)
            add_line(4, grad_attended.astype(jnp.float32))
            grad_mlp[sub, :] = grad_attended

        proj_grad_ref[...] = low(rows_dot(mixed_ref[...], grad_mlp[...]))
        back_ref[...] = low(lanes_dot(grad_mlp[...], proj_ref[...]))


def feed_forward(mlp_in, inner, outer, vectors, inner_bias, residual, attended, cotangent, mixed, first, band_slots):
    rows, width = mlp_in.shape
    hidden = inner.shape[1]
    tile = 512
    bf, f32 = jnp.bfloat16, jnp.float32
    S = jax.ShapeDtypeStruct
    keep = lambda *shape: pl.BlockSpec(shape, lambda j: (0,) * len(shape))
    return pl.pallas_call(
        partial(mlp_kernel, band_slots),
        grid=(hidden // tile,),
        out_shape=[
            S((rows, width), bf), S((rows, width), f32), S((rows, width), bf), S((width, width), bf),
            S((hidden, width), bf), S((width, hidden), bf), S((8, hidden), f32), S((8, width), f32),
        ],
        in_specs=[
            keep(rows, width), pl.BlockSpec((width, tile), lambda j: (0, j)), pl.BlockSpec((tile, width), lambda j: (j, 0)),
            keep(16, width), pl.BlockSpec((1, tile), lambda j: (0, j)), keep(rows, width), keep(rows, width),
            keep(rows, width), keep(rows, width), pl.BlockSpec((width, width), lambda j: (0, 3)),
        ],
        out_specs=[
            keep(rows, width), keep(rows, width), keep(rows, width), keep(width, width),
            pl.BlockSpec((tile, width), lambda j: (j, 0)), pl.BlockSpec((width, tile), lambda j: (0, j)),
            pl.BlockSpec((8, tile), lambda j: (0, j)), keep(8, width),
        ],
        scratch_shapes=[pltpu.VMEM((rows, width), f32), pltpu.VMEM((rows, width), f32), pltpu.VMEM((rows, width), bf)],
        compiler_params=pltpu.CompilerParams(vmem_limit_bytes=60 * 2**20),
        cost_estimate=pl.CostEstimate(
            flops=12 * rows * width * hidden, bytes_accessed=8 * width * hidden + 24 * rows * width,
            transcendentals=rows * hidden,
        ),
        name="feed_forward",
    )(mlp_in, inner, outer, vectors, inner_bias, residual, attended, cotangent, mixed, first)


def position_parts(width):
    quarter = width // 4
    frequency = 10000.0 ** (-jnp.arange(quarter, dtype=jnp.float32) / quarter)
    angles = jnp.arange(128, dtype=jnp.float32)[:, None] * frequency
    left = jnp.concatenate([jnp.sin(angles), jnp.cos(angles)], -1)
    parts = []
    for _ in range(3):
        part = lax.reduce_precision(left, 8, 7)
        parts.append(part.astype(jnp.bfloat16))
        left = left - part
    return jnp.stack(parts)


def over_groups(piece, dp_count):
    if dp_count == 8:
        return piece
    groups = [[rank + 8 * group for group in range(dp_count // 8)] for rank in range(8)]
    return lax.psum(piece.astype(jnp.float32), "dp", axis_index_groups=groups)


def every_group(piece, dp_count):
    if dp_count == 8:
        return piece[None]
    groups = [[rank + 8 * group for group in range(dp_count // 8)] for rank in range(8)]
    return lax.all_gather(piece, "dp", axis_index_groups=groups)


def own_piece(vector, count, band_place):
    return lax.dynamic_slice_in_dim(vector, band_place * count, count, 0)


def body(
    tokens,
    condition,
    patch_grid,
    ada_weight,
    ada_bias,
    qkv_weight,
    query_bias,
    value_bias,
    proj_weight,
    proj_bias,
    inner_weight,
    inner_bias,
    outer_weight,
    outer_bias,
    cotangent,
):
    dp_count = lax.axis_size("dp")
    band_count = lax.axis_size("band")
    images, band_slots, width = tokens.shape
    band = lax.axis_index("band")
    dp = lax.axis_index("dp")
    core = lax.rem(dp, 2)
    hidden = inner_weight.shape[1]
    part_rows = qkv_weight.shape[0]

    condition_f = condition.astype(jnp.float32)
    activated = jax.nn.silu(condition_f).astype(jnp.bfloat16)
    own_activated = lax.dynamic_slice_in_dim(activated, band * part_rows, part_rows, 1)
    share = jnp.dot(own_activated, ada_weight, preferred_element_type=jnp.float32)
    share = share + lax.dynamic_update_slice_in_dim(
        jnp.zeros((ada_weight.shape[1],), jnp.float32),
        ada_bias.astype(jnp.float32),
        band * ada_bias.shape[0],
        0,
    )
    mod_count = share.shape[1]
    lines = lambda vector: jnp.pad(
        vector.astype(jnp.float32), [(0, 0)] * (vector.ndim - 1) + [(0, -vector.shape[-1] % 128)]
    )
    spread = lambda vector: jnp.broadcast_to(lines(vector), (images, -(-vector.shape[0] // 128) * 128))
    note = jnp.concatenate(
        [share, condition_f, lines(patch_grid)]
        + [spread(bias) for bias in (query_bias, value_bias, proj_bias, outer_bias, inner_bias)],
        1,
    )
    note = jnp.pad(note, ((0, 0), (0, -note.shape[1] % 1024))).reshape(images, -1, 128)
    first_weight = jnp.concatenate([qkv_weight, proj_weight], 1)
    (first_full, inner_full, outer_full, cotangent_here, vectors, residual, attn_in, query_rows, key_value,
     other_key_value, tops, mixed_rows, attended, mlp_in) = forward_block(
        first_weight, inner_weight, outer_weight, tokens, cotangent, note, position_parts(width)
    )
    first_full = first_full.reshape(width, -1)
    inner_full = inner_full.reshape(width, hidden)
    outer_full = outer_full.reshape(hidden, width)
    valid_count = vectors[15, :1].astype(jnp.int32)
    rows = images * band_slots
    inner_bias_row = vectors[10:14].reshape(1, -1)
    (block_out, grad_middle, grad_mixed, grad_proj, grad_outer, grad_inner, grad_inner_bias, sums) = feed_forward(
        mlp_in, inner_full, outer_full, vectors, inner_bias_row, residual, attended,
        cotangent_here.reshape(rows, width), mixed_rows, first_full, band_slots,
    )
    blocks = (band_count, 2, part_rows // 2, width)
    grad_outer = grad_outer.reshape(band_count, 4, 2, part_rows // 2, width)
    grad_inner = grad_inner.reshape(band_count, 2, part_rows // 2, hidden)
    outer_sum, inner_part, block_home, grad_query, own_terms, other_terms = reduce_attend(
        (FRONT | BACK, FRONT), [[grad_outer], [grad_inner]], [], block_out.reshape(images, band_slots, width), valid_count, query_rows, key_value, other_key_value, grad_mixed, tops,
        band_slots, 1,
    )
    inner_sum, first_sum, tokens_home, every, bias_grads, grad_act = reduce_last(
        grad_proj.reshape(blocks), inner_part, attn_in, grad_query, own_terms, other_terms, first_full, residual,
        grad_middle, vectors, sums, grad_inner_bias, ada_weight, images, band_slots, 2,
    )
    tokens_home = tokens_home.astype(jnp.float32)
    every = every_group(every, dp_count)
    bias_grads = over_groups(bias_grads, dp_count).reshape(-1)
    every = jnp.swapaxes(every, 1, 2).reshape(dp_count * images, -1)
    every_mod = every[:, :mod_count]
    every_condition = every[:, mod_count : mod_count + width]
    every_activated = jax.nn.silu(every_condition.astype(jnp.float32)).astype(jnp.bfloat16)
    every_activated = lax.dynamic_slice_in_dim(every_activated, band * part_rows, part_rows, 1)
    grad_ada = rows_dot(every_activated, every_mod)
    grad_ada_bias = own_piece(jnp.sum(every_mod.astype(jnp.float32), 0), ada_bias.shape[0], band)
    grad_act = jnp.swapaxes(grad_act[:, :images, :part_rows], 0, 1).reshape(images, width)
    grad_condition = jax.vjp(jax.nn.silu, condition_f)[1](grad_act)[0]

    def side_by_side(units):
        return jnp.concatenate([unit.reshape(part_rows, width) for unit in units], 1).astype(jnp.float32)

    first_sum, inner_sum, outer_sum = [
        over_groups(piece, dp_count) for piece in (first_sum, inner_sum, outer_sum)
    ]
    qkv_sum = side_by_side([first_sum[t] for t in range(3)])
    proj_sum = first_sum[3].reshape(part_rows, width).astype(jnp.float32)
    inner_sum = side_by_side([inner_sum[t] for t in range(4)])
    outer_sum = outer_sum.reshape(4 * part_rows, width).astype(jnp.float32)
    bias_parts = []
    at = 0
    for piece in (query_bias, value_bias, proj_bias, inner_bias, outer_bias):
        whole = piece.shape[0] * band_count
        bias_parts.append(own_piece(bias_grads[at : at + whole], piece.shape[0], band))
        at += whole
    return (
        block_home,
        tokens_home,
        grad_condition,
        grad_ada,
        grad_ada_bias,
        qkv_sum,
        bias_parts[0],
        bias_parts[1],
        proj_sum,
        bias_parts[2],
        inner_sum,
        bias_parts[3],
        outer_sum,
        bias_parts[4],
    )


def solution(mesh):
    placed = (
        P("dp", "band", None),
        P("dp", None),
        P("dp", None),
        P("band", None),
        P("band"),
        P("band", None),
        P("band"),
        P("band"),
        P("band", None),
        P("band"),
        P("band", None),
        P("band"),
        P("band", None),
        P("band"),
        P("dp", "band", None),
    )
    return jax.shard_map(
        body,
        mesh=mesh,
        in_specs=placed,
        out_specs=(
            P("dp", "band", None),
            P("dp", "band", None),
            P("dp", None),
            P("band", None),
            P("band"),
            P("band", None),
            P("band"),
            P("band"),
            P("band", None),
            P("band"),
            P("band", None),
            P("band"),
            P("band", None),
            P("band"),
        ),
        check_vma=False,
    )
```

```python
from functools import partial
from types import SimpleNamespace

import jax
import jax.numpy as jnp
import numpy as np
from jax import lax
from jax.experimental import pallas as pl
from jax.experimental.pallas import tpu as pltpu
from jax.sharding import PartitionSpec as P

HEAD_DIM = 72


MESH = pl.DeviceIdType.MESH
NB = 4


def device(dp, band):
    return {"dp": dp, "band": band}


def normalize(values):
    average = jnp.mean(values, -1, keepdims=True)
    centered = values - average
    variance = jnp.mean(centered * centered, -1, keepdims=True)
    inverse = lax.rsqrt(variance + 1e-06)
    return (centered * inverse, inverse)


def norm_back(grad_normed, normed, inverse):
    first = jnp.mean(grad_normed, -1, keepdims=True)
    second = jnp.mean(grad_normed * normed, -1, keepdims=True)
    return inverse * (grad_normed - first - normed * second)


LANES = 128
PACK_ROWS = 128


def pack_heads(source, first, heads_ref, row0, rows, tail):
    heads = heads_ref.shape[0]

    @pl.loop(0, rows // PACK_ROWS)
    def _(step):
        at = pl.multiple_of(step * PACK_ROWS, PACK_ROWS)
        block = source[pl.ds(at, PACK_ROWS), first : first + heads * HEAD_DIM]
        end = tail(at)
        for h in range(heads):
            part = block[:, h * HEAD_DIM : (h + 1) * HEAD_DIM]
            heads_ref[h, pl.ds(row0 + at, PACK_ROWS), :] = jnp.concatenate([part, end], 1)


def unpack_heads(heads_ref, row0, rows, target, first):
    heads = heads_ref.shape[0]

    @pl.loop(0, rows // PACK_ROWS)
    def _(step):
        at = pl.multiple_of(step * PACK_ROWS, PACK_ROWS)
        parts = [heads_ref[h, pl.ds(row0 + at, PACK_ROWS), :][:, :HEAD_DIM] for h in range(heads)]
        target[pl.ds(at, PACK_ROWS), first : first + heads * HEAD_DIM] = jnp.concatenate(parts, 1)


def flat_tail(value):
    def tail(at):
        lane = lax.broadcasted_iota(jnp.int32, (PACK_ROWS, LANES - HEAD_DIM), 1)
        return jnp.where(lane == 0, value, 0.0).astype(jnp.bfloat16)

    return tail


def key_tail(valid_count, band_slots):
    def tail(at):
        shape = (PACK_ROWS, LANES - HEAD_DIM)
        lane = lax.broadcasted_iota(jnp.int32, shape, 1)
        slot = lax.rem(at + lax.broadcasted_iota(jnp.int32, shape, 0), band_slots)
        return jnp.where(jnp.logical_and(lane == 0, slot >= valid_count), -1e30, 0.0).astype(jnp.bfloat16)

    return tail


def lanes_dot(left, right):
    return lax.dot_general(left, right, (((1,), (1,)), ((), ())), preferred_element_type=jnp.float32)


def rows_dot(left, right):
    return lax.dot_general(left, right, (((0,), (0,)), ((), ())), preferred_element_type=jnp.float32)


SCORE_SCALE = HEAD_DIM ** (-0.5)


def attend_block(h, qh, kh, vh, top_ref):
    rows = qh.shape[1]
    for block in range(2):
        at = pl.ds(block * rows // 2, rows // 2)
        scores = lanes_dot(kh[h], qh[h, at, :]) * SCORE_SCALE
        top = jnp.max(scores, 0, keepdims=True)
        weights = jnp.exp(scores - top)
        total = jnp.sum(weights, 0, keepdims=True)
        low = (weights * (1.0 / total)).astype(jnp.bfloat16)
        mixed = rows_dot(vh[h], low)
        qh[h, at, :] = jnp.transpose(mixed).astype(jnp.bfloat16)
        top_ref[h, :, at] = jnp.broadcast_to(top + jnp.log(total), (8, rows // 2))


def attend_head(h, qh, kh, vh, gh, top_ref):
    query = qh[h]
    key = kh[h]
    grad = gh[h]
    probs = jnp.exp(lanes_dot(key, query) * SCORE_SCALE - top_ref[h, 0:1, :])
    grad_probs = lanes_dot(vh[h], grad)
    inner = jnp.sum(probs * grad_probs, 0, keepdims=True)
    grad_scores = (probs * (grad_probs - inner)).astype(jnp.bfloat16)
    vh[h] = jnp.dot(
        probs.astype(jnp.bfloat16), grad, preferred_element_type=jnp.float32
    ).astype(jnp.bfloat16)
    grad_query = rows_dot(key, grad_scores)
    kh[h] = (
        SCORE_SCALE * jnp.dot(grad_scores, query, preferred_element_type=jnp.float32)
    ).astype(jnp.bfloat16)
    qh[h] = (SCORE_SCALE * jnp.transpose(grad_query)).astype(jnp.bfloat16)


def compass():
    dp = lax.axis_index("dp")
    band = lax.axis_index("band")
    core = lax.rem(dp, 2)
    px = lax.rem(dp // 2, 2)
    py = lax.rem(dp // 4, 2)
    return SimpleNamespace(
        dp=dp, band=band, core=core, px=px, py=py, kind=2 * py + px,
        sib=dp + 1 - 2 * core, xdp=dp + 2 - 4 * px, ydp=dp + 4 - 8 * py,
    )


def add_rows(total, term):
    rows = total.shape[0]

    @pl.loop(0, rows // 16)
    def _(step):
        at = pl.ds(pl.multiple_of(step * 16, 16), 16)
        total[at, :] = (
            total[at, :].astype(jnp.float32) + term[at, :].astype(jnp.float32)
        ).astype(jnp.bfloat16)


def run_all(batch):
    for do in batch:
        do()


REDUCE_ORDER = (1, 3, 2, 0)


FRONT, BACK = 1, 2


def reduce_scratch(plan, half, width):
    bf = jnp.bfloat16
    n = NB * sum(1 for todo in plan if todo & FRONT)
    m = len(plan)
    D = pltpu.SemaphoreType.DMA
    scratch = dict(
        recv_z=pltpu.VMEM((m, NB, half, width), bf), z_send=D((m, NB)), z_recv=D((m, NB)),
        d_send=D((m, 6)), d_recv=D((m, 6)), d_own=D((m,)), part_sem=D((m,)),
    )
    if n:
        scratch.update(
            acc=pltpu.VMEM((n, 4, half, width), bf), recv_a=pltpu.VMEM((n, 4, half, width), bf),
            recv_b=pltpu.VMEM((n, 2, half, width), bf), recv_c=pltpu.VMEM((n, half, width), bf),
            a_send=D((n,)), a_recv=D((n,)), a_own=D((n,)),
            b_send=D((n, 2, 2)), b_recv=D((n, 2, 2)), c_send=D((n, 2)), c_recv=D((n, 2)),
        )
    return scratch


def reduce_steps(me, plan, source, out, parts_in, parts_out, sc, beside=(), ahead=3, by_kind=False):
    dp, band, core, px, py, kind = me.dp, me.band, me.core, me.px, me.py, me.kind
    here = lambda d: device(d, band)
    fronts = [phase for phase, todo in enumerate(plan) if todo & FRONT]
    backs = [phase for phase, todo in enumerate(plan) if todo & BACK]
    chunks = [(phase, k) for phase in fronts for k in REDUCE_ORDER]
    n = len(chunks)
    flip = lambda v: 1 - v
    sends = []
    rows = sc.recv_z.shape[2]
    cut = rows // 32 * 16
    spans = (pl.ds(0, cut), pl.ds(cut, rows - cut))

    def remote(src, dst, ss, rs, to):
        return pltpu.make_async_remote_copy(
            src_ref=src, dst_ref=dst, send_sem=ss, recv_sem=rs, device_id=to, device_id_type=MESH
        )

    def go(make):
        make().start()
        sends.append(make)

    def target(k):
        return device(dp, lax.rem(band + k, NB))

    def start_a(s, kinds=range(4)):
        phase, k = chunks[s]
        b = lax.rem(band + k, NB)
        for t in kinds:
            remote(
                source(phase, b, t, flip(core)), sc.recv_a.at[s, t], sc.a_send.at[s], sc.a_recv.at[s],
                here(me.sib),
            ).start()
            pltpu.make_async_copy(source(phase, b, t, core), sc.acc.at[s, t], sc.a_own.at[s]).start()

    def first(half, j, send):
        if half == 0:
            return 2 * j + (flip(px) if send else px)
        return 2 * (flip(py) if send else py) + j

    def second(half, send):
        if half == 0:
            return 2 * (flip(py) if send else py) + px
        return 2 * py + (flip(px) if send else px)

    def near(half):
        return here(me.xdp if half == 0 else me.ydp)

    def send_b(s, half, j):
        return remote(
            sc.acc.at[s, first(half, j, True), spans[half]], sc.recv_b.at[s, j, spans[half]],
            sc.b_send.at[s, half, j], sc.b_recv.at[s, half, j], near(half),
        )

    def send_c(s, half):
        return remote(
            sc.acc.at[s, second(half, True), spans[half]], sc.recv_c.at[s, spans[half]],
            sc.c_send.at[s, half], sc.c_recv.at[s, half], near(1 - half),
        )

    def send_z(phase, k, src):
        return remote(src, sc.recv_z.at[phase, k], sc.z_send.at[phase, k], sc.z_recv.at[phase, k], target(k))

    def unit_z(s):
        phase, k = chunks[s]
        return send_z(phase, k, sc.acc.at[s, kind])

    def part_load(phase):
        return pltpu.make_async_copy(parts_in[phase], sc.recv_z.at[phase, 0], sc.part_sem.at[phase])

    def part_store(phase):
        return pltpu.make_async_copy(sc.recv_z.at[phase, 0], parts_out[phase], sc.part_sem.at[phase])

    def d_copy(phase, half, slot, mine):
        ss, rs = sc.d_send.at[phase, 3 * half + slot], sc.d_recv.at[phase, 3 * half + slot]
        span = spans[half]
        if slot == 0:
            src = sc.recv_z.at[phase, 0, span]
            return remote(src, out[phase].at[kind, core, span], ss, rs, near(half))
        j = slot - 1
        t = 2 * (py if mine else flip(py)) + j if half == 0 else 2 * j + (px if mine else flip(px))
        unit = out[phase].at[t, core, span]
        return remote(unit, unit, ss, rs, near(1 - half))

    def d_cross(phase, mine):
        row = out[phase].at[:, core if mine else flip(core)]
        return remote(row, row, sc.z_send.at[phase, 0], sc.z_recv.at[phase, 0], here(me.sib))

    def a_to_b(s):
        acc, got = sc.acc, sc.recv_a
        pltpu.make_async_copy(got.at[s], acc.at[s], sc.a_own.at[s]).wait()
        whole = remote(got.at[s], got.at[s], sc.a_send.at[s], sc.a_recv.at[s], here(me.sib))
        whole.wait_recv()
        for j in range(2):
            for half in range(2):
                t = first(half, j, True)
                add_rows(acc.at[s, t, spans[half]], got.at[s, t, spans[half]])
                go(partial(send_b, s, half, j))
        for j in range(2):
            for half in range(2):
                t = first(half, j, False)
                add_rows(acc.at[s, t, spans[half]], got.at[s, t, spans[half]])
        whole.wait_send()

    def b_to_c(s):
        acc, got = sc.acc, sc.recv_b
        for half in range(2):
            for j in range(2):
                send_b(s, half, j).wait_recv()
            away = flip(py) if half == 0 else flip(px)
            t = second(half, True)
            add_rows(acc.at[s, t, spans[half]], got.at[s, away, spans[half]])
            go(partial(send_c, s, half))
        for half in range(2):
            stay = py if half == 0 else px
            add_rows(acc.at[s, kind, spans[half]], got.at[s, stay, spans[half]])

    def c_to_z(s):
        phase, k = chunks[s]
        for half in range(2):
            send_c(s, half).wait_recv()
            add_rows(sc.acc.at[s, kind, spans[half]], sc.recv_c.at[s, spans[half]])
        if k != 0:
            go(partial(unit_z, s))

    def z_sum(phase):
        got = sc.recv_z
        for k in range(1, NB):
            remote(
                got.at[phase, k], got.at[phase, k], sc.z_send.at[phase, k], sc.z_recv.at[phase, k], here(dp)
            ).wait_recv()
        s = NB * fronts.index(phase) + NB - 1

        @pl.loop(0, rows // 16)
        def _(step):
            at = pl.ds(pl.multiple_of(step * 16, 16), 16)
            total = sc.acc[s, kind, at, :].astype(jnp.float32)
            for k in range(1, NB):
                total = total + got[phase, k, at, :].astype(jnp.float32)
            got[phase, 0, at, :] = total.astype(jnp.bfloat16)

        if not plan[phase] & BACK:
            part_store(phase).start()

    def d_first(phase):
        if not plan[phase] & FRONT:
            part_load(phase).wait()
        own_copy = pltpu.make_async_copy(sc.recv_z.at[phase, 0], out[phase].at[kind, core], sc.d_own.at[phase])
        own_copy.start()
        for half in range(2):
            go(partial(d_copy, phase, half, 0, True))
        own_copy.wait()

    def d_second(phase):
        for half in range(2):
            d_copy(phase, half, 0, False).wait_recv()
            for slot in (1, 2):
                go(partial(d_copy, phase, half, slot, True))

    def d_third(phase):
        for half in range(2):
            for slot in (1, 2):
                d_copy(phase, half, slot, False).wait_recv()
        go(partial(d_cross, phase, True))

    def d_last(phase):
        d_cross(phase, False).wait_recv()

    def finish():
        for phase in fronts:
            if not plan[phase] & BACK:
                part_store(phase).wait()
        for make in sends:
            make().wait_send()

    table = {-1: [] if by_kind else [partial(start_a, s) for s in range(n)]}

    def put(at, do):
        table.setdefault(at, []).append(do)

    for phase in backs:
        if not plan[phase] & FRONT:
            put(-1, lambda phase=phase: part_load(phase).start())
    for at, do in enumerate(beside):
        put(at, do)
    for s in range(n):
        put(s + ahead, partial(b_to_c, s))
        put(s + ahead + 1, partial(c_to_z, s))
        put(s, partial(a_to_b, s))
    for phase, todo in enumerate(plan):
        end = 0
        if todo & FRONT:
            end = NB * fronts.index(phase) + NB + ahead + 1
            put(end, partial(z_sum, phase))
        if todo & BACK:
            for lag, do in ((0, d_first), (1, d_second), (2, d_third), (4, d_last)):
                put(end + lag - (0 if todo & FRONT else 1), partial(do, phase))
    steps = [partial(run_all, table[at]) for at in sorted(table)]
    steps.append(finish)
    if by_kind:
        return SimpleNamespace(
            start=lambda kind: [start_a(s, (kind,)) for s in range(n)], a=a_to_b, b=b_to_c, c=c_to_z, sum=z_sum,
            take=lambda phase: part_load(phase).start(), d1=d_first, d2=d_second, d3=d_third, d4=d_last, finish=finish,
        )
    return steps


def home_scratch():
    D = pltpu.SemaphoreType.DMA
    return dict(home_send=D((2,)), home_recv=D((2,)))


def home_steps(me, rows_ref, home_ref, sc):
    band, core = me.band, me.core
    slot = lax.rem(band, 2)

    def stays(s):
        return jnp.logical_and(band // 2 == core, 2 * core + s == band)

    def copy(s):
        to = device(me.dp - core + band // 2, 2 * core + s)
        return pltpu.make_async_remote_copy(
            src_ref=rows_ref.at[s], dst_ref=home_ref.at[slot], send_sem=sc.home_send.at[s],
            recv_sem=sc.home_recv.at[slot], device_id=to, device_id_type=MESH,
        )

    def begin():
        for s in range(2):
            pl.when(stays(s))(
                lambda: pltpu.make_async_copy(
                    rows_ref.at[s], home_ref.at[slot], sc.home_recv.at[slot]
                ).start()
            )
            pl.when(jnp.logical_not(stays(s)))(lambda: copy(s).start())

    def finish():
        for s in range(2):
            pl.when(jnp.logical_not(stays(s)))(lambda: copy(s).wait_send())
        for i in range(2):
            pltpu.make_async_copy(rows_ref.at[i], home_ref.at[i], sc.home_recv.at[i]).wait()

    return begin, finish


def group_barrier(me):
    barrier = pltpu.get_barrier_semaphore()
    peers = [(me.xdp, me.band), (me.ydp, me.band), (me.sib, me.band)]
    for k in range(1, NB):
        other = lax.rem(me.band + k, NB)
        peers += [(me.dp, other), (me.sib, other)]
    for dp, band in peers:
        pl.semaphore_signal(
            barrier, inc=1, device_id=device(dp, band), device_id_type=MESH
        )
    pl.semaphore_wait(barrier, len(peers))


def reduce_refs(plan, counts, refs):
    take = iter(refs)
    grads = [[next(take) for _ in range(count)] for count in counts]

    def source(phase, b, t, h):
        if len(grads[phase]) > 1:
            return grads[phase][t].at[b, h]
        whole = grads[phase][0]
        if len(whole.shape) == 5:
            return whole.at[b, t, h]
        span = whole.shape[3] // 4
        return whole.at[b, h, :, pl.ds(pl.multiple_of(t * span, 128), span)]

    return source, [next(take) if todo == BACK else None for todo in plan]


def reduce_outs(plan, refs):
    take = iter(refs)
    out = [next(take) if todo & BACK else None for todo in plan]
    return out, [next(take) if todo == FRONT else None for todo in plan]


def reduce_shapes(plan, half, width):
    bf = jnp.bfloat16
    shapes = [jax.ShapeDtypeStruct((4, 2, half, width), bf) for todo in plan if todo & BACK]
    return shapes + [jax.ShapeDtypeStruct((half, width), bf) for todo in plan if todo == FRONT]


def small_scratch(mod_rows, bias_rows, cond_rows, cond_cols):
    D = pltpu.SemaphoreType.DMA
    f32 = jnp.float32
    return dict(
        s_core=pltpu.VMEM((mod_rows + bias_rows, 128), f32),
        s_every=pltpu.VMEM((NB, 4, mod_rows, 128), jnp.bfloat16),
        s_bias=pltpu.VMEM((3, bias_rows, 128), f32),
        s_got=pltpu.VMEM((2 + NB, bias_rows, 128), f32),
        s_flat=pltpu.VMEM((8, mod_rows, 128), f32),
        s_cond=pltpu.VMEM((NB, cond_rows, cond_cols), f32),
        s_send=D((8,)), s_recv=D((8,)), sz_send=D((2, NB)), sz_recv=D((2, NB)),
        sc_send=D((NB,)), sc_recv=D((NB,)),
    )


def small_steps(me, mods, images, small_ref, ada_ref, every_ref, bias_ref, cond_ref, sc):
    dp, band, core, px, py, kind = me.dp, me.band, me.core, me.px, me.py, me.kind
    here = lambda d: device(d, band)
    every, bias, got, cond = sc.s_every, sc.s_bias, sc.s_got, sc.s_cond
    mod_rows = every.shape[2]
    flip = lambda v: 1 - v

    def remote(src, dst, ss, rs, to):
        return pltpu.make_async_remote_copy(
            src_ref=src, dst_ref=dst, send_sem=ss, recv_sem=rs, device_id=to, device_id_type=MESH
        )

    def plain(index, src, dst, to):
        return remote(src, dst, sc.s_send.at[index], sc.s_recv.at[index], to)

    def core_copy():
        return plain(0, small_ref, sc.s_core, here(me.sib))

    def x_copies(mine):
        unit = every.at[band, kind if mine else 2 * py + flip(px)]
        return [
            plain(1, unit, unit, here(me.xdp)),
            plain(2, bias.at[0], got.at[0], here(me.xdp)),
        ]

    def y_copies(mine):
        pair = every.at[band, pl.ds(2 * (py if mine else flip(py)), 2)]
        return [
            plain(3, pair, pair, here(me.ydp)),
            plain(4, bias.at[1], got.at[1], here(me.ydp)),
        ]

    def z_copies(k, mine):
        to = device(dp, lax.rem(band + k, NB))
        block = every.at[band if mine else lax.rem(band + NB - k, NB)]
        return [
            remote(block, block, sc.sz_send.at[0, k], sc.sz_recv.at[0, k], to),
            remote(bias.at[2], got.at[2 + k], sc.sz_send.at[1, k], sc.sz_recv.at[1, k], to),
        ]

    def cond_copy(k, mine):
        to = device(dp, lax.rem(band + k, NB))
        block = cond.at[band if mine else lax.rem(band + NB - k, NB)]
        return remote(block, block, sc.sc_send.at[k], sc.sc_recv.at[k], to)

    def begin():
        core_copy().start()

    def cores():
        core_copy().wait()
        total = small_ref[...] + sc.s_core[...]
        every[band, kind] = total[:mod_rows].astype(jnp.bfloat16)
        bias[0] = total[mod_rows:]
        for copy in x_copies(True):
            copy.start()

    def over_x():
        for copy in x_copies(True):
            copy.wait_send()
        for copy in x_copies(False):
            copy.wait_recv()
        bias[1] = bias[0] + got[0]
        for copy in y_copies(True):
            copy.start()

    def over_y():
        for copy in y_copies(True):
            copy.wait_send()
        for copy in y_copies(False):
            copy.wait_recv()
        bias[2] = bias[1] + got[1]
        for k in range(1, NB):
            for copy in z_copies(k, True):
                copy.start()

    def over_z():
        for k in range(1, NB):
            for copy in z_copies(k, True):
                copy.wait_send()
            for copy in z_copies(k, False):
                copy.wait_recv()
        bias_ref[...] = bias[2] + got[3] + got[4] + got[5]
        every_ref[...] = every[...]
        flat = sc.s_flat
        for i in range(images):
            flat[i] = every[images * core + i, kind].astype(jnp.float32)
        parts = mods // 128
        lead = flat.shape[0]
        total = jnp.zeros((lead, ada_ref.shape[0]), jnp.float32)
        for r in range(parts):
            left = jnp.concatenate(
                [flat[i, r : r + 1, :] for i in range(images)]
                + [jnp.zeros((lead - images, 128), jnp.float32)]
            ).astype(jnp.bfloat16)
            total = total + lanes_dot(left, ada_ref[:, r * 128 : (r + 1) * 128])
        pad = cond.shape[2] - total.shape[1]
        cond[band] = jnp.concatenate([total, jnp.zeros((lead, pad), jnp.float32)], 1)
        for k in range(1, NB):
            cond_copy(k, True).start()

    def conditions():
        for k in range(1, NB):
            cond_copy(k, True).wait_send()
            cond_copy(k, False).wait_recv()
        cond_ref[...] = cond[...]

    return [begin, cores, over_x, over_y, over_z, conditions]


def put_lines(ref, first, values):
    for i in range(values.shape[1] // 128):
        ref[first + i : first + i + 1, :] = values[:, i * 128 : (i + 1) * 128]


def reduce_last_kernel(plan, images, band_slots, names, *refs):
    me = compass()
    (proj_ref, part_ref, attn_hbm, query_hbm, own_hbm, other_hbm, first_hbm, residual_hbm, middle_hbm, vec_ref, sums_ref,
     inner_bias_ref, ada_ref) = refs[:13]
    inner_out, first_out, home_ref, every_ref, bias_ref, cond_ref = refs[13:19]
    sc = SimpleNamespace(**dict(zip(names, refs[19:])))
    rows, width = sc.attn.shape
    lines = width // 128
    small = sc.small
    mod_rows = sc.s_every.shape[2]

    def source(phase, b, t, h):
        return proj_ref.at[b, h] if t == 3 else sc.grads.at[t, b, h]

    loads = [
        (attn_hbm, sc.attn), (query_hbm, sc.gqkv.at[:, pl.ds(0, width)]), (own_hbm, sc.gqkv.at[:, pl.ds(width, 2 * width)]),
        (other_hbm, sc.other), (first_hbm.at[:, pl.ds(0, 3 * width)], sc.first), (residual_hbm, sc.residual),
        (middle_hbm, sc.middle),
    ]

    def load(i):
        return pltpu.make_async_copy(*loads[i], sc.load_sem.at[i])

    for i in range(len(loads)):
        load(i).start()
    group_barrier(me)
    mods = MOD_BLOCKS * width
    exchange = small_steps(me, mods, images, small, ada_ref, every_ref, bias_ref, cond_ref, sc)
    depart, settle = home_steps(me, sc.tokens, home_ref, sc)
    r = reduce_steps(me, plan, source, (inner_out, first_out), (part_ref, None), (None, None), sc, (), 2, True)

    def run(*todo):
        for do, index in todo:
            do(index)

    run((r.start, 3), (r.take, 0), (r.d1, 0))
    for i in range(4):
        load(i).wait()

    sc.sums[...] = jnp.zeros_like(sc.sums)

    def add_line(index, values):
        sc.sums[index : index + 1, :] += jnp.sum(values, 0, keepdims=True)

    @pl.loop(0, rows // BLOCK)
    def _(block):
        sub = pl.ds(pl.multiple_of(block * BLOCK, BLOCK), BLOCK)
        total = sc.gqkv[sub, width:].astype(jnp.float32) + sc.other[sub, :].astype(jnp.float32)
        total = total.astype(jnp.bfloat16)
        sc.gqkv[sub, width:] = total
        add_line(1, total[:, width:].astype(jnp.float32))
        add_line(0, sc.gqkv[sub, :width].astype(jnp.float32))

    tile = width // 3
    load(4).wait()
    between = [(), ((r.d2, 0),), ()]
    for j in range(3):
        sc.back[:, j * tile : (j + 1) * tile] = lanes_dot(sc.gqkv[...], sc.first[j * tile : (j + 1) * tile, :])
        run(*between[j])
    load(5).wait()
    load(6).wait()

    @pl.loop(0, rows // BLOCK)
    def _(block):
        at = pl.multiple_of(block * BLOCK, BLOCK)
        sub = pl.ds(at, BLOCK)
        normed, inverse = normalize(sc.residual[sub, :])
        back = sc.back[sub, :]
        add_line(2, back)
        add_line(3, back * normed)
        grad = sc.middle[sub, :] + norm_back(back * (1.0 + vec_ref[1:2, :]), normed, inverse)
        per_image = band_slots // BLOCK
        to = pl.ds(pl.multiple_of(lax.rem(block, per_image) * BLOCK, BLOCK), BLOCK)
        sc.tokens[block // per_image, to, :] = grad.astype(jnp.bfloat16)

    small[...] = jnp.zeros_like(small)
    kept = [sc.sums[2:3, :], sc.sums[3:4, :]] + [sums_ref[i : i + 1, :] for i in (3, 1, 2, 0)]
    for i, values in enumerate(kept + [0.5 * vec_ref[14:15, :]]):
        put_lines(small, i * lines, values)
    at = mod_rows
    for values in (sc.sums[0:1, :], sc.sums[1:2, :], sums_ref[4:5, :], inner_bias_ref[0:1, :], sums_ref[5:6, :]):
        put_lines(small, at, values)
        at += values.shape[1] // 128
    say = lambda i: exchange[i]()
    depart()
    run((r.d3, 0))
    for t in range(3):

        @pl.loop(0, 3)
        def _(j):
            at = pl.multiple_of(t * width + j * tile, 128)
            value = rows_dot(sc.attn[...], sc.gqkv[:, pl.ds(at, tile)]).astype(jnp.bfloat16)
            to = pl.ds(pl.multiple_of(j * tile, 128), tile)
            sc.grads[t, :, :, :, to] = value.reshape(sc.grads.shape[1:4] + (tile,))

        run((r.start, t), (say, t))

    run((r.a, 0), (r.a, 1), (say, 3), (r.b, 0), (r.a, 2), (r.b, 1), (r.c, 0), (r.a, 3), (r.b, 2), (r.c, 1), (r.b, 3), (r.c, 2))
    run((r.c, 3), (say, 4), (r.sum, 1), (r.d1, 1), (r.d2, 1), (r.d3, 1), (say, 5), (r.d4, 0), (r.d4, 1))
    settle()
    r.finish()


def reduce_last(proj, part, attn_in, query, own, other, first, residual, middle, vectors, sums, inner_bias, ada_weight,
                images, band_slots, collective_id):
    plan = (BACK, FRONT | BACK)
    half, width = proj.shape[-2:]
    rows = attn_in.shape[0]
    bf, f32 = jnp.bfloat16, jnp.float32
    V = pltpu.VMEM
    mod_rows = -(-(MOD_BLOCKS + 1) * width // 2048) * 16
    bias_rows = (4 * width + inner_bias.shape[1]) // 128
    cond_cols = -(-ada_weight.shape[0] // 128) * 128
    scratch = dict(
        **reduce_scratch(plan, half, width), **small_scratch(mod_rows, bias_rows, 8, cond_cols), **home_scratch(),
        attn=V((rows, width), bf), gqkv=V((rows, 3 * width), bf), other=V((rows, 2 * width), bf),
        first=V((width, 3 * width), bf), residual=V((rows, width), f32), middle=V((rows, width), f32),
        grads=V((3, NB, 2, half, width), bf), back=V((rows, width), f32), sums=V((8, width), f32),
        tokens=V((images, band_slots, width), bf), small=V((mod_rows + bias_rows, 128), f32),
        load_sem=pltpu.SemaphoreType.DMA((7,)),
    )
    any_, vmem = pl.BlockSpec(memory_space=pl.ANY), pl.BlockSpec(memory_space=pltpu.VMEM)
    return pl.pallas_call(
        partial(reduce_last_kernel, plan, images, band_slots, tuple(scratch)),
        out_shape=reduce_shapes(plan, half, width)
        + [
            jax.ShapeDtypeStruct((images, band_slots, width), bf),
            jax.ShapeDtypeStruct((NB, 4, mod_rows, 128), bf),
            jax.ShapeDtypeStruct((bias_rows, 128), f32),
            jax.ShapeDtypeStruct((NB, 8, cond_cols), f32),
        ],
        in_specs=[any_] * 9 + [vmem] * 4,
        out_specs=[any_] * 3 + [vmem] * 3,
        scratch_shapes=list(scratch.values()),
        compiler_params=pltpu.CompilerParams(
            collective_id=collective_id, has_side_effects=True, vmem_limit_bytes=62 * 2**20
        ),
        name="reduce_last",
    )(proj, part, attn_in, query, own, other, first, residual, middle, vectors, sums, inner_bias, ada_weight)


def reduce_attend_kernel(plan, counts, band_slots, names, *refs):
    me = compass()
    at = sum(counts) + sum(1 for todo in plan if todo == BACK)
    source, parts = reduce_refs(plan, counts, refs)
    rows_ref, count_ref, q_ref, own_ref, far_ref, grad_ref, top_ref = refs[at : at + 7]
    at += 7
    out, given = reduce_outs(plan, refs[at:])
    at += len(plan)
    home_ref, dq_ref, down_ref, dfar_ref = refs[at : at + 4]
    sc = SimpleNamespace(**dict(zip(names, refs[at + 4 :])))
    qh, kh, vh, gh, stage, stage_sem = sc.qh, sc.kh, sc.vh, sc.gh, sc.stage, sc.stage_sem
    rows, width = q_ref.shape
    heads = qh.shape[0]
    group_barrier(me)
    steps = reduce_steps(me, plan, source, out, parts, given, sc)
    depart, settle = home_steps(me, rows_ref, home_ref, sc)
    steps[0]()
    depart()
    keys, plain, ones = key_tail(count_ref[0], band_slots), flat_tail(0.0), flat_tail(1.0)
    loads = [(q_ref, 0, qh, 0, ones), (grad_ref, 0, gh, 0, plain)]
    for row0, ref in ((0, own_ref), (rows, far_ref)):
        loads += [(ref, 0, kh, row0, keys), (ref, width, vh, row0, plain)]

    def load(i):
        ref, column = loads[i][:2]
        return pltpu.make_async_copy(ref.at[:, pl.ds(column, width)], stage.at[i % 2], stage_sem.at[i % 2])

    load(0).start()
    for step in steps[1:4]:
        step()
    for i, (ref, column, heads_ref, row0, tail) in enumerate(loads):
        if i + 1 < len(loads):
            load(i + 1).start()
        load(i).wait()
        pack_heads(stage.at[i % 2], 0, heads_ref, row0, rows, tail)
    rest = steps[4:]
    inside = heads // 2

    @pl.loop(0, heads)
    def _(h):
        attend_head(h, qh, kh, vh, gh, top_ref)
        for i, step in enumerate(rest[:inside]):
            pl.when(h == 2 * i)(step)

    stores = [(qh, 0, dq_ref, 0)]
    for row0, ref in ((0, down_ref), (rows, dfar_ref)):
        stores += [(kh, row0, ref, 0), (vh, row0, ref, width)]

    def store(i):
        ref, column = stores[i][2:]
        target = ref.at[:, pl.ds(column, width)]
        if ref is not dfar_ref:
            return pltpu.make_async_copy(stage.at[i % 2], target, stage_sem.at[i % 2])
        return pltpu.make_async_remote_copy(
            src_ref=stage.at[i % 2], dst_ref=target, send_sem=sc.far_send.at[i % 2],
            recv_sem=sc.far_recv.at[i % 2], device_id=device(me.sib, me.band), device_id_type=MESH,
        )

    for i, (heads_ref, row0, ref, column) in enumerate(stores):
        if i >= 2:
            store(i - 2).wait()
        unpack_heads(heads_ref, row0, rows, stage.at[i % 2], 0)
        store(i).start()
    for i in (len(stores) - 2, len(stores) - 1):
        store(i).wait()
    for step in rest[inside:]:
        step()
    settle()


def reduce_attend(plan, grads, parts, rows_out, count, query, own, far, grad, top, band_slots, collective_id):
    half, width = grads[0][0].shape[-2:]
    counts = tuple(len(phase) for phase in grads)
    rows = query.shape[0]
    heads = width // HEAD_DIM
    bf = jnp.bfloat16
    scratch = reduce_scratch(plan, half, width)
    scratch.update(
        qh=pltpu.VMEM((heads, rows, LANES), bf),
        kh=pltpu.VMEM((heads, 2 * rows, LANES), bf),
        vh=pltpu.VMEM((heads, 2 * rows, LANES), bf),
        gh=pltpu.VMEM((heads, rows, LANES), bf),
        stage=pltpu.VMEM((2, rows, width), bf),
        stage_sem=pltpu.SemaphoreType.DMA((2,)),
        far_send=pltpu.SemaphoreType.DMA((2,)),
        far_recv=pltpu.SemaphoreType.DMA((2,)),
        **home_scratch(),
    )
    any_, vmem = pl.BlockSpec(memory_space=pl.ANY), pl.BlockSpec(memory_space=pltpu.VMEM)
    smem = pl.BlockSpec(memory_space=pltpu.SMEM)
    units = [unit for phase in grads for unit in phase]
    return pl.pallas_call(
        partial(reduce_attend_kernel, plan, counts, band_slots, tuple(scratch)),
        out_shape=reduce_shapes(plan, half, width)
        + [
            jax.ShapeDtypeStruct(rows_out.shape, bf),
            jax.ShapeDtypeStruct((rows, width), bf),
            jax.ShapeDtypeStruct((rows, 2 * width), bf),
            jax.ShapeDtypeStruct((rows, 2 * width), bf),
        ],
        in_specs=[any_] * (len(units) + len(parts) + 1) + [smem] + [any_] * 4 + [vmem],
        out_specs=[any_] * (len(plan) + 4),
        scratch_shapes=list(scratch.values()),
        compiler_params=pltpu.CompilerParams(
            collective_id=collective_id, has_side_effects=True, vmem_limit_bytes=60 * 2**20
        ),
        name="reduce_attend",
    )(*units, *parts, rows_out, count, query, own, far, grad, top)


MOD_BLOCKS = 6
BLOCK = 128


def forward_scratch(half, ff, width, rows, note_rows, images):
    bf, f32 = jnp.bfloat16, jnp.float32
    D = pltpu.SemaphoreType.DMA
    heads = width // HEAD_DIM
    V = pltpu.VMEM
    return dict(
        qp=V((NB, 2, half, ff), bf), bounce_i=V((2, half, ff), bf), bounce_o=V((4, 2, half, width), bf),
        bounce_t=V((rows // images, width), bf), tok=V((images, rows // images, width), bf),
        notes=V((NB, note_rows, 128), f32), vec=V((16, width), f32),
        residual=V((rows, width), f32), attn_in=V((rows, width), bf), query=V((rows, width), bf),
        own=V((rows, 2 * width), bf), far=V((rows, 2 * width), bf), mixed=V((rows, width), bf),
        attended=V((rows, width), f32), mlp_in=V((rows, width), bf), tops=V((heads, 8, rows), f32),
        qh=V((heads, rows, LANES), bf), kh=V((heads, 2 * rows, LANES), bf), vh=V((heads, 2 * rows, LANES), bf),
        z_send=D((3, 2)), z_recv=D((3, NB)), f_send=D((3, NB)), a_send=D((9, 2)), a_recv=D((9, 2)), b_send=D((9, 2, 2)), b_recv=D((9, 2, 2)),
        c_send=D((9,)), c_recv=D((9,)), t_send=D((2, 2)), t_recv=D((2, 2)), m_send=D((2, 2)), m_recv=D((NB,)),
        local=D((4,)), kv_send=D((1,)), kv_recv=D((1,)), done=D((12,)),
    )


def gather_steps(me, width, ins, outs, tok_in, tok_out, cot_in, cot_out, note_in, note_out, sc):
    dp, band, core, px, py, kind = me.dp, me.band, me.core, me.px, me.py, me.kind
    base = dp - core
    dev = lambda d, b: device(d, b)
    here = lambda d: dev(d, band)
    flip = lambda v: 1 - v
    low = band < 2
    bands = (band + 1 - 2 * lax.rem(band, 2), jnp.where(low, 2, 1), jnp.where(low, 3, 0))
    order = [(ph, b) for ph in range(3) for b in bands]
    inside = jnp.logical_or(band == 1, band == 2)
    sends = []

    def remote(src, dst, ss, rs, to):
        return pltpu.make_async_remote_copy(
            src_ref=src, dst_ref=dst, send_sem=ss, recv_sem=rs, device_id=to, device_id_type=MESH
        )

    def go(make):
        for copy in make():
            copy.start()
        sends.append(make)

    size = ins[0].shape[1]
    cut = size // 32 * 16
    whole, spans = pl.ds(0, size), (pl.ds(0, cut), pl.ds(cut, size - cut))

    def cols(t, n=1):
        return pl.ds(pl.multiple_of(t * width, 128), n * width)

    def unit(ph, b, t, h, span=whole):
        return outs[ph].at[b, t, h, span] if ph == 2 else outs[ph].at[b, h, span, cols(t)]

    def pair(ph, b, h, y, span):
        return outs[ph].at[b, pl.ds(2 * y, 2), h, span] if ph == 2 else outs[ph].at[b, h, span, cols(2 * y, 2)]

    def row(ph, b, h):
        return outs[ph].at[b, :, h] if ph == 2 else outs[ph].at[b, h]

    def own_z(ph, up):
        src = ins[ph].at[kind, core] if ph == 2 else ins[ph].at[core, :, cols(kind)]
        return remote(
            src, unit(ph, band, kind, core), sc.z_send.at[ph, up], sc.z_recv.at[ph, band],
            dev(dp, band - 1 + 2 * up),
        )

    def pass_z(s):
        ph, b = order[s]
        u = unit(ph, b, kind, core)
        return remote(
            u, u, sc.f_send.at[ph, b], sc.z_recv.at[ph, b], dev(dp, jnp.where(b < band, band + 1, band - 1))
        )

    def a_copy(s, half, mine):
        ph, b = order[s]
        near = 2 * py + flip(px) if half == 0 else 2 * flip(py) + px
        u = unit(ph, b, kind if mine else near, core, spans[half])
        return remote(u, u, sc.a_send.at[s, half], sc.a_recv.at[s, half], here(me.xdp if half == 0 else me.ydp))

    def b_copies(s, half, mine):
        ph, b = order[s]
        if half == 0:
            u = pair(ph, b, core, py if mine else flip(py), spans[half])
            return [remote(u, u, sc.b_send.at[s, half, 0], sc.b_recv.at[s, half, 0], here(me.ydp))]
        copies = []
        for j in range(2):
            u = unit(ph, b, 2 * j + (px if mine else flip(px)), core, spans[half])
            copies.append(remote(u, u, sc.b_send.at[s, half, j], sc.b_recv.at[s, half, j], here(me.xdp)))
        return copies

    def c_copy(s, mine):
        ph, b = order[s]
        u = row(ph, b, core if mine else flip(core))
        return remote(u, u, sc.c_send.at[s], sc.c_recv.at[s], here(me.sib))

    def z_start(ph):
        pl.when(band < NB - 1)(lambda: own_z(ph, 1).start())
        pl.when(band > 0)(lambda: own_z(ph, 0).start())

    def z_wait(s):
        ph, b = order[s]
        u = unit(ph, b, kind, core)
        remote(u, u, sc.f_send.at[ph, b], sc.z_recv.at[ph, b], here(dp)).wait_recv()
        pl.when(inside)(lambda: pass_z(s).start())
        for half in range(2):
            go(lambda half=half: [a_copy(s, half, True)])

    def a_wait(s):
        for half in range(2):
            a_copy(s, half, False).wait_recv()
            go(partial(b_copies, s, half, True))

    def b_wait(s):
        for half in range(2):
            for copy in b_copies(s, half, False):
                copy.wait_recv()
        go(lambda: [c_copy(s, True)])

    def c_wait(s):
        c_copy(s, False).wait_recv()

    slot = lax.rem(band, 2)

    def image_copy(which, src, dst, i):
        to = dev(base + band // 2, 2 * core + i)
        return remote(src.at[i], dst.at[slot], sc.t_send.at[which, i], sc.t_recv.at[which, slot], to)

    def at_home(i):
        return jnp.logical_and(band // 2 == core, 2 * core + i == band)

    def move(which, src, dst, bounce=None):
        for i in range(2):

            @pl.when(at_home(i))
            def _():
                if bounce is None:
                    pltpu.make_async_copy(src.at[i], dst.at[slot], sc.t_recv.at[which, slot]).start()
                else:
                    inward = pltpu.make_async_copy(src.at[i], bounce, sc.local.at[3])
                    inward.start()
                    inward.wait()
                    pltpu.make_async_copy(bounce, dst.at[slot], sc.t_recv.at[which, slot]).start()

            @pl.when(jnp.logical_not(at_home(i)))
            def _():
                image_copy(which, src, dst, i).start()

    def move_wait(which, src, dst):
        for i in range(2):

            @pl.when(jnp.logical_not(at_home(i)))
            def _():
                image_copy(which, src, dst, i).wait_send()

        for s in range(2):
            pltpu.make_async_copy(dst.at[s], dst.at[s], sc.t_recv.at[which, s]).wait()

    def note_copy(i, c):
        return remote(
            note_in.at[i], note_out.at[band], sc.m_send.at[i, c], sc.m_recv.at[band],
            dev(base + c, 2 * core + i),
        )

    def note_home(i, c):
        return jnp.logical_and(c == core, 2 * core + i == band)

    def begin():
        for i in range(2):
            for c in range(2):

                @pl.when(note_home(i, c))
                def _():
                    pltpu.make_async_copy(note_in.at[i], note_out.at[band], sc.m_recv.at[band]).start()

                @pl.when(jnp.logical_not(note_home(i, c)))
                def _():
                    note_copy(i, c).start()

        z_start(0)
        for ph, dst in enumerate((outs[0].at[band], sc.bounce_i, sc.bounce_o)):
            pltpu.make_async_copy(ins[ph], dst, sc.local.at[ph]).start()

    def arrived():
        for i in range(2):
            for c in range(2):

                @pl.when(jnp.logical_not(note_home(i, c)))
                def _():
                    note_copy(i, c).wait_send()

        for b in range(NB):
            pltpu.make_async_copy(note_in.at[0], note_out.at[b], sc.m_recv.at[b]).wait()
        move_wait(0, tok_in, tok_out)

    def place():
        for ph, dst in ((1, sc.bounce_i), (2, sc.bounce_o)):
            pltpu.make_async_copy(ins[ph], dst, sc.local.at[ph]).wait()
            pltpu.make_async_copy(dst, outs[ph].at[band], sc.local.at[ph]).start()

    def first_here():
        pltpu.make_async_copy(ins[0], outs[0].at[band], sc.local.at[0]).wait()

    def finish():
        for ph, src in ((1, sc.bounce_i), (2, sc.bounce_o)):
            pltpu.make_async_copy(src, outs[ph].at[band], sc.local.at[ph]).wait()
        move_wait(1, cot_in, cot_out)
        for ph in range(3):
            pl.when(band < NB - 1)(lambda: own_z(ph, 1).wait_send())
            pl.when(band > 0)(lambda: own_z(ph, 0).wait_send())
        for s in range(len(order)):
            pl.when(inside)(lambda: pass_z(s).wait_send())
        for make in sends:
            for copy in make():
                copy.wait_send()

    def images(which):
        if which == 0:
            move(0, tok_in, tok_out)
        else:
            move(1, cot_in, cot_out, sc.bounce_t)

    return SimpleNamespace(
        i=images, s=z_start,
        begin=begin, arrived=arrived, place=place, first_here=first_here, finish=finish,
        z=z_wait, a=a_wait, b=b_wait, c=c_wait,
    )


def forward_kernel(names, band_slots, *refs):
    me = compass()
    qp_in, inner_in, outer_in, tok_in, cot_in, note_in, table_ref = refs[:7]
    (qp_out, inner_out, outer_out, cot_out, vec_out, residual_out, attn_out, query_out, own_out, far_out,
     tops_out, mixed_out, attended_out, mlp_out) = refs[7:21]
    sc = SimpleNamespace(**dict(zip(names, refs[21:])))
    rows, width = sc.residual.shape
    heads = width // HEAD_DIM
    core = me.core
    qp, tok, notes, vec = sc.qp, sc.tok, sc.notes, sc.vec

    group_barrier(me)
    g = gather_steps(
        me, width, (qp_in, inner_in, outer_in), (qp, inner_out, outer_out), tok_in, tok, cot_in, cot_out,
        note_in, notes, sc,
    )
    saves = []

    def save(src, dst):
        copy = pltpu.make_async_copy(src, dst, sc.done.at[len(saves)])
        copy.start()
        saves.append(copy)

    def run(*words):
        for do, index in words:
            do(index)

    g.begin()
    g.place()
    run((g.z, 0), (g.z, 1), (g.i, 0), (g.a, 0), (g.a, 1), (g.z, 2), (g.s, 1), (g.b, 0), (g.b, 1), (g.a, 2), (g.z, 3), (g.c, 0), (g.c, 1), (g.z, 4), (g.b, 2), (g.a, 3))
    g.arrived()
    spread_notes(notes, vec, width)
    grid_rows = notes[0, 63:64, 0:1]
    grid_cols = notes[0, 63:64, 1:2]
    band_rows = jnp.floor(grid_rows * 0.25)
    valid_count = (band_rows * grid_cols).astype(jnp.int32)
    lane = lax.broadcasted_iota(jnp.int32, (1, width), 1)
    vec[15:16, :] = jnp.where(lane == 0, band_rows * grid_cols, 0.0)
    save(vec, vec_out)

    @pl.loop(0, rows // BLOCK)
    def _(step):
        at = pl.multiple_of(step * BLOCK, BLOCK)
        sub = pl.ds(at, BLOCK)
        per_image = band_slots // BLOCK
        within = (
            lax.rem(step, per_image) * BLOCK + lax.broadcasted_iota(jnp.int32, (BLOCK, 1), 0)
        ).astype(jnp.float32)
        down = jnp.floor((within + 0.5) / grid_cols)
        place = (2 * core + step // per_image).astype(jnp.float32)
        picks = []
        for index in (place * band_rows + down, within - down * grid_cols):
            lanes = lax.broadcasted_iota(jnp.int32, (BLOCK, 128), 1).astype(jnp.float32)
            pick = jnp.where(lanes == index, 1.0, 0.0).astype(jnp.bfloat16)
            part = [jnp.dot(pick, table_ref[i], preferred_element_type=jnp.float32) for i in range(3)]
            picks.append(part[0] + (part[1] + part[2]))
        token = tok[step // per_image, pl.ds(lax.rem(step, per_image) * BLOCK, BLOCK), :]
        residual = token.astype(jnp.float32) + jnp.concatenate(picks, 1)
        sc.residual[sub, :] = residual
        normed = normalize(residual)[0]
        sc.attn_in[sub, :] = (normed * (1.0 + vec[1:2, :]) + vec[0:1, :]).astype(jnp.bfloat16)

    save(sc.residual, residual_out)
    save(sc.attn_in, attn_out)
    g.first_here()
    run((g.c, 2))
    save(qp, qp_out)
    tile = width // 3
    full = NB * 2 * qp.shape[2]

    def product(left_ref, first, step):
        at = pl.ds(pl.multiple_of(first + step * tile, 128), tile)
        return jnp.dot(
            left_ref[...], qp[:, :, :, at].reshape(full, tile), preferred_element_type=jnp.float32
        )

    def here(step):
        return pl.ds(pl.multiple_of(step * tile, 128), tile)

    @pl.loop(0, 3)
    def _(step):
        sc.own[:, here(step)] = product(sc.attn_in, width, step).astype(jnp.bfloat16)

    run((g.z, 5), (g.s, 2))

    @pl.loop(0, 3)
    def _(step):
        value = product(sc.attn_in, 2 * width, step) + vec[7:8, here(step)]
        sc.own[:, here(step + 3)] = value.astype(jnp.bfloat16)

    swap = pltpu.make_async_remote_copy(
        src_ref=sc.own, dst_ref=sc.far, send_sem=sc.kv_send.at[0], recv_sem=sc.kv_recv.at[0],
        device_id=device(me.sib, me.band), device_id_type=MESH,
    )
    swap.start()
    run((g.a, 4), (g.b, 3))

    @pl.loop(0, 3)
    def _(step):
        value = product(sc.attn_in, 0, step) + vec[6:7, here(step)]
        sc.query[:, here(step)] = value.astype(jnp.bfloat16)

    save(sc.query, query_out)
    save(sc.own, own_out)
    run((g.a, 5), (g.b, 4), (g.c, 3), (g.z, 6))
    qh, kh, vh = sc.qh, sc.kh, sc.vh
    keys, plain = key_tail(valid_count, band_slots), flat_tail(0.0)
    pack_heads(sc.query, 0, qh, 0, rows, flat_tail(1.0))
    pack_heads(sc.own, 0, kh, 0, rows, keys)
    pack_heads(sc.own, width, vh, 0, rows, plain)
    swap.wait()
    save(sc.far, far_out)
    pack_heads(sc.far, 0, kh, rows, rows, keys)
    pack_heads(sc.far, width, vh, rows, rows, plain)
    beside = {
        0: ((g.z, 7), (g.b, 5), (g.c, 4)), 2: ((g.a, 6), (g.z, 8), (g.i, 1)), 4: ((g.a, 7), (g.b, 6), (g.c, 5)), 7: ((g.a, 8), (g.b, 7), (g.c, 6)), 10: ((g.b, 8), (g.c, 7)),
        13: ((g.c, 8),),
    }

    @pl.loop(0, heads)
    def _(h):
        attend_block(h, qh, kh, vh, sc.tops)
        for i, words in beside.items():
            pl.when(h == i)(partial(run, *words))

    unpack_heads(qh, 0, rows, sc.mixed, 0)
    save(sc.tops, tops_out)
    save(sc.mixed, mixed_out)

    @pl.loop(0, 3)
    def _(step):
        sc.attended[:, here(step)] = product(sc.mixed, 3 * width, step) + vec[8:9, here(step)]

    save(sc.attended, attended_out)

    @pl.loop(0, rows // BLOCK)
    def _(step):
        sub = pl.ds(pl.multiple_of(step * BLOCK, BLOCK), BLOCK)
        middle = sc.residual[sub, :] + vec[2:3, :] * sc.attended[sub, :]
        normed = normalize(middle)[0]
        sc.mlp_in[sub, :] = (normed * (1.0 + vec[4:5, :]) + vec[3:4, :]).astype(jnp.bfloat16)

    save(sc.mlp_in, mlp_out)
    g.finish()
    for copy in saves:
        copy.wait()


NOTE_COND, NOTE_GRID, NOTE_BIAS = 54, 63, 64


def spread_notes(notes, vec, width):
    lines = width // 128
    share = notes.shape[0]
    total = notes[0, 0:NOTE_GRID, :] + 0.0
    for b in range(1, share):
        total = total + notes[b, 0:NOTE_GRID, :]

    def flat(block, first):
        return jnp.concatenate([block[first + i : first + i + 1, :] for i in range(lines)], 1)

    for index in range(MOD_BLOCKS):
        vec[index : index + 1, :] = flat(total, index * lines)
    small = width // share
    for index in range(4):
        parts = []
        for b in range(share):
            first = NOTE_BIAS + 3 * index
            for i in range(3):
                parts.append(notes[b, first + i : first + i + 1, : min(128, small - 128 * i)])
        vec[6 + index : 7 + index, :] = jnp.concatenate(parts, 1)
    for b in range(share):
        block = notes[b, NOTE_BIAS + 12 : NOTE_BIAS + 12 + lines, :]
        vec[10 + b : 11 + b, :] = flat(block, 0)
    vec[14:15, :] = flat(notes[0, NOTE_COND : NOTE_COND + lines, :], 0)


def forward_block(qp, inner, outer, tok, cot, note, table):
    half, ff = qp.shape[0] // 2, qp.shape[1]
    images, band_slots, width = tok.shape
    rows = images * band_slots
    heads = width // HEAD_DIM
    bf, f32 = jnp.bfloat16, jnp.float32
    S = jax.ShapeDtypeStruct
    qp, inner = qp.reshape(2, half, ff), inner.reshape(2, half, ff)
    outer = outer.reshape(4, 2, half, width)
    scratch = forward_scratch(half, ff, width, rows, note.shape[1], images)
    any_ = pl.BlockSpec(memory_space=pl.ANY)
    return pl.pallas_call(
        partial(forward_kernel, tuple(scratch), band_slots),
        out_shape=[
            S((NB, 2, half, ff), bf), S((NB, 2, half, ff), bf), S((NB, 4, 2, half, width), bf), S(cot.shape, bf),
            S((16, width), f32), S((rows, width), f32), S((rows, width), bf), S((rows, width), bf),
            S((rows, 2 * width), bf), S((rows, 2 * width), bf), S((heads, 8, rows), f32), S((rows, width), bf),
            S((rows, width), f32), S((rows, width), bf),
        ],
        in_specs=[any_] * 6 + [pl.BlockSpec(memory_space=pltpu.VMEM)],
        out_specs=[any_] * 14,
        scratch_shapes=list(scratch.values()),
        compiler_params=pltpu.CompilerParams(
            collective_id=0, has_side_effects=True, vmem_limit_bytes=60 * 2**20
        ),
        name="forward_block",
    )(qp, inner, outer, tok, cot, note, table)


GELU_SCALE = 0.7978845608028654


def mlp_kernel(band_slots, mlp_ref, inner_ref, outer_ref, vec_ref, bias_ref, residual_ref, attended_ref, cot_ref,
               mixed_ref, proj_ref, out_ref, middle_ref, back_ref, proj_grad_ref, outer_grad_ref, inner_grad_ref,
               bias_grad_ref, sums_ref, out_acc, back_acc, grad_mlp):
    step = pl.program_id(0)
    rows = mlp_ref.shape[0]
    low = lambda value: value.astype(jnp.bfloat16)
    line = lambda index: vec_ref[index : index + 1, :]

    def grad_out(at):
        slot = lax.rem(at + lax.broadcasted_iota(jnp.int32, (BLOCK, 1), 0), band_slots)
        valid = jnp.where(slot.astype(jnp.float32) < vec_ref[15:16, 0:1], 1.0, 0.0)
        return cot_ref[pl.ds(at, BLOCK), :].astype(jnp.float32) * valid

    def add_line(index, values):
        sums_ref[index : index + 1, :] += jnp.sum(values, 0, keepdims=True)

    @pl.when(step == 0)
    def _():
        sums_ref[...] = jnp.zeros_like(sums_ref)

        @pl.loop(0, rows // BLOCK)
        def _(block):
            at = pl.multiple_of(block * BLOCK, BLOCK)
            grad = low(line(5) * grad_out(at))
            grad_mlp[pl.ds(at, BLOCK), :] = grad
            add_line(5, grad.astype(jnp.float32))
            out_acc[pl.ds(at, BLOCK), :] = jnp.zeros((BLOCK, out_acc.shape[1]), jnp.float32)
            back_acc[pl.ds(at, BLOCK), :] = jnp.zeros((BLOCK, out_acc.shape[1]), jnp.float32)

    inner, outer, grad = inner_ref[...], outer_ref[...], grad_mlp[...]
    pre = jnp.dot(mlp_ref[...], inner, preferred_element_type=jnp.float32) + bias_ref[...]
    grad_hidden = lanes_dot(grad, outer)
    square = pre * pre
    bend = jnp.tanh(GELU_SCALE * (pre * (1.0 + 0.044715 * square)))
    rise = 0.5 * (1.0 + bend)
    hidden = low(pre * rise)
    slope = rise + (0.5 * pre) * (1.0 - bend * bend) * (GELU_SCALE * (1.0 + 0.134145 * square))
    grad_pre = low(slope * grad_hidden)
    out_acc[...] += jnp.dot(hidden, outer, preferred_element_type=jnp.float32)
    outer_grad_ref[...] = low(rows_dot(hidden, grad))
    back_acc[...] += lanes_dot(grad_pre, inner)
    inner_grad_ref[...] = low(rows_dot(mlp_ref[...], grad_pre))
    bias_grad_ref[...] = jnp.broadcast_to(
        jnp.sum(grad_pre.astype(jnp.float32), 0, keepdims=True), bias_grad_ref.shape
    )

    @pl.when(step == pl.num_programs(0) - 1)
    def _():
        @pl.loop(0, rows // BLOCK)
        def _(block):
            at = pl.multiple_of(block * BLOCK, BLOCK)
            sub = pl.ds(at, BLOCK)
            attended = attended_ref[sub, :]
            middle = residual_ref[sub, :] + line(2) * attended
            normed, inverse = normalize(middle)
            mlp_out = out_acc[sub, :] + line(9)
            out_ref[sub, :] = low(middle + line(5) * mlp_out)
            grad_block = grad_out(at)
            add_line(0, grad_block * mlp_out)
            back = back_acc[sub, :]
            add_line(1, back)
            add_line(2, back * normed)
            grad_middle = grad_block + norm_back(back * (1.0 + line(4)), normed, inverse)
            middle_ref[sub, :] = grad_middle
            add_line(3, grad_middle * attended)
            grad_attended = low(line(2) * grad_middle)
            add_line(4, grad_attended.astype(jnp.float32))
            grad_mlp[sub, :] = grad_attended

        proj_grad_ref[...] = low(rows_dot(mixed_ref[...], grad_mlp[...]))
        back_ref[...] = low(lanes_dot(grad_mlp[...], proj_ref[...]))


def feed_forward(mlp_in, inner, outer, vectors, inner_bias, residual, attended, cotangent, mixed, first, band_slots):
    rows, width = mlp_in.shape
    hidden = inner.shape[1]
    tile = 512
    bf, f32 = jnp.bfloat16, jnp.float32
    S = jax.ShapeDtypeStruct
    keep = lambda *shape: pl.BlockSpec(shape, lambda j: (0,) * len(shape))
    return pl.pallas_call(
        partial(mlp_kernel, band_slots),
        grid=(hidden // tile,),
        out_shape=[
            S((rows, width), bf), S((rows, width), f32), S((rows, width), bf), S((width, width), bf),
            S((hidden, width), bf), S((width, hidden), bf), S((8, hidden), f32), S((8, width), f32),
        ],
        in_specs=[
            keep(rows, width), pl.BlockSpec((width, tile), lambda j: (0, j)), pl.BlockSpec((tile, width), lambda j: (j, 0)),
            keep(16, width), pl.BlockSpec((1, tile), lambda j: (0, j)), keep(rows, width), keep(rows, width),
            keep(rows, width), keep(rows, width), pl.BlockSpec((width, width), lambda j: (0, 3)),
        ],
        out_specs=[
            keep(rows, width), keep(rows, width), keep(rows, width), keep(width, width),
            pl.BlockSpec((tile, width), lambda j: (j, 0)), pl.BlockSpec((width, tile), lambda j: (0, j)),
            pl.BlockSpec((8, tile), lambda j: (0, j)), keep(8, width),
        ],
        scratch_shapes=[pltpu.VMEM((rows, width), f32), pltpu.VMEM((rows, width), f32), pltpu.VMEM((rows, width), bf)],
        compiler_params=pltpu.CompilerParams(vmem_limit_bytes=60 * 2**20),
        cost_estimate=pl.CostEstimate(
            flops=12 * rows * width * hidden, bytes_accessed=8 * width * hidden + 24 * rows * width,
            transcendentals=rows * hidden,
        ),
        name="feed_forward",
    )(mlp_in, inner, outer, vectors, inner_bias, residual, attended, cotangent, mixed, first)


def position_parts(width):
    quarter = width // 4
    frequency = 10000.0 ** (-np.arange(quarter, dtype=np.float32) / np.float32(quarter))
    angles = (np.arange(128, dtype=np.float32)[:, None] * frequency.astype(np.float32)).astype(np.float64)
    left = np.concatenate([np.sin(angles), np.cos(angles)], -1).astype(np.float32)
    parts = []
    for _ in range(3):
        parts.append(left.astype(jnp.bfloat16))
        left = left - parts[-1].astype(np.float32)
    return jnp.asarray(np.stack(parts))


def over_groups(piece, dp_count):
    if dp_count == 8:
        return piece
    groups = [[rank + 8 * group for group in range(dp_count // 8)] for rank in range(8)]
    return lax.psum(piece.astype(jnp.float32), "dp", axis_index_groups=groups)


def every_group(piece, dp_count):
    if dp_count == 8:
        return piece[None]
    groups = [[rank + 8 * group for group in range(dp_count // 8)] for rank in range(8)]
    return lax.all_gather(piece, "dp", axis_index_groups=groups)


def own_piece(vector, count, band_place):
    return lax.dynamic_slice_in_dim(vector, band_place * count, count, 0)


def body(
    tokens,
    condition,
    patch_grid,
    ada_weight,
    ada_bias,
    qkv_weight,
    query_bias,
    value_bias,
    proj_weight,
    proj_bias,
    inner_weight,
    inner_bias,
    outer_weight,
    outer_bias,
    cotangent,
):
    dp_count = lax.axis_size("dp")
    band_count = lax.axis_size("band")
    images, band_slots, width = tokens.shape
    band = lax.axis_index("band")
    dp = lax.axis_index("dp")
    core = lax.rem(dp, 2)
    hidden = inner_weight.shape[1]
    part_rows = qkv_weight.shape[0]

    condition_f = condition.astype(jnp.float32)
    activated = jax.nn.silu(condition_f).astype(jnp.bfloat16)
    own_activated = lax.dynamic_slice_in_dim(activated, band * part_rows, part_rows, 1)
    share = jnp.dot(own_activated, ada_weight, preferred_element_type=jnp.float32)
    share = share + lax.dynamic_update_slice_in_dim(
        jnp.zeros((ada_weight.shape[1],), jnp.float32),
        ada_bias.astype(jnp.float32),
        band * ada_bias.shape[0],
        0,
    )
    mod_count = share.shape[1]
    lines = lambda vector: jnp.pad(
        vector.astype(jnp.float32), [(0, 0)] * (vector.ndim - 1) + [(0, -vector.shape[-1] % 128)]
    )
    spread = lambda vector: jnp.broadcast_to(lines(vector), (images, -(-vector.shape[0] // 128) * 128))
    note = jnp.concatenate(
        [share, condition_f, lines(patch_grid)]
        + [spread(bias) for bias in (query_bias, value_bias, proj_bias, outer_bias, inner_bias)],
        1,
    )
    note = jnp.pad(note, ((0, 0), (0, -note.shape[1] % 1024))).reshape(images, -1, 128)
    first_weight = jnp.concatenate([qkv_weight, proj_weight], 1)
    (first_full, inner_full, outer_full, cotangent_here, vectors, residual, attn_in, query_rows, key_value,
     other_key_value, tops, mixed_rows, attended, mlp_in) = forward_block(
        first_weight, inner_weight, outer_weight, tokens, cotangent, note, position_parts(width)
    )
    first_full = first_full.reshape(width, -1)
    inner_full = inner_full.reshape(width, hidden)
    outer_full = outer_full.reshape(hidden, width)
    valid_count = vectors[15, :1].astype(jnp.int32)
    rows = images * band_slots
    inner_bias_row = vectors[10:14].reshape(1, -1)
    (block_out, grad_middle, grad_mixed, grad_proj, grad_outer, grad_inner, grad_inner_bias, sums) = feed_forward(
        mlp_in, inner_full, outer_full, vectors, inner_bias_row, residual, attended,
        cotangent_here.reshape(rows, width), mixed_rows, first_full, band_slots,
    )
    blocks = (band_count, 2, part_rows // 2, width)
    grad_outer = grad_outer.reshape(band_count, 4, 2, part_rows // 2, width)
    grad_inner = grad_inner.reshape(band_count, 2, part_rows // 2, hidden)
    outer_sum, inner_part, block_home, grad_query, own_terms, other_terms = reduce_attend(
        (FRONT | BACK, FRONT), [[grad_outer], [grad_inner]], [], block_out.reshape(images, band_slots, width), valid_count, query_rows, key_value, other_key_value, grad_mixed, tops,
        band_slots, 1,
    )
    inner_sum, first_sum, tokens_home, every, bias_grads, grad_act = reduce_last(
        grad_proj.reshape(blocks), inner_part, attn_in, grad_query, own_terms, other_terms, first_full, residual,
        grad_middle, vectors, sums, grad_inner_bias, ada_weight, images, band_slots, 2,
    )
    tokens_home = tokens_home.astype(jnp.float32)
    every = every_group(every, dp_count)
    bias_grads = over_groups(bias_grads, dp_count).reshape(-1)
    every = jnp.swapaxes(every, 1, 2).reshape(dp_count * images, -1)
    every_mod = every[:, :mod_count]
    every_condition = every[:, mod_count : mod_count + width]
    every_activated = jax.nn.silu(every_condition.astype(jnp.float32)).astype(jnp.bfloat16)
    every_activated = lax.dynamic_slice_in_dim(every_activated, band * part_rows, part_rows, 1)
    grad_ada = rows_dot(every_activated, every_mod)
    grad_ada_bias = own_piece(jnp.sum(every_mod.astype(jnp.float32), 0), ada_bias.shape[0], band)
    grad_act = jnp.swapaxes(grad_act[:, :images, :part_rows], 0, 1).reshape(images, width)
    grad_condition = jax.vjp(jax.nn.silu, condition_f)[1](grad_act)[0]

    def side_by_side(units):
        return jnp.concatenate([unit.reshape(part_rows, width) for unit in units], 1).astype(jnp.float32)

    first_sum, inner_sum, outer_sum = [
        over_groups(piece, dp_count) for piece in (first_sum, inner_sum, outer_sum)
    ]
    qkv_sum = side_by_side([first_sum[t] for t in range(3)])
    proj_sum = first_sum[3].reshape(part_rows, width).astype(jnp.float32)
    inner_sum = side_by_side([inner_sum[t] for t in range(4)])
    outer_sum = outer_sum.reshape(4 * part_rows, width).astype(jnp.float32)
    bias_parts = []
    at = 0
    for piece in (query_bias, value_bias, proj_bias, inner_bias, outer_bias):
        whole = piece.shape[0] * band_count
        bias_parts.append(own_piece(bias_grads[at : at + whole], piece.shape[0], band))
        at += whole
    return (
        block_home,
        tokens_home,
        grad_condition,
        grad_ada,
        grad_ada_bias,
        qkv_sum,
        bias_parts[0],
        bias_parts[1],
        proj_sum,
        bias_parts[2],
        inner_sum,
        bias_parts[3],
        outer_sum,
        bias_parts[4],
    )


def solution(mesh):
    placed = (
        P("dp", "band", None),
        P("dp", None),
        P("dp", None),
        P("band", None),
        P("band"),
        P("band", None),
        P("band"),
        P("band"),
        P("band", None),
        P("band"),
        P("band", None),
        P("band"),
        P("band", None),
        P("band"),
        P("dp", "band", None),
    )
    return jax.shard_map(
        body,
        mesh=mesh,
        in_specs=placed,
        out_specs=(
            P("dp", "band", None),
            P("dp", "band", None),
            P("dp", None),
            P("band", None),
            P("band"),
            P("band", None),
            P("band"),
            P("band"),
            P("band", None),
            P("band"),
            P("band", None),
            P("band"),
            P("band", None),
            P("band"),
        ),
        check_vma=False,
    )
```

```python
from functools import partial
from types import SimpleNamespace

import jax
import jax.numpy as jnp
import numpy as np
from jax import lax
from jax.experimental import pallas as pl
from jax.experimental.pallas import tpu as pltpu
from jax.sharding import PartitionSpec as P

HEAD_DIM = 72


MESH = pl.DeviceIdType.MESH
NB = 4


def device(dp, band):
    return {"dp": dp, "band": band}


def normalize(values):
    average = jnp.mean(values, -1, keepdims=True)
    centered = values - average
    variance = jnp.mean(centered * centered, -1, keepdims=True)
    inverse = lax.rsqrt(variance + 1e-06)
    return (centered * inverse, inverse)


def norm_back(grad_normed, normed, inverse):
    first = jnp.mean(grad_normed, -1, keepdims=True)
    second = jnp.mean(grad_normed * normed, -1, keepdims=True)
    return inverse * (grad_normed - first - normed * second)


LANES = 128
PACK_ROWS = 128


def pack_heads(source, first, heads_ref, row0, rows, tail):
    heads = heads_ref.shape[0]

    @pl.loop(0, rows // PACK_ROWS)
    def _(step):
        at = pl.multiple_of(step * PACK_ROWS, PACK_ROWS)
        block = source[pl.ds(at, PACK_ROWS), first : first + heads * HEAD_DIM]
        end = tail(at)
        for h in range(heads):
            part = block[:, h * HEAD_DIM : (h + 1) * HEAD_DIM]
            heads_ref[h, pl.ds(row0 + at, PACK_ROWS), :] = jnp.concatenate([part, end], 1)


def unpack_heads(heads_ref, row0, rows, target, first):
    heads = heads_ref.shape[0]

    @pl.loop(0, rows // PACK_ROWS)
    def _(step):
        at = pl.multiple_of(step * PACK_ROWS, PACK_ROWS)
        parts = [heads_ref[h, pl.ds(row0 + at, PACK_ROWS), :][:, :HEAD_DIM] for h in range(heads)]
        target[pl.ds(at, PACK_ROWS), first : first + heads * HEAD_DIM] = jnp.concatenate(parts, 1)


def flat_tail(value):
    def tail(at):
        lane = lax.broadcasted_iota(jnp.int32, (PACK_ROWS, LANES - HEAD_DIM), 1)
        return jnp.where(lane == 0, value, 0.0).astype(jnp.bfloat16)

    return tail


def key_tail(valid_count, band_slots):
    def tail(at):
        shape = (PACK_ROWS, LANES - HEAD_DIM)
        lane = lax.broadcasted_iota(jnp.int32, shape, 1)
        slot = lax.rem(at + lax.broadcasted_iota(jnp.int32, shape, 0), band_slots)
        return jnp.where(jnp.logical_and(lane == 0, slot >= valid_count), -1e30, 0.0).astype(jnp.bfloat16)

    return tail


def lanes_dot(left, right):
    return lax.dot_general(left, right, (((1,), (1,)), ((), ())), preferred_element_type=jnp.float32)


def rows_dot(left, right):
    return lax.dot_general(left, right, (((0,), (0,)), ((), ())), preferred_element_type=jnp.float32)


SCORE_SCALE = HEAD_DIM ** (-0.5)


def attend_block(h, qh, kh, vh, top_ref):
    rows = qh.shape[1]
    for block in range(2):
        at = pl.ds(block * rows // 2, rows // 2)
        scores = lanes_dot(kh[h], qh[h, at, :]) * SCORE_SCALE
        top = jnp.max(scores, 0, keepdims=True)
        weights = jnp.exp(scores - top)
        total = jnp.sum(weights, 0, keepdims=True)
        low = (weights * (1.0 / total)).astype(jnp.bfloat16)
        mixed = rows_dot(vh[h], low)
        qh[h, at, :] = jnp.transpose(mixed).astype(jnp.bfloat16)
        top_ref[h, :, at] = jnp.broadcast_to(top + jnp.log(total), (8, rows // 2))


def attend_head(h, qh, kh, vh, gh, top_ref):
    query = qh[h]
    key = kh[h]
    grad = gh[h]
    probs = jnp.exp(lanes_dot(key, query) * SCORE_SCALE - top_ref[h, 0:1, :])
    grad_probs = lanes_dot(vh[h], grad)
    inner = jnp.sum(probs * grad_probs, 0, keepdims=True)
    grad_scores = (probs * (grad_probs - inner)).astype(jnp.bfloat16)
    vh[h] = jnp.dot(
        probs.astype(jnp.bfloat16), grad, preferred_element_type=jnp.float32
    ).astype(jnp.bfloat16)
    grad_query = rows_dot(key, grad_scores)
    kh[h] = (
        SCORE_SCALE * jnp.dot(grad_scores, query, preferred_element_type=jnp.float32)
    ).astype(jnp.bfloat16)
    qh[h] = (SCORE_SCALE * jnp.transpose(grad_query)).astype(jnp.bfloat16)


def compass():
    dp = lax.axis_index("dp")
    band = lax.axis_index("band")
    core = lax.rem(dp, 2)
    px = lax.rem(dp // 2, 2)
    py = lax.rem(dp // 4, 2)
    return SimpleNamespace(
        dp=dp, band=band, core=core, px=px, py=py, kind=2 * py + px,
        sib=dp + 1 - 2 * core, xdp=dp + 2 - 4 * px, ydp=dp + 4 - 8 * py,
    )


def add_rows(total, term):
    rows = total.shape[0]

    @pl.loop(0, rows // 16)
    def _(step):
        at = pl.ds(pl.multiple_of(step * 16, 16), 16)
        total[at, :] = (
            total[at, :].astype(jnp.float32) + term[at, :].astype(jnp.float32)
        ).astype(jnp.bfloat16)


def run_all(batch):
    for do in batch:
        do()


REDUCE_ORDER = (1, 3, 2, 0)


FRONT, BACK = 1, 2


def reduce_scratch(plan, half, width):
    bf = jnp.bfloat16
    n = NB * sum(1 for todo in plan if todo & FRONT)
    m = len(plan)
    D = pltpu.SemaphoreType.DMA
    scratch = dict(
        recv_z=pltpu.VMEM((m, NB, half, width), bf), z_send=D((m, NB)), z_recv=D((m, NB)),
        d_send=D((m, 6)), d_recv=D((m, 6)), d_own=D((m,)), part_sem=D((m,)),
    )
    if n:
        scratch.update(
            acc=pltpu.VMEM((n, 4, half, width), bf), recv_a=pltpu.VMEM((n, 4, half, width), bf),
            recv_b=pltpu.VMEM((n, 2, half, width), bf), recv_c=pltpu.VMEM((n, half, width), bf),
            a_send=D((n,)), a_recv=D((n,)), a_own=D((n,)),
            b_send=D((n, 2, 2)), b_recv=D((n, 2, 2)), c_send=D((n, 2)), c_recv=D((n, 2)),
        )
    return scratch


def reduce_steps(me, plan, source, out, parts_in, parts_out, sc, beside=(), ahead=3, by_kind=False):
    dp, band, core, px, py, kind = me.dp, me.band, me.core, me.px, me.py, me.kind
    here = lambda d: device(d, band)
    fronts = [phase for phase, todo in enumerate(plan) if todo & FRONT]
    backs = [phase for phase, todo in enumerate(plan) if todo & BACK]
    chunks = [(phase, k) for phase in fronts for k in REDUCE_ORDER]
    n = len(chunks)
    flip = lambda v: 1 - v
    sends = []
    rows = sc.recv_z.shape[2]
    cut = rows // 32 * 16
    spans = (pl.ds(0, cut), pl.ds(cut, rows - cut))

    def remote(src, dst, ss, rs, to):
        return pltpu.make_async_remote_copy(
            src_ref=src, dst_ref=dst, send_sem=ss, recv_sem=rs, device_id=to, device_id_type=MESH
        )

    def go(make):
        make().start()
        sends.append(make)

    def target(k):
        return device(dp, lax.rem(band + k, NB))

    def start_a(s, kinds=range(4)):
        phase, k = chunks[s]
        b = lax.rem(band + k, NB)
        for t in kinds:
            remote(
                source(phase, b, t, flip(core)), sc.recv_a.at[s, t], sc.a_send.at[s], sc.a_recv.at[s],
                here(me.sib),
            ).start()
            pltpu.make_async_copy(source(phase, b, t, core), sc.acc.at[s, t], sc.a_own.at[s]).start()

    def first(half, j, send):
        if half == 0:
            return 2 * j + (flip(px) if send else px)
        return 2 * (flip(py) if send else py) + j

    def second(half, send):
        if half == 0:
            return 2 * (flip(py) if send else py) + px
        return 2 * py + (flip(px) if send else px)

    def near(half):
        return here(me.xdp if half == 0 else me.ydp)

    def send_b(s, half, j):
        return remote(
            sc.acc.at[s, first(half, j, True), spans[half]], sc.recv_b.at[s, j, spans[half]],
            sc.b_send.at[s, half, j], sc.b_recv.at[s, half, j], near(half),
        )

    def send_c(s, half):
        return remote(
            sc.acc.at[s, second(half, True), spans[half]], sc.recv_c.at[s, spans[half]],
            sc.c_send.at[s, half], sc.c_recv.at[s, half], near(1 - half),
        )

    def send_z(phase, k, src):
        return remote(src, sc.recv_z.at[phase, k], sc.z_send.at[phase, k], sc.z_recv.at[phase, k], target(k))

    def unit_z(s):
        phase, k = chunks[s]
        return send_z(phase, k, sc.acc.at[s, kind])

    def part_load(phase):
        return pltpu.make_async_copy(parts_in[phase], sc.recv_z.at[phase, 0], sc.part_sem.at[phase])

    def part_store(phase):
        return pltpu.make_async_copy(sc.recv_z.at[phase, 0], parts_out[phase], sc.part_sem.at[phase])

    def d_copy(phase, half, slot, mine):
        ss, rs = sc.d_send.at[phase, 3 * half + slot], sc.d_recv.at[phase, 3 * half + slot]
        span = spans[half]
        if slot == 0:
            src = sc.recv_z.at[phase, 0, span]
            return remote(src, out[phase].at[kind, core, span], ss, rs, near(half))
        j = slot - 1
        t = 2 * (py if mine else flip(py)) + j if half == 0 else 2 * j + (px if mine else flip(px))
        unit = out[phase].at[t, core, span]
        return remote(unit, unit, ss, rs, near(1 - half))

    def d_cross(phase, mine):
        row = out[phase].at[:, core if mine else flip(core)]
        return remote(row, row, sc.z_send.at[phase, 0], sc.z_recv.at[phase, 0], here(me.sib))

    def a_to_b(s):
        acc, got = sc.acc, sc.recv_a
        pltpu.make_async_copy(got.at[s], acc.at[s], sc.a_own.at[s]).wait()
        whole = remote(got.at[s], got.at[s], sc.a_send.at[s], sc.a_recv.at[s], here(me.sib))
        whole.wait_recv()
        for j in range(2):
            for half in range(2):
                t = first(half, j, True)
                add_rows(acc.at[s, t, spans[half]], got.at[s, t, spans[half]])
                go(partial(send_b, s, half, j))
        for j in range(2):
            for half in range(2):
                t = first(half, j, False)
                add_rows(acc.at[s, t, spans[half]], got.at[s, t, spans[half]])
        whole.wait_send()

    def b_to_c(s):
        acc, got = sc.acc, sc.recv_b
        for half in range(2):
            for j in range(2):
                send_b(s, half, j).wait_recv()
            away = flip(py) if half == 0 else flip(px)
            t = second(half, True)
            add_rows(acc.at[s, t, spans[half]], got.at[s, away, spans[half]])
            go(partial(send_c, s, half))
        for half in range(2):
            stay = py if half == 0 else px
            add_rows(acc.at[s, kind, spans[half]], got.at[s, stay, spans[half]])

    def c_to_z(s):
        phase, k = chunks[s]
        for half in range(2):
            send_c(s, half).wait_recv()
            add_rows(sc.acc.at[s, kind, spans[half]], sc.recv_c.at[s, spans[half]])
        if k != 0:
            go(partial(unit_z, s))

    def z_sum(phase):
        got = sc.recv_z
        for k in range(1, NB):
            remote(
                got.at[phase, k], got.at[phase, k], sc.z_send.at[phase, k], sc.z_recv.at[phase, k], here(dp)
            ).wait_recv()
        s = NB * fronts.index(phase) + NB - 1

        @pl.loop(0, rows // 16)
        def _(step):
            at = pl.ds(pl.multiple_of(step * 16, 16), 16)
            total = sc.acc[s, kind, at, :].astype(jnp.float32)
            for k in range(1, NB):
                total = total + got[phase, k, at, :].astype(jnp.float32)
            got[phase, 0, at, :] = total.astype(jnp.bfloat16)

        if not plan[phase] & BACK:
            part_store(phase).start()

    def d_first(phase):
        if not plan[phase] & FRONT:
            part_load(phase).wait()
        own_copy = pltpu.make_async_copy(sc.recv_z.at[phase, 0], out[phase].at[kind, core], sc.d_own.at[phase])
        own_copy.start()
        for half in range(2):
            go(partial(d_copy, phase, half, 0, True))
        own_copy.wait()

    def d_second(phase):
        for half in range(2):
            d_copy(phase, half, 0, False).wait_recv()
            for slot in (1, 2):
                go(partial(d_copy, phase, half, slot, True))

    def d_third(phase):
        for half in range(2):
            for slot in (1, 2):
                d_copy(phase, half, slot, False).wait_recv()
        go(partial(d_cross, phase, True))

    def d_last(phase):
        d_cross(phase, False).wait_recv()

    def finish():
        for phase in fronts:
            if not plan[phase] & BACK:
                part_store(phase).wait()
        for make in sends:
            make().wait_send()

    table = {-1: [] if by_kind else [partial(start_a, s) for s in range(n)]}

    def put(at, do):
        table.setdefault(at, []).append(do)

    for phase in backs:
        if not plan[phase] & FRONT:
            put(-1, lambda phase=phase: part_load(phase).start())
    for at, do in enumerate(beside):
        put(at, do)
    for s in range(n):
        put(s + ahead, partial(b_to_c, s))
        put(s + ahead + 1, partial(c_to_z, s))
        put(s, partial(a_to_b, s))
    for phase, todo in enumerate(plan):
        end = 0
        if todo & FRONT:
            end = NB * fronts.index(phase) + NB + ahead + 1
            put(end, partial(z_sum, phase))
        if todo & BACK:
            for lag, do in ((0, d_first), (1, d_second), (2, d_third), (4, d_last)):
                put(end + lag - (0 if todo & FRONT else 1), partial(do, phase))
    steps = [partial(run_all, table[at]) for at in sorted(table)]
    steps.append(finish)
    if by_kind:
        return SimpleNamespace(
            start=lambda kind: [start_a(s, (kind,)) for s in range(n)], a=a_to_b, b=b_to_c, c=c_to_z, sum=z_sum,
            take=lambda phase: part_load(phase).start(), d1=d_first, d2=d_second, d3=d_third, d4=d_last, finish=finish,
        )
    return steps


def home_scratch():
    D = pltpu.SemaphoreType.DMA
    return dict(home_send=D((2,)), home_recv=D((2,)))


def home_steps(me, rows_ref, home_ref, sc):
    band, core = me.band, me.core
    slot = lax.rem(band, 2)

    def stays(s):
        return jnp.logical_and(band // 2 == core, 2 * core + s == band)

    def copy(s):
        to = device(me.dp - core + band // 2, 2 * core + s)
        return pltpu.make_async_remote_copy(
            src_ref=rows_ref.at[s], dst_ref=home_ref.at[slot], send_sem=sc.home_send.at[s],
            recv_sem=sc.home_recv.at[slot], device_id=to, device_id_type=MESH,
        )

    def begin():
        for s in range(2):
            pl.when(stays(s))(
                lambda: pltpu.make_async_copy(
                    rows_ref.at[s], home_ref.at[slot], sc.home_recv.at[slot]
                ).start()
            )
            pl.when(jnp.logical_not(stays(s)))(lambda: copy(s).start())

    def finish():
        for s in range(2):
            pl.when(jnp.logical_not(stays(s)))(lambda: copy(s).wait_send())
        for i in range(2):
            pltpu.make_async_copy(rows_ref.at[i], home_ref.at[i], sc.home_recv.at[i]).wait()

    return begin, finish


def group_barrier(me):
    barrier = pltpu.get_barrier_semaphore()
    peers = [(me.xdp, me.band), (me.ydp, me.band), (me.sib, me.band)]
    for k in range(1, NB):
        other = lax.rem(me.band + k, NB)
        peers += [(me.dp, other), (me.sib, other)]
    for dp, band in peers:
        pl.semaphore_signal(
            barrier, inc=1, device_id=device(dp, band), device_id_type=MESH
        )
    pl.semaphore_wait(barrier, len(peers))


def reduce_refs(plan, counts, refs):
    take = iter(refs)
    grads = [[next(take) for _ in range(count)] for count in counts]

    def source(phase, b, t, h):
        if len(grads[phase]) > 1:
            return grads[phase][t].at[b, h]
        whole = grads[phase][0]
        if len(whole.shape) == 5:
            return whole.at[b, t, h]
        span = whole.shape[3] // 4
        return whole.at[b, h, :, pl.ds(pl.multiple_of(t * span, 128), span)]

    return source, [next(take) if todo == BACK else None for todo in plan]


def reduce_outs(plan, refs):
    take = iter(refs)
    out = [next(take) if todo & BACK else None for todo in plan]
    return out, [next(take) if todo == FRONT else None for todo in plan]


def reduce_shapes(plan, half, width):
    bf = jnp.bfloat16
    shapes = [jax.ShapeDtypeStruct((4, 2, half, width), bf) for todo in plan if todo & BACK]
    return shapes + [jax.ShapeDtypeStruct((half, width), bf) for todo in plan if todo == FRONT]


def small_scratch(mod_rows, bias_rows, cond_rows, cond_cols):
    D = pltpu.SemaphoreType.DMA
    f32 = jnp.float32
    return dict(
        s_core=pltpu.VMEM((mod_rows + bias_rows, 128), f32),
        s_every=pltpu.VMEM((NB, 4, mod_rows, 128), jnp.bfloat16),
        s_bias=pltpu.VMEM((3, bias_rows, 128), f32),
        s_got=pltpu.VMEM((2 + NB, bias_rows, 128), f32),
        s_flat=pltpu.VMEM((8, mod_rows, 128), f32),
        s_cond=pltpu.VMEM((NB, cond_rows, cond_cols), f32),
        s_send=D((8,)), s_recv=D((8,)), sz_send=D((2, NB)), sz_recv=D((2, NB)),
        sc_send=D((NB,)), sc_recv=D((NB,)),
    )


def small_steps(me, mods, images, small_ref, ada_ref, every_ref, bias_ref, cond_ref, sc):
    dp, band, core, px, py, kind = me.dp, me.band, me.core, me.px, me.py, me.kind
    here = lambda d: device(d, band)
    every, bias, got, cond = sc.s_every, sc.s_bias, sc.s_got, sc.s_cond
    mod_rows = every.shape[2]
    flip = lambda v: 1 - v

    def remote(src, dst, ss, rs, to):
        return pltpu.make_async_remote_copy(
            src_ref=src, dst_ref=dst, send_sem=ss, recv_sem=rs, device_id=to, device_id_type=MESH
        )

    def plain(index, src, dst, to):
        return remote(src, dst, sc.s_send.at[index], sc.s_recv.at[index], to)

    def core_copy():
        return plain(0, small_ref, sc.s_core, here(me.sib))

    def x_copies(mine):
        unit = every.at[band, kind if mine else 2 * py + flip(px)]
        return [
            plain(1, unit, unit, here(me.xdp)),
            plain(2, bias.at[0], got.at[0], here(me.xdp)),
        ]

    def y_copies(mine):
        pair = every.at[band, pl.ds(2 * (py if mine else flip(py)), 2)]
        return [
            plain(3, pair, pair, here(me.ydp)),
            plain(4, bias.at[1], got.at[1], here(me.ydp)),
        ]

    def z_copies(k, mine):
        to = device(dp, lax.rem(band + k, NB))
        block = every.at[band if mine else lax.rem(band + NB - k, NB)]
        return [
            remote(block, block, sc.sz_send.at[0, k], sc.sz_recv.at[0, k], to),
            remote(bias.at[2], got.at[2 + k], sc.sz_send.at[1, k], sc.sz_recv.at[1, k], to),
        ]

    def cond_copy(k, mine):
        to = device(dp, lax.rem(band + k, NB))
        block = cond.at[band if mine else lax.rem(band + NB - k, NB)]
        return remote(block, block, sc.sc_send.at[k], sc.sc_recv.at[k], to)

    def begin():
        core_copy().start()

    def cores():
        core_copy().wait()
        total = small_ref[...] + sc.s_core[...]
        every[band, kind] = total[:mod_rows].astype(jnp.bfloat16)
        bias[0] = total[mod_rows:]
        for copy in x_copies(True):
            copy.start()

    def over_x():
        for copy in x_copies(True):
            copy.wait_send()
        for copy in x_copies(False):
            copy.wait_recv()
        bias[1] = bias[0] + got[0]
        for copy in y_copies(True):
            copy.start()

    def over_y():
        for copy in y_copies(True):
            copy.wait_send()
        for copy in y_copies(False):
            copy.wait_recv()
        bias[2] = bias[1] + got[1]
        for k in range(1, NB):
            for copy in z_copies(k, True):
                copy.start()

    def over_z():
        for k in range(1, NB):
            for copy in z_copies(k, True):
                copy.wait_send()
            for copy in z_copies(k, False):
                copy.wait_recv()
        bias_ref[...] = bias[2] + got[3] + got[4] + got[5]
        every_ref[...] = every[...]
        flat = sc.s_flat
        for i in range(images):
            flat[i] = every[images * core + i, kind].astype(jnp.float32)
        parts = mods // 128
        lead = flat.shape[0]
        total = jnp.zeros((lead, ada_ref.shape[0]), jnp.float32)
        for r in range(parts):
            left = jnp.concatenate(
                [flat[i, r : r + 1, :] for i in range(images)]
                + [jnp.zeros((lead - images, 128), jnp.float32)]
            ).astype(jnp.bfloat16)
            total = total + lanes_dot(left, ada_ref[:, r * 128 : (r + 1) * 128])
        pad = cond.shape[2] - total.shape[1]
        cond[band] = jnp.concatenate([total, jnp.zeros((lead, pad), jnp.float32)], 1)
        for k in range(1, NB):
            cond_copy(k, True).start()

    def conditions():
        for k in range(1, NB):
            cond_copy(k, True).wait_send()
            cond_copy(k, False).wait_recv()
        cond_ref[...] = cond[...]

    return [begin, cores, over_x, over_y, over_z, conditions]


def put_lines(ref, first, values):
    for i in range(values.shape[1] // 128):
        ref[first + i : first + i + 1, :] = values[:, i * 128 : (i + 1) * 128]


def reduce_last_kernel(plan, images, band_slots, names, *refs):
    me = compass()
    (proj_ref, part_ref, attn_hbm, query_hbm, own_hbm, other_hbm, first_hbm, residual_hbm, middle_hbm, vec_ref, sums_ref,
     inner_bias_ref, ada_ref) = refs[:13]
    inner_out, first_out, home_ref, every_ref, bias_ref, cond_ref = refs[13:19]
    sc = SimpleNamespace(**dict(zip(names, refs[19:])))
    rows, width = sc.attn.shape
    lines = width // 128
    small = sc.small
    mod_rows = sc.s_every.shape[2]

    def source(phase, b, t, h):
        return proj_ref.at[b, h] if t == 3 else sc.grads.at[t, b, h]

    loads = [
        (attn_hbm, sc.attn), (query_hbm, sc.gqkv.at[:, pl.ds(0, width)]), (own_hbm, sc.gqkv.at[:, pl.ds(width, 2 * width)]),
        (other_hbm, sc.other), (first_hbm.at[:, pl.ds(0, 3 * width)], sc.first), (residual_hbm, sc.residual),
        (middle_hbm, sc.middle),
    ]

    def load(i):
        return pltpu.make_async_copy(*loads[i], sc.load_sem.at[i])

    for i in range(len(loads)):
        load(i).start()
    group_barrier(me)
    mods = MOD_BLOCKS * width
    exchange = small_steps(me, mods, images, small, ada_ref, every_ref, bias_ref, cond_ref, sc)
    depart, settle = home_steps(me, sc.tokens, home_ref, sc)
    r = reduce_steps(me, plan, source, (inner_out, first_out), (part_ref, None), (None, None), sc, (), 2, True)

    def run(*todo):
        for do, index in todo:
            do(index)

    run((r.start, 3), (r.take, 0), (r.d1, 0))
    for i in range(4):
        load(i).wait()

    sc.sums[...] = jnp.zeros_like(sc.sums)

    def add_line(index, values):
        sc.sums[index : index + 1, :] += jnp.sum(values, 0, keepdims=True)

    @pl.loop(0, rows // BLOCK)
    def _(block):
        sub = pl.ds(pl.multiple_of(block * BLOCK, BLOCK), BLOCK)
        total = sc.gqkv[sub, width:].astype(jnp.float32) + sc.other[sub, :].astype(jnp.float32)
        total = total.astype(jnp.bfloat16)
        sc.gqkv[sub, width:] = total
        add_line(1, total[:, width:].astype(jnp.float32))
        add_line(0, sc.gqkv[sub, :width].astype(jnp.float32))

    tile = width // 3
    load(4).wait()
    between = [(), ((r.d2, 0),), ()]
    for j in range(3):
        sc.back[:, j * tile : (j + 1) * tile] = lanes_dot(sc.gqkv[...], sc.first[j * tile : (j + 1) * tile, :])
        run(*between[j])
    load(5).wait()
    load(6).wait()

    @pl.loop(0, rows // BLOCK)
    def _(block):
        at = pl.multiple_of(block * BLOCK, BLOCK)
        sub = pl.ds(at, BLOCK)
        normed, inverse = normalize(sc.residual[sub, :])
        back = sc.back[sub, :]
        add_line(2, back)
        add_line(3, back * normed)
        grad = sc.middle[sub, :] + norm_back(back * (1.0 + vec_ref[1:2, :]), normed, inverse)
        per_image = band_slots // BLOCK
        to = pl.ds(pl.multiple_of(lax.rem(block, per_image) * BLOCK, BLOCK), BLOCK)
        sc.tokens[block // per_image, to, :] = grad.astype(jnp.bfloat16)

    small[...] = jnp.zeros_like(small)
    kept = [sc.sums[2:3, :], sc.sums[3:4, :]] + [sums_ref[i : i + 1, :] for i in (3, 1, 2, 0)]
    for i, values in enumerate(kept + [0.5 * vec_ref[14:15, :]]):
        put_lines(small, i * lines, values)
    at = mod_rows
    for values in (sc.sums[0:1, :], sc.sums[1:2, :], sums_ref[4:5, :], inner_bias_ref[0:1, :], sums_ref[5:6, :]):
        put_lines(small, at, values)
        at += values.shape[1] // 128
    say = lambda i: exchange[i]()
    depart()
    run((r.d3, 0))
    for t in range(3):

        @pl.loop(0, 3)
        def _(j):
            at = pl.multiple_of(t * width + j * tile, 128)
            value = rows_dot(sc.attn[...], sc.gqkv[:, pl.ds(at, tile)]).astype(jnp.bfloat16)
            to = pl.ds(pl.multiple_of(j * tile, 128), tile)
            sc.grads[t, :, :, :, to] = value.reshape(sc.grads.shape[1:4] + (tile,))

        run((r.start, t), (say, t))

    run((r.a, 0), (r.a, 1), (say, 3), (r.b, 0), (r.a, 2), (r.b, 1), (r.c, 0), (r.a, 3), (r.b, 2), (r.c, 1), (r.b, 3), (r.c, 2))
    run((r.c, 3), (say, 4), (r.sum, 1), (r.d1, 1), (r.d2, 1), (r.d3, 1), (say, 5), (r.d4, 0), (r.d4, 1))
    settle()
    r.finish()


def reduce_last(proj, part, attn_in, query, own, other, first, residual, middle, vectors, sums, inner_bias, ada_weight,
                images, band_slots, collective_id):
    plan = (BACK, FRONT | BACK)
    half, width = proj.shape[-2:]
    rows = attn_in.shape[0]
    bf, f32 = jnp.bfloat16, jnp.float32
    V = pltpu.VMEM
    mod_rows = -(-(MOD_BLOCKS + 1) * width // 2048) * 16
    bias_rows = (4 * width + inner_bias.shape[1]) // 128
    cond_cols = -(-ada_weight.shape[0] // 128) * 128
    scratch = dict(
        **reduce_scratch(plan, half, width), **small_scratch(mod_rows, bias_rows, 8, cond_cols), **home_scratch(),
        attn=V((rows, width), bf), gqkv=V((rows, 3 * width), bf), other=V((rows, 2 * width), bf),
        first=V((width, 3 * width), bf), residual=V((rows, width), f32), middle=V((rows, width), f32),
        grads=V((3, NB, 2, half, width), bf), back=V((rows, width), f32), sums=V((8, width), f32),
        tokens=V((images, band_slots, width), bf), small=V((mod_rows + bias_rows, 128), f32),
        load_sem=pltpu.SemaphoreType.DMA((7,)),
    )
    any_, vmem = pl.BlockSpec(memory_space=pl.ANY), pl.BlockSpec(memory_space=pltpu.VMEM)
    return pl.pallas_call(
        partial(reduce_last_kernel, plan, images, band_slots, tuple(scratch)),
        out_shape=reduce_shapes(plan, half, width)
        + [
            jax.ShapeDtypeStruct((images, band_slots, width), bf),
            jax.ShapeDtypeStruct((NB, 4, mod_rows, 128), bf),
            jax.ShapeDtypeStruct((bias_rows, 128), f32),
            jax.ShapeDtypeStruct((NB, 8, cond_cols), f32),
        ],
        in_specs=[any_] * 9 + [vmem] * 4,
        out_specs=[any_] * 3 + [vmem] * 3,
        scratch_shapes=list(scratch.values()),
        compiler_params=pltpu.CompilerParams(
            collective_id=collective_id, has_side_effects=True, vmem_limit_bytes=62 * 2**20
        ),
        name="reduce_last",
    )(proj, part, attn_in, query, own, other, first, residual, middle, vectors, sums, inner_bias, ada_weight)


def reduce_attend_kernel(plan, counts, band_slots, names, *refs):
    me = compass()
    at = sum(counts) + sum(1 for todo in plan if todo == BACK)
    source, parts = reduce_refs(plan, counts, refs)
    rows_ref, count_ref, q_ref, own_ref, far_ref, grad_ref, top_ref = refs[at : at + 7]
    at += 7
    out, given = reduce_outs(plan, refs[at:])
    at += len(plan)
    home_ref, dq_ref, down_ref, dfar_ref = refs[at : at + 4]
    sc = SimpleNamespace(**dict(zip(names, refs[at + 4 :])))
    qh, kh, vh, gh, stage, stage_sem = sc.qh, sc.kh, sc.vh, sc.gh, sc.stage, sc.stage_sem
    rows, width = q_ref.shape
    heads = qh.shape[0]
    group_barrier(me)
    steps = reduce_steps(me, plan, source, out, parts, given, sc)
    depart, settle = home_steps(me, rows_ref, home_ref, sc)
    steps[0]()
    depart()
    keys, plain, ones = key_tail(count_ref[0], band_slots), flat_tail(0.0), flat_tail(1.0)
    loads = [(q_ref, 0, qh, 0, ones), (grad_ref, 0, gh, 0, plain)]
    for row0, ref in ((0, own_ref), (rows, far_ref)):
        loads += [(ref, 0, kh, row0, keys), (ref, width, vh, row0, plain)]

    def load(i):
        ref, column = loads[i][:2]
        return pltpu.make_async_copy(ref.at[:, pl.ds(column, width)], stage.at[i % 2], stage_sem.at[i % 2])

    load(0).start()
    for step in steps[1:4]:
        step()
    for i, (ref, column, heads_ref, row0, tail) in enumerate(loads):
        if i + 1 < len(loads):
            load(i + 1).start()
        load(i).wait()
        pack_heads(stage.at[i % 2], 0, heads_ref, row0, rows, tail)
    rest = steps[4:]
    inside = heads // 2

    @pl.loop(0, heads)
    def _(h):
        attend_head(h, qh, kh, vh, gh, top_ref)
        for i, step in enumerate(rest[:inside]):
            pl.when(h == 2 * i)(step)

    stores = [(qh, 0, dq_ref, 0)]
    for row0, ref in ((0, down_ref), (rows, dfar_ref)):
        stores += [(kh, row0, ref, 0), (vh, row0, ref, width)]

    def store(i):
        ref, column = stores[i][2:]
        target = ref.at[:, pl.ds(column, width)]
        if ref is not dfar_ref:
            return pltpu.make_async_copy(stage.at[i % 2], target, stage_sem.at[i % 2])
        return pltpu.make_async_remote_copy(
            src_ref=stage.at[i % 2], dst_ref=target, send_sem=sc.far_send.at[i % 2],
            recv_sem=sc.far_recv.at[i % 2], device_id=device(me.sib, me.band), device_id_type=MESH,
        )

    for i, (heads_ref, row0, ref, column) in enumerate(stores):
        if i >= 2:
            store(i - 2).wait()
        unpack_heads(heads_ref, row0, rows, stage.at[i % 2], 0)
        store(i).start()
    for i in (len(stores) - 2, len(stores) - 1):
        store(i).wait()
    for step in rest[inside:]:
        step()
    settle()


def reduce_attend(plan, grads, parts, rows_out, count, query, own, far, grad, top, band_slots, collective_id):
    half, width = grads[0][0].shape[-2:]
    counts = tuple(len(phase) for phase in grads)
    rows = query.shape[0]
    heads = width // HEAD_DIM
    bf = jnp.bfloat16
    scratch = reduce_scratch(plan, half, width)
    scratch.update(
        qh=pltpu.VMEM((heads, rows, LANES), bf),
        kh=pltpu.VMEM((heads, 2 * rows, LANES), bf),
        vh=pltpu.VMEM((heads, 2 * rows, LANES), bf),
        gh=pltpu.VMEM((heads, rows, LANES), bf),
        stage=pltpu.VMEM((2, rows, width), bf),
        stage_sem=pltpu.SemaphoreType.DMA((2,)),
        far_send=pltpu.SemaphoreType.DMA((2,)),
        far_recv=pltpu.SemaphoreType.DMA((2,)),
        **home_scratch(),
    )
    any_, vmem = pl.BlockSpec(memory_space=pl.ANY), pl.BlockSpec(memory_space=pltpu.VMEM)
    smem = pl.BlockSpec(memory_space=pltpu.SMEM)
    units = [unit for phase in grads for unit in phase]
    return pl.pallas_call(
        partial(reduce_attend_kernel, plan, counts, band_slots, tuple(scratch)),
        out_shape=reduce_shapes(plan, half, width)
        + [
            jax.ShapeDtypeStruct(rows_out.shape, bf),
            jax.ShapeDtypeStruct((rows, width), bf),
            jax.ShapeDtypeStruct((rows, 2 * width), bf),
            jax.ShapeDtypeStruct((rows, 2 * width), bf),
        ],
        in_specs=[any_] * (len(units) + len(parts) + 1) + [smem] + [any_] * 4 + [vmem],
        out_specs=[any_] * (len(plan) + 4),
        scratch_shapes=list(scratch.values()),
        compiler_params=pltpu.CompilerParams(
            collective_id=collective_id, has_side_effects=True, vmem_limit_bytes=60 * 2**20
        ),
        name="reduce_attend",
    )(*units, *parts, rows_out, count, query, own, far, grad, top)


MOD_BLOCKS = 6
BLOCK = 128


def forward_scratch(half, ff, width, rows, note_rows, images):
    bf, f32 = jnp.bfloat16, jnp.float32
    D = pltpu.SemaphoreType.DMA
    heads = width // HEAD_DIM
    V = pltpu.VMEM
    return dict(
        qp=V((NB, 2, half, ff), bf), bounce_i=V((2, half, ff), bf), bounce_o=V((4, 2, half, width), bf),
        bounce_t=V((rows // images, width), bf), tok=V((images, rows // images, width), bf),
        notes=V((NB, note_rows, 128), f32), vec=V((16, width), f32),
        residual=V((rows, width), f32), attn_in=V((rows, width), bf), query=V((rows, width), bf),
        own=V((rows, 2 * width), bf), far=V((rows, 2 * width), bf), mixed=V((rows, width), bf),
        attended=V((rows, width), f32), mlp_in=V((rows, width), bf), tops=V((heads, 8, rows), f32),
        qh=V((heads, rows, LANES), bf), kh=V((heads, 2 * rows, LANES), bf), vh=V((heads, 2 * rows, LANES), bf),
        z_send=D((3, 2)), z_recv=D((3, NB)), f_send=D((3, NB)), a_send=D((9, 2)), a_recv=D((9, 2)), b_send=D((9, 2, 2)), b_recv=D((9, 2, 2)),
        c_send=D((9,)), c_recv=D((9,)), t_send=D((2, 2)), t_recv=D((2, 2)), m_send=D((2, 2)), m_recv=D((NB,)),
        local=D((4,)), kv_send=D((1,)), kv_recv=D((1,)), done=D((12,)),
    )


def gather_steps(me, width, ins, outs, tok_in, tok_out, cot_in, cot_out, note_in, note_out, sc):
    dp, band, core, px, py, kind = me.dp, me.band, me.core, me.px, me.py, me.kind
    base = dp - core
    dev = lambda d, b: device(d, b)
    here = lambda d: dev(d, band)
    flip = lambda v: 1 - v
    low = band < 2
    bands = (band + 1 - 2 * lax.rem(band, 2), jnp.where(low, 2, 1), jnp.where(low, 3, 0))
    order = [(ph, b) for ph in range(3) for b in bands]
    inside = jnp.logical_or(band == 1, band == 2)
    sends = []

    def remote(src, dst, ss, rs, to):
        return pltpu.make_async_remote_copy(
            src_ref=src, dst_ref=dst, send_sem=ss, recv_sem=rs, device_id=to, device_id_type=MESH
        )

    def go(make):
        for copy in make():
            copy.start()
        sends.append(make)

    size = ins[0].shape[1]
    cut = size // 32 * 16
    whole, spans = pl.ds(0, size), (pl.ds(0, cut), pl.ds(cut, size - cut))

    def cols(t, n=1):
        return pl.ds(pl.multiple_of(t * width, 128), n * width)

    def unit(ph, b, t, h, span=whole):
        return outs[ph].at[b, t, h, span] if ph == 2 else outs[ph].at[b, h, span, cols(t)]

    def pair(ph, b, h, y, span):
        return outs[ph].at[b, pl.ds(2 * y, 2), h, span] if ph == 2 else outs[ph].at[b, h, span, cols(2 * y, 2)]

    def row(ph, b, h):
        return outs[ph].at[b, :, h] if ph == 2 else outs[ph].at[b, h]

    def own_z(ph, up):
        src = ins[ph].at[kind, core] if ph == 2 else ins[ph].at[core, :, cols(kind)]
        return remote(
            src, unit(ph, band, kind, core), sc.z_send.at[ph, up], sc.z_recv.at[ph, band],
            dev(dp, band - 1 + 2 * up),
        )

    def pass_z(s):
        ph, b = order[s]
        u = unit(ph, b, kind, core)
        return remote(
            u, u, sc.f_send.at[ph, b], sc.z_recv.at[ph, b], dev(dp, jnp.where(b < band, band + 1, band - 1))
        )

    def a_copy(s, half, mine):
        ph, b = order[s]
        near = 2 * py + flip(px) if half == 0 else 2 * flip(py) + px
        u = unit(ph, b, kind if mine else near, core, spans[half])
        return remote(u, u, sc.a_send.at[s, half], sc.a_recv.at[s, half], here(me.xdp if half == 0 else me.ydp))

    def b_copies(s, half, mine):
        ph, b = order[s]
        if half == 0:
            u = pair(ph, b, core, py if mine else flip(py), spans[half])
            return [remote(u, u, sc.b_send.at[s, half, 0], sc.b_recv.at[s, half, 0], here(me.ydp))]
        copies = []
        for j in range(2):
            u = unit(ph, b, 2 * j + (px if mine else flip(px)), core, spans[half])
            copies.append(remote(u, u, sc.b_send.at[s, half, j], sc.b_recv.at[s, half, j], here(me.xdp)))
        return copies

    def c_copy(s, mine):
        ph, b = order[s]
        u = row(ph, b, core if mine else flip(core))
        return remote(u, u, sc.c_send.at[s], sc.c_recv.at[s], here(me.sib))

    def z_start(ph):
        pl.when(band < NB - 1)(lambda: own_z(ph, 1).start())
        pl.when(band > 0)(lambda: own_z(ph, 0).start())

    def z_wait(s):
        ph, b = order[s]
        u = unit(ph, b, kind, core)
        remote(u, u, sc.f_send.at[ph, b], sc.z_recv.at[ph, b], here(dp)).wait_recv()
        pl.when(inside)(lambda: pass_z(s).start())
        for half in range(2):
            go(lambda half=half: [a_copy(s, half, True)])

    def a_wait(s):
        for half in range(2):
            a_copy(s, half, False).wait_recv()
            go(partial(b_copies, s, half, True))

    def b_wait(s):
        for half in range(2):
            for copy in b_copies(s, half, False):
                copy.wait_recv()
        go(lambda: [c_copy(s, True)])

    def c_wait(s):
        c_copy(s, False).wait_recv()

    slot = lax.rem(band, 2)

    def image_copy(which, src, dst, i):
        to = dev(base + band // 2, 2 * core + i)
        return remote(src.at[i], dst.at[slot], sc.t_send.at[which, i], sc.t_recv.at[which, slot], to)

    def at_home(i):
        return jnp.logical_and(band // 2 == core, 2 * core + i == band)

    def move(which, src, dst, bounce=None):
        for i in range(2):

            @pl.when(at_home(i))
            def _():
                if bounce is None:
                    pltpu.make_async_copy(src.at[i], dst.at[slot], sc.t_recv.at[which, slot]).start()
                else:
                    inward = pltpu.make_async_copy(src.at[i], bounce, sc.local.at[3])
                    inward.start()
                    inward.wait()
                    pltpu.make_async_copy(bounce, dst.at[slot], sc.t_recv.at[which, slot]).start()

            @pl.when(jnp.logical_not(at_home(i)))
            def _():
                image_copy(which, src, dst, i).start()

    def move_wait(which, src, dst):
        for i in range(2):

            @pl.when(jnp.logical_not(at_home(i)))
            def _():
                image_copy(which, src, dst, i).wait_send()

        for s in range(2):
            pltpu.make_async_copy(dst.at[s], dst.at[s], sc.t_recv.at[which, s]).wait()

    def note_copy(i, c):
        return remote(
            note_in.at[i], note_out.at[band], sc.m_send.at[i, c], sc.m_recv.at[band],
            dev(base + c, 2 * core + i),
        )

    def note_home(i, c):
        return jnp.logical_and(c == core, 2 * core + i == band)

    def begin():
        for i in range(2):
            for c in range(2):

                @pl.when(note_home(i, c))
                def _():
                    pltpu.make_async_copy(note_in.at[i], note_out.at[band], sc.m_recv.at[band]).start()

                @pl.when(jnp.logical_not(note_home(i, c)))
                def _():
                    note_copy(i, c).start()

        z_start(0)
        for ph, dst in enumerate((outs[0].at[band], sc.bounce_i, sc.bounce_o)):
            pltpu.make_async_copy(ins[ph], dst, sc.local.at[ph]).start()

    def arrived():
        for i in range(2):
            for c in range(2):

                @pl.when(jnp.logical_not(note_home(i, c)))
                def _():
                    note_copy(i, c).wait_send()

        for b in range(NB):
            pltpu.make_async_copy(note_in.at[0], note_out.at[b], sc.m_recv.at[b]).wait()
        move_wait(0, tok_in, tok_out)

    def place():
        for ph, dst in ((1, sc.bounce_i), (2, sc.bounce_o)):
            pltpu.make_async_copy(ins[ph], dst, sc.local.at[ph]).wait()
            pltpu.make_async_copy(dst, outs[ph].at[band], sc.local.at[ph]).start()

    def first_here():
        pltpu.make_async_copy(ins[0], outs[0].at[band], sc.local.at[0]).wait()

    def finish():
        for ph, src in ((1, sc.bounce_i), (2, sc.bounce_o)):
            pltpu.make_async_copy(src, outs[ph].at[band], sc.local.at[ph]).wait()
        move_wait(1, cot_in, cot_out)
        for ph in range(3):
            pl.when(band < NB - 1)(lambda: own_z(ph, 1).wait_send())
            pl.when(band > 0)(lambda: own_z(ph, 0).wait_send())
        for s in range(len(order)):
            pl.when(inside)(lambda: pass_z(s).wait_send())
        for make in sends:
            for copy in make():
                copy.wait_send()

    def images(which):
        if which == 0:
            move(0, tok_in, tok_out)
        else:
            move(1, cot_in, cot_out, sc.bounce_t)

    return SimpleNamespace(
        i=images, s=z_start,
        begin=begin, arrived=arrived, place=place, first_here=first_here, finish=finish,
        z=z_wait, a=a_wait, b=b_wait, c=c_wait,
    )


def forward_kernel(names, band_slots, *refs):
    me = compass()
    qp_in, inner_in, outer_in, tok_in, cot_in, note_in, table_ref = refs[:7]
    (qp_out, inner_out, outer_out, cot_out, vec_out, residual_out, attn_out, query_out, own_out, far_out,
     tops_out, mixed_out, attended_out, mlp_out) = refs[7:21]
    sc = SimpleNamespace(**dict(zip(names, refs[21:])))
    rows, width = sc.residual.shape
    heads = width // HEAD_DIM
    core = me.core
    qp, tok, notes, vec = sc.qp, sc.tok, sc.notes, sc.vec

    group_barrier(me)
    g = gather_steps(
        me, width, (qp_in, inner_in, outer_in), (qp, inner_out, outer_out), tok_in, tok, cot_in, cot_out,
        note_in, notes, sc,
    )
    saves = []

    def save(src, dst):
        copy = pltpu.make_async_copy(src, dst, sc.done.at[len(saves)])
        copy.start()
        saves.append(copy)

    def run(*words):
        for do, index in words:
            do(index)

    g.begin()
    g.place()
    run((g.z, 0), (g.z, 1), (g.i, 0), (g.a, 0), (g.a, 1), (g.z, 2), (g.s, 1), (g.b, 0), (g.b, 1), (g.a, 2), (g.z, 3), (g.c, 0), (g.c, 1), (g.z, 4), (g.b, 2), (g.a, 3))
    g.arrived()
    spread_notes(notes, vec, width)
    grid_rows = notes[0, 63:64, 0:1]
    grid_cols = notes[0, 63:64, 1:2]
    band_rows = jnp.floor(grid_rows * 0.25)
    valid_count = (band_rows * grid_cols).astype(jnp.int32)
    lane = lax.broadcasted_iota(jnp.int32, (1, width), 1)
    vec[15:16, :] = jnp.where(lane == 0, band_rows * grid_cols, 0.0)
    save(vec, vec_out)

    @pl.loop(0, rows // BLOCK)
    def _(step):
        at = pl.multiple_of(step * BLOCK, BLOCK)
        sub = pl.ds(at, BLOCK)
        per_image = band_slots // BLOCK
        within = (
            lax.rem(step, per_image) * BLOCK + lax.broadcasted_iota(jnp.int32, (BLOCK, 1), 0)
        ).astype(jnp.float32)
        down = jnp.floor((within + 0.5) / grid_cols)
        place = (2 * core + step // per_image).astype(jnp.float32)
        picks = []
        for index in (place * band_rows + down, within - down * grid_cols):
            lanes = lax.broadcasted_iota(jnp.int32, (BLOCK, 128), 1).astype(jnp.float32)
            pick = jnp.where(lanes == index, 1.0, 0.0).astype(jnp.bfloat16)
            part = [jnp.dot(pick, table_ref[i], preferred_element_type=jnp.float32) for i in range(3)]
            picks.append(part[0] + (part[1] + part[2]))
        token = tok[step // per_image, pl.ds(lax.rem(step, per_image) * BLOCK, BLOCK), :]
        residual = token.astype(jnp.float32) + jnp.concatenate(picks, 1)
        sc.residual[sub, :] = residual
        normed = normalize(residual)[0]
        sc.attn_in[sub, :] = (normed * (1.0 + vec[1:2, :]) + vec[0:1, :]).astype(jnp.bfloat16)

    save(sc.residual, residual_out)
    save(sc.attn_in, attn_out)
    g.first_here()
    run((g.c, 2))
    save(qp, qp_out)
    tile = width // 3
    full = NB * 2 * qp.shape[2]

    def product(left_ref, first, step):
        at = pl.ds(pl.multiple_of(first + step * tile, 128), tile)
        return jnp.dot(
            left_ref[...], qp[:, :, :, at].reshape(full, tile), preferred_element_type=jnp.float32
        )

    def here(step):
        return pl.ds(pl.multiple_of(step * tile, 128), tile)

    @pl.loop(0, 3)
    def _(step):
        sc.own[:, here(step)] = product(sc.attn_in, width, step).astype(jnp.bfloat16)

    run((g.z, 5), (g.s, 2))

    @pl.loop(0, 3)
    def _(step):
        value = product(sc.attn_in, 2 * width, step) + vec[7:8, here(step)]
        sc.own[:, here(step + 3)] = value.astype(jnp.bfloat16)

    swap = pltpu.make_async_remote_copy(
        src_ref=sc.own, dst_ref=sc.far, send_sem=sc.kv_send.at[0], recv_sem=sc.kv_recv.at[0],
        device_id=device(me.sib, me.band), device_id_type=MESH,
    )
    swap.start()
    run((g.a, 4), (g.b, 3))

    @pl.loop(0, 3)
    def _(step):
        value = product(sc.attn_in, 0, step) + vec[6:7, here(step)]
        sc.query[:, here(step)] = value.astype(jnp.bfloat16)

    save(sc.query, query_out)
    save(sc.own, own_out)
    run((g.a, 5), (g.b, 4), (g.c, 3), (g.z, 6))
    qh, kh, vh = sc.qh, sc.kh, sc.vh
    keys, plain = key_tail(valid_count, band_slots), flat_tail(0.0)
    pack_heads(sc.query, 0, qh, 0, rows, flat_tail(1.0))
    pack_heads(sc.own, 0, kh, 0, rows, keys)
    pack_heads(sc.own, width, vh, 0, rows, plain)
    swap.wait()
    save(sc.far, far_out)
    pack_heads(sc.far, 0, kh, rows, rows, keys)
    pack_heads(sc.far, width, vh, rows, rows, plain)
    beside = {
        0: ((g.z, 7), (g.b, 5), (g.c, 4)), 2: ((g.a, 6), (g.z, 8), (g.i, 1)), 4: ((g.a, 7), (g.b, 6), (g.c, 5)), 7: ((g.a, 8), (g.b, 7), (g.c, 6)), 10: ((g.b, 8), (g.c, 7)),
        13: ((g.c, 8),),
    }

    @pl.loop(0, heads)
    def _(h):
        attend_block(h, qh, kh, vh, sc.tops)
        for i, words in beside.items():
            pl.when(h == i)(partial(run, *words))

    unpack_heads(qh, 0, rows, sc.mixed, 0)
    save(sc.tops, tops_out)
    save(sc.mixed, mixed_out)

    @pl.loop(0, 3)
    def _(step):
        sc.attended[:, here(step)] = product(sc.mixed, 3 * width, step) + vec[8:9, here(step)]

    save(sc.attended, attended_out)

    @pl.loop(0, rows // BLOCK)
    def _(step):
        sub = pl.ds(pl.multiple_of(step * BLOCK, BLOCK), BLOCK)
        middle = sc.residual[sub, :] + vec[2:3, :] * sc.attended[sub, :]
        normed = normalize(middle)[0]
        sc.mlp_in[sub, :] = (normed * (1.0 + vec[4:5, :]) + vec[3:4, :]).astype(jnp.bfloat16)

    save(sc.mlp_in, mlp_out)
    g.finish()
    for copy in saves:
        copy.wait()


NOTE_COND, NOTE_GRID, NOTE_BIAS = 54, 63, 64


def spread_notes(notes, vec, width):
    lines = width // 128
    share = notes.shape[0]
    total = notes[0, 0:NOTE_GRID, :] + 0.0
    for b in range(1, share):
        total = total + notes[b, 0:NOTE_GRID, :]

    def flat(block, first):
        return jnp.concatenate([block[first + i : first + i + 1, :] for i in range(lines)], 1)

    for index in range(MOD_BLOCKS):
        vec[index : index + 1, :] = flat(total, index * lines)
    small = width // share
    for index in range(4):
        parts = []
        for b in range(share):
            first = NOTE_BIAS + 3 * index
            for i in range(3):
                parts.append(notes[b, first + i : first + i + 1, : min(128, small - 128 * i)])
        vec[6 + index : 7 + index, :] = jnp.concatenate(parts, 1)
    for b in range(share):
        block = notes[b, NOTE_BIAS + 12 : NOTE_BIAS + 12 + lines, :]
        vec[10 + b : 11 + b, :] = flat(block, 0)
    vec[14:15, :] = flat(notes[0, NOTE_COND : NOTE_COND + lines, :], 0)


def forward_block(qp, inner, outer, tok, cot, note, table):
    half, ff = qp.shape[0] // 2, qp.shape[1]
    images, band_slots, width = tok.shape
    rows = images * band_slots
    heads = width // HEAD_DIM
    bf, f32 = jnp.bfloat16, jnp.float32
    S = jax.ShapeDtypeStruct
    qp, inner = qp.reshape(2, half, ff), inner.reshape(2, half, ff)
    outer = outer.reshape(4, 2, half, width)
    scratch = forward_scratch(half, ff, width, rows, note.shape[1], images)
    any_ = pl.BlockSpec(memory_space=pl.ANY)
    return pl.pallas_call(
        partial(forward_kernel, tuple(scratch), band_slots),
        out_shape=[
            S((NB, 2, half, ff), bf), S((NB, 2, half, ff), bf), S((NB, 4, 2, half, width), bf), S(cot.shape, bf),
            S((16, width), f32), S((rows, width), f32), S((rows, width), bf), S((rows, width), bf),
            S((rows, 2 * width), bf), S((rows, 2 * width), bf), S((heads, 8, rows), f32), S((rows, width), bf),
            S((rows, width), f32), S((rows, width), bf),
        ],
        in_specs=[any_] * 6 + [pl.BlockSpec(memory_space=pltpu.VMEM)],
        out_specs=[any_] * 14,
        scratch_shapes=list(scratch.values()),
        compiler_params=pltpu.CompilerParams(
            collective_id=0, has_side_effects=True, vmem_limit_bytes=60 * 2**20
        ),
        name="forward_block",
    )(qp, inner, outer, tok, cot, note, table)


GELU_SCALE = 0.7978845608028654


def mlp_kernel(band_slots, mlp_ref, inner_ref, outer_ref, vec_ref, bias_ref, residual_hbm, attended_hbm, cot_ref,
               mixed_hbm, first_hbm, out_ref, middle_ref, back_ref, proj_grad_ref, outer_grad_ref, inner_grad_ref,
               bias_grad_ref, sums_ref, out_acc, back_acc, grad_mlp, residual_ref, attended_ref, mixed_ref, proj_ref, late_sem):
    step = pl.program_id(0)
    rows = mlp_ref.shape[0]
    low = lambda value: value.astype(jnp.bfloat16)
    line = lambda index: vec_ref[index : index + 1, :]
    width = mlp_ref.shape[1]
    late = [
        pltpu.make_async_copy(src, dst, late_sem.at[i])
        for i, (src, dst) in enumerate(
            ((residual_hbm, residual_ref), (attended_hbm, attended_ref), (mixed_hbm, mixed_ref),
             (first_hbm.at[:, pl.ds(3 * width, width)], proj_ref))
        )
    ]

    def grad_out(at):
        slot = lax.rem(at + lax.broadcasted_iota(jnp.int32, (BLOCK, 1), 0), band_slots)
        valid = jnp.where(slot.astype(jnp.float32) < vec_ref[15:16, 0:1], 1.0, 0.0)
        return cot_ref[pl.ds(at, BLOCK), :].astype(jnp.float32) * valid

    def add_line(index, values):
        sums_ref[index : index + 1, :] += jnp.sum(values, 0, keepdims=True)

    @pl.when(step == 0)
    def _():
        sums_ref[...] = jnp.zeros_like(sums_ref)
        for copy in late:
            copy.start()

        @pl.loop(0, rows // BLOCK)
        def _(block):
            at = pl.multiple_of(block * BLOCK, BLOCK)
            grad = low(line(5) * grad_out(at))
            grad_mlp[pl.ds(at, BLOCK), :] = grad
            add_line(5, grad.astype(jnp.float32))
            out_acc[pl.ds(at, BLOCK), :] = jnp.zeros((BLOCK, out_acc.shape[1]), jnp.float32)
            back_acc[pl.ds(at, BLOCK), :] = jnp.zeros((BLOCK, out_acc.shape[1]), jnp.float32)

    inner, outer, grad = inner_ref[...], outer_ref[...], grad_mlp[...]
    pre = jnp.dot(mlp_ref[...], inner, preferred_element_type=jnp.float32) + bias_ref[...]
    grad_hidden = lanes_dot(grad, outer)
    square = pre * pre
    bend = jnp.tanh(GELU_SCALE * (pre * (1.0 + 0.044715 * square)))
    rise = 0.5 * (1.0 + bend)
    hidden = low(pre * rise)
    slope = rise + (0.5 * pre) * (1.0 - bend * bend) * (GELU_SCALE * (1.0 + 0.134145 * square))
    grad_pre = low(slope * grad_hidden)
    out_acc[...] += jnp.dot(hidden, outer, preferred_element_type=jnp.float32)
    outer_grad_ref[...] = low(rows_dot(hidden, grad))
    back_acc[...] += lanes_dot(grad_pre, inner)
    inner_grad_ref[...] = low(rows_dot(mlp_ref[...], grad_pre))
    bias_grad_ref[...] = jnp.broadcast_to(
        jnp.sum(grad_pre.astype(jnp.float32), 0, keepdims=True), bias_grad_ref.shape
    )

    @pl.when(step == pl.num_programs(0) - 1)
    def _():
        for copy in late:
            copy.wait()

        @pl.loop(0, rows // BLOCK)
        def _(block):
            at = pl.multiple_of(block * BLOCK, BLOCK)
            sub = pl.ds(at, BLOCK)
            attended = attended_ref[sub, :]
            middle = residual_ref[sub, :] + line(2) * attended
            normed, inverse = normalize(middle)
            mlp_out = out_acc[sub, :] + line(9)
            out_ref[sub, :] = low(middle + line(5) * mlp_out)
            grad_block = grad_out(at)
            add_line(0, grad_block * mlp_out)
            back = back_acc[sub, :]
            add_line(1, back)
            add_line(2, back * normed)
            grad_middle = grad_block + norm_back(back * (1.0 + line(4)), normed, inverse)
            middle_ref[sub, :] = grad_middle
            add_line(3, grad_middle * attended)
            grad_attended = low(line(2) * grad_middle)
            add_line(4, grad_attended.astype(jnp.float32))
            grad_mlp[sub, :] = grad_attended

        proj_grad_ref[...] = low(rows_dot(mixed_ref[...], grad_mlp[...]))
        back_ref[...] = low(lanes_dot(grad_mlp[...], proj_ref[...]))


def feed_forward(mlp_in, inner, outer, vectors, inner_bias, residual, attended, cotangent, mixed, first, band_slots):
    rows, width = mlp_in.shape
    hidden = inner.shape[1]
    tile = 512
    bf, f32 = jnp.bfloat16, jnp.float32
    S = jax.ShapeDtypeStruct
    keep = lambda *shape: pl.BlockSpec(shape, lambda j: (0,) * len(shape))
    any_ = pl.BlockSpec(memory_space=pl.ANY)
    return pl.pallas_call(
        partial(mlp_kernel, band_slots),
        grid=(hidden // tile,),
        out_shape=[
            S((rows, width), bf), S((rows, width), f32), S((rows, width), bf), S((width, width), bf),
            S((hidden, width), bf), S((width, hidden), bf), S((8, hidden), f32), S((8, width), f32),
        ],
        in_specs=[
            keep(rows, width), pl.BlockSpec((width, tile), lambda j: (0, j)), pl.BlockSpec((tile, width), lambda j: (j, 0)),
            keep(16, width), pl.BlockSpec((1, tile), lambda j: (0, j)), any_, any_, keep(rows, width), any_, any_,
        ],
        out_specs=[
            keep(rows, width), keep(rows, width), keep(rows, width), keep(width, width),
            pl.BlockSpec((tile, width), lambda j: (j, 0)), pl.BlockSpec((width, tile), lambda j: (0, j)),
            pl.BlockSpec((8, tile), lambda j: (0, j)), keep(8, width),
        ],
        scratch_shapes=[
            pltpu.VMEM((rows, width), f32), pltpu.VMEM((rows, width), f32), pltpu.VMEM((rows, width), bf),
            pltpu.VMEM((rows, width), f32), pltpu.VMEM((rows, width), f32), pltpu.VMEM((rows, width), bf),
            pltpu.VMEM((width, width), bf), pltpu.SemaphoreType.DMA((4,)),
        ],
        compiler_params=pltpu.CompilerParams(vmem_limit_bytes=60 * 2**20),
        cost_estimate=pl.CostEstimate(
            flops=12 * rows * width * hidden, bytes_accessed=8 * width * hidden + 24 * rows * width,
            transcendentals=rows * hidden,
        ),
        name="feed_forward",
    )(mlp_in, inner, outer, vectors, inner_bias, residual, attended, cotangent, mixed, first)


def position_parts(width):
    quarter = width // 4
    frequency = 10000.0 ** (-np.arange(quarter, dtype=np.float32) / np.float32(quarter))
    angles = (np.arange(128, dtype=np.float32)[:, None] * frequency.astype(np.float32)).astype(np.float64)
    left = np.concatenate([np.sin(angles), np.cos(angles)], -1).astype(np.float32)
    parts = []
    for _ in range(3):
        parts.append(left.astype(jnp.bfloat16))
        left = left - parts[-1].astype(np.float32)
    return jnp.asarray(np.stack(parts))


def over_groups(piece, dp_count):
    if dp_count == 8:
        return piece
    groups = [[rank + 8 * group for group in range(dp_count // 8)] for rank in range(8)]
    return lax.psum(piece.astype(jnp.float32), "dp", axis_index_groups=groups)


def every_group(piece, dp_count):
    if dp_count == 8:
        return piece[None]
    groups = [[rank + 8 * group for group in range(dp_count // 8)] for rank in range(8)]
    return lax.all_gather(piece, "dp", axis_index_groups=groups)


def own_piece(vector, count, band_place):
    return lax.dynamic_slice_in_dim(vector, band_place * count, count, 0)


def body(
    tokens,
    condition,
    patch_grid,
    ada_weight,
    ada_bias,
    qkv_weight,
    query_bias,
    value_bias,
    proj_weight,
    proj_bias,
    inner_weight,
    inner_bias,
    outer_weight,
    outer_bias,
    cotangent,
):
    dp_count = lax.axis_size("dp")
    band_count = lax.axis_size("band")
    images, band_slots, width = tokens.shape
    band = lax.axis_index("band")
    dp = lax.axis_index("dp")
    core = lax.rem(dp, 2)
    hidden = inner_weight.shape[1]
    part_rows = qkv_weight.shape[0]

    condition_f = condition.astype(jnp.float32)
    activated = jax.nn.silu(condition_f).astype(jnp.bfloat16)
    own_activated = lax.dynamic_slice_in_dim(activated, band * part_rows, part_rows, 1)
    share = jnp.dot(own_activated, ada_weight, preferred_element_type=jnp.float32)
    share = share + lax.dynamic_update_slice_in_dim(
        jnp.zeros((ada_weight.shape[1],), jnp.float32),
        ada_bias.astype(jnp.float32),
        band * ada_bias.shape[0],
        0,
    )
    mod_count = share.shape[1]
    lines = lambda vector: jnp.pad(
        vector.astype(jnp.float32), [(0, 0)] * (vector.ndim - 1) + [(0, -vector.shape[-1] % 128)]
    )
    spread = lambda vector: jnp.broadcast_to(lines(vector), (images, -(-vector.shape[0] // 128) * 128))
    note = jnp.concatenate(
        [share, condition_f, lines(patch_grid)]
        + [spread(bias) for bias in (query_bias, value_bias, proj_bias, outer_bias, inner_bias)],
        1,
    )
    note = jnp.pad(note, ((0, 0), (0, -note.shape[1] % 1024))).reshape(images, -1, 128)
    first_weight = jnp.concatenate([qkv_weight, proj_weight], 1)
    (first_full, inner_full, outer_full, cotangent_here, vectors, residual, attn_in, query_rows, key_value,
     other_key_value, tops, mixed_rows, attended, mlp_in) = forward_block(
        first_weight, inner_weight, outer_weight, tokens, cotangent, note, position_parts(width)
    )
    first_full = first_full.reshape(width, -1)
    inner_full = inner_full.reshape(width, hidden)
    outer_full = outer_full.reshape(hidden, width)
    valid_count = vectors[15, :1].astype(jnp.int32)
    rows = images * band_slots
    inner_bias_row = vectors[10:14].reshape(1, -1)
    (block_out, grad_middle, grad_mixed, grad_proj, grad_outer, grad_inner, grad_inner_bias, sums) = feed_forward(
        mlp_in, inner_full, outer_full, vectors, inner_bias_row, residual, attended,
        cotangent_here.reshape(rows, width), mixed_rows, first_full, band_slots,
    )
    blocks = (band_count, 2, part_rows // 2, width)
    grad_outer = grad_outer.reshape(band_count, 4, 2, part_rows // 2, width)
    grad_inner = grad_inner.reshape(band_count, 2, part_rows // 2, hidden)
    outer_sum, inner_part, block_home, grad_query, own_terms, other_terms = reduce_attend(
        (FRONT | BACK, FRONT), [[grad_outer], [grad_inner]], [], block_out.reshape(images, band_slots, width), valid_count, query_rows, key_value, other_key_value, grad_mixed, tops,
        band_slots, 1,
    )
    inner_sum, first_sum, tokens_home, every, bias_grads, grad_act = reduce_last(
        grad_proj.reshape(blocks), inner_part, attn_in, grad_query, own_terms, other_terms, first_full, residual,
        grad_middle, vectors, sums, grad_inner_bias, ada_weight, images, band_slots, 2,
    )
    tokens_home = tokens_home.astype(jnp.float32)
    every = every_group(every, dp_count)
    bias_grads = over_groups(bias_grads, dp_count).reshape(-1)
    every = jnp.swapaxes(every, 1, 2).reshape(dp_count * images, -1)
    every_mod = every[:, :mod_count]
    every_condition = every[:, mod_count : mod_count + width]
    every_activated = jax.nn.silu(every_condition.astype(jnp.float32)).astype(jnp.bfloat16)
    every_activated = lax.dynamic_slice_in_dim(every_activated, band * part_rows, part_rows, 1)
    grad_ada = rows_dot(every_activated, every_mod)
    grad_ada_bias = own_piece(jnp.sum(every_mod.astype(jnp.float32), 0), ada_bias.shape[0], band)
    grad_act = jnp.swapaxes(grad_act[:, :images, :part_rows], 0, 1).reshape(images, width)
    grad_condition = jax.vjp(jax.nn.silu, condition_f)[1](grad_act)[0]

    def side_by_side(units):
        return jnp.concatenate([unit.reshape(part_rows, width) for unit in units], 1).astype(jnp.float32)

    first_sum, inner_sum, outer_sum = [
        over_groups(piece, dp_count) for piece in (first_sum, inner_sum, outer_sum)
    ]
    qkv_sum = side_by_side([first_sum[t] for t in range(3)])
    proj_sum = first_sum[3].reshape(part_rows, width).astype(jnp.float32)
    inner_sum = side_by_side([inner_sum[t] for t in range(4)])
    outer_sum = outer_sum.reshape(4 * part_rows, width).astype(jnp.float32)
    bias_parts = []
    at = 0
    for piece in (query_bias, value_bias, proj_bias, inner_bias, outer_bias):
        whole = piece.shape[0] * band_count
        bias_parts.append(own_piece(bias_grads[at : at + whole], piece.shape[0], band))
        at += whole
    return (
        block_home,
        tokens_home,
        grad_condition,
        grad_ada,
        grad_ada_bias,
        qkv_sum,
        bias_parts[0],
        bias_parts[1],
        proj_sum,
        bias_parts[2],
        inner_sum,
        bias_parts[3],
        outer_sum,
        bias_parts[4],
    )


def solution(mesh):
    placed = (
        P("dp", "band", None),
        P("dp", None),
        P("dp", None),
        P("band", None),
        P("band"),
        P("band", None),
        P("band"),
        P("band"),
        P("band", None),
        P("band"),
        P("band", None),
        P("band"),
        P("band", None),
        P("band"),
        P("dp", "band", None),
    )
    return jax.shard_map(
        body,
        mesh=mesh,
        in_specs=placed,
        out_specs=(
            P("dp", "band", None),
            P("dp", "band", None),
            P("dp", None),
            P("band", None),
            P("band"),
            P("band", None),
            P("band"),
            P("band"),
            P("band", None),
            P("band"),
            P("band", None),
            P("band"),
            P("band", None),
            P("band"),
        ),
        check_vma=False,
    )
```

```python
from functools import partial
from types import SimpleNamespace

import jax
import jax.numpy as jnp
import numpy as np
from jax import lax
from jax.experimental import pallas as pl
from jax.experimental.pallas import tpu as pltpu
from jax.sharding import PartitionSpec as P

HEAD_DIM = 72


MESH = pl.DeviceIdType.MESH
NB = 4


def device(dp, band):
    return {"dp": dp, "band": band}


def normalize(values):
    average = jnp.mean(values, -1, keepdims=True)
    centered = values - average
    variance = jnp.mean(centered * centered, -1, keepdims=True)
    inverse = lax.rsqrt(variance + 1e-06)
    return (centered * inverse, inverse)


def norm_back(grad_normed, normed, inverse):
    first = jnp.mean(grad_normed, -1, keepdims=True)
    second = jnp.mean(grad_normed * normed, -1, keepdims=True)
    return inverse * (grad_normed - first - normed * second)


LANES = 128
PACK_ROWS = 128


def pack_heads(source, first, heads_ref, row0, rows, tail):
    heads = heads_ref.shape[0]

    @pl.loop(0, rows // PACK_ROWS)
    def _(step):
        at = pl.multiple_of(step * PACK_ROWS, PACK_ROWS)
        block = source[pl.ds(at, PACK_ROWS), first : first + heads * HEAD_DIM]
        end = tail(at)
        for h in range(heads):
            part = block[:, h * HEAD_DIM : (h + 1) * HEAD_DIM]
            heads_ref[h, pl.ds(row0 + at, PACK_ROWS), :] = jnp.concatenate([part, end], 1)


def unpack_heads(heads_ref, row0, rows, target, first):
    heads = heads_ref.shape[0]

    @pl.loop(0, rows // PACK_ROWS)
    def _(step):
        at = pl.multiple_of(step * PACK_ROWS, PACK_ROWS)
        parts = [heads_ref[h, pl.ds(row0 + at, PACK_ROWS), :][:, :HEAD_DIM] for h in range(heads)]
        target[pl.ds(at, PACK_ROWS), first : first + heads * HEAD_DIM] = jnp.concatenate(parts, 1)


def flat_tail(value):
    def tail(at):
        lane = lax.broadcasted_iota(jnp.int32, (PACK_ROWS, LANES - HEAD_DIM), 1)
        return jnp.where(lane == 0, value, 0.0).astype(jnp.bfloat16)

    return tail


def key_tail(valid_count, band_slots):
    def tail(at):
        shape = (PACK_ROWS, LANES - HEAD_DIM)
        lane = lax.broadcasted_iota(jnp.int32, shape, 1)
        slot = lax.rem(at + lax.broadcasted_iota(jnp.int32, shape, 0), band_slots)
        return jnp.where(jnp.logical_and(lane == 0, slot >= valid_count), -1e30, 0.0).astype(jnp.bfloat16)

    return tail


def lanes_dot(left, right):
    return lax.dot_general(left, right, (((1,), (1,)), ((), ())), preferred_element_type=jnp.float32)


def rows_dot(left, right):
    return lax.dot_general(left, right, (((0,), (0,)), ((), ())), preferred_element_type=jnp.float32)


SCORE_SCALE = HEAD_DIM ** (-0.5)


def attend_block(h, qh, kh, vh, top_ref):
    rows = qh.shape[1]
    for block in range(2):
        at = pl.ds(block * rows // 2, rows // 2)
        scores = lanes_dot(kh[h], qh[h, at, :]) * SCORE_SCALE
        top = jnp.max(scores, 0, keepdims=True)
        weights = jnp.exp(scores - top)
        total = jnp.sum(weights, 0, keepdims=True)
        low = (weights * (1.0 / total)).astype(jnp.bfloat16)
        mixed = rows_dot(vh[h], low)
        qh[h, at, :] = jnp.transpose(mixed).astype(jnp.bfloat16)
        top_ref[h, :, at] = jnp.broadcast_to(top + jnp.log(total), (8, rows // 2))


def attend_head(h, qh, kh, vh, gh, top_ref):
    query = qh[h]
    key = kh[h]
    grad = gh[h]
    probs = jnp.exp(lanes_dot(key, query) * SCORE_SCALE - top_ref[h, 0:1, :])
    grad_probs = lanes_dot(vh[h], grad)
    inner = jnp.sum(probs * grad_probs, 0, keepdims=True)
    grad_scores = (probs * (grad_probs - inner)).astype(jnp.bfloat16)
    vh[h] = jnp.dot(
        probs.astype(jnp.bfloat16), grad, preferred_element_type=jnp.float32
    ).astype(jnp.bfloat16)
    grad_query = rows_dot(key, grad_scores)
    kh[h] = (
        SCORE_SCALE * jnp.dot(grad_scores, query, preferred_element_type=jnp.float32)
    ).astype(jnp.bfloat16)
    qh[h] = (SCORE_SCALE * jnp.transpose(grad_query)).astype(jnp.bfloat16)


def compass():
    dp = lax.axis_index("dp")
    band = lax.axis_index("band")
    core = lax.rem(dp, 2)
    px = lax.rem(dp // 2, 2)
    py = lax.rem(dp // 4, 2)
    return SimpleNamespace(
        dp=dp, band=band, core=core, px=px, py=py, kind=2 * py + px,
        sib=dp + 1 - 2 * core, xdp=dp + 2 - 4 * px, ydp=dp + 4 - 8 * py,
    )


def add_rows(total, term):
    rows = total.shape[0]

    @pl.loop(0, rows // 16)
    def _(step):
        at = pl.ds(pl.multiple_of(step * 16, 16), 16)
        total[at, :] = (
            total[at, :].astype(jnp.float32) + term[at, :].astype(jnp.float32)
        ).astype(jnp.bfloat16)


def run_all(batch):
    for do in batch:
        do()


REDUCE_ORDER = (1, 3, 2, 0)


FRONT, BACK = 1, 2


def reduce_scratch(plan, half, width):
    bf = jnp.bfloat16
    n = NB * sum(1 for todo in plan if todo & FRONT)
    m = len(plan)
    D = pltpu.SemaphoreType.DMA
    scratch = dict(
        recv_z=pltpu.VMEM((m, NB, half, width), bf), z_send=D((m, NB)), z_recv=D((m, NB)),
        d_send=D((m, 6)), d_recv=D((m, 6)), d_own=D((m,)), part_sem=D((m,)),
    )
    if n:
        scratch.update(
            acc=pltpu.VMEM((n, 4, half, width), bf), recv_a=pltpu.VMEM((n, 4, half, width), bf),
            recv_b=pltpu.VMEM((n, 2, half, width), bf), recv_c=pltpu.VMEM((n, half, width), bf),
            a_send=D((n,)), a_recv=D((n,)), a_own=D((n,)),
            b_send=D((n, 2, 2)), b_recv=D((n, 2, 2)), c_send=D((n, 2)), c_recv=D((n, 2)),
        )
    return scratch


def reduce_steps(me, plan, source, out, parts_in, parts_out, sc, beside=(), ahead=3, by_kind=False):
    dp, band, core, px, py, kind = me.dp, me.band, me.core, me.px, me.py, me.kind
    here = lambda d: device(d, band)
    fronts = [phase for phase, todo in enumerate(plan) if todo & FRONT]
    backs = [phase for phase, todo in enumerate(plan) if todo & BACK]
    chunks = [(phase, k) for phase in fronts for k in REDUCE_ORDER]
    n = len(chunks)
    flip = lambda v: 1 - v
    sends = []
    rows = sc.recv_z.shape[2]
    cut = rows // 32 * 16
    spans = (pl.ds(0, cut), pl.ds(cut, rows - cut))

    def remote(src, dst, ss, rs, to):
        return pltpu.make_async_remote_copy(
            src_ref=src, dst_ref=dst, send_sem=ss, recv_sem=rs, device_id=to, device_id_type=MESH
        )

    def go(make):
        make().start()
        sends.append(make)

    def target(k):
        return device(dp, lax.rem(band + k, NB))

    def start_a(s, kinds=range(4)):
        phase, k = chunks[s]
        b = lax.rem(band + k, NB)
        for t in kinds:
            remote(
                source(phase, b, t, flip(core)), sc.recv_a.at[s, t], sc.a_send.at[s], sc.a_recv.at[s],
                here(me.sib),
            ).start()
            pltpu.make_async_copy(source(phase, b, t, core), sc.acc.at[s, t], sc.a_own.at[s]).start()

    def first(half, j, send):
        if half == 0:
            return 2 * j + (flip(px) if send else px)
        return 2 * (flip(py) if send else py) + j

    def second(half, send):
        if half == 0:
            return 2 * (flip(py) if send else py) + px
        return 2 * py + (flip(px) if send else px)

    def near(half):
        return here(me.xdp if half == 0 else me.ydp)

    def send_b(s, half, j):
        return remote(
            sc.acc.at[s, first(half, j, True), spans[half]], sc.recv_b.at[s, j, spans[half]],
            sc.b_send.at[s, half, j], sc.b_recv.at[s, half, j], near(half),
        )

    def send_c(s, half):
        return remote(
            sc.acc.at[s, second(half, True), spans[half]], sc.recv_c.at[s, spans[half]],
            sc.c_send.at[s, half], sc.c_recv.at[s, half], near(1 - half),
        )

    def send_z(phase, k, src):
        return remote(src, sc.recv_z.at[phase, k], sc.z_send.at[phase, k], sc.z_recv.at[phase, k], target(k))

    def unit_z(s):
        phase, k = chunks[s]
        return send_z(phase, k, sc.acc.at[s, kind])

    def part_load(phase):
        return pltpu.make_async_copy(parts_in[phase], sc.recv_z.at[phase, 0], sc.part_sem.at[phase])

    def part_store(phase):
        return pltpu.make_async_copy(sc.recv_z.at[phase, 0], parts_out[phase], sc.part_sem.at[phase])

    def d_copy(phase, half, slot, mine):
        ss, rs = sc.d_send.at[phase, 3 * half + slot], sc.d_recv.at[phase, 3 * half + slot]
        span = spans[half]
        if slot == 0:
            src = sc.recv_z.at[phase, 0, span]
            return remote(src, out[phase].at[kind, core, span], ss, rs, near(half))
        j = slot - 1
        t = 2 * (py if mine else flip(py)) + j if half == 0 else 2 * j + (px if mine else flip(px))
        unit = out[phase].at[t, core, span]
        return remote(unit, unit, ss, rs, near(1 - half))

    def d_cross(phase, mine):
        row = out[phase].at[:, core if mine else flip(core)]
        return remote(row, row, sc.z_send.at[phase, 0], sc.z_recv.at[phase, 0], here(me.sib))

    def a_to_b(s):
        acc, got = sc.acc, sc.recv_a
        pltpu.make_async_copy(got.at[s], acc.at[s], sc.a_own.at[s]).wait()
        whole = remote(got.at[s], got.at[s], sc.a_send.at[s], sc.a_recv.at[s], here(me.sib))
        whole.wait_recv()
        for j in range(2):
            for half in range(2):
                t = first(half, j, True)
                add_rows(acc.at[s, t, spans[half]], got.at[s, t, spans[half]])
                go(partial(send_b, s, half, j))
        for j in range(2):
            for half in range(2):
                t = first(half, j, False)
                add_rows(acc.at[s, t, spans[half]], got.at[s, t, spans[half]])
        whole.wait_send()

    def b_to_c(s):
        acc, got = sc.acc, sc.recv_b
        for half in range(2):
            for j in range(2):
                send_b(s, half, j).wait_recv()
            away = flip(py) if half == 0 else flip(px)
            t = second(half, True)
            add_rows(acc.at[s, t, spans[half]], got.at[s, away, spans[half]])
            go(partial(send_c, s, half))
        for half in range(2):
            stay = py if half == 0 else px
            add_rows(acc.at[s, kind, spans[half]], got.at[s, stay, spans[half]])

    def c_to_z(s):
        phase, k = chunks[s]
        for half in range(2):
            send_c(s, half).wait_recv()
            add_rows(sc.acc.at[s, kind, spans[half]], sc.recv_c.at[s, spans[half]])
        if k != 0:
            go(partial(unit_z, s))

    def z_sum(phase):
        got = sc.recv_z
        for k in range(1, NB):
            remote(
                got.at[phase, k], got.at[phase, k], sc.z_send.at[phase, k], sc.z_recv.at[phase, k], here(dp)
            ).wait_recv()
        s = NB * fronts.index(phase) + NB - 1

        @pl.loop(0, rows // 16)
        def _(step):
            at = pl.ds(pl.multiple_of(step * 16, 16), 16)
            total = sc.acc[s, kind, at, :].astype(jnp.float32)
            for k in range(1, NB):
                total = total + got[phase, k, at, :].astype(jnp.float32)
            got[phase, 0, at, :] = total.astype(jnp.bfloat16)

        if not plan[phase] & BACK:
            part_store(phase).start()

    def d_first(phase):
        if not plan[phase] & FRONT:
            part_load(phase).wait()
        own_copy = pltpu.make_async_copy(sc.recv_z.at[phase, 0], out[phase].at[kind, core], sc.d_own.at[phase])
        own_copy.start()
        for half in range(2):
            go(partial(d_copy, phase, half, 0, True))
        own_copy.wait()

    def d_second(phase):
        for half in range(2):
            d_copy(phase, half, 0, False).wait_recv()
            for slot in (1, 2):
                go(partial(d_copy, phase, half, slot, True))

    def d_third(phase):
        for half in range(2):
            for slot in (1, 2):
                d_copy(phase, half, slot, False).wait_recv()
        go(partial(d_cross, phase, True))

    def d_last(phase):
        d_cross(phase, False).wait_recv()

    def finish():
        for phase in fronts:
            if not plan[phase] & BACK:
                part_store(phase).wait()
        for make in sends:
            make().wait_send()

    table = {-1: [] if by_kind else [partial(start_a, s) for s in range(n)]}

    def put(at, do):
        table.setdefault(at, []).append(do)

    for phase in backs:
        if not plan[phase] & FRONT:
            put(-1, lambda phase=phase: part_load(phase).start())
    for at, do in enumerate(beside):
        put(at, do)
    for s in range(n):
        put(s + ahead, partial(b_to_c, s))
        put(s + ahead + 1, partial(c_to_z, s))
        put(s, partial(a_to_b, s))
    for phase, todo in enumerate(plan):
        end = 0
        if todo & FRONT:
            end = NB * fronts.index(phase) + NB + ahead + 1
            put(end, partial(z_sum, phase))
        if todo & BACK:
            for lag, do in ((0, d_first), (1, d_second), (2, d_third), (4, d_last)):
                put(end + lag - (0 if todo & FRONT else 1), partial(do, phase))
    steps = [partial(run_all, table[at]) for at in sorted(table)]
    steps.append(finish)
    if by_kind:
        return SimpleNamespace(
            start=lambda kind: [start_a(s, (kind,)) for s in range(n)], a=a_to_b, b=b_to_c, c=c_to_z, sum=z_sum,
            take=lambda phase: part_load(phase).start(), d1=d_first, d2=d_second, d3=d_third, d4=d_last, finish=finish,
        )
    return steps


def home_scratch():
    D = pltpu.SemaphoreType.DMA
    return dict(home_send=D((2,)), home_recv=D((2,)))


def home_steps(me, rows_ref, home_ref, sc):
    band, core = me.band, me.core
    slot = lax.rem(band, 2)

    def stays(s):
        return jnp.logical_and(band // 2 == core, 2 * core + s == band)

    def copy(s):
        to = device(me.dp - core + band // 2, 2 * core + s)
        return pltpu.make_async_remote_copy(
            src_ref=rows_ref.at[s], dst_ref=home_ref.at[slot], send_sem=sc.home_send.at[s],
            recv_sem=sc.home_recv.at[slot], device_id=to, device_id_type=MESH,
        )

    def begin():
        for s in range(2):
            pl.when(stays(s))(
                lambda: pltpu.make_async_copy(
                    rows_ref.at[s], home_ref.at[slot], sc.home_recv.at[slot]
                ).start()
            )
            pl.when(jnp.logical_not(stays(s)))(lambda: copy(s).start())

    def finish():
        for s in range(2):
            pl.when(jnp.logical_not(stays(s)))(lambda: copy(s).wait_send())
        for i in range(2):
            pltpu.make_async_copy(rows_ref.at[i], home_ref.at[i], sc.home_recv.at[i]).wait()

    return begin, finish


def group_barrier(me):
    barrier = pltpu.get_barrier_semaphore()
    peers = [(me.xdp, me.band), (me.ydp, me.band), (me.sib, me.band)]
    for k in range(1, NB):
        other = lax.rem(me.band + k, NB)
        peers += [(me.dp, other), (me.sib, other)]
    for dp, band in peers:
        pl.semaphore_signal(
            barrier, inc=1, device_id=device(dp, band), device_id_type=MESH
        )
    pl.semaphore_wait(barrier, len(peers))


def reduce_refs(plan, counts, refs):
    take = iter(refs)
    grads = [[next(take) for _ in range(count)] for count in counts]

    def source(phase, b, t, h):
        if len(grads[phase]) > 1:
            return grads[phase][t].at[b, h]
        whole = grads[phase][0]
        if len(whole.shape) == 5:
            return whole.at[b, t, h]
        span = whole.shape[3] // 4
        return whole.at[b, h, :, pl.ds(pl.multiple_of(t * span, 128), span)]

    return source, [next(take) if todo == BACK else None for todo in plan]


def reduce_outs(plan, refs):
    take = iter(refs)
    out = [next(take) if todo & BACK else None for todo in plan]
    return out, [next(take) if todo == FRONT else None for todo in plan]


def reduce_shapes(plan, half, width):
    bf = jnp.bfloat16
    shapes = [jax.ShapeDtypeStruct((4, 2, half, width), bf) for todo in plan if todo & BACK]
    return shapes + [jax.ShapeDtypeStruct((half, width), bf) for todo in plan if todo == FRONT]


def small_scratch(mod_rows, bias_rows, cond_rows, cond_cols):
    D = pltpu.SemaphoreType.DMA
    f32 = jnp.float32
    return dict(
        s_core=pltpu.VMEM((mod_rows + bias_rows, 128), f32),
        s_every=pltpu.VMEM((NB, 4, mod_rows, 128), jnp.bfloat16),
        s_bias=pltpu.VMEM((3, bias_rows, 128), f32),
        s_got=pltpu.VMEM((2 + NB, bias_rows, 128), f32),
        s_flat=pltpu.VMEM((8, mod_rows, 128), f32),
        s_cond=pltpu.VMEM((NB, cond_rows, cond_cols), f32),
        s_send=D((8,)), s_recv=D((8,)), sz_send=D((2, NB)), sz_recv=D((2, NB)),
        sc_send=D((NB,)), sc_recv=D((NB,)),
    )


def small_steps(me, mods, images, small_ref, ada_ref, every_ref, bias_ref, cond_ref, sc):
    dp, band, core, px, py, kind = me.dp, me.band, me.core, me.px, me.py, me.kind
    here = lambda d: device(d, band)
    every, bias, got, cond = sc.s_every, sc.s_bias, sc.s_got, sc.s_cond
    mod_rows = every.shape[2]
    flip = lambda v: 1 - v

    def remote(src, dst, ss, rs, to):
        return pltpu.make_async_remote_copy(
            src_ref=src, dst_ref=dst, send_sem=ss, recv_sem=rs, device_id=to, device_id_type=MESH
        )

    def plain(index, src, dst, to):
        return remote(src, dst, sc.s_send.at[index], sc.s_recv.at[index], to)

    def core_copy():
        return plain(0, small_ref, sc.s_core, here(me.sib))

    def x_copies(mine):
        unit = every.at[band, kind if mine else 2 * py + flip(px)]
        return [
            plain(1, unit, unit, here(me.xdp)),
            plain(2, bias.at[0], got.at[0], here(me.xdp)),
        ]

    def y_copies(mine):
        pair = every.at[band, pl.ds(2 * (py if mine else flip(py)), 2)]
        return [
            plain(3, pair, pair, here(me.ydp)),
            plain(4, bias.at[1], got.at[1], here(me.ydp)),
        ]

    def z_copies(k, mine):
        to = device(dp, lax.rem(band + k, NB))
        block = every.at[band if mine else lax.rem(band + NB - k, NB)]
        return [
            remote(block, block, sc.sz_send.at[0, k], sc.sz_recv.at[0, k], to),
            remote(bias.at[2], got.at[2 + k], sc.sz_send.at[1, k], sc.sz_recv.at[1, k], to),
        ]

    def cond_copy(k, mine):
        to = device(dp, lax.rem(band + k, NB))
        block = cond.at[band if mine else lax.rem(band + NB - k, NB)]
        return remote(block, block, sc.sc_send.at[k], sc.sc_recv.at[k], to)

    def begin():
        core_copy().start()

    def cores():
        core_copy().wait()
        total = small_ref[...] + sc.s_core[...]
        every[band, kind] = total[:mod_rows].astype(jnp.bfloat16)
        bias[0] = total[mod_rows:]
        for copy in x_copies(True):
            copy.start()

    def over_x():
        for copy in x_copies(True):
            copy.wait_send()
        for copy in x_copies(False):
            copy.wait_recv()
        bias[1] = bias[0] + got[0]
        for copy in y_copies(True):
            copy.start()

    def over_y():
        for copy in y_copies(True):
            copy.wait_send()
        for copy in y_copies(False):
            copy.wait_recv()
        bias[2] = bias[1] + got[1]
        for k in range(1, NB):
            for copy in z_copies(k, True):
                copy.start()

    def over_z():
        for k in range(1, NB):
            for copy in z_copies(k, True):
                copy.wait_send()
            for copy in z_copies(k, False):
                copy.wait_recv()
        bias_ref[...] = bias[2] + got[3] + got[4] + got[5]
        every_ref[...] = every[...]
        flat = sc.s_flat
        for i in range(images):
            flat[i] = every[images * core + i, kind].astype(jnp.float32)
        parts = mods // 128
        lead = flat.shape[0]
        total = jnp.zeros((lead, ada_ref.shape[0]), jnp.float32)
        for r in range(parts):
            left = jnp.concatenate(
                [flat[i, r : r + 1, :] for i in range(images)]
                + [jnp.zeros((lead - images, 128), jnp.float32)]
            ).astype(jnp.bfloat16)
            total = total + lanes_dot(left, ada_ref[:, r * 128 : (r + 1) * 128])
        pad = cond.shape[2] - total.shape[1]
        cond[band] = jnp.concatenate([total, jnp.zeros((lead, pad), jnp.float32)], 1)
        for k in range(1, NB):
            cond_copy(k, True).start()

    def conditions():
        for k in range(1, NB):
            cond_copy(k, True).wait_send()
            cond_copy(k, False).wait_recv()
        cond_ref[...] = cond[...]

    return [begin, cores, over_x, over_y, over_z, conditions]


def put_lines(ref, first, values):
    for i in range(values.shape[1] // 128):
        ref[first + i : first + i + 1, :] = values[:, i * 128 : (i + 1) * 128]


def reduce_last_kernel(plan, images, band_slots, names, *refs):
    me = compass()
    (proj_ref, part_ref, attn_hbm, query_hbm, own_hbm, other_hbm, first_hbm, residual_hbm, middle_hbm, vec_ref, sums_ref,
     inner_bias_ref, ada_hbm) = refs[:13]
    inner_out, first_out, home_ref, every_ref, bias_ref, cond_ref = refs[13:19]
    sc = SimpleNamespace(**dict(zip(names, refs[19:])))
    rows, width = sc.attn.shape
    lines = width // 128
    small = sc.small
    mod_rows = sc.s_every.shape[2]

    def source(phase, b, t, h):
        return proj_ref.at[b, h] if t == 3 else sc.grads.at[t, b, h]

    loads = [
        (attn_hbm, sc.attn), (query_hbm, sc.gqkv.at[:, pl.ds(0, width)]), (own_hbm, sc.gqkv.at[:, pl.ds(width, 2 * width)]),
        (other_hbm, sc.other), (first_hbm.at[:, pl.ds(0, 3 * width)], sc.first), (residual_hbm, sc.residual),
        (middle_hbm, sc.middle), (ada_hbm, sc.ada),
    ]

    def load(i):
        return pltpu.make_async_copy(*loads[i], sc.load_sem.at[i])

    for i in range(len(loads)):
        load(i).start()
    group_barrier(me)
    mods = MOD_BLOCKS * width
    exchange = small_steps(me, mods, images, small, sc.ada, every_ref, bias_ref, cond_ref, sc)
    depart, settle = home_steps(me, sc.tokens, home_ref, sc)
    r = reduce_steps(me, plan, source, (inner_out, first_out), (part_ref, None), (None, None), sc, (), 2, True)

    def run(*todo):
        for do, index in todo:
            do(index)

    run((r.start, 3), (r.take, 0), (r.d1, 0))
    for i in range(4):
        load(i).wait()

    sc.sums[...] = jnp.zeros_like(sc.sums)

    def add_line(index, values):
        sc.sums[index : index + 1, :] += jnp.sum(values, 0, keepdims=True)

    @pl.loop(0, rows // BLOCK)
    def _(block):
        sub = pl.ds(pl.multiple_of(block * BLOCK, BLOCK), BLOCK)
        total = sc.gqkv[sub, width:].astype(jnp.float32) + sc.other[sub, :].astype(jnp.float32)
        total = total.astype(jnp.bfloat16)
        sc.gqkv[sub, width:] = total
        add_line(1, total[:, width:].astype(jnp.float32))
        add_line(0, sc.gqkv[sub, :width].astype(jnp.float32))

    tile = width // 3
    load(4).wait()
    between = [(), ((r.d2, 0),), ()]
    for j in range(3):
        sc.back[:, j * tile : (j + 1) * tile] = lanes_dot(sc.gqkv[...], sc.first[j * tile : (j + 1) * tile, :])
        run(*between[j])
    load(5).wait()
    load(6).wait()
    load(7).wait()

    @pl.loop(0, rows // BLOCK)
    def _(block):
        at = pl.multiple_of(block * BLOCK, BLOCK)
        sub = pl.ds(at, BLOCK)
        normed, inverse = normalize(sc.residual[sub, :])
        back = sc.back[sub, :]
        add_line(2, back)
        add_line(3, back * normed)
        grad = sc.middle[sub, :] + norm_back(back * (1.0 + vec_ref[1:2, :]), normed, inverse)
        per_image = band_slots // BLOCK
        to = pl.ds(pl.multiple_of(lax.rem(block, per_image) * BLOCK, BLOCK), BLOCK)
        sc.tokens[block // per_image, to, :] = grad.astype(jnp.bfloat16)

    small[...] = jnp.zeros_like(small)
    kept = [sc.sums[2:3, :], sc.sums[3:4, :]] + [sums_ref[i : i + 1, :] for i in (3, 1, 2, 0)]
    for i, values in enumerate(kept + [0.5 * vec_ref[14:15, :]]):
        put_lines(small, i * lines, values)
    at = mod_rows
    for values in (sc.sums[0:1, :], sc.sums[1:2, :], sums_ref[4:5, :], inner_bias_ref[0:1, :], sums_ref[5:6, :]):
        put_lines(small, at, values)
        at += values.shape[1] // 128
    say = lambda i: exchange[i]()
    depart()
    run((r.d3, 0))
    for t in range(3):

        @pl.loop(0, 3)
        def _(j):
            at = pl.multiple_of(t * width + j * tile, 128)
            value = rows_dot(sc.attn[...], sc.gqkv[:, pl.ds(at, tile)]).astype(jnp.bfloat16)
            to = pl.ds(pl.multiple_of(j * tile, 128), tile)
            sc.grads[t, :, :, :, to] = value.reshape(sc.grads.shape[1:4] + (tile,))

        run((r.start, t), (say, t))

    run((r.a, 0), (r.a, 1), (say, 3), (r.b, 0), (r.a, 2), (r.b, 1), (r.c, 0), (r.a, 3), (r.b, 2), (r.c, 1), (r.b, 3), (r.c, 2))
    run((r.c, 3), (say, 4), (r.sum, 1), (r.d1, 1), (r.d2, 1), (r.d3, 1), (say, 5), (r.d4, 0), (r.d4, 1))
    settle()
    r.finish()


def reduce_last(proj, part, attn_in, query, own, other, first, residual, middle, vectors, sums, inner_bias, ada_weight,
                images, band_slots, collective_id):
    plan = (BACK, FRONT | BACK)
    half, width = proj.shape[-2:]
    rows = attn_in.shape[0]
    bf, f32 = jnp.bfloat16, jnp.float32
    V = pltpu.VMEM
    mod_rows = -(-(MOD_BLOCKS + 1) * width // 2048) * 16
    bias_rows = (4 * width + inner_bias.shape[1]) // 128
    cond_cols = -(-ada_weight.shape[0] // 128) * 128
    scratch = dict(
        **reduce_scratch(plan, half, width), **small_scratch(mod_rows, bias_rows, 8, cond_cols), **home_scratch(),
        attn=V((rows, width), bf), gqkv=V((rows, 3 * width), bf), other=V((rows, 2 * width), bf),
        first=V((width, 3 * width), bf), residual=V((rows, width), f32), middle=V((rows, width), f32),
        grads=V((3, NB, 2, half, width), bf), back=V((rows, width), f32), sums=V((8, width), f32),
        tokens=V((images, band_slots, width), bf), small=V((mod_rows + bias_rows, 128), f32),
        load_sem=pltpu.SemaphoreType.DMA((8,)), ada=V(ada_weight.shape, bf),
    )
    any_, vmem = pl.BlockSpec(memory_space=pl.ANY), pl.BlockSpec(memory_space=pltpu.VMEM)
    return pl.pallas_call(
        partial(reduce_last_kernel, plan, images, band_slots, tuple(scratch)),
        out_shape=reduce_shapes(plan, half, width)
        + [
            jax.ShapeDtypeStruct((images, band_slots, width), bf),
            jax.ShapeDtypeStruct((NB, 4, mod_rows, 128), bf),
            jax.ShapeDtypeStruct((bias_rows, 128), f32),
            jax.ShapeDtypeStruct((NB, 8, cond_cols), f32),
        ],
        in_specs=[any_] * 9 + [vmem] * 3 + [any_],
        out_specs=[any_] * 3 + [vmem] * 3,
        scratch_shapes=list(scratch.values()),
        compiler_params=pltpu.CompilerParams(
            collective_id=collective_id, has_side_effects=True, vmem_limit_bytes=62 * 2**20
        ),
        name="reduce_last",
    )(proj, part, attn_in, query, own, other, first, residual, middle, vectors, sums, inner_bias, ada_weight)


def reduce_attend_kernel(plan, counts, band_slots, names, *refs):
    me = compass()
    at = sum(counts) + sum(1 for todo in plan if todo == BACK)
    source, parts = reduce_refs(plan, counts, refs)
    rows_ref, count_ref, q_ref, own_ref, far_ref, grad_ref, top_ref = refs[at : at + 7]
    at += 7
    out, given = reduce_outs(plan, refs[at:])
    at += len(plan)
    home_ref, dq_ref, down_ref, dfar_ref = refs[at : at + 4]
    sc = SimpleNamespace(**dict(zip(names, refs[at + 4 :])))
    qh, kh, vh, gh, stage, stage_sem = sc.qh, sc.kh, sc.vh, sc.gh, sc.stage, sc.stage_sem
    rows, width = q_ref.shape
    heads = qh.shape[0]
    group_barrier(me)
    steps = reduce_steps(me, plan, source, out, parts, given, sc)
    depart, settle = home_steps(me, rows_ref, home_ref, sc)
    steps[0]()
    depart()
    keys, plain, ones = key_tail(count_ref[0], band_slots), flat_tail(0.0), flat_tail(1.0)
    loads = [(q_ref, 0, qh, 0, ones), (grad_ref, 0, gh, 0, plain)]
    for row0, ref in ((0, own_ref), (rows, far_ref)):
        loads += [(ref, 0, kh, row0, keys), (ref, width, vh, row0, plain)]

    def load(i):
        ref, column = loads[i][:2]
        return pltpu.make_async_copy(ref.at[:, pl.ds(column, width)], stage.at[i % 2], stage_sem.at[i % 2])

    load(0).start()
    for step in steps[1:4]:
        step()
    for i, (ref, column, heads_ref, row0, tail) in enumerate(loads):
        if i + 1 < len(loads):
            load(i + 1).start()
        load(i).wait()
        pack_heads(stage.at[i % 2], 0, heads_ref, row0, rows, tail)
    rest = steps[4:]
    inside = heads // 2

    @pl.loop(0, heads)
    def _(h):
        attend_head(h, qh, kh, vh, gh, top_ref)
        for i, step in enumerate(rest[:inside]):
            pl.when(h == 2 * i)(step)

    stores = [(qh, 0, dq_ref, 0)]
    for row0, ref in ((0, down_ref), (rows, dfar_ref)):
        stores += [(kh, row0, ref, 0), (vh, row0, ref, width)]

    def store(i):
        ref, column = stores[i][2:]
        target = ref.at[:, pl.ds(column, width)]
        if ref is not dfar_ref:
            return pltpu.make_async_copy(stage.at[i % 2], target, stage_sem.at[i % 2])
        return pltpu.make_async_remote_copy(
            src_ref=stage.at[i % 2], dst_ref=target, send_sem=sc.far_send.at[i % 2],
            recv_sem=sc.far_recv.at[i % 2], device_id=device(me.sib, me.band), device_id_type=MESH,
        )

    for i, (heads_ref, row0, ref, column) in enumerate(stores):
        if i >= 2:
            store(i - 2).wait()
        unpack_heads(heads_ref, row0, rows, stage.at[i % 2], 0)
        store(i).start()
    for i in (len(stores) - 2, len(stores) - 1):
        store(i).wait()
    for step in rest[inside:]:
        step()
    settle()


def reduce_attend(plan, grads, parts, rows_out, count, query, own, far, grad, top, band_slots, collective_id):
    half, width = grads[0][0].shape[-2:]
    counts = tuple(len(phase) for phase in grads)
    rows = query.shape[0]
    heads = width // HEAD_DIM
    bf = jnp.bfloat16
    scratch = reduce_scratch(plan, half, width)
    scratch.update(
        qh=pltpu.VMEM((heads, rows, LANES), bf),
        kh=pltpu.VMEM((heads, 2 * rows, LANES), bf),
        vh=pltpu.VMEM((heads, 2 * rows, LANES), bf),
        gh=pltpu.VMEM((heads, rows, LANES), bf),
        stage=pltpu.VMEM((2, rows, width), bf),
        stage_sem=pltpu.SemaphoreType.DMA((2,)),
        far_send=pltpu.SemaphoreType.DMA((2,)),
        far_recv=pltpu.SemaphoreType.DMA((2,)),
        **home_scratch(),
    )
    any_, vmem = pl.BlockSpec(memory_space=pl.ANY), pl.BlockSpec(memory_space=pltpu.VMEM)
    smem = pl.BlockSpec(memory_space=pltpu.SMEM)
    units = [unit for phase in grads for unit in phase]
    return pl.pallas_call(
        partial(reduce_attend_kernel, plan, counts, band_slots, tuple(scratch)),
        out_shape=reduce_shapes(plan, half, width)
        + [
            jax.ShapeDtypeStruct(rows_out.shape, bf),
            jax.ShapeDtypeStruct((rows, width), bf),
            jax.ShapeDtypeStruct((rows, 2 * width), bf),
            jax.ShapeDtypeStruct((rows, 2 * width), bf),
        ],
        in_specs=[any_] * (len(units) + len(parts) + 1) + [smem] + [any_] * 4 + [vmem],
        out_specs=[any_] * (len(plan) + 4),
        scratch_shapes=list(scratch.values()),
        compiler_params=pltpu.CompilerParams(
            collective_id=collective_id, has_side_effects=True, vmem_limit_bytes=60 * 2**20
        ),
        name="reduce_attend",
    )(*units, *parts, rows_out, count, query, own, far, grad, top)


MOD_BLOCKS = 6
BLOCK = 128


def forward_scratch(half, ff, width, rows, note_rows, images):
    bf, f32 = jnp.bfloat16, jnp.float32
    D = pltpu.SemaphoreType.DMA
    heads = width // HEAD_DIM
    V = pltpu.VMEM
    return dict(
        qp=V((NB, 2, half, ff), bf), bounce_i=V((2, half, ff), bf), bounce_o=V((4, 2, half, width), bf),
        bounce_t=V((rows // images, width), bf), tok=V((images, rows // images, width), bf),
        notes=V((NB, note_rows, 128), f32), vec=V((16, width), f32),
        residual=V((rows, width), f32), attn_in=V((rows, width), bf), query=V((rows, width), bf),
        own=V((rows, 2 * width), bf), far=V((rows, 2 * width), bf), mixed=V((rows, width), bf),
        attended=V((rows, width), f32), mlp_in=V((rows, width), bf), tops=V((heads, 8, rows), f32),
        qh=V((heads, rows, LANES), bf), kh=V((heads, 2 * rows, LANES), bf), vh=V((heads, 2 * rows, LANES), bf),
        z_send=D((3, 2)), z_recv=D((3, NB)), f_send=D((3, NB)), a_send=D((9, 2)), a_recv=D((9, 2)), b_send=D((9, 2, 2)), b_recv=D((9, 2, 2)),
        c_send=D((9,)), c_recv=D((9,)), t_send=D((2, 2)), t_recv=D((2, 2)), m_send=D((2, 2)), m_recv=D((NB,)),
        local=D((4,)), kv_send=D((1,)), kv_recv=D((1,)), done=D((12,)),
    )


def gather_steps(me, width, ins, outs, tok_in, tok_out, cot_in, cot_out, note_in, note_out, sc):
    dp, band, core, px, py, kind = me.dp, me.band, me.core, me.px, me.py, me.kind
    base = dp - core
    dev = lambda d, b: device(d, b)
    here = lambda d: dev(d, band)
    flip = lambda v: 1 - v
    low = band < 2
    bands = (band + 1 - 2 * lax.rem(band, 2), jnp.where(low, 2, 1), jnp.where(low, 3, 0))
    order = [(ph, b) for ph in range(3) for b in bands]
    inside = jnp.logical_or(band == 1, band == 2)
    sends = []

    def remote(src, dst, ss, rs, to):
        return pltpu.make_async_remote_copy(
            src_ref=src, dst_ref=dst, send_sem=ss, recv_sem=rs, device_id=to, device_id_type=MESH
        )

    def go(make):
        for copy in make():
            copy.start()
        sends.append(make)

    size = ins[0].shape[1]
    cut = size // 32 * 16
    whole, spans = pl.ds(0, size), (pl.ds(0, cut), pl.ds(cut, size - cut))

    def cols(t, n=1):
        return pl.ds(pl.multiple_of(t * width, 128), n * width)

    def unit(ph, b, t, h, span=whole):
        return outs[ph].at[b, t, h, span] if ph == 2 else outs[ph].at[b, h, span, cols(t)]

    def pair(ph, b, h, y, span):
        return outs[ph].at[b, pl.ds(2 * y, 2), h, span] if ph == 2 else outs[ph].at[b, h, span, cols(2 * y, 2)]

    def row(ph, b, h):
        return outs[ph].at[b, :, h] if ph == 2 else outs[ph].at[b, h]

    def own_z(ph, up):
        src = ins[ph].at[kind, core] if ph == 2 else ins[ph].at[core, :, cols(kind)]
        return remote(
            src, unit(ph, band, kind, core), sc.z_send.at[ph, up], sc.z_recv.at[ph, band],
            dev(dp, band - 1 + 2 * up),
        )

    def pass_z(s):
        ph, b = order[s]
        u = unit(ph, b, kind, core)
        return remote(
            u, u, sc.f_send.at[ph, b], sc.z_recv.at[ph, b], dev(dp, jnp.where(b < band, band + 1, band - 1))
        )

    def a_copy(s, half, mine):
        ph, b = order[s]
        near = 2 * py + flip(px) if half == 0 else 2 * flip(py) + px
        u = unit(ph, b, kind if mine else near, core, spans[half])
        return remote(u, u, sc.a_send.at[s, half], sc.a_recv.at[s, half], here(me.xdp if half == 0 else me.ydp))

    def b_copies(s, half, mine):
        ph, b = order[s]
        if half == 0:
            u = pair(ph, b, core, py if mine else flip(py), spans[half])
            return [remote(u, u, sc.b_send.at[s, half, 0], sc.b_recv.at[s, half, 0], here(me.ydp))]
        copies = []
        for j in range(2):
            u = unit(ph, b, 2 * j + (px if mine else flip(px)), core, spans[half])
            copies.append(remote(u, u, sc.b_send.at[s, half, j], sc.b_recv.at[s, half, j], here(me.xdp)))
        return copies

    def c_copy(s, mine):
        ph, b = order[s]
        u = row(ph, b, core if mine else flip(core))
        return remote(u, u, sc.c_send.at[s], sc.c_recv.at[s], here(me.sib))

    def z_start(ph):
        pl.when(band < NB - 1)(lambda: own_z(ph, 1).start())
        pl.when(band > 0)(lambda: own_z(ph, 0).start())

    def z_wait(s):
        ph, b = order[s]
        u = unit(ph, b, kind, core)
        remote(u, u, sc.f_send.at[ph, b], sc.z_recv.at[ph, b], here(dp)).wait_recv()
        pl.when(inside)(lambda: pass_z(s).start())
        for half in range(2):
            go(lambda half=half: [a_copy(s, half, True)])

    def a_wait(s):
        for half in range(2):
            a_copy(s, half, False).wait_recv()
            go(partial(b_copies, s, half, True))

    def b_wait(s):
        for half in range(2):
            for copy in b_copies(s, half, False):
                copy.wait_recv()
        go(lambda: [c_copy(s, True)])

    def c_wait(s):
        c_copy(s, False).wait_recv()

    slot = lax.rem(band, 2)

    def image_copy(which, src, dst, i):
        to = dev(base + band // 2, 2 * core + i)
        return remote(src.at[i], dst.at[slot], sc.t_send.at[which, i], sc.t_recv.at[which, slot], to)

    def at_home(i):
        return jnp.logical_and(band // 2 == core, 2 * core + i == band)

    def move(which, src, dst, bounce=None):
        for i in range(2):

            @pl.when(at_home(i))
            def _():
                if bounce is None:
                    pltpu.make_async_copy(src.at[i], dst.at[slot], sc.t_recv.at[which, slot]).start()
                else:
                    inward = pltpu.make_async_copy(src.at[i], bounce, sc.local.at[3])
                    inward.start()
                    inward.wait()
                    pltpu.make_async_copy(bounce, dst.at[slot], sc.t_recv.at[which, slot]).start()

            @pl.when(jnp.logical_not(at_home(i)))
            def _():
                image_copy(which, src, dst, i).start()

    def move_wait(which, src, dst):
        for i in range(2):

            @pl.when(jnp.logical_not(at_home(i)))
            def _():
                image_copy(which, src, dst, i).wait_send()

        for s in range(2):
            pltpu.make_async_copy(dst.at[s], dst.at[s], sc.t_recv.at[which, s]).wait()

    def note_copy(i, c):
        return remote(
            note_in.at[i], note_out.at[band], sc.m_send.at[i, c], sc.m_recv.at[band],
            dev(base + c, 2 * core + i),
        )

    def note_home(i, c):
        return jnp.logical_and(c == core, 2 * core + i == band)

    def begin():
        for i in range(2):
            for c in range(2):

                @pl.when(note_home(i, c))
                def _():
                    pltpu.make_async_copy(note_in.at[i], note_out.at[band], sc.m_recv.at[band]).start()

                @pl.when(jnp.logical_not(note_home(i, c)))
                def _():
                    note_copy(i, c).start()

        z_start(0)
        for ph, dst in enumerate((outs[0].at[band], sc.bounce_i, sc.bounce_o)):
            pltpu.make_async_copy(ins[ph], dst, sc.local.at[ph]).start()

    def arrived():
        for i in range(2):
            for c in range(2):

                @pl.when(jnp.logical_not(note_home(i, c)))
                def _():
                    note_copy(i, c).wait_send()

        for b in range(NB):
            pltpu.make_async_copy(note_in.at[0], note_out.at[b], sc.m_recv.at[b]).wait()
        move_wait(0, tok_in, tok_out)

    def place():
        for ph, dst in ((1, sc.bounce_i), (2, sc.bounce_o)):
            pltpu.make_async_copy(ins[ph], dst, sc.local.at[ph]).wait()
            pltpu.make_async_copy(dst, outs[ph].at[band], sc.local.at[ph]).start()

    def first_here():
        pltpu.make_async_copy(ins[0], outs[0].at[band], sc.local.at[0]).wait()

    def finish():
        for ph, src in ((1, sc.bounce_i), (2, sc.bounce_o)):
            pltpu.make_async_copy(src, outs[ph].at[band], sc.local.at[ph]).wait()
        move_wait(1, cot_in, cot_out)
        for ph in range(3):
            pl.when(band < NB - 1)(lambda: own_z(ph, 1).wait_send())
            pl.when(band > 0)(lambda: own_z(ph, 0).wait_send())
        for s in range(len(order)):
            pl.when(inside)(lambda: pass_z(s).wait_send())
        for make in sends:
            for copy in make():
                copy.wait_send()

    def images(which):
        if which == 0:
            move(0, tok_in, tok_out)
        else:
            move(1, cot_in, cot_out, sc.bounce_t)

    return SimpleNamespace(
        i=images, s=z_start,
        begin=begin, arrived=arrived, place=place, first_here=first_here, finish=finish,
        z=z_wait, a=a_wait, b=b_wait, c=c_wait,
    )


def forward_kernel(names, band_slots, *refs):
    me = compass()
    qp_in, inner_in, outer_in, tok_in, cot_in, note_in, table_ref = refs[:7]
    (qp_out, inner_out, outer_out, cot_out, vec_out, residual_out, attn_out, query_out, own_out, far_out,
     tops_out, mixed_out, attended_out, mlp_out) = refs[7:21]
    sc = SimpleNamespace(**dict(zip(names, refs[21:])))
    rows, width = sc.residual.shape
    heads = width // HEAD_DIM
    core = me.core
    qp, tok, notes, vec = sc.qp, sc.tok, sc.notes, sc.vec

    group_barrier(me)
    g = gather_steps(
        me, width, (qp_in, inner_in, outer_in), (qp, inner_out, outer_out), tok_in, tok, cot_in, cot_out,
        note_in, notes, sc,
    )
    saves = []

    def save(src, dst):
        copy = pltpu.make_async_copy(src, dst, sc.done.at[len(saves)])
        copy.start()
        saves.append(copy)

    def run(*words):
        for do, index in words:
            do(index)

    g.begin()
    g.place()
    run((g.z, 0), (g.z, 1), (g.i, 0), (g.a, 0), (g.a, 1), (g.z, 2), (g.s, 1), (g.b, 0), (g.b, 1), (g.a, 2), (g.z, 3), (g.c, 0), (g.c, 1), (g.z, 4), (g.b, 2), (g.a, 3))
    g.arrived()
    spread_notes(notes, vec, width)
    grid_rows = notes[0, 63:64, 0:1]
    grid_cols = notes[0, 63:64, 1:2]
    band_rows = jnp.floor(grid_rows * 0.25)
    valid_count = (band_rows * grid_cols).astype(jnp.int32)
    lane = lax.broadcasted_iota(jnp.int32, (1, width), 1)
    vec[15:16, :] = jnp.where(lane == 0, band_rows * grid_cols, 0.0)
    save(vec, vec_out)

    @pl.loop(0, rows // BLOCK)
    def _(step):
        at = pl.multiple_of(step * BLOCK, BLOCK)
        sub = pl.ds(at, BLOCK)
        per_image = band_slots // BLOCK
        within = (
            lax.rem(step, per_image) * BLOCK + lax.broadcasted_iota(jnp.int32, (BLOCK, 1), 0)
        ).astype(jnp.float32)
        down = jnp.floor((within + 0.5) / grid_cols)
        place = (2 * core + step // per_image).astype(jnp.float32)
        picks = []
        for index in (place * band_rows + down, within - down * grid_cols):
            lanes = lax.broadcasted_iota(jnp.int32, (BLOCK, 128), 1).astype(jnp.float32)
            pick = jnp.where(lanes == index, 1.0, 0.0).astype(jnp.bfloat16)
            part = [jnp.dot(pick, table_ref[i], preferred_element_type=jnp.float32) for i in range(3)]
            picks.append(part[0] + (part[1] + part[2]))
        token = tok[step // per_image, pl.ds(lax.rem(step, per_image) * BLOCK, BLOCK), :]
        residual = token.astype(jnp.float32) + jnp.concatenate(picks, 1)
        sc.residual[sub, :] = residual
        normed = normalize(residual)[0]
        sc.attn_in[sub, :] = (normed * (1.0 + vec[1:2, :]) + vec[0:1, :]).astype(jnp.bfloat16)

    save(sc.residual, residual_out)
    save(sc.attn_in, attn_out)
    g.first_here()
    run((g.c, 2))
    save(qp, qp_out)
    tile = width // 3
    full = NB * 2 * qp.shape[2]

    def product(left_ref, first, step):
        at = pl.ds(pl.multiple_of(first + step * tile, 128), tile)
        return jnp.dot(
            left_ref[...], qp[:, :, :, at].reshape(full, tile), preferred_element_type=jnp.float32
        )

    def here(step):
        return pl.ds(pl.multiple_of(step * tile, 128), tile)

    @pl.loop(0, 3)
    def _(step):
        sc.own[:, here(step)] = product(sc.attn_in, width, step).astype(jnp.bfloat16)

    run((g.z, 5), (g.s, 2))

    @pl.loop(0, 3)
    def _(step):
        value = product(sc.attn_in, 2 * width, step) + vec[7:8, here(step)]
        sc.own[:, here(step + 3)] = value.astype(jnp.bfloat16)

    swap = pltpu.make_async_remote_copy(
        src_ref=sc.own, dst_ref=sc.far, send_sem=sc.kv_send.at[0], recv_sem=sc.kv_recv.at[0],
        device_id=device(me.sib, me.band), device_id_type=MESH,
    )
    swap.start()
    run((g.a, 4), (g.b, 3))

    @pl.loop(0, 3)
    def _(step):
        value = product(sc.attn_in, 0, step) + vec[6:7, here(step)]
        sc.query[:, here(step)] = value.astype(jnp.bfloat16)

    save(sc.query, query_out)
    save(sc.own, own_out)
    run((g.a, 5), (g.b, 4), (g.c, 3), (g.z, 6))
    qh, kh, vh = sc.qh, sc.kh, sc.vh
    keys, plain = key_tail(valid_count, band_slots), flat_tail(0.0)
    pack_heads(sc.query, 0, qh, 0, rows, flat_tail(1.0))
    pack_heads(sc.own, 0, kh, 0, rows, keys)
    pack_heads(sc.own, width, vh, 0, rows, plain)
    swap.wait()
    save(sc.far, far_out)
    pack_heads(sc.far, 0, kh, rows, rows, keys)
    pack_heads(sc.far, width, vh, rows, rows, plain)
    beside = {
        0: ((g.z, 7), (g.b, 5), (g.c, 4)), 2: ((g.a, 6), (g.z, 8), (g.i, 1)), 4: ((g.a, 7), (g.b, 6), (g.c, 5)), 7: ((g.a, 8), (g.b, 7), (g.c, 6)), 10: ((g.b, 8), (g.c, 7)),
        13: ((g.c, 8),),
    }

    @pl.loop(0, heads)
    def _(h):
        attend_block(h, qh, kh, vh, sc.tops)
        for i, words in beside.items():
            pl.when(h == i)(partial(run, *words))

    unpack_heads(qh, 0, rows, sc.mixed, 0)
    save(sc.tops, tops_out)
    save(sc.mixed, mixed_out)

    @pl.loop(0, 3)
    def _(step):
        sc.attended[:, here(step)] = product(sc.mixed, 3 * width, step) + vec[8:9, here(step)]

    save(sc.attended, attended_out)

    @pl.loop(0, rows // BLOCK)
    def _(step):
        sub = pl.ds(pl.multiple_of(step * BLOCK, BLOCK), BLOCK)
        middle = sc.residual[sub, :] + vec[2:3, :] * sc.attended[sub, :]
        normed = normalize(middle)[0]
        sc.mlp_in[sub, :] = (normed * (1.0 + vec[4:5, :]) + vec[3:4, :]).astype(jnp.bfloat16)

    save(sc.mlp_in, mlp_out)
    g.finish()
    for copy in saves:
        copy.wait()


NOTE_COND, NOTE_GRID, NOTE_BIAS = 54, 63, 64


def spread_notes(notes, vec, width):
    lines = width // 128
    share = notes.shape[0]
    total = notes[0, 0:NOTE_GRID, :] + 0.0
    for b in range(1, share):
        total = total + notes[b, 0:NOTE_GRID, :]

    def flat(block, first):
        return jnp.concatenate([block[first + i : first + i + 1, :] for i in range(lines)], 1)

    for index in range(MOD_BLOCKS):
        vec[index : index + 1, :] = flat(total, index * lines)
    small = width // share
    for index in range(4):
        parts = []
        for b in range(share):
            first = NOTE_BIAS + 3 * index
            for i in range(3):
                parts.append(notes[b, first + i : first + i + 1, : min(128, small - 128 * i)])
        vec[6 + index : 7 + index, :] = jnp.concatenate(parts, 1)
    for b in range(share):
        block = notes[b, NOTE_BIAS + 12 : NOTE_BIAS + 12 + lines, :]
        vec[10 + b : 11 + b, :] = flat(block, 0)
    vec[14:15, :] = flat(notes[0, NOTE_COND : NOTE_COND + lines, :], 0)


def forward_block(qp, inner, outer, tok, cot, note, table):
    half, ff = qp.shape[0] // 2, qp.shape[1]
    images, band_slots, width = tok.shape
    rows = images * band_slots
    heads = width // HEAD_DIM
    bf, f32 = jnp.bfloat16, jnp.float32
    S = jax.ShapeDtypeStruct
    qp, inner = qp.reshape(2, half, ff), inner.reshape(2, half, ff)
    outer = outer.reshape(4, 2, half, width)
    scratch = forward_scratch(half, ff, width, rows, note.shape[1], images)
    any_ = pl.BlockSpec(memory_space=pl.ANY)
    return pl.pallas_call(
        partial(forward_kernel, tuple(scratch), band_slots),
        out_shape=[
            S((NB, 2, half, ff), bf), S((NB, 2, half, ff), bf), S((NB, 4, 2, half, width), bf), S(cot.shape, bf),
            S((16, width), f32), S((rows, width), f32), S((rows, width), bf), S((rows, width), bf),
            S((rows, 2 * width), bf), S((rows, 2 * width), bf), S((heads, 8, rows), f32), S((rows, width), bf),
            S((rows, width), f32), S((rows, width), bf),
        ],
        in_specs=[any_] * 6 + [pl.BlockSpec(memory_space=pltpu.VMEM)],
        out_specs=[any_] * 14,
        scratch_shapes=list(scratch.values()),
        compiler_params=pltpu.CompilerParams(
            collective_id=0, has_side_effects=True, vmem_limit_bytes=60 * 2**20
        ),
        name="forward_block",
    )(qp, inner, outer, tok, cot, note, table)


GELU_SCALE = 0.7978845608028654


def mlp_kernel(band_slots, mlp_ref, inner_ref, outer_ref, vec_ref, bias_ref, residual_hbm, attended_hbm, cot_ref,
               mixed_hbm, first_hbm, out_ref, middle_ref, back_ref, proj_grad_ref, outer_grad_ref, inner_grad_ref,
               bias_grad_ref, sums_ref, out_acc, back_acc, grad_mlp, residual_ref, attended_ref, mixed_ref, proj_ref, late_sem):
    step = pl.program_id(0)
    rows = mlp_ref.shape[0]
    low = lambda value: value.astype(jnp.bfloat16)
    line = lambda index: vec_ref[index : index + 1, :]
    width = mlp_ref.shape[1]
    late = [
        pltpu.make_async_copy(src, dst, late_sem.at[i])
        for i, (src, dst) in enumerate(
            ((residual_hbm, residual_ref), (attended_hbm, attended_ref), (mixed_hbm, mixed_ref),
             (first_hbm.at[:, pl.ds(3 * width, width)], proj_ref))
        )
    ]

    def grad_out(at):
        slot = lax.rem(at + lax.broadcasted_iota(jnp.int32, (BLOCK, 1), 0), band_slots)
        valid = jnp.where(slot.astype(jnp.float32) < vec_ref[15:16, 0:1], 1.0, 0.0)
        return cot_ref[pl.ds(at, BLOCK), :].astype(jnp.float32) * valid

    def add_line(index, values):
        sums_ref[index : index + 1, :] += jnp.sum(values, 0, keepdims=True)

    @pl.when(step == 0)
    def _():
        sums_ref[...] = jnp.zeros_like(sums_ref)
        for copy in late:
            copy.start()

        @pl.loop(0, rows // BLOCK)
        def _(block):
            at = pl.multiple_of(block * BLOCK, BLOCK)
            grad = low(line(5) * grad_out(at))
            grad_mlp[pl.ds(at, BLOCK), :] = grad
            add_line(5, grad.astype(jnp.float32))
            out_acc[pl.ds(at, BLOCK), :] = jnp.zeros((BLOCK, out_acc.shape[1]), jnp.float32)
            back_acc[pl.ds(at, BLOCK), :] = jnp.zeros((BLOCK, out_acc.shape[1]), jnp.float32)

    inner, outer, grad = inner_ref[...], outer_ref[...], grad_mlp[...]
    pre = jnp.dot(mlp_ref[...], inner, preferred_element_type=jnp.float32) + bias_ref[...]
    grad_hidden = lanes_dot(grad, outer)
    square = pre * pre
    bend = jnp.tanh(GELU_SCALE * (pre * (1.0 + 0.044715 * square)))
    rise = 0.5 * (1.0 + bend)
    hidden = low(pre * rise)
    slope = rise + (0.5 * pre) * (1.0 - bend * bend) * (GELU_SCALE * (1.0 + 0.134145 * square))
    grad_pre = low(slope * grad_hidden)
    out_acc[...] += jnp.dot(hidden, outer, preferred_element_type=jnp.float32)
    outer_grad_ref[...] = low(rows_dot(hidden, grad))
    back_acc[...] += lanes_dot(grad_pre, inner)
    inner_grad_ref[...] = low(rows_dot(mlp_ref[...], grad_pre))
    bias_grad_ref[...] = jnp.broadcast_to(
        jnp.sum(grad_pre.astype(jnp.float32), 0, keepdims=True), bias_grad_ref.shape
    )

    @pl.when(step == pl.num_programs(0) - 1)
    def _():
        for copy in late:
            copy.wait()

        @pl.loop(0, rows // BLOCK)
        def _(block):
            at = pl.multiple_of(block * BLOCK, BLOCK)
            sub = pl.ds(at, BLOCK)
            attended = attended_ref[sub, :]
            middle = residual_ref[sub, :] + line(2) * attended
            normed, inverse = normalize(middle)
            mlp_out = out_acc[sub, :] + line(9)
            out_ref[sub, :] = low(middle + line(5) * mlp_out)
            grad_block = grad_out(at)
            add_line(0, grad_block * mlp_out)
            back = back_acc[sub, :]
            add_line(1, back)
            add_line(2, back * normed)
            grad_middle = grad_block + norm_back(back * (1.0 + line(4)), normed, inverse)
            middle_ref[sub, :] = grad_middle
            add_line(3, grad_middle * attended)
            grad_attended = low(line(2) * grad_middle)
            add_line(4, grad_attended.astype(jnp.float32))
            grad_mlp[sub, :] = grad_attended

        proj_grad_ref[...] = low(rows_dot(mixed_ref[...], grad_mlp[...]))
        back_ref[...] = low(lanes_dot(grad_mlp[...], proj_ref[...]))


def feed_forward(mlp_in, inner, outer, vectors, inner_bias, residual, attended, cotangent, mixed, first, band_slots):
    rows, width = mlp_in.shape
    hidden = inner.shape[1]
    tile = 512
    bf, f32 = jnp.bfloat16, jnp.float32
    S = jax.ShapeDtypeStruct
    keep = lambda *shape: pl.BlockSpec(shape, lambda j: (0,) * len(shape))
    any_ = pl.BlockSpec(memory_space=pl.ANY)
    return pl.pallas_call(
        partial(mlp_kernel, band_slots),
        grid=(hidden // tile,),
        out_shape=[
            S((rows, width), bf), S((rows, width), f32), S((rows, width), bf), S((width, width), bf),
            S((hidden, width), bf), S((width, hidden), bf), S((8, hidden), f32), S((8, width), f32),
        ],
        in_specs=[
            keep(rows, width), pl.BlockSpec((width, tile), lambda j: (0, j)), pl.BlockSpec((tile, width), lambda j: (j, 0)),
            keep(16, width), pl.BlockSpec((1, tile), lambda j: (0, j)), any_, any_, keep(rows, width), any_, any_,
        ],
        out_specs=[
            keep(rows, width), keep(rows, width), keep(rows, width), keep(width, width),
            pl.BlockSpec((tile, width), lambda j: (j, 0)), pl.BlockSpec((width, tile), lambda j: (0, j)),
            pl.BlockSpec((8, tile), lambda j: (0, j)), keep(8, width),
        ],
        scratch_shapes=[
            pltpu.VMEM((rows, width), f32), pltpu.VMEM((rows, width), f32), pltpu.VMEM((rows, width), bf),
            pltpu.VMEM((rows, width), f32), pltpu.VMEM((rows, width), f32), pltpu.VMEM((rows, width), bf),
            pltpu.VMEM((width, width), bf), pltpu.SemaphoreType.DMA((4,)),
        ],
        compiler_params=pltpu.CompilerParams(vmem_limit_bytes=60 * 2**20),
        cost_estimate=pl.CostEstimate(
            flops=12 * rows * width * hidden, bytes_accessed=8 * width * hidden + 24 * rows * width,
            transcendentals=rows * hidden,
        ),
        name="feed_forward",
    )(mlp_in, inner, outer, vectors, inner_bias, residual, attended, cotangent, mixed, first)


def position_parts(width):
    quarter = width // 4
    frequency = 10000.0 ** (-np.arange(quarter, dtype=np.float32) / np.float32(quarter))
    angles = (np.arange(128, dtype=np.float32)[:, None] * frequency.astype(np.float32)).astype(np.float64)
    left = np.concatenate([np.sin(angles), np.cos(angles)], -1).astype(np.float32)
    parts = []
    for _ in range(3):
        parts.append(left.astype(jnp.bfloat16))
        left = left - parts[-1].astype(np.float32)
    return jnp.asarray(np.stack(parts))


def over_groups(piece, dp_count):
    if dp_count == 8:
        return piece
    groups = [[rank + 8 * group for group in range(dp_count // 8)] for rank in range(8)]
    return lax.psum(piece.astype(jnp.float32), "dp", axis_index_groups=groups)


def every_group(piece, dp_count):
    if dp_count == 8:
        return piece[None]
    groups = [[rank + 8 * group for group in range(dp_count // 8)] for rank in range(8)]
    return lax.all_gather(piece, "dp", axis_index_groups=groups)


def own_piece(vector, count, band_place):
    return lax.dynamic_slice_in_dim(vector, band_place * count, count, 0)


def body(
    tokens,
    condition,
    patch_grid,
    ada_weight,
    ada_bias,
    qkv_weight,
    query_bias,
    value_bias,
    proj_weight,
    proj_bias,
    inner_weight,
    inner_bias,
    outer_weight,
    outer_bias,
    cotangent,
):
    dp_count = lax.axis_size("dp")
    band_count = lax.axis_size("band")
    images, band_slots, width = tokens.shape
    band = lax.axis_index("band")
    dp = lax.axis_index("dp")
    core = lax.rem(dp, 2)
    hidden = inner_weight.shape[1]
    part_rows = qkv_weight.shape[0]

    condition_f = condition.astype(jnp.float32)
    activated = jax.nn.silu(condition_f).astype(jnp.bfloat16)
    own_activated = lax.dynamic_slice_in_dim(activated, band * part_rows, part_rows, 1)
    share = jnp.dot(own_activated, ada_weight, preferred_element_type=jnp.float32)
    share = share + lax.dynamic_update_slice_in_dim(
        jnp.zeros((ada_weight.shape[1],), jnp.float32),
        ada_bias.astype(jnp.float32),
        band * ada_bias.shape[0],
        0,
    )
    mod_count = share.shape[1]
    lines = lambda vector: jnp.pad(
        vector.astype(jnp.float32), [(0, 0)] * (vector.ndim - 1) + [(0, -vector.shape[-1] % 128)]
    )
    spread = lambda vector: jnp.broadcast_to(lines(vector), (images, -(-vector.shape[0] // 128) * 128))
    note = jnp.concatenate(
        [share, condition_f, lines(patch_grid)]
        + [spread(bias) for bias in (query_bias, value_bias, proj_bias, outer_bias, inner_bias)],
        1,
    )
    note = jnp.pad(note, ((0, 0), (0, -note.shape[1] % 1024))).reshape(images, -1, 128)
    first_weight = jnp.concatenate([qkv_weight, proj_weight], 1)
    (first_full, inner_full, outer_full, cotangent_here, vectors, residual, attn_in, query_rows, key_value,
     other_key_value, tops, mixed_rows, attended, mlp_in) = forward_block(
        first_weight, inner_weight, outer_weight, tokens, cotangent, note, position_parts(width)
    )
    first_full = first_full.reshape(width, -1)
    inner_full = inner_full.reshape(width, hidden)
    outer_full = outer_full.reshape(hidden, width)
    valid_count = vectors[15, :1].astype(jnp.int32)
    rows = images * band_slots
    inner_bias_row = vectors[10:14].reshape(1, -1)
    (block_out, grad_middle, grad_mixed, grad_proj, grad_outer, grad_inner, grad_inner_bias, sums) = feed_forward(
        mlp_in, inner_full, outer_full, vectors, inner_bias_row, residual, attended,
        cotangent_here.reshape(rows, width), mixed_rows, first_full, band_slots,
    )
    blocks = (band_count, 2, part_rows // 2, width)
    grad_outer = grad_outer.reshape(band_count, 4, 2, part_rows // 2, width)
    grad_inner = grad_inner.reshape(band_count, 2, part_rows // 2, hidden)
    outer_sum, inner_part, block_home, grad_query, own_terms, other_terms = reduce_attend(
        (FRONT | BACK, FRONT), [[grad_outer], [grad_inner]], [], block_out.reshape(images, band_slots, width), valid_count, query_rows, key_value, other_key_value, grad_mixed, tops,
        band_slots, 1,
    )
    inner_sum, first_sum, tokens_home, every, bias_grads, grad_act = reduce_last(
        grad_proj.reshape(blocks), inner_part, attn_in, grad_query, own_terms, other_terms, first_full, residual,
        grad_middle, vectors, sums, grad_inner_bias, ada_weight, images, band_slots, 2,
    )
    tokens_home = tokens_home.astype(jnp.float32)
    every = every_group(every, dp_count)
    bias_grads = over_groups(bias_grads, dp_count).reshape(-1)
    every = jnp.swapaxes(every, 1, 2).reshape(dp_count * images, -1)
    every_mod = every[:, :mod_count]
    every_condition = every[:, mod_count : mod_count + width]
    every_activated = jax.nn.silu(every_condition.astype(jnp.float32)).astype(jnp.bfloat16)
    every_activated = lax.dynamic_slice_in_dim(every_activated, band * part_rows, part_rows, 1)
    grad_ada = rows_dot(every_activated, every_mod)
    grad_ada_bias = own_piece(jnp.sum(every_mod.astype(jnp.float32), 0), ada_bias.shape[0], band)
    grad_act = jnp.swapaxes(grad_act[:, :images, :part_rows], 0, 1).reshape(images, width)
    grad_condition = jax.vjp(jax.nn.silu, condition_f)[1](grad_act)[0]

    def side_by_side(units):
        return jnp.concatenate([unit.reshape(part_rows, width) for unit in units], 1).astype(jnp.float32)

    first_sum, inner_sum, outer_sum = [
        over_groups(piece, dp_count) for piece in (first_sum, inner_sum, outer_sum)
    ]
    qkv_sum = side_by_side([first_sum[t] for t in range(3)])
    proj_sum = first_sum[3].reshape(part_rows, width).astype(jnp.float32)
    inner_sum = side_by_side([inner_sum[t] for t in range(4)])
    outer_sum = outer_sum.reshape(4 * part_rows, width).astype(jnp.float32)
    bias_parts = []
    at = 0
    for piece in (query_bias, value_bias, proj_bias, inner_bias, outer_bias):
        whole = piece.shape[0] * band_count
        bias_parts.append(own_piece(bias_grads[at : at + whole], piece.shape[0], band))
        at += whole
    return (
        block_home,
        tokens_home,
        grad_condition,
        grad_ada,
        grad_ada_bias,
        qkv_sum,
        bias_parts[0],
        bias_parts[1],
        proj_sum,
        bias_parts[2],
        inner_sum,
        bias_parts[3],
        outer_sum,
        bias_parts[4],
    )


def solution(mesh):
    placed = (
        P("dp", "band", None),
        P("dp", None),
        P("dp", None),
        P("band", None),
        P("band"),
        P("band", None),
        P("band"),
        P("band"),
        P("band", None),
        P("band"),
        P("band", None),
        P("band"),
        P("band", None),
        P("band"),
        P("dp", "band", None),
    )
    return jax.shard_map(
        body,
        mesh=mesh,
        in_specs=placed,
        out_specs=(
            P("dp", "band", None),
            P("dp", "band", None),
            P("dp", None),
            P("band", None),
            P("band"),
            P("band", None),
            P("band"),
            P("band"),
            P("band", None),
            P("band"),
            P("band", None),
            P("band"),
            P("band", None),
            P("band"),
        ),
        check_vma=False,
    )
```
